32 devices in a mesh: head: 4 (over y, core), blk: 8 (over z, x).
Axes of the slice: x: 2, y: 2, z: 4, core: 2. Of those that a mesh axis runs over, the one named last changes fastest.
Arguments:
- tokens: bfloat16 [48, 512, 1024], P('blk', 'head'), may hold values from -6 to 6
- wq: bfloat16 [1024, 1024], P(('head', 'blk')), may hold values from -0.1875 to 0.1875
- wk: bfloat16 [1024, 1024], P(('head', 'blk')), may hold values from -0.1875 to 0.1875
- wv: bfloat16 [1024, 1024], P(('head', 'blk')), may hold values from -0.1875 to 0.1875
- wo: bfloat16 [1024, 1024], P(('head', 'blk')), may hold values from -0.75 to 0.75
- w_up: bfloat16 [1024, 4096], P(None, ('head', 'blk')), may hold values from -0.1875 to 0.1875
- w_down: bfloat16 [4096, 1024], P(('head', 'blk')), may hold values from -0.125 to 0.125
- gain_one: bfloat16 [1024], P(('head', 'blk')), may hold values from 0.5 to 1.5
- gain_two: bfloat16 [1024], P(('head', 'blk')), may hold values from 0.5 to 1.5
- w_comp: bfloat16 [3, 1024, 1024], P(None, ('head', 'blk')), may hold values from -0.109375 to 0.109375
- lengths: int32 [8], replicated, may hold values from 2 to 11, as said below
- grad_out: bfloat16 [48, 512, 1024], P('blk', 'head'), may hold values from -8 to 8
Outputs:
- out: bfloat16 [48, 512, 1024], P('blk', 'head')
- compressed: bfloat16 [48, 170, 1024], P('blk', None, 'head')
- grad_tokens: bfloat16 [48, 512, 1024], P('blk', 'head')
- grad_wq: float32 [1024, 1024], P(('head', 'blk'))
- grad_wk: float32 [1024, 1024], P(('head', 'blk'))
- grad_wv: float32 [1024, 1024], P(('head', 'blk'))
- grad_wo: float32 [1024, 1024], P(('head', 'blk'))
- grad_up: float32 [1024, 4096], P(None, ('head', 'blk'))
- grad_down: float32 [4096, 1024], P(('head', 'blk'))
- grad_gain_one: float32 [1024], P(('head', 'blk'))
- grad_gain_two: float32 [1024], P(('head', 'blk'))
- grad_comp: float32 [3, 1024, 1024], P(None, ('head', 'blk'))
The draws below stay inside these ranges and needn't reach their ends.
Inputs may be any that keep to these rules, and one draw needn't show every extreme that they name: lengths of the 8 sequences in segments of 512 tokens, taken in order; they sum to 48; the first is the longest with exactly 11; no sequence but the first begins at a segment index that is a multiple of 6.
All inputs are finite; a program needn't handle non-finite values.
Results may differ from the reference program's by a relative error of at most 0.018.
Values may be sent and summed in bfloat16 or wider, within the bound.
No kernel may reach another device: no remote copies, remote signals or barrier semaphores. Data moves between devices by JAX's collectives and lax.ppermute only.
A program may use at most 320 MiB of HBM per device.

```python
import jax
import jax.numpy as jnp
from jax import lax

D = 1024
HEADS = 8
HD = 128
FF = 4096
SEG = 512
RATE = 3
CSEGS = 3
SEG_DEV = 6
SEGS = 48
CROWS = 170
NSEQ = 8


def draw_lengths(key, part):
    offset_key = jax.random.fold_in(key, 5)
    offsets = jax.random.randint(offset_key, (NSEQ - 1,), 1, SEG_DEV, dtype=jnp.int32)
    index = jnp.arange(NSEQ - 1, dtype=jnp.int32)
    offsets = jnp.where(index == 0, SEG_DEV - 1, offsets)
    offsets = jnp.where(index == NSEQ - 2, 1, offsets)
    bounds = SEG_DEV * (index + 1) + offsets
    edges = jnp.concatenate([jnp.zeros((1,), jnp.int32), bounds, jnp.full((1,), SEGS, jnp.int32)])
    return (edges[1:] - edges[:-1]).astype(jnp.int32)


def draw_grad_out(key, part):
    noise_key = jax.random.fold_in(key, 11)
    common_key = jax.random.fold_in(key, 23)
    common = jax.random.normal(common_key, (SEGS, 1, D), jnp.float32)
    noise = jax.random.normal(noise_key, (SEGS, SEG, D), jnp.float32)
    return jnp.clip(noise + common, -8.0, 8.0).astype(jnp.bfloat16)


def levels(stream_key, shape, split, low, top_value):
    level = 1.0
    for position, parts in split:
        draws = jax.random.uniform(jax.random.fold_in(jax.random.fold_in(stream_key, 6), position), (parts,), jnp.float32, low / len(split), top_value / len(split))
        level = level * jnp.repeat(jnp.exp(draws), shape[position] // parts).reshape((-1,) + (1,) * (len(shape) - 1 - position))
    return level


def bell_draw(stream_key, shape, width, limit, split=(), kind=jnp.bfloat16):
    values = width * jax.random.normal(stream_key, shape, jnp.float32)
    if split:
        values = values * levels(stream_key, shape, split, -0.22, 0.18)
    return jnp.clip(values, -limit, limit).astype(kind)


def setup_inputs(seed: int = 0) -> dict:
    key_list = jax.random.split(jax.random.key(seed), 13)
    tokens = bell_draw(key_list[0], (SEGS, SEG, D), 1.0, 6.0, ((0, 8), (1, 4)))
    wq = bell_draw(key_list[1], (D, D), D ** -0.5, 0.1875, ((0, 32),))
    wk = bell_draw(key_list[2], (D, D), D ** -0.5, 0.1875, ((0, 32),))
    wv = bell_draw(key_list[3], (D, D), D ** -0.5, 0.1875, ((0, 32),))
    wo = bell_draw(key_list[4], (D, D), (D // 16) ** -0.5, 0.75, ((0, 32),))
    w_up = bell_draw(key_list[5], (D, FF), D ** -0.5, 0.1875, ((1, 32),))
    w_down = bell_draw(key_list[6], (FF, D), (FF // 2) ** -0.5, 0.125, ((0, 32),))
    gain_one = jnp.clip(1.0 + 0.1 * jax.random.normal(key_list[7], (D,), jnp.float32), 0.5, 1.5).astype(jnp.bfloat16)
    gain_two = jnp.clip(1.0 + 0.1 * jax.random.normal(key_list[8], (D,), jnp.float32), 0.5, 1.5).astype(jnp.bfloat16)
    w_comp = bell_draw(key_list[9], (RATE, D, D), (RATE * D) ** -0.5, 0.109375, ((1, 32),))
    lengths = draw_lengths(jax.random.fold_in(key_list[12], 71), 0)
    grad_out = draw_grad_out(jax.random.fold_in(key_list[12], 71), 0)
    return {"tokens": tokens, "wq": wq, "wk": wk, "wv": wv, "wo": wo, "w_up": w_up, "w_down": w_down, "gain_one": gain_one, "gain_two": gain_two, "w_comp": w_comp, "lengths": lengths, "grad_out": grad_out}


@jax.custom_vjp
def low(v):
    return lax.optimization_barrier(v.astype(jnp.bfloat16)).astype(jnp.float32)

@jax.custom_vjp
def low_back(v):
    return v

def low_keep(v):
    return (low(v), None)

def low_pass(kept, grad):
    return (grad,)

def back_keep(v):
    return (v, None)

def back_low(kept, grad):
    return (low(grad),)
low.defvjp(low_keep, low_pass)
low_back.defvjp(back_keep, back_low)
HIGH = lax.Precision.HIGHEST
EPS = 1e-05
NEG = -1e+30

def matmul(left, right):
    return jnp.dot(left, right, precision=HIGH, preferred_element_type=jnp.float32)

def layer_norm(values, gain):
    average = lax.optimization_barrier(jnp.mean(values, axis=-1, keepdims=True))
    center = values - average
    variance = lax.optimization_barrier(jnp.mean(center * center, axis=-1, keepdims=True))
    return center * lax.rsqrt(variance + EPS) * gain

def key_layout(seg_len, comp_rows, comp_segs, rate):
    groups = []
    places = []
    for lag in range(comp_segs + 1, 1, -1):
        groups.append(jnp.full((comp_rows,), lag, jnp.int32))
        places.append(rate * jnp.arange(comp_rows, dtype=jnp.int32) + rate // 2 - lag * seg_len)
    groups.append(jnp.full((seg_len,), 1, jnp.int32))
    places.append(jnp.arange(seg_len, dtype=jnp.int32) - seg_len)
    groups.append(jnp.zeros((seg_len,), jnp.int32))
    places.append(jnp.arange(seg_len, dtype=jnp.int32))
    return (jnp.concatenate(groups), jnp.concatenate(places))

def attend(args):
    query, mem_key, own_key, mem_value, own_value, comp_keys, comp_values, seg_place = args
    group, place = key_layout(SEG, CROWS, CSEGS, RATE)
    keys = jnp.concatenate([comp_keys.reshape(CSEGS * CROWS, D), mem_key, own_key], 0)
    values = jnp.concatenate([comp_values.reshape(CSEGS * CROWS, D), mem_value, own_value], 0)
    positions = jnp.arange(SEG, dtype=jnp.int32)
    allowed = (group[None, :] <= seg_place) & (place[None, :] <= positions[:, None])
    distance = (positions[:, None] - place[None, :]).astype(jnp.float32)
    slopes = jnp.exp2(-jnp.arange(HEADS).astype(jnp.float32)) / 64.0
    query_heads = query.reshape(SEG, HEADS, HD)
    key_heads = keys.reshape(-1, HEADS, HD)
    value_heads = values.reshape(-1, HEADS, HD)
    raw = jnp.einsum('qhd,khd->hqk', query_heads, key_heads, precision=HIGH)
    scores = low_back(raw * HD ** (-0.5) - slopes[:, None, None] * distance[None])
    scores = jnp.where(allowed[None], scores, NEG)
    row_top = lax.optimization_barrier(jnp.max(scores, axis=-1, keepdims=True))
    weights = jnp.exp(scores - row_top)
    probs = weights / lax.optimization_barrier(jnp.sum(weights, axis=-1, keepdims=True))
    result = jnp.einsum('hqk,khd->qhd', low(probs), value_heads, precision=HIGH)
    return result.reshape(SEG, D)

def forward(tokens, wq, wk, wv, wo, w_up, w_down, gain_one, gain_two, w_comp, seg_place):
    token_rows = tokens.reshape(SEGS * SEG, D)
    normed = low(layer_norm(token_rows, gain_one))
    sent = low_back(normed)
    query = low_back(low(matmul(normed, wq)))
    key = low_back(low(matmul(normed, wk)))
    value = low_back(low(matmul(normed, wv)))
    grouped = sent.reshape(SEGS, SEG, D)[:, :RATE * CROWS].reshape(SEGS * CROWS, RATE * D)
    packed = low_back(low(matmul(grouped, w_comp.reshape(RATE * D, D))))
    comp_key = low_back(low(matmul(packed, wk))).reshape(SEGS, CROWS, D)
    comp_value = low_back(low(matmul(packed, wv))).reshape(SEGS, CROWS, D)
    key_seg = key.reshape(SEGS, SEG, D)
    value_seg = value.reshape(SEGS, SEG, D)
    zero_seg = jnp.zeros((1, SEG, D), jnp.float32)
    mem_key = jnp.concatenate([zero_seg, key_seg[:-1]], 0)
    mem_value = jnp.concatenate([zero_seg, value_seg[:-1]], 0)
    zero_comp = jnp.zeros((CSEGS + 1, CROWS, D), jnp.float32)
    ext_key = jnp.concatenate([zero_comp, comp_key], 0)
    ext_value = jnp.concatenate([zero_comp, comp_value], 0)
    comp_keys = jnp.stack([ext_key[CSEGS + 1 - lag:CSEGS + 1 - lag + SEGS] for lag in range(CSEGS + 1, 1, -1)], 1)
    comp_values = jnp.stack([ext_value[CSEGS + 1 - lag:CSEGS + 1 - lag + SEGS] for lag in range(CSEGS + 1, 1, -1)], 1)
    attended = lax.map(jax.checkpoint(attend), (query.reshape(SEGS, SEG, D), mem_key, key_seg, mem_value, value_seg, comp_keys, comp_values, seg_place))
    mixed = low_back(low(attended.reshape(SEGS * SEG, D)))
    branch = low_back(matmul(mixed, wo))
    hidden = token_rows + branch
    normed_two = low(layer_norm(hidden, gain_two))
    lifted = low_back(matmul(normed_two, w_up))
    active = low(jax.nn.silu(lifted))
    result = hidden + matmul(active, w_down)
    return (result.reshape(SEGS, SEG, D), packed.reshape(SEGS, CROWS, D))

def reference(tokens, wq, wk, wv, wo, w_up, w_down, gain_one, gain_two, w_comp, lengths, grad_out):
    starts = (jnp.cumsum(lengths) - lengths).astype(jnp.int32)
    seg_index = jnp.arange(SEGS, dtype=jnp.int32)
    seg_place = seg_index - lax.optimization_barrier(jnp.max(jnp.where(starts[None, :] <= seg_index[:, None], starts[None, :], 0), axis=1)).astype(jnp.int32)
    floats = tuple((item.astype(jnp.float32) for item in (tokens, wq, wk, wv, wo, w_up, w_down, gain_one, gain_two, w_comp)))

    def forward_fn(*values):
        return forward(*values, seg_place)
    (result, packed), pullback = jax.vjp(forward_fn, *floats)
    gradients = pullback((grad_out.astype(jnp.float32), jnp.zeros_like(packed)))
    return (result.astype(jnp.bfloat16), packed.astype(jnp.bfloat16), gradients[0].astype(jnp.bfloat16), gradients[1], gradients[2], gradients[3], gradients[4], gradients[5], gradients[6], gradients[7], gradients[8], gradients[9])
```

```python
import jax
import jax.numpy as jnp
from jax import lax
from jax.sharding import PartitionSpec as P

HD = 128
RATE = 3
CSEGS = 3


EPS = 1e-05
NEG = -1e30
ROWS_IN = (((0,), (0,)), ((), ()))
COLS_IN = (((1,), (1,)), ((), ()))


def passed_along(value, axis, steps):
    count = lax.axis_size(axis)
    leading, last = (max(0, -steps), min(count, count - steps))
    return lax.ppermute(value, axis, [(source, source + steps) for source in range(leading, last)])


def layer_norm(values, gain):
    average = jnp.mean(values, axis=-1, keepdims=True)
    center = values - average
    variance = jnp.mean(center * center, axis=-1, keepdims=True)
    return center * lax.rsqrt(variance + EPS) * gain


def silu_slope(values):
    sig = jax.nn.sigmoid(values)
    return sig * (1.0 + values * (1.0 - sig))


def key_layout(seg_len, comp_rows, comp_segs, rate):
    groups = []
    places = []
    for lag in range(comp_segs + 1, 1, -1):
        groups.append(jnp.full((comp_rows,), lag, jnp.int32))
        places.append(rate * jnp.arange(comp_rows, dtype=jnp.int32) + rate // 2 - lag * seg_len)
    groups.append(jnp.full((seg_len,), 1, jnp.int32))
    places.append(jnp.arange(seg_len, dtype=jnp.int32) - seg_len)
    groups.append(jnp.zeros((seg_len,), jnp.int32))
    places.append(jnp.arange(seg_len, dtype=jnp.int32))
    return (jnp.concatenate(groups), jnp.concatenate(places))


def make_scores(query_heads, key_heads, group, place, seg_place, slopes):
    seg_len = query_heads.shape[0]
    positions = jnp.arange(seg_len, dtype=jnp.int32)
    allowed = (group[None, :] <= seg_place) & (place[None, :] <= positions[:, None])
    distance = (positions[:, None] - place[None, :]).astype(jnp.float32)
    raw = jnp.einsum("qhd,khd->hqk", query_heads, key_heads, preferred_element_type=jnp.float32)
    scores = raw * HD ** (-0.5) - slopes[:, None, None] * distance[None]
    return jnp.where(allowed[None], scores, NEG)


def per_device(tokens, wq, wk, wv, wo, w_up, w_down, gain_one, gain_two, w_comp, lengths, grad_out):
    seg_count, quarter, width = tokens.shape
    head_groups = lax.axis_size("head")
    seg_len = quarter * head_groups
    head_cols = width // head_groups
    local_heads = head_cols // HD
    comp_rows = seg_len // RATE
    window = CSEGS + 1
    head_index = lax.axis_index("head")
    blk_index = lax.axis_index("blk")
    col_start = head_index * head_cols
    token_count = seg_count * quarter
    gathered = (
        lax.all_gather(wq, ("head", "blk"), axis=0, tiled=True),
        lax.all_gather(wk, ("head", "blk"), axis=0, tiled=True),
        lax.all_gather(wv, ("head", "blk"), axis=0, tiled=True),
        lax.all_gather(wo, ("head", "blk"), axis=0, tiled=True),
        lax.all_gather(gain_one, ("head", "blk"), axis=0, tiled=True),
        lax.all_gather(gain_two, ("head", "blk"), axis=0, tiled=True),
    )
    wq_all, wk_all, wv_all, wo_all, gain_first, gain_second = gathered
    up_cols, down_rows, comp_part = (
        lax.all_gather(w_up, "blk", axis=1, tiled=True),
        lax.all_gather(w_down, "blk", axis=0, tiled=True),
        lax.all_gather(w_comp, "blk", axis=1, tiled=True),
    )
    comp_matrix = comp_part.reshape(RATE * head_cols, width)
    gain_first = gain_first.astype(jnp.float32)
    gain_second = gain_second.astype(jnp.float32)
    up_all, down_all = (
        lax.all_gather(up_cols, "head", axis=1, tiled=True),
        lax.all_gather(down_rows, "head", axis=0, tiled=True),
    )
    token_rows = tokens.reshape(token_count, width).astype(jnp.float32)
    normed = layer_norm(token_rows, gain_first).astype(jnp.bfloat16)
    query = jnp.dot(normed, wq_all, preferred_element_type=jnp.float32).astype(jnp.bfloat16)
    key = jnp.dot(normed, wk_all, preferred_element_type=jnp.float32).astype(jnp.bfloat16)
    value = jnp.dot(normed, wv_all, preferred_element_type=jnp.float32).astype(jnp.bfloat16)
    split_shape = (seg_count, quarter, head_groups, head_cols)
    heads_q, heads_k, heads_v, heads_x = (
        lax.all_to_all(query.reshape(split_shape), "head", split_axis=2, concat_axis=1, tiled=True),
        lax.all_to_all(key.reshape(split_shape), "head", split_axis=2, concat_axis=1, tiled=True),
        lax.all_to_all(value.reshape(split_shape), "head", split_axis=2, concat_axis=1, tiled=True),
        lax.all_to_all(
            normed.reshape(split_shape), "head", split_axis=2, concat_axis=1, tiled=True
        ),
    )
    local_shape = (seg_count, seg_len, head_cols)
    heads_q = heads_q.reshape(local_shape)
    heads_k = heads_k.reshape(local_shape)
    heads_v = heads_v.reshape(local_shape)
    heads_x = heads_x.reshape(local_shape)
    grouped = heads_x[:, : RATE * comp_rows].reshape(seg_count * comp_rows, RATE * head_cols)
    packed_part = jnp.dot(grouped, comp_matrix, preferred_element_type=jnp.float32)
    packed = lax.psum(packed_part.astype(jnp.bfloat16), "head")
    wk_mine = lax.dynamic_slice_in_dim(wk_all, col_start, head_cols, 1)
    wv_mine = lax.dynamic_slice_in_dim(wv_all, col_start, head_cols, 1)
    comp_key = jnp.dot(packed, wk_mine, preferred_element_type=jnp.float32).astype(jnp.bfloat16)
    comp_value = jnp.dot(packed, wv_mine, preferred_element_type=jnp.float32).astype(jnp.bfloat16)
    comp_pair = jnp.concatenate([comp_key, comp_value], 1).reshape(
        seg_count, comp_rows, 2 * head_cols
    )
    own_pair = jnp.concatenate([heads_k, heads_v], 2)
    recv_mem = jnp.zeros((1, seg_len, 2 * head_cols), jnp.bfloat16)
    recv_comp = jnp.zeros((window, comp_rows, 2 * head_cols), jnp.bfloat16)
    tail_mem = jnp.concatenate([recv_mem, own_pair], 0)[seg_count:]
    tail_comp = jnp.concatenate([recv_comp, comp_pair], 0)[seg_count:]
    recv_mem, recv_comp = passed_along((tail_mem, tail_comp), "blk", 1)
    comp_ext = jnp.concatenate([recv_comp, comp_pair], 0)
    mem_ext = jnp.concatenate([recv_mem, own_pair], 0)
    pieces = [comp_ext[window - lag : window - lag + seg_count] for lag in range(CSEGS + 1, 1, -1)]
    pairs = jnp.concatenate(pieces + [mem_ext[:seg_count], own_pair], 1)
    order = jnp.arange(lengths.shape[0], dtype=jnp.int32)
    starts = jnp.sum(jnp.where(order[None, :] < order[:, None], lengths[None, :], 0), axis=1)
    seg_ids = blk_index * seg_count + jnp.arange(seg_count, dtype=jnp.int32)
    seg_place = seg_ids - jnp.max(
        jnp.where(starts[None, :] <= seg_ids[:, None], starts[None, :], 0), axis=1
    )
    head_ids = head_index * local_heads + jnp.arange(local_heads, dtype=jnp.int32)
    slopes = jnp.exp2(-head_ids.astype(jnp.float32)) / 64.0
    group, place = key_layout(seg_len, comp_rows, CSEGS, RATE)

    def attend_fwd(args):
        query_seg, pair_seg, place_seg = args
        query_heads = query_seg.reshape(seg_len, local_heads, HD)
        key_heads = pair_seg[:, :head_cols].reshape(-1, local_heads, HD)
        value_heads = pair_seg[:, head_cols:].reshape(-1, local_heads, HD)
        scores = make_scores(query_heads, key_heads, group, place, place_seg, slopes)
        row_top = jnp.max(scores, axis=-1, keepdims=True)
        weights = jnp.exp(scores - row_top)
        total = jnp.sum(weights, axis=-1, keepdims=True)
        probs = (weights / total).astype(jnp.bfloat16)
        result = jnp.einsum("hqk,khd->qhd", probs, value_heads, preferred_element_type=jnp.float32)
        return (result.reshape(seg_len, head_cols).astype(jnp.bfloat16), row_top + jnp.log(total))

    attn_out, log_total = lax.map(attend_fwd, (heads_q, pairs, seg_place))
    mixed = lax.all_to_all(
        attn_out.reshape(seg_count, seg_len, 1, head_cols),
        "head",
        split_axis=1,
        concat_axis=2,
        tiled=True,
    ).reshape(token_count, width)
    branch = jnp.dot(mixed, wo_all, preferred_element_type=jnp.float32)
    hidden = token_rows + branch
    normed_two = layer_norm(hidden, gain_second).astype(jnp.bfloat16)
    lifted = jnp.dot(normed_two, up_all, preferred_element_type=jnp.float32)
    active = jax.nn.silu(lifted).astype(jnp.bfloat16)
    ffn_term = jnp.dot(active, down_all, preferred_element_type=jnp.float32)
    result_rows = hidden + ffn_term
    out_tokens = result_rows.astype(jnp.bfloat16).reshape(tokens.shape)
    compressed = lax.dynamic_slice_in_dim(packed, col_start, head_cols, 1).reshape(
        seg_count, comp_rows, head_cols
    )
    upstream = grad_out.reshape(token_count, width)
    grad_down_full = lax.dot_general(active, upstream, ROWS_IN, preferred_element_type=jnp.float32)
    grad_active = lax.dot_general(upstream, down_all, COLS_IN, preferred_element_type=jnp.float32)
    grad_lifted = (grad_active * silu_slope(lifted)).astype(jnp.bfloat16)
    grad_up_full = lax.dot_general(
        normed_two, grad_lifted, ROWS_IN, preferred_element_type=jnp.float32
    )
    grad_normed_two = lax.dot_general(
        grad_lifted, up_all, COLS_IN, preferred_element_type=jnp.float32
    )
    up_part, down_part = (
        lax.psum_scatter(
            grad_up_full.astype(jnp.bfloat16), "head", scatter_dimension=1, tiled=True
        ).astype(jnp.float32),
        lax.psum_scatter(
            grad_down_full.astype(jnp.bfloat16), "head", scatter_dimension=0, tiled=True
        ).astype(jnp.float32),
    )
    second_value, second_pull = jax.vjp(layer_norm, hidden, gain_second)
    grad_hidden_norm, grad_gain_two = second_pull(grad_normed_two)
    grad_hidden = upstream.astype(jnp.float32) + grad_hidden_norm
    grad_branch = grad_hidden.astype(jnp.bfloat16)
    grad_wo = lax.dot_general(mixed, grad_branch, ROWS_IN, preferred_element_type=jnp.float32)
    grad_mixed = lax.dot_general(
        grad_branch, wo_all, COLS_IN, preferred_element_type=jnp.float32
    ).astype(jnp.bfloat16)
    grad_heads = lax.all_to_all(
        grad_mixed.reshape(split_shape), "head", split_axis=2, concat_axis=1, tiled=True
    ).reshape(local_shape)

    def attend_back(args):
        query_seg, pair_seg, place_seg, lse_seg, grad_seg = args
        query_heads = query_seg.reshape(seg_len, local_heads, HD)
        key_heads = pair_seg[:, :head_cols].reshape(-1, local_heads, HD)
        value_heads = pair_seg[:, head_cols:].reshape(-1, local_heads, HD)
        scores = make_scores(query_heads, key_heads, group, place, place_seg, slopes)
        probs = jnp.exp(scores - lse_seg)
        grad_seg_heads = grad_seg.reshape(seg_len, local_heads, HD)
        grad_probs = jnp.einsum(
            "qhd,khd->hqk", grad_seg_heads, value_heads, preferred_element_type=jnp.float32
        )
        grad_scores = (
            probs * (grad_probs - jnp.sum(probs * grad_probs, axis=-1, keepdims=True))
        ).astype(jnp.bfloat16)
        grad_query_seg = jnp.einsum(
            "hqk,khd->qhd", grad_scores, key_heads, preferred_element_type=jnp.float32
        ) * HD ** (-0.5)
        grad_key_seg = jnp.einsum(
            "hqk,qhd->khd", grad_scores, query_heads, preferred_element_type=jnp.float32
        ) * HD ** (-0.5)
        grad_value_seg = jnp.einsum(
            "hqk,qhd->khd",
            probs.astype(jnp.bfloat16),
            grad_seg_heads,
            preferred_element_type=jnp.float32,
        )
        key_count = pair_seg.shape[0]
        grad_pair_seg = jnp.concatenate(
            [
                grad_key_seg.reshape(key_count, head_cols),
                grad_value_seg.reshape(key_count, head_cols),
            ],
            1,
        )
        return (grad_query_seg.reshape(seg_len, head_cols).astype(jnp.bfloat16), grad_pair_seg)

    grad_query, grad_pairs = lax.map(
        attend_back, (heads_q, pairs, seg_place, log_total, grad_heads)
    )
    grad_comp_ext = jnp.zeros((window + seg_count, comp_rows, 2 * head_cols), jnp.float32)
    for piece_index in range(CSEGS):
        lag = CSEGS + 1 - piece_index
        piece = grad_pairs[:, piece_index * comp_rows : (piece_index + 1) * comp_rows]
        grad_comp_ext = grad_comp_ext + jnp.pad(piece, ((window - lag, lag), (0, 0), (0, 0)))
    mem_start = CSEGS * comp_rows
    grad_mem = grad_pairs[:, mem_start : mem_start + seg_len]
    grad_own = grad_pairs[:, mem_start + seg_len :]
    grad_mem_ext = jnp.pad(grad_mem, ((0, 1), (0, 0), (0, 0))) + jnp.pad(
        grad_own, ((1, 0), (0, 0), (0, 0))
    )
    back_mem = grad_mem_ext[:1]
    own_pair_grad = grad_mem_ext[1:]
    back_comp = grad_comp_ext[:window]
    comp_pair_grad = grad_comp_ext[window:]
    got_mem = passed_along(back_mem.astype(jnp.bfloat16), "blk", -1).astype(back_mem.dtype)
    got_comp = passed_along(back_comp.astype(jnp.bfloat16), "blk", -1).astype(back_comp.dtype)
    joined_mem = jnp.pad(got_mem, ((seg_count, 0), (0, 0), (0, 0)))
    own_pair_grad = own_pair_grad + joined_mem[1:]
    joined_comp = jnp.pad(got_comp, ((seg_count, 0), (0, 0), (0, 0)))
    comp_pair_grad = comp_pair_grad + joined_comp[window:]
    grad_key_heads = own_pair_grad[..., :head_cols].astype(jnp.bfloat16)
    grad_value_heads = own_pair_grad[..., head_cols:].astype(jnp.bfloat16)
    comp_grad_rows = comp_pair_grad.reshape(seg_count * comp_rows, 2 * head_cols).astype(
        jnp.bfloat16
    )
    grad_comp_key = comp_grad_rows[:, :head_cols]
    grad_comp_value = comp_grad_rows[:, head_cols:]
    grad_packed_part = lax.dot_general(
        grad_comp_key, wk_mine, COLS_IN, preferred_element_type=jnp.float32
    ) + lax.dot_general(grad_comp_value, wv_mine, COLS_IN, preferred_element_type=jnp.float32)
    grad_packed = lax.psum(grad_packed_part.astype(jnp.bfloat16), "head")
    comp_key_term = lax.dot_general(
        packed, grad_comp_key, ROWS_IN, preferred_element_type=jnp.float32
    )
    comp_value_term = lax.dot_general(
        packed, grad_comp_value, ROWS_IN, preferred_element_type=jnp.float32
    )
    grad_grouped = lax.dot_general(
        grad_packed, comp_matrix, COLS_IN, preferred_element_type=jnp.float32
    ).astype(jnp.bfloat16)
    grad_comp_term = lax.dot_general(
        grouped, grad_packed, ROWS_IN, preferred_element_type=jnp.float32
    ).reshape(RATE, head_cols, width)
    grad_sent = jnp.pad(
        grad_grouped.reshape(seg_count, RATE * comp_rows, head_cols),
        ((0, 0), (0, seg_len - RATE * comp_rows), (0, 0)),
    )
    back_shape = (seg_count, seg_len, 1, head_cols)
    token_q, token_k, token_v, token_x = (
        lax.all_to_all(
            grad_query.reshape(back_shape), "head", split_axis=1, concat_axis=2, tiled=True
        ),
        lax.all_to_all(
            grad_key_heads.reshape(back_shape), "head", split_axis=1, concat_axis=2, tiled=True
        ),
        lax.all_to_all(
            grad_value_heads.reshape(back_shape), "head", split_axis=1, concat_axis=2, tiled=True
        ),
        lax.all_to_all(
            grad_sent.reshape(back_shape), "head", split_axis=1, concat_axis=2, tiled=True
        ),
    )
    token_q = token_q.reshape(token_count, width)
    token_k = token_k.reshape(token_count, width)
    token_v = token_v.reshape(token_count, width)
    token_x = token_x.reshape(token_count, width)
    grad_normed = lax.dot_general(token_q, wq_all, COLS_IN, preferred_element_type=jnp.float32)
    grad_normed = grad_normed + lax.dot_general(
        token_k, wk_all, COLS_IN, preferred_element_type=jnp.float32
    )
    grad_normed = grad_normed + lax.dot_general(
        token_v, wv_all, COLS_IN, preferred_element_type=jnp.float32
    )
    grad_normed = grad_normed + token_x.astype(jnp.float32)
    first_value, first_pull = jax.vjp(layer_norm, token_rows, gain_first)
    grad_rows_norm, grad_gain_one = first_pull(grad_normed)
    grad_tokens = (grad_hidden + grad_rows_norm).astype(jnp.bfloat16).reshape(tokens.shape)
    grad_wq = lax.dot_general(normed, token_q, ROWS_IN, preferred_element_type=jnp.float32)
    grad_wk = lax.dot_general(normed, token_k, ROWS_IN, preferred_element_type=jnp.float32)
    grad_wv = lax.dot_general(normed, token_v, ROWS_IN, preferred_element_type=jnp.float32)
    grad_wk = grad_wk + lax.dynamic_update_slice_in_dim(
        jnp.zeros_like(grad_wk), comp_key_term, col_start, 1
    )
    grad_wv = grad_wv + lax.dynamic_update_slice_in_dim(
        jnp.zeros_like(grad_wv), comp_value_term, col_start, 1
    )
    blk_summed = (
        lax.psum_scatter(
            up_part.astype(jnp.bfloat16), "blk", scatter_dimension=1, tiled=True
        ).astype(jnp.float32),
        lax.psum_scatter(
            down_part.astype(jnp.bfloat16), "blk", scatter_dimension=0, tiled=True
        ).astype(jnp.float32),
        lax.psum_scatter(
            grad_comp_term.astype(jnp.bfloat16), "blk", scatter_dimension=1, tiled=True
        ).astype(jnp.float32),
    )
    summed = (
        lax.psum_scatter(grad_wq, ("head", "blk"), scatter_dimension=0, tiled=True),
        lax.psum_scatter(grad_wk, ("head", "blk"), scatter_dimension=0, tiled=True),
        lax.psum_scatter(grad_wv, ("head", "blk"), scatter_dimension=0, tiled=True),
        lax.psum_scatter(grad_wo, ("head", "blk"), scatter_dimension=0, tiled=True),
        lax.psum_scatter(grad_gain_one, ("head", "blk"), scatter_dimension=0, tiled=True),
        lax.psum_scatter(grad_gain_two, ("head", "blk"), scatter_dimension=0, tiled=True),
    )
    return (
        out_tokens,
        compressed,
        grad_tokens,
        summed[0],
        summed[1],
        summed[2],
        summed[3],
        blk_summed[0],
        blk_summed[1],
        summed[4],
        summed[5],
        blk_summed[2],
    )


def solution(mesh):
    return jax.shard_map(
        per_device,
        mesh=mesh,
        in_specs=(
            P("blk", "head", None),
            P(("head", "blk"), None),
            P(("head", "blk"), None),
            P(("head", "blk"), None),
            P(("head", "blk"), None),
            P(None, ("head", "blk")),
            P(("head", "blk"), None),
            P(("head", "blk")),
            P(("head", "blk")),
            P(None, ("head", "blk"), None),
            P(),
            P("blk", "head", None),
        ),
        out_specs=(
            P("blk", "head", None),
            P("blk", None, "head"),
            P("blk", "head", None),
            P(("head", "blk"), None),
            P(("head", "blk"), None),
            P(("head", "blk"), None),
            P(("head", "blk"), None),
            P(None, ("head", "blk")),
            P(("head", "blk"), None),
            P(("head", "blk")),
            P(("head", "blk")),
            P(None, ("head", "blk"), None),
        ),
        check_vma=False,
    )
```

```python
import jax
import jax.numpy as jnp
from jax import lax
from jax.sharding import PartitionSpec as P

HD = 128
RATE = 3
CSEGS = 3


EPS = 1e-05
NEG = -1e30
ROWS_IN = (((0,), (0,)), ((), ()))
COLS_IN = (((1,), (1,)), ((), ()))


def passed_along(value, axis, steps):
    count = lax.axis_size(axis)
    leading, last = (max(0, -steps), min(count, count - steps))
    return lax.ppermute(value, axis, [(source, source + steps) for source in range(leading, last)])


def layer_norm(values, gain):
    average = jnp.mean(values, axis=-1, keepdims=True)
    center = values - average
    variance = jnp.mean(center * center, axis=-1, keepdims=True)
    return center * lax.rsqrt(variance + EPS) * gain


def silu_slope(values):
    sig = jax.nn.sigmoid(values)
    return sig * (1.0 + values * (1.0 - sig))


def key_layout(seg_len, comp_rows, comp_segs, rate):
    groups = []
    places = []
    for lag in range(comp_segs + 1, 1, -1):
        groups.append(jnp.full((comp_rows,), lag, jnp.int32))
        places.append(rate * jnp.arange(comp_rows, dtype=jnp.int32) + rate // 2 - lag * seg_len)
    groups.append(jnp.full((seg_len,), 1, jnp.int32))
    places.append(jnp.arange(seg_len, dtype=jnp.int32) - seg_len)
    groups.append(jnp.zeros((seg_len,), jnp.int32))
    places.append(jnp.arange(seg_len, dtype=jnp.int32))
    return (jnp.concatenate(groups), jnp.concatenate(places))


def make_scores(query_heads, key_heads, group, place, seg_place, slopes):
    seg_len = query_heads.shape[0]
    positions = jnp.arange(seg_len, dtype=jnp.int32)
    allowed = (group[None, :] <= seg_place) & (place[None, :] <= positions[:, None])
    distance = (positions[:, None] - place[None, :]).astype(jnp.float32)
    raw = jnp.einsum("qhd,khd->hqk", query_heads, key_heads, preferred_element_type=jnp.float32)
    scores = raw * HD ** (-0.5) - slopes[:, None, None] * distance[None]
    return jnp.where(allowed[None], scores, NEG)


def head_swap(value, bit):
    count = lax.axis_size("head")
    return lax.ppermute(value, "head", [(source, source ^ bit) for source in range(count)])


def gather_over_head(value):
    seg_count, quarter, width = value.shape
    head_index = lax.axis_index("head")
    far = head_swap(value, 2)
    near = head_swap(value, 1)
    far_near = head_swap(far, 1)
    blocks = lax.axis_size("head")
    whole = jnp.zeros((seg_count, blocks, quarter, width), value.dtype)
    for block, held in ((0, value), (1, near), (2, far), (3, far_near)):
        whole = lax.dynamic_update_slice(
            whole, held[:, None], (0, jnp.bitwise_xor(head_index, block), 0, 0)
        )
    return whole.reshape(seg_count, blocks * quarter, width)


def scatter_over_head(pieces):
    head_index = lax.axis_index("head")

    def term(bits):
        return pieces(jnp.bitwise_xor(head_index, bits))

    sent = jnp.stack([term(1), term(3)]).astype(jnp.bfloat16)
    got = head_swap(sent, 1).astype(jnp.float32)
    far = (term(2) + got[1]).astype(jnp.bfloat16)
    return term(0) + got[0] + head_swap(far, 2).astype(jnp.float32)


def per_device(tokens, wq, wk, wv, wo, w_up, w_down, gain_one, gain_two, w_comp, lengths, grad_out):
    seg_count, quarter, width = tokens.shape
    head_groups = lax.axis_size("head")
    blk_count = lax.axis_size("blk")
    devices = head_groups * blk_count
    seg_len = quarter * head_groups
    head_cols = width // head_groups
    local_heads = head_cols // HD
    comp_rows = seg_len // RATE
    window = CSEGS + 1
    head_index = lax.axis_index("head")
    blk_index = lax.axis_index("blk")
    col_start = head_index * head_cols
    token_count = seg_count * quarter
    full_count = seg_count * seg_len
    comp_count = seg_count * comp_rows
    part = wq.shape[0]
    ff_part = w_down.shape[0]
    both = ("head", "blk")
    gains = jnp.pad(jnp.concatenate([gain_one, gain_two])[None], ((0, 7), (0, width - 2 * part)))
    first_pack = jnp.concatenate([wq, wk, wv, w_comp.reshape(RATE * part, width), gains], 0)
    second_pack = jnp.concatenate([wo, w_up.T, w_down], 0)
    first_all = lax.all_gather(first_pack, both, axis=0)
    second_all = lax.all_gather(second_pack, both, axis=0)
    full_tokens = gather_over_head(tokens)
    gain_first = first_all[:, 6 * part, :part].reshape(width).astype(jnp.float32)
    gain_second = first_all[:, 6 * part, part : 2 * part].reshape(width).astype(jnp.float32)
    mine = lax.dynamic_slice_in_dim(first_all[:, : 3 * part], col_start, head_cols, 2)
    wqkv = (
        mine.reshape(devices, 3, part, head_cols)
        .transpose(0, 2, 1, 3)
        .reshape(width, 3 * head_cols)
    )
    wkv = wqkv[:, head_cols:]
    comp_matrix = (
        first_all[:, 3 * part : 6 * part]
        .reshape(devices, RATE, part, width)
        .transpose(1, 0, 2, 3)
        .reshape(RATE * width, width)
    )
    wo_all = second_all[:, :part].reshape(width, width)
    up_all = second_all[:, part : part + ff_part].reshape(devices * ff_part, width)
    down_all = second_all[:, part + ff_part :].reshape(devices * ff_part, width)

    full_rows = full_tokens.reshape(full_count, width).astype(jnp.float32)
    normed = layer_norm(full_rows, gain_first).astype(jnp.bfloat16)
    heads = jnp.dot(normed, wqkv, preferred_element_type=jnp.float32).astype(jnp.bfloat16)
    heads = heads.reshape(seg_count, seg_len, 3 * head_cols)
    heads_q = heads[..., :head_cols]
    own_pair = heads[..., head_cols:]
    grouped = normed.reshape(seg_count, seg_len, width)[:, : RATE * comp_rows].reshape(
        comp_count, RATE * width
    )
    packed = jnp.dot(grouped, comp_matrix, preferred_element_type=jnp.float32).astype(jnp.bfloat16)
    comp_pair = (
        jnp.dot(packed, wkv, preferred_element_type=jnp.float32)
        .astype(jnp.bfloat16)
        .reshape(seg_count, comp_rows, 2 * head_cols)
    )
    compressed = lax.dynamic_slice_in_dim(packed, col_start, head_cols, 1).reshape(
        seg_count, comp_rows, head_cols
    )
    recv_mem, recv_comp = passed_along(
        (own_pair[seg_count - 1 :], comp_pair[seg_count - window :]), "blk", 1
    )
    comp_ext = jnp.concatenate([recv_comp, comp_pair], 0)
    mem_ext = jnp.concatenate([recv_mem, own_pair], 0)
    order = jnp.arange(lengths.shape[0], dtype=jnp.int32)
    starts = jnp.sum(jnp.where(order[None, :] < order[:, None], lengths[None, :], 0), axis=1)
    seg_ids = blk_index * seg_count + jnp.arange(seg_count, dtype=jnp.int32)
    seg_place = seg_ids - jnp.max(
        jnp.where(starts[None, :] <= seg_ids[:, None], starts[None, :], 0), axis=1
    )
    pieces = [comp_ext[window - lag : window - lag + seg_count] for lag in range(CSEGS + 1, 1, -1)]
    pairs = jnp.concatenate(pieces + [mem_ext[:seg_count], own_pair], 1)
    head_ids = head_index * local_heads + jnp.arange(local_heads, dtype=jnp.int32)
    slopes = jnp.exp2(-head_ids.astype(jnp.float32)) / 64.0
    group, place = key_layout(seg_len, comp_rows, CSEGS, RATE)

    def attend_fwd(args):
        query_seg, pair_seg, place_seg = args
        query_heads = query_seg.reshape(seg_len, local_heads, HD)
        key_heads = pair_seg[:, :head_cols].reshape(-1, local_heads, HD)
        value_heads = pair_seg[:, head_cols:].reshape(-1, local_heads, HD)
        scores = make_scores(query_heads, key_heads, group, place, place_seg, slopes)
        row_top = jnp.max(scores, axis=-1, keepdims=True)
        weights = jnp.exp(scores - row_top)
        total = jnp.sum(weights, axis=-1, keepdims=True)
        probs = (weights / total).astype(jnp.bfloat16)
        result = jnp.einsum("hqk,khd->qhd", probs, value_heads, preferred_element_type=jnp.float32)
        return (result.reshape(seg_len, head_cols).astype(jnp.bfloat16), row_top + jnp.log(total))

    attn_out, log_total = lax.map(attend_fwd, (heads_q, pairs, seg_place))
    mixed = lax.all_to_all(
        attn_out.reshape(seg_count, seg_len, 1, head_cols),
        "head",
        split_axis=1,
        concat_axis=2,
        tiled=True,
    ).reshape(token_count, width)
    token_rows = tokens.reshape(token_count, width).astype(jnp.float32)
    branch = jnp.dot(mixed, wo_all, preferred_element_type=jnp.float32)
    hidden = token_rows + branch
    normed_two = layer_norm(hidden, gain_second).astype(jnp.bfloat16)
    lifted = lax.dot_general(normed_two, up_all, COLS_IN, preferred_element_type=jnp.float32)
    active = jax.nn.silu(lifted).astype(jnp.bfloat16)
    ffn_term = jnp.dot(active, down_all, preferred_element_type=jnp.float32)
    out_tokens = (hidden + ffn_term).astype(jnp.bfloat16).reshape(tokens.shape)
    upstream = grad_out.reshape(token_count, width)
    grad_down = lax.dot_general(active, upstream, ROWS_IN, preferred_element_type=jnp.float32)
    grad_active = lax.dot_general(upstream, down_all, COLS_IN, preferred_element_type=jnp.float32)
    grad_lifted = (grad_active * silu_slope(lifted)).astype(jnp.bfloat16)
    grad_up = lax.dot_general(grad_lifted, normed_two, ROWS_IN, preferred_element_type=jnp.float32)
    grad_normed_two = jnp.dot(grad_lifted, up_all, preferred_element_type=jnp.float32)
    second_value, second_pull = jax.vjp(layer_norm, hidden, gain_second)
    grad_hidden_norm, grad_gain_two = second_pull(grad_normed_two)
    grad_hidden = upstream.astype(jnp.float32) + grad_hidden_norm
    grad_branch = grad_hidden.astype(jnp.bfloat16)
    grad_wo = lax.dot_general(mixed, grad_branch, ROWS_IN, preferred_element_type=jnp.float32)
    first_grads = jnp.concatenate(
        [
            grad_wo.astype(jnp.bfloat16).reshape(devices, part, width),
            grad_up.astype(jnp.bfloat16).reshape(devices, ff_part, width),
            grad_down.astype(jnp.bfloat16).reshape(devices, ff_part, width),
        ],
        1,
    )
    first_sum = lax.psum_scatter(first_grads, both, scatter_dimension=0).astype(jnp.float32)
    grad_mixed = lax.dot_general(
        grad_branch, wo_all, COLS_IN, preferred_element_type=jnp.float32
    ).astype(jnp.bfloat16)
    grad_heads = lax.all_to_all(
        grad_mixed.reshape(seg_count, quarter, head_groups, head_cols),
        "head",
        split_axis=2,
        concat_axis=1,
        tiled=True,
    ).reshape(seg_count, seg_len, head_cols)
    def attend_back(args):
        query_seg, pair_seg, place_seg, lse_seg, grad_seg = args
        query_heads = query_seg.reshape(seg_len, local_heads, HD)
        key_heads = pair_seg[:, :head_cols].reshape(-1, local_heads, HD)
        value_heads = pair_seg[:, head_cols:].reshape(-1, local_heads, HD)
        scores = make_scores(query_heads, key_heads, group, place, place_seg, slopes)
        probs = jnp.exp(scores - lse_seg)
        grad_seg_heads = grad_seg.reshape(seg_len, local_heads, HD)
        grad_probs = jnp.einsum(
            "qhd,khd->hqk", grad_seg_heads, value_heads, preferred_element_type=jnp.float32
        )
        grad_scores = (
            probs * (grad_probs - jnp.sum(probs * grad_probs, axis=-1, keepdims=True))
        ).astype(jnp.bfloat16)
        grad_query_seg = jnp.einsum(
            "hqk,khd->qhd", grad_scores, key_heads, preferred_element_type=jnp.float32
        ) * HD ** (-0.5)
        grad_key_seg = jnp.einsum(
            "hqk,qhd->khd", grad_scores, query_heads, preferred_element_type=jnp.float32
        ) * HD ** (-0.5)
        grad_value_seg = jnp.einsum(
            "hqk,qhd->khd",
            probs.astype(jnp.bfloat16),
            grad_seg_heads,
            preferred_element_type=jnp.float32,
        )
        key_count = pair_seg.shape[0]
        grad_pair_seg = jnp.concatenate(
            [
                grad_key_seg.reshape(key_count, head_cols),
                grad_value_seg.reshape(key_count, head_cols),
            ],
            1,
        )
        return (grad_query_seg.reshape(seg_len, head_cols).astype(jnp.bfloat16), grad_pair_seg)

    grad_query, grad_pairs = lax.map(
        attend_back, (heads_q, pairs, seg_place, log_total, grad_heads)
    )
    grad_comp_ext = jnp.zeros((window + seg_count, comp_rows, 2 * head_cols), jnp.float32)
    for piece_index in range(CSEGS):
        lag = CSEGS + 1 - piece_index
        piece = grad_pairs[:, piece_index * comp_rows : (piece_index + 1) * comp_rows]
        grad_comp_ext = grad_comp_ext + jnp.pad(piece, ((window - lag, lag), (0, 0), (0, 0)))
    mem_start = CSEGS * comp_rows
    grad_mem = grad_pairs[:, mem_start : mem_start + seg_len]
    grad_own = grad_pairs[:, mem_start + seg_len :]
    grad_mem_ext = jnp.pad(grad_mem, ((0, 1), (0, 0), (0, 0))) + jnp.pad(
        grad_own, ((1, 0), (0, 0), (0, 0))
    )
    back_mem = grad_mem_ext[:1]
    own_pair_grad = grad_mem_ext[1:]
    back_comp = grad_comp_ext[:window]
    comp_pair_grad = grad_comp_ext[window:]
    got_mem = passed_along(back_mem.astype(jnp.bfloat16), "blk", -1).astype(back_mem.dtype)
    got_comp = passed_along(back_comp.astype(jnp.bfloat16), "blk", -1).astype(back_comp.dtype)
    joined_mem = jnp.pad(got_mem, ((seg_count, 0), (0, 0), (0, 0)))
    own_pair_grad = own_pair_grad + joined_mem[1:]
    joined_comp = jnp.pad(got_comp, ((seg_count, 0), (0, 0), (0, 0)))
    comp_pair_grad = comp_pair_grad + joined_comp[window:]
    grad_qkv = jnp.concatenate([grad_query, own_pair_grad.astype(jnp.bfloat16)], 2).reshape(
        full_count, 3 * head_cols
    )
    comp_grad_rows = comp_pair_grad.reshape(comp_count, 2 * head_cols).astype(jnp.bfloat16)
    grad_packed_part = lax.dot_general(
        comp_grad_rows, wkv, COLS_IN, preferred_element_type=jnp.float32
    )
    grad_packed_mine = scatter_over_head(
        lambda block: lax.dynamic_slice_in_dim(grad_packed_part, block * head_cols, head_cols, 1)
    ).astype(jnp.bfloat16)
    grad_grouped = lax.dot_general(
        grad_packed_part.astype(jnp.bfloat16), comp_matrix, COLS_IN, preferred_element_type=jnp.float32
    ).astype(jnp.bfloat16)
    grad_sent = jnp.pad(
        grad_grouped.reshape(seg_count, RATE * comp_rows, width),
        ((0, 0), (0, seg_len - RATE * comp_rows), (0, 0)),
    )
    grad_normed_part = lax.dot_general(
        grad_qkv, wqkv, COLS_IN, preferred_element_type=jnp.float32
    ).reshape(seg_count, head_groups, quarter, width) + grad_sent.reshape(
        seg_count, head_groups, quarter, width
    ).astype(jnp.float32)
    average = jnp.mean(full_rows, axis=-1, keepdims=True)
    center = full_rows - average
    spread = lax.rsqrt(jnp.mean(center * center, axis=-1, keepdims=True) + EPS)
    grad_gain_one = jnp.sum(grad_normed_part.reshape(full_count, width) * (center * spread), axis=0)
    grad_normed = scatter_over_head(
        lambda block: lax.dynamic_slice_in_dim(grad_normed_part, block, 1, 1)
    ).reshape(token_count, width)
    first_value, first_pull = jax.vjp(lambda rows: layer_norm(rows, gain_first), token_rows)
    (grad_rows_norm,) = first_pull(grad_normed)
    grad_tokens = (grad_hidden + grad_rows_norm).astype(jnp.bfloat16).reshape(tokens.shape)
    comp_term = lax.dot_general(packed, comp_grad_rows, ROWS_IN, preferred_element_type=jnp.float32)
    grad_wqkv = lax.dot_general(normed, grad_qkv, ROWS_IN, preferred_element_type=jnp.float32)
    grad_wqkv = grad_wqkv + jnp.pad(comp_term, ((0, 0), (head_cols, 0)))
    grad_comp = lax.dot_general(
        grouped, grad_packed_mine, ROWS_IN, preferred_element_type=jnp.float32
    )

    def by_owner(value, kinds):
        return value.astype(jnp.bfloat16).reshape(
            kinds, head_groups, blk_count, part, head_cols
        ).transpose(2, 1, 0, 3, 4).reshape(blk_count, head_groups, kinds * part, head_cols)

    gain_rows = jnp.stack(
        [grad_gain_one.reshape(head_groups, blk_count, part), grad_gain_two.reshape(head_groups, blk_count, part)], 2
    ).transpose(1, 0, 2, 3).astype(jnp.bfloat16)
    second_grads = jnp.concatenate(
        [
            by_owner(jnp.concatenate([grad_wqkv[:, i * head_cols : (i + 1) * head_cols] for i in range(3)], 0), 3),
            by_owner(grad_comp, RATE),
            jnp.pad(gain_rows, ((0, 0), (0, 0), (0, 14), (0, head_cols - part))),
        ],
        2,
    )
    second_part = lax.psum_scatter(second_grads, "blk", scatter_dimension=0)
    second_sum = lax.all_to_all(second_part, "head", split_axis=0, concat_axis=0, tiled=True).astype(
        jnp.float32
    )
    gain_sum = jnp.sum(second_sum[:, 6 * part : 6 * part + 2, :part], axis=0)
    weight_sum = (
        second_sum[:, : 6 * part]
        .reshape(head_groups, 6, part, head_cols)
        .transpose(1, 2, 0, 3)
        .reshape(6, part, width)
    )
    return (
        out_tokens,
        compressed,
        grad_tokens,
        weight_sum[0],
        weight_sum[1],
        weight_sum[2],
        first_sum[:part],
        first_sum[part : part + ff_part].T,
        first_sum[part + ff_part :],
        gain_sum[0],
        gain_sum[1],
        weight_sum[3:],
    )


def solution(mesh):
    return jax.shard_map(
        per_device,
        mesh=mesh,
        in_specs=(
            P("blk", "head", None),
            P(("head", "blk"), None),
            P(("head", "blk"), None),
            P(("head", "blk"), None),
            P(("head", "blk"), None),
            P(None, ("head", "blk")),
            P(("head", "blk"), None),
            P(("head", "blk")),
            P(("head", "blk")),
            P(None, ("head", "blk"), None),
            P(),
            P("blk", "head", None),
        ),
        out_specs=(
            P("blk", "head", None),
            P("blk", None, "head"),
            P("blk", "head", None),
            P(("head", "blk"), None),
            P(("head", "blk"), None),
            P(("head", "blk"), None),
            P(("head", "blk"), None),
            P(None, ("head", "blk")),
            P(("head", "blk"), None),
            P(("head", "blk")),
            P(("head", "blk")),
            P(None, ("head", "blk"), None),
        ),
        check_vma=False,
    )
```

```python
import jax
import jax.numpy as jnp
from jax import lax
from jax.experimental import pallas as pl
from jax.experimental.pallas import tpu as pltpu
from jax.sharding import PartitionSpec as P

HD = 128
RATE = 3
CSEGS = 3


EPS = 1e-05
NEG = -1e30
ROWS_IN = (((0,), (0,)), ((), ()))
COLS_IN = (((1,), (1,)), ((), ()))


def passed_along(value, axis, steps):
    count = lax.axis_size(axis)
    leading, last = (max(0, -steps), min(count, count - steps))
    return lax.ppermute(value, axis, [(source, source + steps) for source in range(leading, last)])


def layer_norm(values, gain):
    average = jnp.mean(values, axis=-1, keepdims=True)
    center = values - average
    variance = jnp.mean(center * center, axis=-1, keepdims=True)
    return center * lax.rsqrt(variance + EPS) * gain


def silu_slope(values):
    sig = jax.nn.sigmoid(values)
    return sig * (1.0 + values * (1.0 - sig))


LOG2E = 1.4426950408889634
PAD_ROWS = 176
VMEM_LIMIT = 56 * 1024 * 1024


def key_bias(rows, base, step, valid_rows, open_, slope):
    row = lax.broadcasted_iota(jnp.int32, (rows, 1), 0)
    place = (base + step * row).astype(jnp.float32)
    return jnp.where((row < valid_rows) & open_, place * slope, NEG)


def fwd_kernel(place_ref, slope_ref, q_ref, own_ref, prev_ref, recv_ref, comp_ref, out_ref, lse_ref):
    step = pl.program_id(0)
    place = place_ref[step]
    seg_len = q_ref.shape[1]
    half = seg_len // 2
    pad_rows = comp_ref.shape[1]
    local_heads = q_ref.shape[2] // HD
    values_at = local_heads * HD
    factor = HD ** (-0.5) * LOG2E
    lower = lax.broadcasted_iota(jnp.int32, (half, half), 0) <= lax.broadcasted_iota(
        jnp.int32, (half, half), 1
    )
    for h in range(local_heads):
        kc = slice(h * HD, (h + 1) * HD)
        vc = slice(values_at + h * HD, values_at + (h + 1) * HD)
        slope = slope_ref[h]
        parts = []
        for piece in range(CSEGS):
            lag = CSEGS + 1 - piece
            bias = key_bias(pad_rows, RATE // 2 - lag * seg_len, RATE, seg_len // RATE, place >= lag, slope)
            parts.append((comp_ref[step + piece, :, kc], comp_ref[step + piece, :, vc], bias))
        bias = key_bias(seg_len, -seg_len, 1, seg_len, place >= 1, slope)
        is_first = step == 0
        parts.append(
            (
                jnp.where(is_first, recv_ref[0, :, kc], prev_ref[0, :, kc]),
                jnp.where(is_first, recv_ref[0, :, vc], prev_ref[0, :, vc]),
                bias,
            )
        )
        own_bias = [
            key_bias(half, n * half, 1, half, place >= 0, slope) for n in range(2)
        ]
        for n in range(2):
            query = q_ref[0, n * half : (n + 1) * half, kc]
            group = list(parts)
            for m in range(n + 1):
                rows = slice(m * half, (m + 1) * half)
                group.append((own_ref[0, rows, kc], own_ref[0, rows, vc], own_bias[m]))
            scores = []
            top = None
            for index, (k, v, bias) in enumerate(group):
                raw = lax.dot_general(k, query, COLS_IN, preferred_element_type=jnp.float32)
                raw = raw * factor + bias
                if index == len(group) - 1:
                    raw = jnp.where(lower, raw, NEG)
                scores.append(raw)
                peak = jnp.max(raw, axis=0, keepdims=True)
                top = peak if top is None else jnp.maximum(top, peak)
            total = jnp.zeros_like(top)
            result = jnp.zeros((HD, half), jnp.float32)
            for raw, (k, v, bias) in zip(scores, group):
                weight = jnp.exp2(raw - top)
                total = total + jnp.sum(weight, axis=0, keepdims=True)
                result = result + lax.dot_general(
                    v, weight.astype(jnp.bfloat16), ROWS_IN, preferred_element_type=jnp.float32
                )
            result = result * (1.0 / total)
            out_ref[0, n * half : (n + 1) * half, kc] = result.T.astype(jnp.bfloat16)
            lse_ref[0, h : h + 1, n * half : (n + 1) * half] = top + jnp.log(total) * LOG2E


def bwd_kernel(
    place_ref, slope_ref, q_ref, own_ref, prev_ref, recv_ref, comp_ref, grad_ref, att_ref, lse_ref,
    gq_ref, gkv_ref, tail_ref, gcomp_ref,
):
    step = pl.program_id(0)
    place = place_ref[step]
    seg_len = q_ref.shape[1]
    half = seg_len // 2
    pad_rows = comp_ref.shape[1]
    local_heads = q_ref.shape[2] // HD
    values_at = local_heads * HD
    scale = HD ** (-0.5)
    factor = scale * LOG2E
    is_first = step == 0
    lower = lax.broadcasted_iota(jnp.int32, (half, half), 0) <= lax.broadcasted_iota(
        jnp.int32, (half, half), 1
    )

    @pl.when(is_first)
    def _():
        tail_ref[...] = jnp.zeros_like(tail_ref)
        gcomp_ref[...] = jnp.zeros_like(gcomp_ref)

    for h in range(local_heads):
        kc = slice(h * HD, (h + 1) * HD)
        vc = slice(values_at + h * HD, values_at + (h + 1) * HD)
        slope = slope_ref[h]
        query = q_ref[0, :, kc]
        grad = grad_ref[0, :, kc]
        lse = lse_ref[0, h : h + 1, :]
        product = grad.astype(jnp.float32) * att_ref[0, :, kc].astype(jnp.float32)
        delta = jnp.sum(product.T, axis=0, keepdims=True)

        def part(k, v, bias, cols, masked):
            raw = lax.dot_general(k, query[cols], COLS_IN, preferred_element_type=jnp.float32)
            raw = raw * factor + bias
            if masked:
                raw = jnp.where(lower, raw, NEG)
            prob = jnp.exp2(raw - lse[:, cols])
            grad_prob = lax.dot_general(v, grad[cols], COLS_IN, preferred_element_type=jnp.float32)
            grad_score = (prob * (grad_prob - delta[:, cols])).astype(jnp.bfloat16)
            gk = jnp.dot(grad_score, query[cols], preferred_element_type=jnp.float32) * scale
            gv = jnp.dot(prob.astype(jnp.bfloat16), grad[cols], preferred_element_type=jnp.float32)
            gq = lax.dot_general(k, grad_score, ROWS_IN, preferred_element_type=jnp.float32)
            return gk, gv, gq

        every = slice(0, seg_len)
        total = jnp.zeros((HD, seg_len), jnp.float32)
        for piece in range(CSEGS):
            lag = CSEGS + 1 - piece
            bias = key_bias(pad_rows, RATE // 2 - lag * seg_len, RATE, seg_len // RATE, place >= lag, slope)
            gk, gv, gq = part(comp_ref[step + piece, :, kc], comp_ref[step + piece, :, vc], bias, every, False)
            gcomp_ref[step + piece, :, kc] += gk
            gcomp_ref[step + piece, :, vc] += gv
            total = total + gq
        for n in range(2):
            rows = slice(n * half, (n + 1) * half)
            bias = key_bias(half, n * half - seg_len, 1, half, place >= 1, slope)
            k = jnp.where(is_first, recv_ref[0, rows, kc], prev_ref[0, rows, kc])
            v = jnp.where(is_first, recv_ref[0, rows, vc], prev_ref[0, rows, vc])
            gk, gv, gq = part(k, v, bias, every, False)
            gkv_ref[0, rows, kc] = (tail_ref[rows, kc] + gk).astype(jnp.bfloat16)
            gkv_ref[0, rows, vc] = (tail_ref[rows, vc] + gv).astype(jnp.bfloat16)
            total = total + gq
        lo, hi = slice(0, half), slice(half, seg_len)
        bias_lo = key_bias(half, 0, 1, half, place >= 0, slope)
        bias_hi = key_bias(half, half, 1, half, place >= 0, slope)
        gk0, gv0, gq0 = part(own_ref[0, lo, kc], own_ref[0, lo, vc], bias_lo, lo, True)
        gk1, gv1, gq1 = part(own_ref[0, lo, kc], own_ref[0, lo, vc], bias_lo, hi, False)
        gk2, gv2, gq2 = part(own_ref[0, hi, kc], own_ref[0, hi, vc], bias_hi, hi, True)
        tail_ref[lo, kc] = gk0 + gk1
        tail_ref[lo, vc] = gv0 + gv1
        tail_ref[hi, kc] = gk2
        tail_ref[hi, vc] = gv2
        gq_ref[0, lo, kc] = ((total[:, lo] + gq0) * scale).T.astype(jnp.bfloat16)
        gq_ref[0, hi, kc] = ((total[:, hi] + gq1 + gq2) * scale).T.astype(jnp.bfloat16)


def attention_specs(seg_len, head_cols, comp_shape):
    pair = 2 * head_cols
    return [
        pl.BlockSpec(memory_space=pltpu.SMEM),
        pl.BlockSpec(memory_space=pltpu.SMEM),
        pl.BlockSpec((1, seg_len, head_cols), lambda s: (s, 0, 2)),
        pl.BlockSpec((1, seg_len, pair), lambda s: (s, 0, 0)),
        pl.BlockSpec((1, seg_len, pair), lambda s: (jnp.maximum(s - 1, 0), 0, 0)),
        pl.BlockSpec((1, seg_len, pair), lambda s: (0, 0, 0)),
        pl.BlockSpec(comp_shape, lambda s: (0, 0, 0)),
    ]


def attend_fwd(place, slope, heads, recv_mem, comp_ext, head_cols):
    seg_count, seg_len, _ = heads.shape
    local_heads = head_cols // HD
    return pl.pallas_call(
        fwd_kernel,
        grid=(seg_count,),
        in_specs=attention_specs(seg_len, head_cols, comp_ext.shape),
        out_specs=[
            pl.BlockSpec((1, seg_len, head_cols), lambda s: (s, 0, 0)),
            pl.BlockSpec((1, local_heads, seg_len), lambda s: (s, 0, 0)),
        ],
        out_shape=[
            jax.ShapeDtypeStruct((seg_count, seg_len, head_cols), jnp.bfloat16),
            jax.ShapeDtypeStruct((seg_count, local_heads, seg_len), jnp.float32),
        ],
        compiler_params=pltpu.CompilerParams(vmem_limit_bytes=VMEM_LIMIT),
        cost_estimate=pl.CostEstimate(flops=5 * 10**9, bytes_accessed=16 * 10**6, transcendentals=10**7),
        name="attend_fwd",
    )(place, slope, heads, heads, heads, recv_mem, comp_ext)


def attend_bwd(place, slope, heads, recv_mem, comp_ext, grad_heads, attn_out, lse, head_cols):
    seg_count, seg_len, _ = heads.shape
    local_heads = head_cols // HD
    pair = 2 * head_cols
    blocks = seg_count + 1
    return pl.pallas_call(
        bwd_kernel,
        grid=(seg_count,),
        in_specs=attention_specs(seg_len, head_cols, comp_ext.shape)
        + [
            pl.BlockSpec((1, seg_len, head_cols), lambda s: (s, 0, 0)),
            pl.BlockSpec((1, seg_len, head_cols), lambda s: (s, 0, 0)),
            pl.BlockSpec((1, local_heads, seg_len), lambda s: (s, 0, 0)),
        ],
        out_specs=[
            pl.BlockSpec((1, seg_len, head_cols), lambda s: (s, 0, 0)),
            pl.BlockSpec((1, seg_len, pair), lambda s: (lax.rem(s + blocks - 1, blocks), 0, 0)),
            pl.BlockSpec((seg_len, pair), lambda s: (0, 0)),
            pl.BlockSpec(comp_ext.shape, lambda s: (0, 0, 0)),
        ],
        out_shape=[
            jax.ShapeDtypeStruct((seg_count, seg_len, head_cols), jnp.bfloat16),
            jax.ShapeDtypeStruct((blocks, seg_len, pair), jnp.bfloat16),
            jax.ShapeDtypeStruct((seg_len, pair), jnp.float32),
            jax.ShapeDtypeStruct(comp_ext.shape, jnp.float32),
        ],
        compiler_params=pltpu.CompilerParams(vmem_limit_bytes=VMEM_LIMIT),
        cost_estimate=pl.CostEstimate(flops=12 * 10**9, bytes_accessed=24 * 10**6, transcendentals=10**7),
        name="attend_bwd",
    )(place, slope, heads, heads, heads, recv_mem, comp_ext, grad_heads, attn_out, lse)


def head_swap(value, bit):
    count = lax.axis_size("head")
    return lax.ppermute(value, "head", [(source, source ^ bit) for source in range(count)])


def gather_over_head(value):
    seg_count, quarter, width = value.shape
    head_index = lax.axis_index("head")
    far = head_swap(value, 2)
    near = head_swap(value, 1)
    far_near = head_swap(far, 1)
    blocks = lax.axis_size("head")
    whole = jnp.zeros((seg_count, blocks, quarter, width), value.dtype)
    for block, held in ((0, value), (1, near), (2, far), (3, far_near)):
        whole = lax.dynamic_update_slice(
            whole, held[:, None], (0, jnp.bitwise_xor(head_index, block), 0, 0)
        )
    return whole.reshape(seg_count, blocks * quarter, width)


def scatter_over_head(pieces):
    head_index = lax.axis_index("head")

    def term(bits):
        return pieces(jnp.bitwise_xor(head_index, bits))

    sent = jnp.stack([term(1), term(3)]).astype(jnp.bfloat16)
    got = head_swap(sent, 1).astype(jnp.float32)
    far = (term(2) + got[1]).astype(jnp.bfloat16)
    return term(0) + got[0] + head_swap(far, 2).astype(jnp.float32)


def per_device(tokens, wq, wk, wv, wo, w_up, w_down, gain_one, gain_two, w_comp, lengths, grad_out):
    seg_count, quarter, width = tokens.shape
    head_groups = lax.axis_size("head")
    blk_count = lax.axis_size("blk")
    devices = head_groups * blk_count
    seg_len = quarter * head_groups
    head_cols = width // head_groups
    local_heads = head_cols // HD
    comp_rows = seg_len // RATE
    pad_rows = (comp_rows + 15) // 16 * 16
    window = CSEGS + 1
    head_index = lax.axis_index("head")
    blk_index = lax.axis_index("blk")
    col_start = head_index * head_cols
    token_count = seg_count * quarter
    full_count = seg_count * seg_len
    comp_count = seg_count * pad_rows
    part = wq.shape[0]
    ff_part = w_down.shape[0]
    both = ("head", "blk")
    gains = jnp.pad(jnp.concatenate([gain_one, gain_two])[None], ((0, 7), (0, width - 2 * part)))
    first_pack = jnp.concatenate([wk, wv, wq, w_comp.reshape(RATE * part, width), gains], 0)
    second_pack = jnp.concatenate([wo, w_up.T, w_down], 0)
    first_all = lax.all_gather(first_pack, both, axis=0)
    second_all = lax.all_gather(second_pack, both, axis=0)
    full_tokens = gather_over_head(tokens)
    gain_first = first_all[:, 6 * part, :part].reshape(width).astype(jnp.float32)
    gain_second = first_all[:, 6 * part, part : 2 * part].reshape(width).astype(jnp.float32)
    mine = lax.dynamic_slice_in_dim(first_all[:, : 3 * part], col_start, head_cols, 2)
    wkvq = (
        mine.reshape(devices, 3, part, head_cols)
        .transpose(0, 2, 1, 3)
        .reshape(width, 3 * head_cols)
    )
    wkv = wkvq[:, : 2 * head_cols]
    wq_mine = wkvq[:, 2 * head_cols :]
    comp_matrix = (
        first_all[:, 3 * part : 6 * part]
        .reshape(devices, RATE, part, width)
        .transpose(1, 0, 2, 3)
        .reshape(RATE * width, width)
    )
    wo_all = second_all[:, :part].reshape(width, width)
    up_all = second_all[:, part : part + ff_part].reshape(devices * ff_part, width)
    down_all = second_all[:, part + ff_part :].reshape(devices * ff_part, width)

    full_rows = full_tokens.reshape(full_count, width).astype(jnp.float32)
    normed = layer_norm(full_rows, gain_first).astype(jnp.bfloat16)
    heads = jnp.dot(normed, wkvq, preferred_element_type=jnp.float32).astype(jnp.bfloat16)
    heads = heads.reshape(seg_count, seg_len, 3 * head_cols)
    grouped = normed.reshape(seg_count, seg_len, width)[:, : RATE * comp_rows].reshape(
        seg_count, comp_rows, RATE * width
    )
    grouped = jnp.pad(grouped, ((0, 0), (0, pad_rows - comp_rows), (0, 0))).reshape(
        comp_count, RATE * width
    )
    packed = jnp.dot(grouped, comp_matrix, preferred_element_type=jnp.float32).astype(jnp.bfloat16)
    comp_pair = (
        jnp.dot(packed, wkv, preferred_element_type=jnp.float32)
        .astype(jnp.bfloat16)
        .reshape(seg_count, pad_rows, 2 * head_cols)
    )
    compressed = lax.dynamic_slice_in_dim(packed, col_start, head_cols, 1).reshape(
        seg_count, pad_rows, head_cols
    )[:, :comp_rows]
    recv_mem, recv_comp = passed_along(
        (heads[seg_count - 1 :, :, : 2 * head_cols], comp_pair[seg_count - window :]), "blk", 1
    )
    comp_ext = jnp.concatenate([recv_comp, comp_pair], 0)
    order = jnp.arange(lengths.shape[0], dtype=jnp.int32)
    starts = jnp.sum(jnp.where(order[None, :] < order[:, None], lengths[None, :], 0), axis=1)
    seg_ids = blk_index * seg_count + jnp.arange(seg_count, dtype=jnp.int32)
    seg_place = seg_ids - jnp.max(
        jnp.where(starts[None, :] <= seg_ids[:, None], starts[None, :], 0), axis=1
    )
    head_ids = head_index * local_heads + jnp.arange(local_heads, dtype=jnp.int32)
    slopes = jnp.exp2(-head_ids.astype(jnp.float32)) / 64.0 * LOG2E
    attn_out, lse = attend_fwd(seg_place, slopes, heads, recv_mem, comp_ext, head_cols)
    mixed = lax.all_to_all(
        attn_out.reshape(seg_count, seg_len, 1, head_cols),
        "head",
        split_axis=1,
        concat_axis=2,
        tiled=True,
    ).reshape(token_count, width)
    token_rows = tokens.reshape(token_count, width).astype(jnp.float32)
    branch = jnp.dot(mixed, wo_all, preferred_element_type=jnp.float32)
    hidden = token_rows + branch
    normed_two = layer_norm(hidden, gain_second).astype(jnp.bfloat16)
    lifted = lax.dot_general(normed_two, up_all, COLS_IN, preferred_element_type=jnp.float32)
    active = jax.nn.silu(lifted).astype(jnp.bfloat16)
    ffn_term = jnp.dot(active, down_all, preferred_element_type=jnp.float32)
    out_tokens = (hidden + ffn_term).astype(jnp.bfloat16).reshape(tokens.shape)
    upstream = grad_out.reshape(token_count, width)
    grad_down = lax.dot_general(active, upstream, ROWS_IN, preferred_element_type=jnp.float32)
    grad_active = lax.dot_general(upstream, down_all, COLS_IN, preferred_element_type=jnp.float32)
    grad_lifted = (grad_active * silu_slope(lifted)).astype(jnp.bfloat16)
    grad_up = lax.dot_general(grad_lifted, normed_two, ROWS_IN, preferred_element_type=jnp.float32)
    grad_normed_two = jnp.dot(grad_lifted, up_all, preferred_element_type=jnp.float32)
    second_value, second_pull = jax.vjp(layer_norm, hidden, gain_second)
    grad_hidden_norm, grad_gain_two = second_pull(grad_normed_two)
    grad_hidden = upstream.astype(jnp.float32) + grad_hidden_norm
    grad_branch = grad_hidden.astype(jnp.bfloat16)
    grad_wo = lax.dot_general(mixed, grad_branch, ROWS_IN, preferred_element_type=jnp.float32)
    first_grads = jnp.concatenate(
        [
            grad_wo.astype(jnp.bfloat16).reshape(devices, part, width),
            grad_up.astype(jnp.bfloat16).reshape(devices, ff_part, width),
            grad_down.astype(jnp.bfloat16).reshape(devices, ff_part, width),
        ],
        1,
    )
    grad_mixed = lax.dot_general(
        grad_branch, wo_all, COLS_IN, preferred_element_type=jnp.float32
    ).astype(jnp.bfloat16)
    grad_mixed, first_grads = lax.optimization_barrier((grad_mixed, first_grads))
    first_sum = lax.psum_scatter(first_grads, both, scatter_dimension=0).astype(jnp.float32)
    grad_heads = lax.all_to_all(
        grad_mixed.reshape(seg_count, quarter, head_groups, head_cols),
        "head",
        split_axis=2,
        concat_axis=1,
        tiled=True,
    ).reshape(seg_count, seg_len, head_cols)
    grad_query, grad_pair, tail, grad_comp_ext = attend_bwd(
        seg_place, slopes, heads, recv_mem, comp_ext, grad_heads, attn_out, lse, head_cols
    )
    got_mem, got_comp = passed_along(
        (grad_pair[seg_count], grad_comp_ext[:window].astype(jnp.bfloat16)), "blk", -1
    )
    last_pair = (tail + got_mem.astype(jnp.float32)).astype(jnp.bfloat16)
    grad_pair = lax.dynamic_update_slice(grad_pair, last_pair[None], (seg_count - 1, 0, 0))
    comp_pair_grad = grad_comp_ext[window:] + jnp.pad(
        got_comp.astype(jnp.float32), ((seg_count - window, 0), (0, 0), (0, 0))
    )
    grad_kv = grad_pair[:seg_count].reshape(full_count, 2 * head_cols)
    grad_q = grad_query.reshape(full_count, head_cols)
    comp_grad_rows = comp_pair_grad.reshape(comp_count, 2 * head_cols).astype(jnp.bfloat16)
    grad_packed_part = lax.dot_general(
        comp_grad_rows, wkv, COLS_IN, preferred_element_type=jnp.float32
    )
    grad_packed_mine = scatter_over_head(
        lambda block: lax.dynamic_slice_in_dim(grad_packed_part, block * head_cols, head_cols, 1)
    ).astype(jnp.bfloat16)
    grad_grouped = lax.dot_general(
        grad_packed_part.astype(jnp.bfloat16), comp_matrix, COLS_IN, preferred_element_type=jnp.float32
    ).astype(jnp.bfloat16)
    grad_sent = jnp.pad(
        grad_grouped.reshape(seg_count, pad_rows, RATE * width)[:, :comp_rows].reshape(
            seg_count, RATE * comp_rows, width
        ),
        ((0, 0), (0, seg_len - RATE * comp_rows), (0, 0)),
    )
    grad_normed_part = (
        lax.dot_general(grad_q, wq_mine, COLS_IN, preferred_element_type=jnp.float32)
        + lax.dot_general(grad_kv, wkv, COLS_IN, preferred_element_type=jnp.float32)
    ).reshape(seg_count, head_groups, quarter, width) + grad_sent.reshape(
        seg_count, head_groups, quarter, width
    ).astype(jnp.float32)
    average = jnp.mean(full_rows, axis=-1, keepdims=True)
    center = full_rows - average
    spread = lax.rsqrt(jnp.mean(center * center, axis=-1, keepdims=True) + EPS)
    grad_gain_one = jnp.sum(grad_normed_part.reshape(full_count, width) * (center * spread), axis=0)
    grad_normed = scatter_over_head(
        lambda block: lax.dynamic_slice_in_dim(grad_normed_part, block, 1, 1)
    ).reshape(token_count, width)
    first_value, first_pull = jax.vjp(lambda rows: layer_norm(rows, gain_first), token_rows)
    (grad_rows_norm,) = first_pull(grad_normed)
    grad_tokens = (grad_hidden + grad_rows_norm).astype(jnp.bfloat16).reshape(tokens.shape)
    comp_term = lax.dot_general(packed, comp_grad_rows, ROWS_IN, preferred_element_type=jnp.float32)
    grad_wq = lax.dot_general(normed, grad_q, ROWS_IN, preferred_element_type=jnp.float32)
    grad_wkv = lax.dot_general(normed, grad_kv, ROWS_IN, preferred_element_type=jnp.float32) + comp_term
    grad_comp = lax.dot_general(
        grouped, grad_packed_mine, ROWS_IN, preferred_element_type=jnp.float32
    )

    def by_owner(value, kinds):
        return value.astype(jnp.bfloat16).reshape(
            kinds, head_groups, blk_count, part, head_cols
        ).transpose(2, 1, 0, 3, 4).reshape(blk_count, head_groups, kinds * part, head_cols)

    gain_rows = jnp.stack(
        [grad_gain_one.reshape(head_groups, blk_count, part), grad_gain_two.reshape(head_groups, blk_count, part)], 2
    ).transpose(1, 0, 2, 3).astype(jnp.bfloat16)
    second_grads = jnp.concatenate(
        [
            by_owner(jnp.concatenate([grad_wq, grad_wkv[:, :head_cols], grad_wkv[:, head_cols:]], 0), 3),
            by_owner(grad_comp, RATE),
            jnp.pad(gain_rows, ((0, 0), (0, 0), (0, 14), (0, head_cols - part))),
        ],
        2,
    )
    second_part = lax.psum_scatter(second_grads, "blk", scatter_dimension=0)
    second_sum = lax.all_to_all(second_part, "head", split_axis=0, concat_axis=0, tiled=True).astype(
        jnp.float32
    )
    gain_sum = jnp.sum(second_sum[:, 6 * part : 6 * part + 2, :part], axis=0)
    weight_sum = (
        second_sum[:, : 6 * part]
        .reshape(head_groups, 6, part, head_cols)
        .transpose(1, 2, 0, 3)
        .reshape(6, part, width)
    )
    return (
        out_tokens,
        compressed,
        grad_tokens,
        weight_sum[0],
        weight_sum[1],
        weight_sum[2],
        first_sum[:part],
        first_sum[part : part + ff_part].T,
        first_sum[part + ff_part :],
        gain_sum[0],
        gain_sum[1],
        weight_sum[3:],
    )


def solution(mesh):
    return jax.shard_map(
        per_device,
        mesh=mesh,
        in_specs=(
            P("blk", "head", None),
            P(("head", "blk"), None),
            P(("head", "blk"), None),
            P(("head", "blk"), None),
            P(("head", "blk"), None),
            P(None, ("head", "blk")),
            P(("head", "blk"), None),
            P(("head", "blk")),
            P(("head", "blk")),
            P(None, ("head", "blk"), None),
            P(),
            P("blk", "head", None),
        ),
        out_specs=(
            P("blk", "head", None),
            P("blk", None, "head"),
            P("blk", "head", None),
            P(("head", "blk"), None),
            P(("head", "blk"), None),
            P(("head", "blk"), None),
            P(("head", "blk"), None),
            P(None, ("head", "blk")),
            P(("head", "blk"), None),
            P(("head", "blk")),
            P(("head", "blk")),
            P(None, ("head", "blk"), None),
        ),
        check_vma=False,
    )
```

```python
import jax
import jax.numpy as jnp
from jax import lax
from jax.experimental import pallas as pl
from jax.experimental.pallas import tpu as pltpu
from jax.sharding import PartitionSpec as P

HD = 128
RATE = 3
CSEGS = 3


EPS = 1e-05
NEG = -1e30
ROWS_IN = (((0,), (0,)), ((), ()))
COLS_IN = (((1,), (1,)), ((), ()))


def passed_along(value, axis, steps):
    count = lax.axis_size(axis)
    leading, last = (max(0, -steps), min(count, count - steps))
    return lax.ppermute(value, axis, [(source, source + steps) for source in range(leading, last)])


def layer_norm(values, gain):
    average = jnp.mean(values, axis=-1, keepdims=True)
    center = values - average
    variance = jnp.mean(center * center, axis=-1, keepdims=True)
    return center * lax.rsqrt(variance + EPS) * gain


LOG2E = 1.4426950408889634
PAD_ROWS = 176
VMEM_LIMIT = 56 * 1024 * 1024


def key_bias(rows, base, step, valid_rows, open_, slope):
    row = lax.broadcasted_iota(jnp.int32, (rows, 1), 0)
    place = (base + step * row).astype(jnp.float32)
    return jnp.where((row < valid_rows) & open_, place * slope, NEG)


def fwd_kernel(place_ref, slope_ref, q_ref, own_ref, prev_ref, recv_ref, comp_ref, out_ref, lse_ref):
    step = pl.program_id(0)
    place = place_ref[step]
    seg_len = q_ref.shape[1]
    half = seg_len // 2
    pad_rows = comp_ref.shape[1]
    local_heads = q_ref.shape[2] // HD
    values_at = local_heads * HD
    factor = HD ** (-0.5) * LOG2E
    lower = lax.broadcasted_iota(jnp.int32, (half, half), 0) <= lax.broadcasted_iota(
        jnp.int32, (half, half), 1
    )
    for h in range(local_heads):
        kc = slice(h * HD, (h + 1) * HD)
        vc = slice(values_at + h * HD, values_at + (h + 1) * HD)
        slope = slope_ref[h]
        parts = []
        for piece in range(CSEGS):
            lag = CSEGS + 1 - piece
            bias = key_bias(pad_rows, RATE // 2 - lag * seg_len, RATE, seg_len // RATE, place >= lag, slope)
            parts.append((comp_ref[step + piece, :, kc], comp_ref[step + piece, :, vc], bias))
        bias = key_bias(seg_len, -seg_len, 1, seg_len, place >= 1, slope)
        is_first = step == 0
        parts.append(
            (
                jnp.where(is_first, recv_ref[0, :, kc], prev_ref[0, :, kc]),
                jnp.where(is_first, recv_ref[0, :, vc], prev_ref[0, :, vc]),
                bias,
            )
        )
        own_bias = [
            key_bias(half, n * half, 1, half, place >= 0, slope) for n in range(2)
        ]
        for n in range(2):
            query = q_ref[0, n * half : (n + 1) * half, kc]
            group = list(parts)
            for m in range(n + 1):
                rows = slice(m * half, (m + 1) * half)
                group.append((own_ref[0, rows, kc], own_ref[0, rows, vc], own_bias[m]))
            scores = []
            top = None
            for index, (k, v, bias) in enumerate(group):
                raw = lax.dot_general(k, query, COLS_IN, preferred_element_type=jnp.float32)
                raw = raw * factor + bias
                if index == len(group) - 1:
                    raw = jnp.where(lower, raw, NEG)
                scores.append(raw)
                peak = jnp.max(raw, axis=0, keepdims=True)
                top = peak if top is None else jnp.maximum(top, peak)
            total = jnp.zeros_like(top)
            result = jnp.zeros((HD, half), jnp.float32)
            for raw, (k, v, bias) in zip(scores, group):
                weight = jnp.exp2(raw - top)
                total = total + jnp.sum(weight, axis=0, keepdims=True)
                result = result + lax.dot_general(
                    v, weight.astype(jnp.bfloat16), ROWS_IN, preferred_element_type=jnp.float32
                )
            result = result * (1.0 / total)
            out_ref[0, n * half : (n + 1) * half, kc] = result.T.astype(jnp.bfloat16)
            lse_ref[0, h : h + 1, n * half : (n + 1) * half] = top + jnp.log(total) * LOG2E


def bwd_kernel(
    place_ref, slope_ref, q_ref, own_ref, prev_ref, recv_ref, comp_ref, grad_ref, att_ref, lse_ref,
    gq_ref, gkv_ref, tail_ref, gcomp_ref,
):
    step = pl.program_id(0)
    place = place_ref[step]
    seg_len = q_ref.shape[1]
    half = seg_len // 2
    pad_rows = comp_ref.shape[1]
    local_heads = q_ref.shape[2] // HD
    values_at = local_heads * HD
    scale = HD ** (-0.5)
    factor = scale * LOG2E
    is_first = step == 0
    lower = lax.broadcasted_iota(jnp.int32, (half, half), 0) <= lax.broadcasted_iota(
        jnp.int32, (half, half), 1
    )

    @pl.when(is_first)
    def _():
        tail_ref[...] = jnp.zeros_like(tail_ref)
        gcomp_ref[...] = jnp.zeros_like(gcomp_ref)

    for h in range(local_heads):
        kc = slice(h * HD, (h + 1) * HD)
        vc = slice(values_at + h * HD, values_at + (h + 1) * HD)
        slope = slope_ref[h]
        query = q_ref[0, :, kc]
        grad = grad_ref[0, :, kc]
        lse = lse_ref[0, h : h + 1, :]
        product = grad.astype(jnp.float32) * att_ref[0, :, kc].astype(jnp.float32)
        delta = jnp.sum(product.T, axis=0, keepdims=True)

        def part(k, v, bias, cols, masked):
            raw = lax.dot_general(k, query[cols], COLS_IN, preferred_element_type=jnp.float32)
            raw = raw * factor + bias
            if masked:
                raw = jnp.where(lower, raw, NEG)
            prob = jnp.exp2(raw - lse[:, cols])
            grad_prob = lax.dot_general(v, grad[cols], COLS_IN, preferred_element_type=jnp.float32)
            grad_score = (prob * (grad_prob - delta[:, cols])).astype(jnp.bfloat16)
            gk = jnp.dot(grad_score, query[cols], preferred_element_type=jnp.float32) * scale
            gv = jnp.dot(prob.astype(jnp.bfloat16), grad[cols], preferred_element_type=jnp.float32)
            gq = lax.dot_general(k, grad_score, ROWS_IN, preferred_element_type=jnp.float32)
            return gk, gv, gq

        every = slice(0, seg_len)
        total = jnp.zeros((HD, seg_len), jnp.float32)
        for piece in range(CSEGS):
            lag = CSEGS + 1 - piece
            bias = key_bias(pad_rows, RATE // 2 - lag * seg_len, RATE, seg_len // RATE, place >= lag, slope)
            gk, gv, gq = part(comp_ref[step + piece, :, kc], comp_ref[step + piece, :, vc], bias, every, False)
            gcomp_ref[step + piece, :, kc] += gk
            gcomp_ref[step + piece, :, vc] += gv
            total = total + gq
        for n in range(2):
            rows = slice(n * half, (n + 1) * half)
            bias = key_bias(half, n * half - seg_len, 1, half, place >= 1, slope)
            k = jnp.where(is_first, recv_ref[0, rows, kc], prev_ref[0, rows, kc])
            v = jnp.where(is_first, recv_ref[0, rows, vc], prev_ref[0, rows, vc])
            gk, gv, gq = part(k, v, bias, every, False)
            gkv_ref[0, rows, kc] = (tail_ref[rows, kc] + gk).astype(jnp.bfloat16)
            gkv_ref[0, rows, vc] = (tail_ref[rows, vc] + gv).astype(jnp.bfloat16)
            total = total + gq
        lo, hi = slice(0, half), slice(half, seg_len)
        bias_lo = key_bias(half, 0, 1, half, place >= 0, slope)
        bias_hi = key_bias(half, half, 1, half, place >= 0, slope)
        gk0, gv0, gq0 = part(own_ref[0, lo, kc], own_ref[0, lo, vc], bias_lo, lo, True)
        gk1, gv1, gq1 = part(own_ref[0, lo, kc], own_ref[0, lo, vc], bias_lo, hi, False)
        gk2, gv2, gq2 = part(own_ref[0, hi, kc], own_ref[0, hi, vc], bias_hi, hi, True)
        tail_ref[lo, kc] = gk0 + gk1
        tail_ref[lo, vc] = gv0 + gv1
        tail_ref[hi, kc] = gk2
        tail_ref[hi, vc] = gv2
        gq_ref[0, lo, kc] = ((total[:, lo] + gq0) * scale).T.astype(jnp.bfloat16)
        gq_ref[0, hi, kc] = ((total[:, hi] + gq1 + gq2) * scale).T.astype(jnp.bfloat16)


def attention_specs(seg_len, head_cols, comp_shape):
    pair = 2 * head_cols
    return [
        pl.BlockSpec(memory_space=pltpu.SMEM),
        pl.BlockSpec(memory_space=pltpu.SMEM),
        pl.BlockSpec((1, seg_len, head_cols), lambda s: (s, 0, 2)),
        pl.BlockSpec((1, seg_len, pair), lambda s: (s, 0, 0)),
        pl.BlockSpec((1, seg_len, pair), lambda s: (jnp.maximum(s - 1, 0), 0, 0)),
        pl.BlockSpec((1, seg_len, pair), lambda s: (0, 0, 0)),
        pl.BlockSpec(comp_shape, lambda s: (0, 0, 0)),
    ]


def attend_fwd(place, slope, heads, recv_mem, comp_ext, head_cols):
    seg_count, seg_len, _ = heads.shape
    local_heads = head_cols // HD
    return pl.pallas_call(
        fwd_kernel,
        grid=(seg_count,),
        in_specs=attention_specs(seg_len, head_cols, comp_ext.shape),
        out_specs=[
            pl.BlockSpec((1, seg_len, head_cols), lambda s: (s, 0, 0)),
            pl.BlockSpec((1, local_heads, seg_len), lambda s: (s, 0, 0)),
        ],
        out_shape=[
            jax.ShapeDtypeStruct((seg_count, seg_len, head_cols), jnp.bfloat16),
            jax.ShapeDtypeStruct((seg_count, local_heads, seg_len), jnp.float32),
        ],
        compiler_params=pltpu.CompilerParams(vmem_limit_bytes=VMEM_LIMIT),
        cost_estimate=pl.CostEstimate(flops=5 * 10**9, bytes_accessed=16 * 10**6, transcendentals=10**7),
        name="attend_fwd",
    )(place, slope, heads, heads, heads, recv_mem, comp_ext)


def attend_bwd(place, slope, heads, recv_mem, comp_ext, grad_heads, attn_out, lse, head_cols):
    seg_count, seg_len, _ = heads.shape
    local_heads = head_cols // HD
    pair = 2 * head_cols
    blocks = seg_count + 1
    return pl.pallas_call(
        bwd_kernel,
        grid=(seg_count,),
        in_specs=attention_specs(seg_len, head_cols, comp_ext.shape)
        + [
            pl.BlockSpec((1, seg_len, head_cols), lambda s: (s, 0, 0)),
            pl.BlockSpec((1, seg_len, head_cols), lambda s: (s, 0, 0)),
            pl.BlockSpec((1, local_heads, seg_len), lambda s: (s, 0, 0)),
        ],
        out_specs=[
            pl.BlockSpec((1, seg_len, head_cols), lambda s: (s, 0, 0)),
            pl.BlockSpec((1, seg_len, pair), lambda s: (lax.rem(s + blocks - 1, blocks), 0, 0)),
            pl.BlockSpec((seg_len, pair), lambda s: (0, 0)),
            pl.BlockSpec(comp_ext.shape, lambda s: (0, 0, 0)),
        ],
        out_shape=[
            jax.ShapeDtypeStruct((seg_count, seg_len, head_cols), jnp.bfloat16),
            jax.ShapeDtypeStruct((blocks, seg_len, pair), jnp.bfloat16),
            jax.ShapeDtypeStruct((seg_len, pair), jnp.float32),
            jax.ShapeDtypeStruct(comp_ext.shape, jnp.float32),
        ],
        compiler_params=pltpu.CompilerParams(vmem_limit_bytes=VMEM_LIMIT),
        cost_estimate=pl.CostEstimate(flops=12 * 10**9, bytes_accessed=24 * 10**6, transcendentals=10**7),
        name="attend_bwd",
    )(place, slope, heads, heads, heads, recv_mem, comp_ext, grad_heads, attn_out, lse)


def row_norm(values):
    average = jnp.mean(values, axis=-1, keepdims=True)
    center = values - average
    spread = lax.rsqrt(jnp.mean(center * center, axis=-1, keepdims=True) + EPS)
    return center * spread, spread


def norm_back(grad, unit, spread, gain):
    scaled = grad * gain
    along = jnp.mean(scaled * unit, axis=-1, keepdims=True)
    return spread * (scaled - jnp.mean(scaled, axis=-1, keepdims=True) - unit * along)


def ffn_kernel(
    up_ref, down_ref, wo_ref, mixed_ref, tokens_ref, grad_ref, gain_ref,
    out_ref, pack_ref, g_hidden_ref, g_gain_ref, g_mixed_ref, g_wo_ref,
    hidden, normed, result, g_normed,
):
    step = pl.program_id(0)
    width = mixed_ref.shape[1]
    ff_part = up_ref.shape[1]
    block = up_ref.shape[0] * ff_part

    @pl.when(step == 0)
    def _():
        branch = jnp.dot(
            mixed_ref[...], wo_ref[...].reshape(width, width), preferred_element_type=jnp.float32
        )
        rows = tokens_ref[...].astype(jnp.float32) + branch
        hidden[...] = rows
        unit, spread = row_norm(rows)
        normed[...] = (unit * gain_ref[...]).astype(jnp.bfloat16)
        result[...] = rows
        g_normed[...] = jnp.zeros_like(g_normed)

    up = up_ref[...].reshape(block, width)
    down = down_ref[...].reshape(block, width)
    grad = grad_ref[...]
    lifted = lax.dot_general(up, normed[...], COLS_IN, preferred_element_type=jnp.float32)
    sig = 0.5 * jnp.tanh(0.5 * lifted) + 0.5
    smooth = lifted * sig
    active = smooth.astype(jnp.bfloat16)
    g_active = lax.dot_general(down, grad, COLS_IN, preferred_element_type=jnp.float32)
    g_lifted = (g_active * (sig + smooth * (1.0 - sig))).astype(jnp.bfloat16)
    g_down = jnp.dot(active, grad, preferred_element_type=jnp.float32).astype(jnp.bfloat16)
    g_up = jnp.dot(g_lifted, normed[...], preferred_element_type=jnp.float32).astype(jnp.bfloat16)
    pack_ref[:, :ff_part] = g_up.reshape(up_ref.shape)
    pack_ref[:, ff_part : 2 * ff_part] = g_down.reshape(up_ref.shape)
    result[...] += lax.dot_general(active, down, ROWS_IN, preferred_element_type=jnp.float32)
    g_normed[...] += lax.dot_general(g_lifted, up, ROWS_IN, preferred_element_type=jnp.float32)

    @pl.when(step == pl.num_programs(0) - 1)
    def _():
        out_ref[...] = result[...].astype(jnp.bfloat16)
        unit, spread = row_norm(hidden[...])
        gn = g_normed[...]
        g_gain_ref[...] = jnp.sum(gn * unit, axis=0, keepdims=True)
        g_hidden = grad_ref[...].astype(jnp.float32) + norm_back(gn, unit, spread, gain_ref[...])
        g_hidden_ref[...] = g_hidden
        g_branch = g_hidden.astype(jnp.bfloat16)
        g_mixed_ref[...] = lax.dot_general(
            g_branch, wo_ref[...].reshape(width, width), COLS_IN, preferred_element_type=jnp.float32
        ).astype(jnp.bfloat16)
        g_wo_ref[...] = lax.dot_general(
            mixed_ref[...], g_branch, ROWS_IN, preferred_element_type=jnp.float32
        ).astype(jnp.bfloat16)


def feed_forward(pack, wo_part, ff_part, mixed, tokens, grad, gain):
    devices, pack_rows, width = pack.shape
    rows = mixed.shape[0]
    per_step = 512 // ff_part
    steps = devices // per_step
    if wo_part % 16 == 0:
        wo, wo_spec = pack, pl.BlockSpec(
            (devices, wo_part, width), lambda j: (0, 2 * ff_part // wo_part, 0)
        )
    else:
        wo = pack[:, 2 * ff_part :].reshape(width, width)
        wo_spec = pl.BlockSpec((width, width), lambda j: (0, 0))

    def fixed(shape):
        return pl.BlockSpec(shape, lambda j: (0,) * len(shape))

    flat = (rows, width)
    return pl.pallas_call(
        ffn_kernel,
        grid=(steps,),
        in_specs=[
            pl.BlockSpec((per_step, ff_part, width), lambda j: (j, 0, 0)),
            pl.BlockSpec((per_step, ff_part, width), lambda j: (j, 1, 0)),
            wo_spec,
            fixed(flat),
            fixed(flat),
            fixed(flat),
            fixed((1, width)),
        ],
        out_specs=[
            fixed(flat),
            pl.BlockSpec((per_step, pack_rows, width), lambda j: (j, 0, 0)),
            fixed(flat),
            fixed((1, width)),
            fixed(flat),
            fixed((width, width)),
        ],
        out_shape=[
            jax.ShapeDtypeStruct(flat, jnp.bfloat16),
            jax.ShapeDtypeStruct(pack.shape, jnp.bfloat16),
            jax.ShapeDtypeStruct(flat, jnp.float32),
            jax.ShapeDtypeStruct((1, width), jnp.float32),
            jax.ShapeDtypeStruct(flat, jnp.bfloat16),
            jax.ShapeDtypeStruct((width, width), jnp.bfloat16),
        ],
        scratch_shapes=[
            pltpu.VMEM(flat, jnp.float32),
            pltpu.VMEM(flat, jnp.bfloat16),
            pltpu.VMEM(flat, jnp.float32),
            pltpu.VMEM(flat, jnp.float32),
        ],
        compiler_params=pltpu.CompilerParams(vmem_limit_bytes=VMEM_LIMIT),
        cost_estimate=pl.CostEstimate(flops=42 * 10**9, bytes_accessed=50 * 10**6, transcendentals=4 * 10**6),
        name="feed_forward",
    )(pack, pack, wo, mixed, tokens, grad, gain)


def head_swap(value, bit):
    count = lax.axis_size("head")
    return lax.ppermute(value, "head", [(source, source ^ bit) for source in range(count)])


def gather_over_head(value):
    seg_count, quarter, width = value.shape
    head_index = lax.axis_index("head")
    far = head_swap(value, 2)
    near = head_swap(value, 1)
    far_near = head_swap(far, 1)
    blocks = lax.axis_size("head")
    whole = jnp.zeros((seg_count, blocks, quarter, width), value.dtype)
    for block, held in ((0, value), (1, near), (2, far), (3, far_near)):
        whole = lax.dynamic_update_slice(
            whole, held[:, None], (0, jnp.bitwise_xor(head_index, block), 0, 0)
        )
    return whole.reshape(seg_count, blocks * quarter, width)


def scatter_over_head(pieces):
    head_index = lax.axis_index("head")

    def term(bits):
        return pieces(jnp.bitwise_xor(head_index, bits))

    sent = jnp.stack([term(1), term(3)]).astype(jnp.bfloat16)
    got = head_swap(sent, 1).astype(jnp.float32)
    far = (term(2) + got[1]).astype(jnp.bfloat16)
    return term(0) + got[0] + head_swap(far, 2).astype(jnp.float32)


def per_device(tokens, wq, wk, wv, wo, w_up, w_down, gain_one, gain_two, w_comp, lengths, grad_out):
    seg_count, quarter, width = tokens.shape
    head_groups = lax.axis_size("head")
    blk_count = lax.axis_size("blk")
    devices = head_groups * blk_count
    seg_len = quarter * head_groups
    head_cols = width // head_groups
    local_heads = head_cols // HD
    comp_rows = seg_len // RATE
    pad_rows = (comp_rows + 15) // 16 * 16
    window = CSEGS + 1
    head_index = lax.axis_index("head")
    blk_index = lax.axis_index("blk")
    col_start = head_index * head_cols
    token_count = seg_count * quarter
    full_count = seg_count * seg_len
    comp_count = seg_count * pad_rows
    part = wq.shape[0]
    ff_part = w_down.shape[0]
    both = ("head", "blk")
    gains = jnp.pad(jnp.concatenate([gain_one, gain_two])[None], ((0, 7), (0, width - 2 * part)))
    first_pack = jnp.concatenate([wk, wv, wq, w_comp.reshape(RATE * part, width), gains], 0)
    second_pack = jnp.concatenate([w_up.T, w_down, wo], 0)
    first_all = lax.all_gather(first_pack, both, axis=0)
    second_all = lax.all_gather(second_pack, both, axis=0)
    full_tokens = gather_over_head(tokens)
    gain_first = first_all[:, 6 * part, :part].reshape(width).astype(jnp.float32)
    gain_second = first_all[:, 6 * part, part : 2 * part].reshape(width).astype(jnp.float32)
    mine = lax.dynamic_slice_in_dim(first_all[:, : 3 * part], col_start, head_cols, 2)
    wkvq = (
        mine.reshape(devices, 3, part, head_cols)
        .transpose(0, 2, 1, 3)
        .reshape(width, 3 * head_cols)
    )
    wkv = wkvq[:, : 2 * head_cols]
    wq_mine = wkvq[:, 2 * head_cols :]
    comp_matrix = (
        first_all[:, 3 * part : 6 * part]
        .reshape(devices, RATE, part, width)
        .transpose(1, 0, 2, 3)
        .reshape(RATE * width, width)
    )
    full_rows = full_tokens.reshape(full_count, width).astype(jnp.float32)
    normed = layer_norm(full_rows, gain_first).astype(jnp.bfloat16)
    heads = jnp.dot(normed, wkvq, preferred_element_type=jnp.float32).astype(jnp.bfloat16)
    heads = heads.reshape(seg_count, seg_len, 3 * head_cols)
    grouped = normed.reshape(seg_count, seg_len, width)[:, : RATE * comp_rows].reshape(
        seg_count, comp_rows, RATE * width
    )
    grouped = jnp.pad(grouped, ((0, 0), (0, pad_rows - comp_rows), (0, 0))).reshape(
        comp_count, RATE * width
    )
    packed = jnp.dot(grouped, comp_matrix, preferred_element_type=jnp.float32).astype(jnp.bfloat16)
    comp_pair = (
        jnp.dot(packed, wkv, preferred_element_type=jnp.float32)
        .astype(jnp.bfloat16)
        .reshape(seg_count, pad_rows, 2 * head_cols)
    )
    compressed = lax.dynamic_slice_in_dim(packed, col_start, head_cols, 1).reshape(
        seg_count, pad_rows, head_cols
    )[:, :comp_rows]
    recv_mem, recv_comp = passed_along(
        (heads[seg_count - 1 :, :, : 2 * head_cols], comp_pair[seg_count - window :]), "blk", 1
    )
    comp_ext = jnp.concatenate([recv_comp, comp_pair], 0)
    order = jnp.arange(lengths.shape[0], dtype=jnp.int32)
    starts = jnp.sum(jnp.where(order[None, :] < order[:, None], lengths[None, :], 0), axis=1)
    seg_ids = blk_index * seg_count + jnp.arange(seg_count, dtype=jnp.int32)
    seg_place = seg_ids - jnp.max(
        jnp.where(starts[None, :] <= seg_ids[:, None], starts[None, :], 0), axis=1
    )
    head_ids = head_index * local_heads + jnp.arange(local_heads, dtype=jnp.int32)
    slopes = jnp.exp2(-head_ids.astype(jnp.float32)) / 64.0 * LOG2E
    attn_out, lse = attend_fwd(seg_place, slopes, heads, recv_mem, comp_ext, head_cols)
    mixed = lax.all_to_all(
        attn_out.reshape(seg_count, seg_len, 1, head_cols),
        "head",
        split_axis=1,
        concat_axis=2,
        tiled=True,
    ).reshape(token_count, width)
    token_rows = tokens.reshape(token_count, width).astype(jnp.float32)
    result_rows, first_grads, grad_hidden, grad_gain_two, grad_mixed, grad_wo = feed_forward(
        second_all,
        part,
        ff_part,
        mixed,
        tokens.reshape(token_count, width),
        grad_out.reshape(token_count, width),
        gain_second[None],
    )
    out_tokens = result_rows.reshape(tokens.shape)
    first_grads = lax.dynamic_update_slice(
        first_grads, grad_wo.reshape(devices, part, width), (0, 2 * ff_part, 0)
    )
    grad_mixed, first_grads = lax.optimization_barrier((grad_mixed, first_grads))
    first_sum = lax.psum_scatter(first_grads, both, scatter_dimension=0)
    grad_heads = lax.all_to_all(
        grad_mixed.reshape(seg_count, quarter, head_groups, head_cols),
        "head",
        split_axis=2,
        concat_axis=1,
        tiled=True,
    ).reshape(seg_count, seg_len, head_cols)
    grad_query, grad_pair, tail, grad_comp_ext = attend_bwd(
        seg_place, slopes, heads, recv_mem, comp_ext, grad_heads, attn_out, lse, head_cols
    )
    got_mem, got_comp = passed_along(
        (grad_pair[seg_count], grad_comp_ext[:window].astype(jnp.bfloat16)), "blk", -1
    )
    last_pair = (tail + got_mem.astype(jnp.float32)).astype(jnp.bfloat16)
    grad_pair = lax.dynamic_update_slice(grad_pair, last_pair[None], (seg_count - 1, 0, 0))
    comp_pair_grad = grad_comp_ext[window:] + jnp.pad(
        got_comp.astype(jnp.float32), ((seg_count - window, 0), (0, 0), (0, 0))
    )
    grad_kv = grad_pair[:seg_count].reshape(full_count, 2 * head_cols)
    grad_q = grad_query.reshape(full_count, head_cols)
    comp_grad_rows = comp_pair_grad.reshape(comp_count, 2 * head_cols).astype(jnp.bfloat16)
    grad_packed_part = lax.dot_general(
        comp_grad_rows, wkv, COLS_IN, preferred_element_type=jnp.float32
    )
    grad_packed_mine = scatter_over_head(
        lambda block: lax.dynamic_slice_in_dim(grad_packed_part, block * head_cols, head_cols, 1)
    ).astype(jnp.bfloat16)
    grad_grouped = lax.dot_general(
        grad_packed_part.astype(jnp.bfloat16), comp_matrix, COLS_IN, preferred_element_type=jnp.float32
    ).astype(jnp.bfloat16)
    grad_sent = jnp.pad(
        grad_grouped.reshape(seg_count, pad_rows, RATE * width)[:, :comp_rows].reshape(
            seg_count, RATE * comp_rows, width
        ),
        ((0, 0), (0, seg_len - RATE * comp_rows), (0, 0)),
    )
    grad_normed_part = (
        lax.dot_general(grad_q, wq_mine, COLS_IN, preferred_element_type=jnp.float32)
        + lax.dot_general(grad_kv, wkv, COLS_IN, preferred_element_type=jnp.float32)
    ).reshape(seg_count, head_groups, quarter, width) + grad_sent.reshape(
        seg_count, head_groups, quarter, width
    ).astype(jnp.float32)
    average = jnp.mean(full_rows, axis=-1, keepdims=True)
    center = full_rows - average
    spread = lax.rsqrt(jnp.mean(center * center, axis=-1, keepdims=True) + EPS)
    grad_gain_one = jnp.sum(grad_normed_part.reshape(full_count, width) * (center * spread), axis=0)
    grad_normed = scatter_over_head(
        lambda block: lax.dynamic_slice_in_dim(grad_normed_part, block, 1, 1)
    ).reshape(token_count, width)
    first_value, first_pull = jax.vjp(lambda rows: layer_norm(rows, gain_first), token_rows)
    (grad_rows_norm,) = first_pull(grad_normed)
    grad_tokens = (grad_hidden + grad_rows_norm).astype(jnp.bfloat16).reshape(tokens.shape)
    comp_term = lax.dot_general(packed, comp_grad_rows, ROWS_IN, preferred_element_type=jnp.float32)
    grad_wq = lax.dot_general(normed, grad_q, ROWS_IN, preferred_element_type=jnp.float32)
    grad_wkv = lax.dot_general(normed, grad_kv, ROWS_IN, preferred_element_type=jnp.float32) + comp_term
    grad_comp = lax.dot_general(
        grouped, grad_packed_mine, ROWS_IN, preferred_element_type=jnp.float32
    )

    def by_owner(value, kinds):
        return value.astype(jnp.bfloat16).reshape(
            kinds, head_groups, blk_count, part, head_cols
        ).transpose(2, 1, 0, 3, 4).reshape(blk_count, head_groups, kinds * part, head_cols)

    gain_rows = jnp.stack(
        [grad_gain_one.reshape(head_groups, blk_count, part), grad_gain_two.reshape(head_groups, blk_count, part)], 2
    ).transpose(1, 0, 2, 3).astype(jnp.bfloat16)
    second_grads = jnp.concatenate(
        [
            by_owner(jnp.concatenate([grad_wq, grad_wkv[:, :head_cols], grad_wkv[:, head_cols:]], 0), 3),
            by_owner(grad_comp, RATE),
            jnp.pad(gain_rows, ((0, 0), (0, 0), (0, 14), (0, head_cols - part))),
        ],
        2,
    )
    second_grads, first_sum = lax.optimization_barrier((second_grads, first_sum))
    first_sum = first_sum.astype(jnp.float32)
    second_part = lax.psum_scatter(second_grads, "blk", scatter_dimension=0)
    second_sum = lax.all_to_all(second_part, "head", split_axis=0, concat_axis=0, tiled=True).astype(
        jnp.float32
    )
    gain_sum = jnp.sum(second_sum[:, 6 * part : 6 * part + 2, :part], axis=0)
    weight_sum = (
        second_sum[:, : 6 * part]
        .reshape(head_groups, 6, part, head_cols)
        .transpose(1, 2, 0, 3)
        .reshape(6, part, width)
    )
    return (
        out_tokens,
        compressed,
        grad_tokens,
        weight_sum[0],
        weight_sum[1],
        weight_sum[2],
        first_sum[2 * ff_part :],
        first_sum[:ff_part].T,
        first_sum[ff_part : 2 * ff_part],
        gain_sum[0],
        gain_sum[1],
        weight_sum[3:],
    )


def solution(mesh):
    return jax.shard_map(
        per_device,
        mesh=mesh,
        in_specs=(
            P("blk", "head", None),
            P(("head", "blk"), None),
            P(("head", "blk"), None),
            P(("head", "blk"), None),
            P(("head", "blk"), None),
            P(None, ("head", "blk")),
            P(("head", "blk"), None),
            P(("head", "blk")),
            P(("head", "blk")),
            P(None, ("head", "blk"), None),
            P(),
            P("blk", "head", None),
        ),
        out_specs=(
            P("blk", "head", None),
            P("blk", None, "head"),
            P("blk", "head", None),
            P(("head", "blk"), None),
            P(("head", "blk"), None),
            P(("head", "blk"), None),
            P(("head", "blk"), None),
            P(None, ("head", "blk")),
            P(("head", "blk"), None),
            P(("head", "blk")),
            P(("head", "blk")),
            P(None, ("head", "blk"), None),
        ),
        check_vma=False,
    )
```

```python
import jax
import jax.numpy as jnp
from jax import lax
from jax.experimental import pallas as pl
from jax.experimental.pallas import tpu as pltpu
from jax.sharding import PartitionSpec as P

HD = 128
RATE = 3
CSEGS = 3


EPS = 1e-05
NEG = -1e30
ROWS_IN = (((0,), (0,)), ((), ()))
COLS_IN = (((1,), (1,)), ((), ()))


def passed_along(value, axis, steps):
    count = lax.axis_size(axis)
    leading, last = (max(0, -steps), min(count, count - steps))
    return lax.ppermute(value, axis, [(source, source + steps) for source in range(leading, last)])


LOG2E = 1.4426950408889634
PAD_ROWS = 176
VMEM_LIMIT = 56 * 1024 * 1024


def key_bias(rows, base, step, valid_rows, open_, slope):
    row = lax.broadcasted_iota(jnp.int32, (rows, 1), 0)
    place = (base + step * row).astype(jnp.float32)
    return jnp.where((row < valid_rows) & open_, place * slope, NEG)


def fwd_kernel(place_ref, slope_ref, q_ref, own_ref, prev_ref, recv_ref, comp_ref, out_ref, lse_ref):
    step = pl.program_id(0)
    place = place_ref[step]
    seg_len = q_ref.shape[1]
    half = seg_len // 2
    pad_rows = comp_ref.shape[1]
    local_heads = q_ref.shape[2] // HD
    values_at = local_heads * HD
    factor = HD ** (-0.5) * LOG2E
    lower = lax.broadcasted_iota(jnp.int32, (half, half), 0) <= lax.broadcasted_iota(
        jnp.int32, (half, half), 1
    )
    for h in range(local_heads):
        kc = slice(h * HD, (h + 1) * HD)
        vc = slice(values_at + h * HD, values_at + (h + 1) * HD)
        slope = slope_ref[h]
        parts = []
        for piece in range(CSEGS):
            lag = CSEGS + 1 - piece
            bias = key_bias(pad_rows, RATE // 2 - lag * seg_len, RATE, seg_len // RATE, place >= lag, slope)
            parts.append((comp_ref[step + piece, :, kc], comp_ref[step + piece, :, vc], bias))
        bias = key_bias(seg_len, -seg_len, 1, seg_len, place >= 1, slope)
        is_first = step == 0
        parts.append(
            (
                jnp.where(is_first, recv_ref[0, :, kc], prev_ref[0, :, kc]),
                jnp.where(is_first, recv_ref[0, :, vc], prev_ref[0, :, vc]),
                bias,
            )
        )
        own_bias = [
            key_bias(half, n * half, 1, half, place >= 0, slope) for n in range(2)
        ]
        for n in range(2):
            query = q_ref[0, n * half : (n + 1) * half, kc]
            group = list(parts)
            for m in range(n + 1):
                rows = slice(m * half, (m + 1) * half)
                group.append((own_ref[0, rows, kc], own_ref[0, rows, vc], own_bias[m]))
            scores = []
            top = None
            for index, (k, v, bias) in enumerate(group):
                raw = lax.dot_general(k, query, COLS_IN, preferred_element_type=jnp.float32)
                raw = raw * factor + bias
                if index == len(group) - 1:
                    raw = jnp.where(lower, raw, NEG)
                scores.append(raw)
                peak = jnp.max(raw, axis=0, keepdims=True)
                top = peak if top is None else jnp.maximum(top, peak)
            total = jnp.zeros_like(top)
            result = jnp.zeros((HD, half), jnp.float32)
            for raw, (k, v, bias) in zip(scores, group):
                weight = jnp.exp2(raw - top)
                total = total + jnp.sum(weight, axis=0, keepdims=True)
                result = result + lax.dot_general(
                    v, weight.astype(jnp.bfloat16), ROWS_IN, preferred_element_type=jnp.float32
                )
            result = result * (1.0 / total)
            out_ref[0, n * half : (n + 1) * half, kc] = result.T.astype(jnp.bfloat16)
            lse_ref[0, h : h + 1, n * half : (n + 1) * half] = top + jnp.log(total) * LOG2E


def bwd_kernel(
    place_ref, slope_ref, q_ref, own_ref, prev_ref, recv_ref, comp_ref, head_ref, g0, g1, g2, g3, att_ref, lse_ref,
    gq_ref, gkv_ref, tail_ref, gcomp_ref, grad_ref,
):
    step = pl.program_id(0)
    place = place_ref[step]
    seg_len = q_ref.shape[1]
    half = seg_len // 2
    pad_rows = comp_ref.shape[1]
    local_heads = q_ref.shape[2] // HD
    values_at = local_heads * HD
    scale = HD ** (-0.5)
    factor = scale * LOG2E
    is_first = step == 0
    lower = lax.broadcasted_iota(jnp.int32, (half, half), 0) <= lax.broadcasted_iota(
        jnp.int32, (half, half), 1
    )

    @pl.when(is_first)
    def _():
        tail_ref[...] = jnp.zeros_like(tail_ref)
        gcomp_ref[...] = jnp.zeros_like(gcomp_ref)

    place_rows(head_ref[0], (g0, g1, g2, g3), grad_ref)
    for h in range(local_heads):
        kc = slice(h * HD, (h + 1) * HD)
        vc = slice(values_at + h * HD, values_at + (h + 1) * HD)
        slope = slope_ref[h]
        query = q_ref[0, :, kc]
        grad = grad_ref[:, kc]
        lse = lse_ref[0, h : h + 1, :]
        product = grad.astype(jnp.float32) * att_ref[0, :, kc].astype(jnp.float32)
        delta = jnp.sum(product.T, axis=0, keepdims=True)

        def part(k, v, bias, cols, masked):
            raw = lax.dot_general(k, query[cols], COLS_IN, preferred_element_type=jnp.float32)
            raw = raw * factor + bias
            if masked:
                raw = jnp.where(lower, raw, NEG)
            prob = jnp.exp2(raw - lse[:, cols])
            grad_prob = lax.dot_general(v, grad[cols], COLS_IN, preferred_element_type=jnp.float32)
            grad_score = (prob * (grad_prob - delta[:, cols])).astype(jnp.bfloat16)
            gk = jnp.dot(grad_score, query[cols], preferred_element_type=jnp.float32) * scale
            gv = jnp.dot(prob.astype(jnp.bfloat16), grad[cols], preferred_element_type=jnp.float32)
            gq = lax.dot_general(k, grad_score, ROWS_IN, preferred_element_type=jnp.float32)
            return gk, gv, gq

        every = slice(0, seg_len)
        total = jnp.zeros((HD, seg_len), jnp.float32)
        for piece in range(CSEGS):
            lag = CSEGS + 1 - piece
            bias = key_bias(pad_rows, RATE // 2 - lag * seg_len, RATE, seg_len // RATE, place >= lag, slope)
            gk, gv, gq = part(comp_ref[step + piece, :, kc], comp_ref[step + piece, :, vc], bias, every, False)
            gcomp_ref[step + piece, :, kc] += gk
            gcomp_ref[step + piece, :, vc] += gv
            total = total + gq
        for n in range(2):
            rows = slice(n * half, (n + 1) * half)
            bias = key_bias(half, n * half - seg_len, 1, half, place >= 1, slope)
            k = jnp.where(is_first, recv_ref[0, rows, kc], prev_ref[0, rows, kc])
            v = jnp.where(is_first, recv_ref[0, rows, vc], prev_ref[0, rows, vc])
            gk, gv, gq = part(k, v, bias, every, False)
            gkv_ref[0, rows, kc] = (tail_ref[rows, kc] + gk).astype(jnp.bfloat16)
            gkv_ref[0, rows, vc] = (tail_ref[rows, vc] + gv).astype(jnp.bfloat16)
            total = total + gq
        lo, hi = slice(0, half), slice(half, seg_len)
        bias_lo = key_bias(half, 0, 1, half, place >= 0, slope)
        bias_hi = key_bias(half, half, 1, half, place >= 0, slope)
        gk0, gv0, gq0 = part(own_ref[0, lo, kc], own_ref[0, lo, vc], bias_lo, lo, True)
        gk1, gv1, gq1 = part(own_ref[0, lo, kc], own_ref[0, lo, vc], bias_lo, hi, False)
        gk2, gv2, gq2 = part(own_ref[0, hi, kc], own_ref[0, hi, vc], bias_hi, hi, True)
        tail_ref[lo, kc] = gk0 + gk1
        tail_ref[lo, vc] = gv0 + gv1
        tail_ref[hi, kc] = gk2
        tail_ref[hi, vc] = gv2
        gq_ref[0, lo, kc] = ((total[:, lo] + gq0) * scale).T.astype(jnp.bfloat16)
        gq_ref[0, hi, kc] = ((total[:, hi] + gq1 + gq2) * scale).T.astype(jnp.bfloat16)


def attention_specs(seg_len, head_cols, comp_shape):
    pair = 2 * head_cols
    return [
        pl.BlockSpec(memory_space=pltpu.SMEM),
        pl.BlockSpec(memory_space=pltpu.SMEM),
        pl.BlockSpec((1, seg_len, head_cols), lambda s: (s, 0, 2)),
        pl.BlockSpec((1, seg_len, pair), lambda s: (s, 0, 0)),
        pl.BlockSpec((1, seg_len, pair), lambda s: (jnp.maximum(s - 1, 0), 0, 0)),
        pl.BlockSpec((1, seg_len, pair), lambda s: (0, 0, 0)),
        pl.BlockSpec(comp_shape, lambda s: (0, 0, 0)),
    ]


def attend_fwd(place, slope, heads, recv_mem, comp_ext, head_cols):
    seg_count, seg_len, _ = heads.shape
    local_heads = head_cols // HD
    return pl.pallas_call(
        fwd_kernel,
        grid=(seg_count,),
        in_specs=attention_specs(seg_len, head_cols, comp_ext.shape),
        out_specs=[
            pl.BlockSpec((1, seg_len, head_cols), lambda s: (s, 0, 0)),
            pl.BlockSpec((1, local_heads, seg_len), lambda s: (s, 0, 0)),
        ],
        out_shape=[
            jax.ShapeDtypeStruct((seg_count, seg_len, head_cols), jnp.bfloat16),
            jax.ShapeDtypeStruct((seg_count, local_heads, seg_len), jnp.float32),
        ],
        compiler_params=pltpu.CompilerParams(vmem_limit_bytes=VMEM_LIMIT),
        cost_estimate=pl.CostEstimate(flops=5 * 10**9, bytes_accessed=16 * 10**6, transcendentals=10**7),
        name="attend_fwd",
    )(place, slope, heads, heads, heads, recv_mem, comp_ext)


def attend_bwd(head, place, slope, heads, recv_mem, comp_ext, grad_mixed, attn_out, lse, head_cols):
    seg_count, seg_len, _ = heads.shape
    local_heads = head_cols // HD
    pair = 2 * head_cols
    blocks = seg_count + 1
    return pl.pallas_call(
        bwd_kernel,
        grid=(seg_count,),
        in_specs=attention_specs(seg_len, head_cols, comp_ext.shape)
        + [pl.BlockSpec(memory_space=pltpu.SMEM)]
        + [by_segment(grad_mixed[0].shape[1:])] * 4
        + [by_segment((seg_len, head_cols)), by_segment((local_heads, seg_len))],
        out_specs=[
            pl.BlockSpec((1, seg_len, head_cols), lambda s: (s, 0, 0)),
            pl.BlockSpec((1, seg_len, pair), lambda s: (lax.rem(s + blocks - 1, blocks), 0, 0)),
            pl.BlockSpec((seg_len, pair), lambda s: (0, 0)),
            pl.BlockSpec(comp_ext.shape, lambda s: (0, 0, 0)),
        ],
        out_shape=[
            jax.ShapeDtypeStruct((seg_count, seg_len, head_cols), jnp.bfloat16),
            jax.ShapeDtypeStruct((blocks, seg_len, pair), jnp.bfloat16),
            jax.ShapeDtypeStruct((seg_len, pair), jnp.float32),
            jax.ShapeDtypeStruct(comp_ext.shape, jnp.float32),
        ],
        scratch_shapes=[pltpu.VMEM((seg_len, head_cols), jnp.bfloat16)],
        compiler_params=pltpu.CompilerParams(vmem_limit_bytes=VMEM_LIMIT),
        cost_estimate=pl.CostEstimate(flops=12 * 10**9, bytes_accessed=24 * 10**6, transcendentals=10**7),
        name="attend_bwd",
    )(place, slope, heads, heads, heads, recv_mem, comp_ext, head, *grad_mixed, attn_out, lse)


def row_norm(values):
    average = jnp.mean(values, axis=-1, keepdims=True)
    center = values - average
    spread = lax.rsqrt(jnp.mean(center * center, axis=-1, keepdims=True) + EPS)
    return center * spread, spread


def norm_back(grad, unit, spread, gain):
    scaled = grad * gain
    along = jnp.mean(scaled * unit, axis=-1, keepdims=True)
    return spread * (scaled - jnp.mean(scaled, axis=-1, keepdims=True) - unit * along)


def place_rows(head, pieces, target):
    for bits, piece in enumerate(pieces):
        rows = piece.shape[1]
        at = pl.multiple_of(jnp.bitwise_xor(head, bits) * rows, rows)
        target[pl.ds(at, rows), :] = piece[0].astype(target.dtype)


def hand_out(head, source, keep_ref, sent_ref):
    rows = keep_ref.shape[2]
    for bits, (ref, slot) in enumerate(
        ((keep_ref, 0), (sent_ref, 0), (keep_ref, 1), (sent_ref, 1))
    ):
        at = pl.multiple_of(jnp.bitwise_xor(head, bits) * rows, rows)
        ref[slot, 0] = source[pl.ds(at, rows), :].astype(ref.dtype)


def prep_kernel(
    head_ref, t0, t1, t2, t3, gain_ref, w_ref, heads_ref, normed_ref, grouped_ref, packed_ref, spread
):
    head = head_ref[0]
    quarter, width = t0.shape[1:]
    seg_len = heads_ref.shape[1]
    head_cols = w_ref.shape[2]
    pad_rows = grouped_ref.shape[1]
    tiles = width // 128
    for bits, piece in enumerate((t0, t1, t2, t3)):
        unit, _ = row_norm(piece[0].astype(jnp.float32))
        normed = (unit * gain_ref[...]).astype(jnp.bfloat16)
        at = pl.multiple_of(jnp.bitwise_xor(head, bits) * quarter, quarter)
        normed_ref[0, pl.ds(at, quarter), :] = normed
        wide = normed.astype(jnp.float32)
        for c in range(tiles):
            spread[c, pl.ds(at, quarter), :] = wide[:, c * 128 : (c + 1) * 128]
    last = spread[:, seg_len - 8 : seg_len, :]
    row = lax.broadcasted_iota(jnp.int32, last.shape, 1)
    spread[:, seg_len - 8 : seg_len, :] = jnp.where(row < 8 - seg_len % RATE, last, 0.0)
    spread[:, seg_len:, :] = jnp.zeros((tiles, spread.shape[1] - seg_len, 128), jnp.float32)
    rows = normed_ref[0]
    for n in range(3):
        heads_ref[0, :, n * head_cols : (n + 1) * head_cols] = jnp.dot(
            rows, w_ref[n], preferred_element_type=jnp.float32
        ).astype(jnp.bfloat16)
    total = jnp.zeros((pad_rows, head_cols), jnp.float32)
    for tap in range(RATE):
        for c in range(tiles):
            at = tap * width + c * 128
            grouped_ref[0, :, at : at + 128] = spread[
                c, pl.ds(tap, pad_rows, stride=RATE), :
            ].astype(jnp.bfloat16)
        total = total + jnp.dot(
            grouped_ref[0, :, tap * width : (tap + 1) * width],
            w_ref[3 + tap],
            preferred_element_type=jnp.float32,
        )
    packed_ref[0] = total.astype(jnp.bfloat16)


def fixed(shape):
    return pl.BlockSpec(shape, lambda s: (0,) * len(shape), pipeline_mode=pl.Buffered(1))


def by_segment(shape):
    return pl.BlockSpec((1,) + shape, lambda s: (s,) + (0,) * len(shape))


def piece_specs(quarter, width):
    spec = pl.BlockSpec((2, 1, quarter, width), lambda s: (0, s, 0, 0))
    return [spec, spec]


def piece_shapes(seg_count, quarter, width):
    shape = jax.ShapeDtypeStruct((2, seg_count, quarter, width), jnp.bfloat16)
    return [shape, shape]


def prepare(head, tokens, gain, weights, pad_rows):
    seg_count, quarter, width = tokens[0].shape
    seg_len = quarter * len(tokens)
    head_cols = weights.shape[2]
    bf16 = jnp.bfloat16
    return pl.pallas_call(
        prep_kernel,
        grid=(seg_count,),
        in_specs=[pl.BlockSpec(memory_space=pltpu.SMEM)]
        + [by_segment((quarter, width))] * 4
        + [fixed((1, width)), fixed(weights.shape)],
        out_specs=[
            by_segment((seg_len, 3 * head_cols)),
            by_segment((seg_len, width)),
            by_segment((pad_rows, RATE * width)),
            by_segment((pad_rows, head_cols)),
        ],
        out_shape=[
            jax.ShapeDtypeStruct((seg_count, seg_len, 3 * head_cols), bf16),
            jax.ShapeDtypeStruct((seg_count, seg_len, width), bf16),
            jax.ShapeDtypeStruct((seg_count, pad_rows, RATE * width), bf16),
            jax.ShapeDtypeStruct((seg_count, pad_rows, head_cols), bf16),
        ],
        scratch_shapes=[pltpu.VMEM((width // 128, RATE * pad_rows, 128), jnp.float32)],
        compiler_params=pltpu.CompilerParams(vmem_limit_bytes=VMEM_LIMIT),
        cost_estimate=pl.CostEstimate(flops=7 * 10**9, bytes_accessed=30 * 10**6, transcendentals=3072),
        name="prepare",
    )(head, *tokens, gain, weights)


def ffn_kernel(
    head_ref, a0, a1, a2, a3, o0, o1, o2, o3, t0, t1, t2, t3, g0, g1, g2, g3, gain_ref, up_ref, down_ref,
    f_keep, f_sent, n_keep, n_sent, hidden_ref, pack_ref,
    rows, grads, acc_up, acc_down,
):
    step = pl.program_id(0)
    head = head_ref[0]
    quarter, width = t0.shape[1:]
    ff_part = up_ref.shape[1]
    parts = up_ref.shape[0] // 2
    block = parts * ff_part

    @pl.when(step == 0)
    def _():
        acc_up[...] = jnp.zeros_like(acc_up)
        acc_down[...] = jnp.zeros_like(acc_down)

    place_rows(head, (t0, t1, t2, t3), rows)
    place_rows(head, (g0, g1, g2, g3), grads)
    hidden = rows[...]
    for a, o in ((a0, o0), (a1, o1), (a2, o2), (a3, o3)):
        hidden = hidden + jnp.dot(a[0], o[...], preferred_element_type=jnp.float32)
    rows[...] = hidden
    at = pl.multiple_of(head * quarter, quarter)
    hidden_ref[0] = rows[pl.ds(at, quarter), :]
    unit, _ = row_norm(hidden)
    normed = (unit * gain_ref[...]).astype(jnp.bfloat16)
    grad = grads[...]
    result = jnp.zeros(hidden.shape, jnp.float32)
    g_normed = jnp.zeros(hidden.shape, jnp.float32)
    for n in range(2):
        own = slice(n * parts, (n + 1) * parts)
        up = up_ref[own].reshape(block, width)
        down = down_ref[own].reshape(block, width)
        lifted = lax.dot_general(normed, up, COLS_IN, preferred_element_type=jnp.float32)
        sig = 0.5 * jnp.tanh(0.5 * lifted) + 0.5
        smooth = lifted * sig
        active = smooth.astype(jnp.bfloat16)
        g_active = lax.dot_general(grad, down, COLS_IN, preferred_element_type=jnp.float32)
        g_lifted = (g_active * (sig + smooth * (1.0 - sig))).astype(jnp.bfloat16)
        result = result + jnp.dot(active, down, preferred_element_type=jnp.float32)
        g_normed = g_normed + jnp.dot(g_lifted, up, preferred_element_type=jnp.float32)
        acc_down[n] += lax.dot_general(active, grad, ROWS_IN, preferred_element_type=jnp.float32)
        acc_up[n] += lax.dot_general(g_lifted, normed, ROWS_IN, preferred_element_type=jnp.float32)
    rows[...] = g_normed
    hand_out(head, rows, n_keep, n_sent)
    rows[...] = result
    hand_out(head, rows, f_keep, f_sent)

    @pl.when(step == pl.num_programs(0) - 1)
    def _():
        for n in range(2):
            own = slice(n * parts, (n + 1) * parts)
            shape = (parts, ff_part, width)
            pack_ref[own, :ff_part] = acc_up[n].astype(jnp.bfloat16).reshape(shape)
            pack_ref[own, ff_part:] = acc_down[n].astype(jnp.bfloat16).reshape(shape)


def feed_forward(head, attended, wo, tokens, grads, gain, pack, ff_part):
    seg_count, quarter, width = tokens[0].shape
    seg_len, head_cols = attended[0].shape[1:]
    blks = pack.shape[0]
    half = blks // 2 * ff_part
    pieces = piece_specs(quarter, width)
    shapes = piece_shapes(seg_count, quarter, width)

    def weight(index):
        return pl.BlockSpec(
            (blks, ff_part, width), lambda s: (0, index, 0), pipeline_mode=pl.Buffered(1)
        )

    return pl.pallas_call(
        ffn_kernel,
        grid=(seg_count,),
        in_specs=[pl.BlockSpec(memory_space=pltpu.SMEM)]
        + [by_segment((seg_len, head_cols))] * 4
        + [fixed((head_cols, width))] * 4
        + [by_segment((quarter, width))] * 8
        + [fixed((1, width)), weight(0), weight(1)],
        out_specs=pieces + pieces
        + [
            by_segment((quarter, width)),
            pl.BlockSpec((blks, 2 * ff_part, width), lambda s: (0, 0, 0)),
        ],
        out_shape=shapes + shapes
        + [
            jax.ShapeDtypeStruct((seg_count, quarter, width), jnp.float32),
            jax.ShapeDtypeStruct((blks, 2 * ff_part, width), jnp.bfloat16),
        ],
        scratch_shapes=[
            pltpu.VMEM((seg_len, width), jnp.float32),
            pltpu.VMEM((seg_len, width), jnp.bfloat16),
            pltpu.VMEM((2, half, width), jnp.float32),
            pltpu.VMEM((2, half, width), jnp.float32),
        ],
        compiler_params=pltpu.CompilerParams(vmem_limit_bytes=VMEM_LIMIT),
        cost_estimate=pl.CostEstimate(flops=45 * 10**9, bytes_accessed=60 * 10**6, transcendentals=4 * 10**6),
        name="feed_forward",
    )(head, *attended, *wo, *tokens, *grads, gain, pack, pack)


def g_normed_kernel(head_ref, gq_ref, gkv_ref, gp_ref, w_ref, keep_ref, sent_ref, spread, rows):
    head = head_ref[0]
    seg_len, head_cols = gq_ref.shape[1:]
    pad_rows = gp_ref.shape[1]
    width = w_ref.shape[1]
    total = lax.dot_general(gq_ref[0], w_ref[2], COLS_IN, preferred_element_type=jnp.float32)
    for n in range(2):
        part = gkv_ref[0, :, n * head_cols : (n + 1) * head_cols]
        total = total + lax.dot_general(part, w_ref[n], COLS_IN, preferred_element_type=jnp.float32)
    for tap in range(RATE):
        sent = lax.dot_general(gp_ref[0], w_ref[3 + tap], COLS_IN, preferred_element_type=jnp.float32)
        for c in range(width // 128):
            spread[c, pl.ds(tap, pad_rows, stride=RATE), :] = sent[:, c * 128 : (c + 1) * 128]
    for c in range(width // 128):
        own = slice(c * 128, (c + 1) * 128)
        rows[:, own] = total[:, own] + spread[c, :seg_len, :]
    hand_out(head, rows, keep_ref, sent_ref)


def g_normed_parts(head, grad_query, grad_pair, grad_packed, weights, quarter):
    seg_count, seg_len, head_cols = grad_query.shape
    width = weights.shape[1]
    pad_rows = grad_packed.shape[1]
    return pl.pallas_call(
        g_normed_kernel,
        grid=(seg_count,),
        in_specs=[
            pl.BlockSpec(memory_space=pltpu.SMEM),
            by_segment((seg_len, head_cols)),
            by_segment((seg_len, 2 * head_cols)),
            by_segment((pad_rows, head_cols)),
            fixed(weights.shape),
        ],
        out_specs=piece_specs(quarter, width),
        out_shape=piece_shapes(seg_count, quarter, width),
        scratch_shapes=[
            pltpu.VMEM((width // 128, RATE * pad_rows, 128), jnp.float32),
            pltpu.VMEM((seg_len, width), jnp.float32),
        ],
        compiler_params=pltpu.CompilerParams(vmem_limit_bytes=VMEM_LIMIT),
        cost_estimate=pl.CostEstimate(flops=7 * 10**9, bytes_accessed=20 * 10**6, transcendentals=0),
        name="g_normed",
    )(head, grad_query, grad_pair, grad_packed, weights)


def head_swap(value, bit):
    count = lax.axis_size("head")
    return lax.ppermute(value, "head", [(source, source ^ bit) for source in range(count)])


def to_all_heads(value):
    far = head_swap(value, 2)
    return value, head_swap(value, 1), far, head_swap(far, 1)


def sum_over_heads(keep, sent):
    got = head_swap(sent, 1).astype(jnp.float32)
    far = (keep[1].astype(jnp.float32) + got[1]).astype(jnp.bfloat16)
    return keep[0].astype(jnp.float32) + got[0] + head_swap(far, 2).astype(jnp.float32)


def per_device(tokens, wq, wk, wv, wo, w_up, w_down, gain_one, gain_two, w_comp, lengths, grad_out):
    seg_count, quarter, width = tokens.shape
    head_groups = lax.axis_size("head")
    blk_count = lax.axis_size("blk")
    seg_len = quarter * head_groups
    head_cols = width // head_groups
    local_heads = head_cols // HD
    comp_rows = seg_len // RATE
    pad_rows = (comp_rows + 15) // 16 * 16
    window = CSEGS + 1
    head_index = lax.axis_index("head")
    blk_index = lax.axis_index("blk")
    token_count = seg_count * quarter
    full_count = seg_count * seg_len
    comp_count = seg_count * pad_rows
    part = wq.shape[0]
    ff_part = w_down.shape[0]
    bf16 = jnp.bfloat16
    head = head_index[None].astype(jnp.int32)

    columns = (
        jnp.concatenate([wk, wv, wq, w_comp.reshape(RATE * part, width)], 0)
        .reshape(6 * part, head_groups, head_cols)
        .transpose(1, 0, 2)
    )
    gains = jnp.pad(
        jnp.concatenate([gain_one, gain_two])[None], ((0, 15), (0, head_cols - 2 * part))
    )
    columns = jnp.concatenate(
        [columns, jnp.broadcast_to(gains, (head_groups, 16, head_cols))], 1
    )
    columns = lax.all_to_all(columns, "head", split_axis=0, concat_axis=0, tiled=True)
    columns, tokens_held = lax.optimization_barrier((columns, tokens))
    first_all = lax.all_gather(columns, "blk", axis=0)
    second_all = lax.all_gather(jnp.concatenate([w_up.T, w_down, wo], 0), "blk", axis=0)
    token_pieces = to_all_heads(tokens_held)
    grad_held, tokens_far = lax.optimization_barrier((grad_out, token_pieces[2]))
    token_pieces = token_pieces[:2] + (tokens_far,) + token_pieces[3:]
    grad_pieces = to_all_heads(grad_held)
    gain_pair = first_all[:, :, 6 * part, : 2 * part].reshape(
        blk_count, head_groups, 2, part
    ).transpose(2, 1, 0, 3).reshape(2, 1, width).astype(jnp.float32)
    gain_first, gain_second = gain_pair[0], gain_pair[1]
    weights = (
        first_all[:, :, : 6 * part]
        .reshape(blk_count, head_groups, 6, part, head_cols)
        .transpose(2, 1, 0, 3, 4)
        .reshape(6, width, head_cols)
    )
    wkv = jnp.concatenate([weights[0], weights[1]], 1)
    wo_mine = second_all[:, 2 * ff_part :].reshape(head_cols, width)
    wo_pieces = to_all_heads(wo_mine)

    heads, normed, grouped, packed_mine = prepare(
        head, token_pieces, gain_first, weights, pad_rows
    )
    compressed = packed_mine[:, :comp_rows]
    packed = jnp.zeros((comp_count, width), bf16)
    for bits, piece in enumerate(to_all_heads(packed_mine.reshape(comp_count, head_cols))):
        packed = lax.dynamic_update_slice(
            packed, piece, (0, jnp.bitwise_xor(head_index, bits) * head_cols)
        )
    comp_pair = (
        jnp.dot(packed, wkv, preferred_element_type=jnp.float32)
        .astype(bf16)
        .reshape(seg_count, pad_rows, 2 * head_cols)
    )
    recv_mem, recv_comp = passed_along(
        (heads[seg_count - 1 :, :, : 2 * head_cols], comp_pair[seg_count - window :]), "blk", 1
    )
    comp_ext = jnp.concatenate([recv_comp, comp_pair], 0)
    order = jnp.arange(lengths.shape[0], dtype=jnp.int32)
    starts = jnp.sum(jnp.where(order[None, :] < order[:, None], lengths[None, :], 0), axis=1)
    seg_ids = blk_index * seg_count + jnp.arange(seg_count, dtype=jnp.int32)
    seg_place = seg_ids - jnp.max(
        jnp.where(starts[None, :] <= seg_ids[:, None], starts[None, :], 0), axis=1
    )
    head_ids = head_index * local_heads + jnp.arange(local_heads, dtype=jnp.int32)
    slopes = jnp.exp2(-head_ids.astype(jnp.float32)) / 64.0 * LOG2E
    attn_out, lse = attend_fwd(seg_place, slopes, heads, recv_mem, comp_ext, head_cols)

    attended = to_all_heads(attn_out)
    f_keep, f_sent, n_keep, n_sent, hidden, first_grads = feed_forward(
        head, attended, wo_pieces, token_pieces, grad_pieces, gain_second, second_all, ff_part
    )
    first_sum = lax.psum_scatter(first_grads, "blk", scatter_dimension=0)
    grad_normed_two = sum_over_heads(n_keep, n_sent).reshape(token_count, width)
    hidden = hidden.reshape(token_count, width)
    unit, spread = row_norm(hidden)
    grad_gain_two = jnp.sum(grad_normed_two * unit, axis=0)
    grad_hidden = grad_out.reshape(token_count, width).astype(jnp.float32) + norm_back(
        grad_normed_two, unit, spread, gain_second
    )
    grad_branch = grad_hidden.astype(bf16)
    grad_mixed = [
        head_swap(
            lax.dot_general(grad_branch, block, COLS_IN, preferred_element_type=jnp.float32)
            .astype(bf16)
            .reshape(seg_count, quarter, head_cols),
            bits,
        )
        if bits
        else lax.dot_general(grad_branch, block, COLS_IN, preferred_element_type=jnp.float32)
        .astype(bf16)
        .reshape(seg_count, quarter, head_cols)
        for bits, block in enumerate(wo_pieces)
    ]
    f_sent, grad_mixed = lax.optimization_barrier((f_sent, grad_mixed))
    out_tokens = (
        (hidden.reshape(tokens.shape) + sum_over_heads(f_keep, f_sent)).astype(bf16)
    )
    grad_wo = [
        lax.dot_general(
            lax.dynamic_slice_in_dim(block, head_index * quarter, quarter, 1).reshape(
                token_count, head_cols
            ),
            grad_branch,
            ROWS_IN,
            preferred_element_type=jnp.float32,
        ).astype(bf16)
        for block in attended
    ]
    grad_query, grad_pair, tail, grad_comp_ext = attend_bwd(
        head, seg_place, slopes, heads, recv_mem, comp_ext, grad_mixed, attn_out, lse, head_cols
    )
    got_mem, got_comp = passed_along(
        (grad_pair[seg_count], grad_comp_ext[:window].astype(bf16)), "blk", -1
    )
    last_pair = (tail + got_mem.astype(jnp.float32)).astype(bf16)
    grad_pair = lax.dynamic_update_slice(grad_pair, last_pair[None], (seg_count - 1, 0, 0))
    comp_pair_grad = grad_comp_ext[window:] + jnp.pad(
        got_comp.astype(jnp.float32), ((seg_count - window, 0), (0, 0), (0, 0))
    )
    comp_grad_rows = comp_pair_grad.reshape(comp_count, 2 * head_cols).astype(bf16)
    grad_packed_part = lax.dot_general(
        comp_grad_rows, wkv, COLS_IN, preferred_element_type=jnp.float32
    ).astype(bf16)

    def columns_of(bits):
        start = jnp.bitwise_xor(head_index, bits) * head_cols
        return lax.dynamic_slice_in_dim(grad_packed_part, start, head_cols, 1)

    grad_packed = sum_over_heads(
        (columns_of(0), columns_of(2)), jnp.stack([columns_of(1), columns_of(3)])
    ).astype(bf16)
    keep, sent = g_normed_parts(
        head,
        grad_query,
        grad_pair,
        grad_packed.reshape(seg_count, pad_rows, head_cols),
        weights,
        quarter,
    )
    grad_normed = sum_over_heads(keep, sent).reshape(token_count, width)
    unit_one, spread_one = row_norm(tokens.reshape(token_count, width).astype(jnp.float32))
    grad_tokens = (
        (grad_hidden + norm_back(grad_normed, unit_one, spread_one, gain_first))
        .astype(bf16)
        .reshape(tokens.shape)
    )
    normed = normed.reshape(full_count, width)
    grad_kv = grad_pair[:seg_count].reshape(full_count, 2 * head_cols)
    grad_wq = lax.dot_general(
        normed, grad_query.reshape(full_count, head_cols), ROWS_IN, preferred_element_type=jnp.float32
    )
    grad_wkv = lax.dot_general(normed, grad_kv, ROWS_IN, preferred_element_type=jnp.float32)
    comp_term = lax.dot_general(packed, comp_grad_rows, ROWS_IN, preferred_element_type=jnp.float32)
    grad_comp = lax.dot_general(
        grouped.reshape(comp_count, RATE * width),
        grad_packed,
        ROWS_IN,
        preferred_element_type=jnp.float32,
    ).reshape(RATE, width, head_cols)
    grad_gain_one = (
        jnp.sum(grad_wq * weights[2].astype(jnp.float32), axis=1)
        + jnp.sum(grad_wkv * wkv.astype(jnp.float32), axis=1)
        + jnp.sum(grad_comp * weights[3:].astype(jnp.float32), axis=(0, 2))
    ) / gain_first[0]
    grad_wkv = grad_wkv + comp_term
    grad_wo = sum_over_heads((grad_wo[0], grad_wo[2]), jnp.stack([grad_wo[1], grad_wo[3]]))

    def by_owner(value):
        return value.astype(bf16).reshape(
            head_groups, blk_count, part, value.shape[1]
        ).transpose(1, 0, 2, 3)

    gain_rows = (
        jnp.stack([grad_gain_one, grad_gain_two])
        .reshape(2, head_groups, blk_count, part)
        .transpose(2, 1, 0, 3)
        .astype(bf16)
    )
    second_grads = jnp.concatenate(
        [
            by_owner(grad_wq),
            by_owner(grad_wkv[:, :head_cols]),
            by_owner(grad_wkv[:, head_cols:]),
            by_owner(grad_comp[0]),
            by_owner(grad_comp[1]),
            by_owner(grad_comp[2]),
            jnp.pad(gain_rows, ((0, 0), (0, 0), (0, 14), (0, head_cols - part))),
            grad_wo.astype(bf16)
            .reshape(blk_count, part, head_groups, head_cols)
            .transpose(0, 2, 1, 3),
        ],
        2,
    )
    second_grads, first_sum = lax.optimization_barrier((second_grads, first_sum))
    first_sum = first_sum.astype(jnp.float32)
    own_rows = 6 * part + 16
    second_part = lax.psum_scatter(
        second_grads.reshape(-1, head_cols), "blk", scatter_dimension=0, tiled=True
    ).reshape(head_groups, own_rows + part, head_cols)
    second_sum = lax.all_to_all(
        second_part[:, :own_rows], "head", split_axis=0, concat_axis=0, tiled=True
    ).astype(jnp.float32)
    gain_sum = jnp.sum(second_sum[:, 6 * part : 6 * part + 2, :part], axis=0)
    weight_sum = (
        second_sum[:, : 6 * part]
        .reshape(head_groups, 6, part, head_cols)
        .transpose(1, 2, 0, 3)
        .reshape(6, part, width)
    )
    wo_sum = second_part[:, own_rows:].astype(jnp.float32).transpose(1, 0, 2).reshape(part, width)
    return (
        out_tokens,
        compressed,
        grad_tokens,
        weight_sum[0],
        weight_sum[1],
        weight_sum[2],
        wo_sum,
        first_sum[:ff_part].T,
        first_sum[ff_part:],
        gain_sum[0],
        gain_sum[1],
        weight_sum[3:],
    )


def solution(mesh):
    return jax.shard_map(
        per_device,
        mesh=mesh,
        in_specs=(
            P("blk", "head", None),
            P(("head", "blk"), None),
            P(("head", "blk"), None),
            P(("head", "blk"), None),
            P(("head", "blk"), None),
            P(None, ("head", "blk")),
            P(("head", "blk"), None),
            P(("head", "blk")),
            P(("head", "blk")),
            P(None, ("head", "blk"), None),
            P(),
            P("blk", "head", None),
        ),
        out_specs=(
            P("blk", "head", None),
            P("blk", None, "head"),
            P("blk", "head", None),
            P(("head", "blk"), None),
            P(("head", "blk"), None),
            P(("head", "blk"), None),
            P(("head", "blk"), None),
            P(None, ("head", "blk")),
            P(("head", "blk"), None),
            P(("head", "blk")),
            P(("head", "blk")),
            P(None, ("head", "blk"), None),
        ),
        check_vma=False,
    )
```

```python
import functools

import jax
import jax.numpy as jnp
from jax import lax
from jax.experimental import pallas as pl
from jax.experimental.pallas import tpu as pltpu
from jax.sharding import PartitionSpec as P

HD = 128
RATE = 3
CSEGS = 3


EPS = 1e-05
NEG = -1e30
ROWS_IN = (((0,), (0,)), ((), ()))
COLS_IN = (((1,), (1,)), ((), ()))


def passed_along(value, axis, steps):
    count = lax.axis_size(axis)
    leading, last = (max(0, -steps), min(count, count - steps))
    return lax.ppermute(value, axis, [(source, source + steps) for source in range(leading, last)])


LOG2E = 1.4426950408889634
PAD_ROWS = 176
VMEM_LIMIT = 56 * 1024 * 1024


def key_bias(rows, base, step, valid_rows, open_, slope):
    row = lax.broadcasted_iota(jnp.int32, (rows, 1), 0)
    place = (base + step * row).astype(jnp.float32)
    return jnp.where((row < valid_rows) & open_, place * slope, NEG)


def fwd_kernel(first, place_ref, slope_ref, q_ref, own_ref, prev_ref, recv_ref, comp_ref, out_ref, lse_ref):
    step = pl.program_id(0) + first
    place = place_ref[step]
    seg_len = q_ref.shape[1]
    half = seg_len // 2
    pad_rows = comp_ref.shape[1]
    local_heads = q_ref.shape[2] // HD
    values_at = local_heads * HD
    factor = HD ** (-0.5) * LOG2E
    lower = lax.broadcasted_iota(jnp.int32, (half, half), 0) <= lax.broadcasted_iota(
        jnp.int32, (half, half), 1
    )
    for h in range(local_heads):
        kc = slice(h * HD, (h + 1) * HD)
        vc = slice(values_at + h * HD, values_at + (h + 1) * HD)
        slope = slope_ref[h]
        parts = []
        for piece in range(CSEGS):
            lag = CSEGS + 1 - piece
            bias = key_bias(pad_rows, RATE // 2 - lag * seg_len, RATE, seg_len // RATE, place >= lag, slope)
            parts.append((comp_ref[step + piece, :, kc], comp_ref[step + piece, :, vc], bias))
        bias = key_bias(seg_len, -seg_len, 1, seg_len, place >= 1, slope)
        is_first = step == 0
        parts.append(
            (
                jnp.where(is_first, recv_ref[0, :, kc], prev_ref[0, :, kc]),
                jnp.where(is_first, recv_ref[0, :, vc], prev_ref[0, :, vc]),
                bias,
            )
        )
        own_bias = [
            key_bias(half, n * half, 1, half, place >= 0, slope) for n in range(2)
        ]
        for n in range(2):
            query = q_ref[0, n * half : (n + 1) * half, kc]
            group = list(parts)
            for m in range(n + 1):
                rows = slice(m * half, (m + 1) * half)
                group.append((own_ref[0, rows, kc], own_ref[0, rows, vc], own_bias[m]))
            scores = []
            top = None
            for index, (k, v, bias) in enumerate(group):
                raw = lax.dot_general(k, query, COLS_IN, preferred_element_type=jnp.float32)
                raw = raw * factor + bias
                if index == len(group) - 1:
                    raw = jnp.where(lower, raw, NEG)
                scores.append(raw)
                peak = jnp.max(raw, axis=0, keepdims=True)
                top = peak if top is None else jnp.maximum(top, peak)
            total = jnp.zeros_like(top)
            result = jnp.zeros((HD, half), jnp.float32)
            for raw, (k, v, bias) in zip(scores, group):
                weight = jnp.exp2(raw - top)
                total = total + jnp.sum(weight, axis=0, keepdims=True)
                result = result + lax.dot_general(
                    v, weight.astype(jnp.bfloat16), ROWS_IN, preferred_element_type=jnp.float32
                )
            result = result * (1.0 / total)
            out_ref[0, n * half : (n + 1) * half, kc] = result.T.astype(jnp.bfloat16)
            lse_ref[0, h : h + 1, n * half : (n + 1) * half] = top + jnp.log(total) * LOG2E


def bwd_kernel(
    first, place_ref, slope_ref, q_ref, own_ref, prev_ref, recv_ref, comp_ref, head_ref, g0, g1, g2, g3, att_ref, lse_ref, held_ref,
    gq_ref, gkv_ref, tail_ref, gcomp_ref, grad_ref,
):
    step = pl.program_id(0) + first
    place = place_ref[step]
    seg_len = q_ref.shape[1]
    half = seg_len // 2
    pad_rows = comp_ref.shape[1]
    local_heads = q_ref.shape[2] // HD
    values_at = local_heads * HD
    scale = HD ** (-0.5)
    factor = scale * LOG2E
    is_first = step == 0
    lower = lax.broadcasted_iota(jnp.int32, (half, half), 0) <= lax.broadcasted_iota(
        jnp.int32, (half, half), 1
    )

    at_start = pl.program_id(0) == 0

    @pl.when(at_start)
    def _():
        tail_ref[...] = held_ref[...]
        gcomp_ref[...] = jnp.zeros_like(gcomp_ref)

    place_rows(head_ref[0], (g0, g1, g2, g3), grad_ref)
    for h in range(local_heads):
        kc = slice(h * HD, (h + 1) * HD)
        vc = slice(values_at + h * HD, values_at + (h + 1) * HD)
        slope = slope_ref[h]
        query = q_ref[0, :, kc]
        grad = grad_ref[:, kc]
        lse = lse_ref[0, h : h + 1, :]
        product = grad.astype(jnp.float32) * att_ref[0, :, kc].astype(jnp.float32)
        delta = jnp.sum(product.T, axis=0, keepdims=True)

        def part(k, v, bias, cols, masked):
            raw = lax.dot_general(k, query[cols], COLS_IN, preferred_element_type=jnp.float32)
            raw = raw * factor + bias
            if masked:
                raw = jnp.where(lower, raw, NEG)
            prob = jnp.exp2(raw - lse[:, cols])
            grad_prob = lax.dot_general(v, grad[cols], COLS_IN, preferred_element_type=jnp.float32)
            grad_score = (prob * (grad_prob - delta[:, cols])).astype(jnp.bfloat16)
            gk = jnp.dot(grad_score, query[cols], preferred_element_type=jnp.float32) * scale
            gv = jnp.dot(prob.astype(jnp.bfloat16), grad[cols], preferred_element_type=jnp.float32)
            gq = lax.dot_general(k, grad_score, ROWS_IN, preferred_element_type=jnp.float32)
            return gk, gv, gq

        every = slice(0, seg_len)
        total = jnp.zeros((HD, seg_len), jnp.float32)
        for piece in range(CSEGS):
            lag = CSEGS + 1 - piece
            bias = key_bias(pad_rows, RATE // 2 - lag * seg_len, RATE, seg_len // RATE, place >= lag, slope)
            gk, gv, gq = part(comp_ref[step + piece, :, kc], comp_ref[step + piece, :, vc], bias, every, False)
            gcomp_ref[step - first + piece, :, kc] += gk
            gcomp_ref[step - first + piece, :, vc] += gv
            total = total + gq
        for n in range(2):
            rows = slice(n * half, (n + 1) * half)
            bias = key_bias(half, n * half - seg_len, 1, half, place >= 1, slope)
            k = jnp.where(is_first, recv_ref[0, rows, kc], prev_ref[0, rows, kc])
            v = jnp.where(is_first, recv_ref[0, rows, vc], prev_ref[0, rows, vc])
            gk, gv, gq = part(k, v, bias, every, False)
            gkv_ref[0, rows, kc] = (tail_ref[rows, kc] + gk).astype(jnp.bfloat16)
            gkv_ref[0, rows, vc] = (tail_ref[rows, vc] + gv).astype(jnp.bfloat16)
            total = total + gq
        lo, hi = slice(0, half), slice(half, seg_len)
        bias_lo = key_bias(half, 0, 1, half, place >= 0, slope)
        bias_hi = key_bias(half, half, 1, half, place >= 0, slope)
        gk0, gv0, gq0 = part(own_ref[0, lo, kc], own_ref[0, lo, vc], bias_lo, lo, True)
        gk1, gv1, gq1 = part(own_ref[0, lo, kc], own_ref[0, lo, vc], bias_lo, hi, False)
        gk2, gv2, gq2 = part(own_ref[0, hi, kc], own_ref[0, hi, vc], bias_hi, hi, True)
        tail_ref[lo, kc] = gk0 + gk1
        tail_ref[lo, vc] = gv0 + gv1
        tail_ref[hi, kc] = gk2
        tail_ref[hi, vc] = gv2
        gq_ref[0, lo, kc] = ((total[:, lo] + gq0) * scale).T.astype(jnp.bfloat16)
        gq_ref[0, hi, kc] = ((total[:, hi] + gq1 + gq2) * scale).T.astype(jnp.bfloat16)


def attention_specs(first, seg_len, head_cols, comp_shape):
    pair = 2 * head_cols
    return [
        pl.BlockSpec(memory_space=pltpu.SMEM),
        pl.BlockSpec(memory_space=pltpu.SMEM),
        pl.BlockSpec((1, seg_len, head_cols), lambda s: (s + first, 0, 2)),
        pl.BlockSpec((1, seg_len, pair), lambda s: (s + first, 0, 0)),
        pl.BlockSpec((1, seg_len, pair), lambda s: (jnp.maximum(s + first - 1, 0), 0, 0)),
        fixed((1, seg_len, pair)),
        fixed(comp_shape),
    ]


def attend_fwd(first, count, place, slope, heads, recv_mem, comp_ext, head_cols):
    seg_len = heads.shape[1]
    local_heads = head_cols // HD
    return pl.pallas_call(
        functools.partial(fwd_kernel, first),
        grid=(count,),
        in_specs=attention_specs(first, seg_len, head_cols, comp_ext.shape),
        out_specs=[by_segment((seg_len, head_cols)), by_segment((local_heads, seg_len))],
        out_shape=[
            jax.ShapeDtypeStruct((count, seg_len, head_cols), jnp.bfloat16),
            jax.ShapeDtypeStruct((count, local_heads, seg_len), jnp.float32),
        ],
        compiler_params=pltpu.CompilerParams(vmem_limit_bytes=VMEM_LIMIT),
        cost_estimate=pl.CostEstimate(
            flops=count * 10**9, bytes_accessed=count * 3 * 10**6, transcendentals=count * 16 * 10**5
        ),
        name="attend_fwd",
    )(place, slope, heads, heads, heads, recv_mem, comp_ext)


def attend_bwd(
    first, head, place, slope, heads, recv_mem, comp_ext, grad_mixed, attn_out, lse, held, head_cols
):
    count, seg_len, _ = attn_out.shape
    local_heads = head_cols // HD
    pair = 2 * head_cols
    window = (count + CSEGS - 1,) + comp_ext.shape[1:]
    return pl.pallas_call(
        functools.partial(bwd_kernel, first),
        grid=(count,),
        in_specs=attention_specs(first, seg_len, head_cols, comp_ext.shape)
        + [pl.BlockSpec(memory_space=pltpu.SMEM)]
        + [by_segment(grad_mixed[0].shape[1:])] * 4
        + [
            by_segment((seg_len, head_cols)),
            by_segment((local_heads, seg_len)),
            fixed((seg_len, pair)),
        ],
        out_specs=[
            by_segment((seg_len, head_cols)),
            by_segment((seg_len, pair)),
            pl.BlockSpec((seg_len, pair), lambda s: (0, 0)),
            pl.BlockSpec(window, lambda s: (0, 0, 0)),
        ],
        out_shape=[
            jax.ShapeDtypeStruct((count, seg_len, head_cols), jnp.bfloat16),
            jax.ShapeDtypeStruct((count, seg_len, pair), jnp.bfloat16),
            jax.ShapeDtypeStruct((seg_len, pair), jnp.float32),
            jax.ShapeDtypeStruct(window, jnp.float32),
        ],
        scratch_shapes=[pltpu.VMEM((seg_len, head_cols), jnp.bfloat16)],
        compiler_params=pltpu.CompilerParams(vmem_limit_bytes=VMEM_LIMIT),
        cost_estimate=pl.CostEstimate(
            flops=count * 2 * 10**9, bytes_accessed=count * 4 * 10**6, transcendentals=count * 16 * 10**5
        ),
        name="attend_bwd",
    )(place, slope, heads, heads, heads, recv_mem, comp_ext, head, *grad_mixed, attn_out, lse, held)


def row_norm(values):
    average = jnp.mean(values, axis=-1, keepdims=True)
    center = values - average
    spread = lax.rsqrt(jnp.mean(center * center, axis=-1, keepdims=True) + EPS)
    return center * spread, spread


def norm_back(grad, unit, spread, gain):
    scaled = grad * gain
    along = jnp.mean(scaled * unit, axis=-1, keepdims=True)
    return spread * (scaled - jnp.mean(scaled, axis=-1, keepdims=True) - unit * along)


def place_rows(head, pieces, target):
    for bits, piece in enumerate(pieces):
        rows = piece.shape[1]
        at = pl.multiple_of(jnp.bitwise_xor(head, bits) * rows, rows)
        target[pl.ds(at, rows), :] = piece[0].astype(target.dtype)


def hand_out(head, source, keep_ref, sent_ref):
    rows = keep_ref.shape[2]
    for bits, (ref, slot) in enumerate(
        ((keep_ref, 0), (sent_ref, 0), (keep_ref, 1), (sent_ref, 1))
    ):
        at = pl.multiple_of(jnp.bitwise_xor(head, bits) * rows, rows)
        ref[slot, 0] = source[pl.ds(at, rows), :].astype(ref.dtype)


def prep_kernel(
    head_ref, t0, t1, t2, t3, gain_ref, w_ref, heads_ref, normed_ref, grouped_ref, packed_ref, spread
):
    head = head_ref[0]
    quarter, width = t0.shape[1:]
    seg_len = heads_ref.shape[1]
    head_cols = w_ref.shape[2]
    pad_rows = grouped_ref.shape[1]
    tiles = width // 128
    for bits, piece in enumerate((t0, t1, t2, t3)):
        unit, _ = row_norm(piece[0].astype(jnp.float32))
        normed = (unit * gain_ref[...]).astype(jnp.bfloat16)
        at = pl.multiple_of(jnp.bitwise_xor(head, bits) * quarter, quarter)
        normed_ref[0, pl.ds(at, quarter), :] = normed
        wide = normed.astype(jnp.float32)
        for c in range(tiles):
            spread[c, pl.ds(at, quarter), :] = wide[:, c * 128 : (c + 1) * 128]
    last = spread[:, seg_len - 8 : seg_len, :]
    row = lax.broadcasted_iota(jnp.int32, last.shape, 1)
    spread[:, seg_len - 8 : seg_len, :] = jnp.where(row < 8 - seg_len % RATE, last, 0.0)
    spread[:, seg_len:, :] = jnp.zeros((tiles, spread.shape[1] - seg_len, 128), jnp.float32)
    rows = normed_ref[0]
    for n in range(3):
        heads_ref[0, :, n * head_cols : (n + 1) * head_cols] = jnp.dot(
            rows, w_ref[n], preferred_element_type=jnp.float32
        ).astype(jnp.bfloat16)
    total = jnp.zeros((pad_rows, head_cols), jnp.float32)
    for tap in range(RATE):
        for c in range(tiles):
            at = tap * width + c * 128
            grouped_ref[0, :, at : at + 128] = spread[
                c, pl.ds(tap, pad_rows, stride=RATE), :
            ].astype(jnp.bfloat16)
        total = total + jnp.dot(
            grouped_ref[0, :, tap * width : (tap + 1) * width],
            w_ref[3 + tap],
            preferred_element_type=jnp.float32,
        )
    packed_ref[0] = total.astype(jnp.bfloat16)


def fixed(shape):
    return pl.BlockSpec(shape, lambda s: (0,) * len(shape), pipeline_mode=pl.Buffered(1))


def by_segment(shape):
    return pl.BlockSpec((1,) + shape, lambda s: (s,) + (0,) * len(shape))


def piece_specs(quarter, width):
    spec = pl.BlockSpec((2, 1, quarter, width), lambda s: (0, s, 0, 0))
    return [spec, spec]


def piece_shapes(seg_count, quarter, width):
    shape = jax.ShapeDtypeStruct((2, seg_count, quarter, width), jnp.bfloat16)
    return [shape, shape]


def prepare(head, tokens, gain, weights, pad_rows):
    seg_count, quarter, width = tokens[0].shape
    seg_len = quarter * len(tokens)
    head_cols = weights.shape[2]
    bf16 = jnp.bfloat16
    return pl.pallas_call(
        prep_kernel,
        grid=(seg_count,),
        in_specs=[pl.BlockSpec(memory_space=pltpu.SMEM)]
        + [by_segment((quarter, width))] * 4
        + [fixed((1, width)), fixed(weights.shape)],
        out_specs=[
            by_segment((seg_len, 3 * head_cols)),
            by_segment((seg_len, width)),
            by_segment((pad_rows, RATE * width)),
            by_segment((pad_rows, head_cols)),
        ],
        out_shape=[
            jax.ShapeDtypeStruct((seg_count, seg_len, 3 * head_cols), bf16),
            jax.ShapeDtypeStruct((seg_count, seg_len, width), bf16),
            jax.ShapeDtypeStruct((seg_count, pad_rows, RATE * width), bf16),
            jax.ShapeDtypeStruct((seg_count, pad_rows, head_cols), bf16),
        ],
        scratch_shapes=[pltpu.VMEM((width // 128, RATE * pad_rows, 128), jnp.float32)],
        compiler_params=pltpu.CompilerParams(vmem_limit_bytes=VMEM_LIMIT),
        cost_estimate=pl.CostEstimate(flops=7 * 10**9, bytes_accessed=30 * 10**6, transcendentals=3072),
        name="prepare",
    )(head, *tokens, gain, weights)


def ffn_kernel(
    chained, head_ref, a0, a1, a2, a3, o0, o1, o2, o3, t0, t1, t2, t3, g0, g1, g2, g3, gain_ref,
    up_ref, down_ref, earlier_ref, f_keep, f_sent, n_keep, n_sent, hidden_ref, pack_ref,
    rows, grads, acc_up, acc_down,
):
    step = pl.program_id(0)
    head = head_ref[0]
    quarter, width = t0.shape[1:]
    ff_part = up_ref.shape[1]
    parts = up_ref.shape[0] // 2
    block = parts * ff_part

    @pl.when(step == 0)
    def _():
        if chained:
            for n in range(2):
                own = slice(n * parts, (n + 1) * parts)
                acc_up[n] = earlier_ref[own, :ff_part].reshape(block, width).astype(jnp.float32)
                acc_down[n] = earlier_ref[own, ff_part:].reshape(block, width).astype(jnp.float32)
        else:
            acc_up[...] = jnp.zeros_like(acc_up)
            acc_down[...] = jnp.zeros_like(acc_down)

    place_rows(head, (t0, t1, t2, t3), rows)
    place_rows(head, (g0, g1, g2, g3), grads)
    hidden = rows[...]
    for a, o in ((a0, o0), (a1, o1), (a2, o2), (a3, o3)):
        hidden = hidden + jnp.dot(
            a[0], o[...].reshape(a.shape[2], width), preferred_element_type=jnp.float32
        )
    rows[...] = hidden
    at = pl.multiple_of(head * quarter, quarter)
    hidden_ref[0] = rows[pl.ds(at, quarter), :]
    unit, _ = row_norm(hidden)
    normed = (unit * gain_ref[...]).astype(jnp.bfloat16)
    grad = grads[...]
    result = jnp.zeros(hidden.shape, jnp.float32)
    g_normed = jnp.zeros(hidden.shape, jnp.float32)
    for n in range(2):
        own = slice(n * parts, (n + 1) * parts)
        up = up_ref[own].reshape(block, width)
        down = down_ref[own].reshape(block, width)
        lifted = lax.dot_general(normed, up, COLS_IN, preferred_element_type=jnp.float32)
        sig = 0.5 * jnp.tanh(0.5 * lifted) + 0.5
        smooth = lifted * sig
        active = smooth.astype(jnp.bfloat16)
        g_active = lax.dot_general(grad, down, COLS_IN, preferred_element_type=jnp.float32)
        g_lifted = (g_active * (sig + smooth * (1.0 - sig))).astype(jnp.bfloat16)
        result = result + jnp.dot(active, down, preferred_element_type=jnp.float32)
        g_normed = g_normed + jnp.dot(g_lifted, up, preferred_element_type=jnp.float32)
        acc_down[n] += lax.dot_general(active, grad, ROWS_IN, preferred_element_type=jnp.float32)
        acc_up[n] += lax.dot_general(g_lifted, normed, ROWS_IN, preferred_element_type=jnp.float32)
    rows[...] = g_normed
    hand_out(head, rows, n_keep, n_sent)
    rows[...] = result
    hand_out(head, rows, f_keep, f_sent)

    @pl.when(step == pl.num_programs(0) - 1)
    def _():
        for n in range(2):
            own = slice(n * parts, (n + 1) * parts)
            shape = (parts, ff_part, width)
            pack_ref[own, :ff_part] = acc_up[n].astype(jnp.bfloat16).reshape(shape)
            pack_ref[own, ff_part:] = acc_down[n].astype(jnp.bfloat16).reshape(shape)


def wo_blocks(pack, part, ff_part, head_groups):
    blks, _, width = pack.shape
    start = 2 * ff_part
    if part % 16 == 0:
        specs = [
            pl.BlockSpec(
                (blks, part, width),
                functools.partial(lambda index, s: (0, index, 0), start // part + n),
                pipeline_mode=pl.Buffered(1),
            )
            for n in range(head_groups)
        ]
        return [pack] * head_groups, specs
    blocks = [
        pack[:, start + n * part : start + (n + 1) * part].reshape(blks * part, width)
        for n in range(head_groups)
    ]
    return blocks, [fixed((blks * part, width))] * head_groups


def feed_forward(first, head, attended, wo, wo_specs, tokens, grads, gain, pack, ff_part, earlier):
    quarter, width = tokens[0].shape[1:]
    count, seg_len, head_cols = attended[0].shape
    blks = pack.shape[0]
    half = blks // 2 * ff_part
    grad_shape = (blks, 2 * ff_part, width)
    pieces = piece_specs(quarter, width)
    shapes = piece_shapes(count, quarter, width)
    chained = earlier is not None
    if not chained:
        earlier, earlier_spec = head, pl.BlockSpec(memory_space=pltpu.SMEM)
    else:
        earlier_spec = fixed(grad_shape)

    def weight(index):
        return pl.BlockSpec(
            (blks, ff_part, width), lambda s: (0, index, 0), pipeline_mode=pl.Buffered(1)
        )

    return pl.pallas_call(
        functools.partial(ffn_kernel, chained),
        grid=(count,),
        in_specs=[pl.BlockSpec(memory_space=pltpu.SMEM)]
        + [by_segment((seg_len, head_cols))] * 4
        + wo_specs
        + [pl.BlockSpec((1, quarter, width), lambda s: (s + first, 0, 0))] * 8
        + [fixed((1, width)), weight(0), weight(1), earlier_spec],
        out_specs=pieces + pieces
        + [by_segment((quarter, width)), pl.BlockSpec(grad_shape, lambda s: (0, 0, 0))],
        out_shape=shapes + shapes
        + [
            jax.ShapeDtypeStruct((count, quarter, width), jnp.float32),
            jax.ShapeDtypeStruct(grad_shape, jnp.bfloat16),
        ],
        scratch_shapes=[
            pltpu.VMEM((seg_len, width), jnp.float32),
            pltpu.VMEM((seg_len, width), jnp.bfloat16),
            pltpu.VMEM((2, half, width), jnp.float32),
            pltpu.VMEM((2, half, width), jnp.float32),
        ],
        compiler_params=pltpu.CompilerParams(vmem_limit_bytes=VMEM_LIMIT),
        cost_estimate=pl.CostEstimate(
            flops=count * 75 * 10**8, bytes_accessed=2 * 10**7 + count * 5 * 10**6, transcendentals=10**6
        ),
        name="feed_forward",
    )(head, *attended, *wo, *tokens, *grads, gain, pack, pack, earlier)


def middle_kernel(
    keep_ref, got_ref, far_ref, hidden_ref, grad_ref, gain_ref, o0, o1, o2, o3,
    g_hidden_ref, g_branch_ref, g_gain_ref, m0, m1, m2, m3,
):
    count, quarter, width = hidden_ref.shape
    flat = (count * quarter, width)
    gn = (
        keep_ref[0].astype(jnp.float32)
        + got_ref[0].astype(jnp.float32)
        + far_ref[...].astype(jnp.float32)
    ).reshape(flat)
    unit, spread = row_norm(hidden_ref[...].reshape(flat))
    g_gain_ref[...] = jnp.sum(gn * unit, axis=0, keepdims=True)
    g_hidden = grad_ref[...].astype(jnp.float32).reshape(flat) + norm_back(
        gn, unit, spread, gain_ref[...]
    )
    g_hidden_ref[...] = g_hidden.reshape(g_hidden_ref.shape)
    g_branch = g_hidden.astype(jnp.bfloat16)
    g_branch_ref[...] = g_branch.reshape(g_branch_ref.shape)
    for o, m in ((o0, m0), (o1, m1), (o2, m2), (o3, m3)):
        m[...] = (
            lax.dot_general(
                g_branch, o[...].reshape(m.shape[2], width), COLS_IN, preferred_element_type=jnp.float32
            )
            .astype(jnp.bfloat16)
            .reshape(m.shape)
        )


def middle(first, keep, got, far, hidden, grad, gain, wo, wo_specs, head_cols):
    count, quarter, width = hidden.shape
    whole = (count, quarter, width)
    piece = pl.BlockSpec((1,) + whole, lambda s: (0, 0, 0, 0))
    block = pl.BlockSpec(whole, lambda s: (0, 0, 0))
    mixed = (count, quarter, head_cols)
    return pl.pallas_call(
        middle_kernel,
        grid=(1,),
        in_specs=[
            piece,
            piece,
            block,
            block,
            pl.BlockSpec(whole, lambda s: (first // count, 0, 0)),
            fixed((1, width)),
        ]
        + wo_specs,
        out_specs=[block, block, pl.BlockSpec((1, width), lambda s: (0, 0))]
        + [pl.BlockSpec(mixed, lambda s: (0, 0, 0))] * 4,
        out_shape=[
            jax.ShapeDtypeStruct(whole, jnp.float32),
            jax.ShapeDtypeStruct(whole, jnp.bfloat16),
            jax.ShapeDtypeStruct((1, width), jnp.float32),
        ]
        + [jax.ShapeDtypeStruct(mixed, jnp.bfloat16)] * 4,
        compiler_params=pltpu.CompilerParams(vmem_limit_bytes=VMEM_LIMIT),
        cost_estimate=pl.CostEstimate(flops=count * 27 * 10**7, bytes_accessed=8 * 10**6, transcendentals=0),
        name="middle",
    )(keep, got, far, hidden, grad, gain, *wo)


def g_normed_kernel(head_ref, gq_ref, gkv_ref, gp_ref, w_ref, keep_ref, sent_ref, spread, rows):
    head = head_ref[0]
    seg_len, head_cols = gq_ref.shape[1:]
    pad_rows = gp_ref.shape[1]
    width = w_ref.shape[1]
    total = lax.dot_general(gq_ref[0], w_ref[2], COLS_IN, preferred_element_type=jnp.float32)
    for n in range(2):
        part = gkv_ref[0, :, n * head_cols : (n + 1) * head_cols]
        total = total + lax.dot_general(part, w_ref[n], COLS_IN, preferred_element_type=jnp.float32)
    for tap in range(RATE):
        sent = lax.dot_general(gp_ref[0], w_ref[3 + tap], COLS_IN, preferred_element_type=jnp.float32)
        for c in range(width // 128):
            spread[c, pl.ds(tap, pad_rows, stride=RATE), :] = sent[:, c * 128 : (c + 1) * 128]
    for c in range(width // 128):
        own = slice(c * 128, (c + 1) * 128)
        rows[:, own] = total[:, own] + spread[c, :seg_len, :]
    hand_out(head, rows, keep_ref, sent_ref)


def g_normed_parts(head, grad_query, grad_pair, grad_packed, weights, quarter):
    seg_count, seg_len, head_cols = grad_query.shape
    width = weights.shape[1]
    pad_rows = grad_packed.shape[1]
    return pl.pallas_call(
        g_normed_kernel,
        grid=(seg_count,),
        in_specs=[
            pl.BlockSpec(memory_space=pltpu.SMEM),
            by_segment((seg_len, head_cols)),
            by_segment((seg_len, 2 * head_cols)),
            by_segment((pad_rows, head_cols)),
            fixed(weights.shape),
        ],
        out_specs=piece_specs(quarter, width),
        out_shape=piece_shapes(seg_count, quarter, width),
        scratch_shapes=[
            pltpu.VMEM((width // 128, RATE * pad_rows, 128), jnp.float32),
            pltpu.VMEM((seg_len, width), jnp.float32),
        ],
        compiler_params=pltpu.CompilerParams(vmem_limit_bytes=VMEM_LIMIT),
        cost_estimate=pl.CostEstimate(flops=7 * 10**9, bytes_accessed=20 * 10**6, transcendentals=0),
        name="g_normed",
    )(head, grad_query, grad_pair, grad_packed, weights)


def head_swap(value, bit):
    count = lax.axis_size("head")
    return lax.ppermute(value, "head", [(source, source ^ bit) for source in range(count)])


def to_all_heads(value):
    far = head_swap(value, 2)
    return value, head_swap(value, 1), far, head_swap(far, 1)


def sum_over_heads(keep, sent):
    got = head_swap(sent, 1).astype(jnp.float32)
    far = (keep[1].astype(jnp.float32) + got[1]).astype(jnp.bfloat16)
    return keep[0].astype(jnp.float32) + got[0] + head_swap(far, 2).astype(jnp.float32)


def per_device(tokens, wq, wk, wv, wo, w_up, w_down, gain_one, gain_two, w_comp, lengths, grad_out):
    seg_count, quarter, width = tokens.shape
    head_groups = lax.axis_size("head")
    blk_count = lax.axis_size("blk")
    seg_len = quarter * head_groups
    head_cols = width // head_groups
    local_heads = head_cols // HD
    comp_rows = seg_len // RATE
    pad_rows = (comp_rows + 15) // 16 * 16
    window = CSEGS + 1
    head_index = lax.axis_index("head")
    blk_index = lax.axis_index("blk")
    token_count = seg_count * quarter
    full_count = seg_count * seg_len
    comp_count = seg_count * pad_rows
    part = wq.shape[0]
    ff_part = w_down.shape[0]
    bf16 = jnp.bfloat16
    head = head_index[None].astype(jnp.int32)

    columns = (
        jnp.concatenate([wk, wv, wq, w_comp.reshape(RATE * part, width)], 0)
        .reshape(6 * part, head_groups, head_cols)
        .transpose(1, 0, 2)
    )
    gains = jnp.pad(
        jnp.concatenate([gain_one, gain_two])[None], ((0, 15), (0, head_cols - 2 * part))
    )
    columns = jnp.concatenate(
        [columns, jnp.broadcast_to(gains, (head_groups, 16, head_cols))], 1
    )
    columns = lax.all_to_all(columns, "head", split_axis=0, concat_axis=0, tiled=True)
    columns, tokens_held = lax.optimization_barrier((columns, tokens))
    first_all = lax.all_gather(columns, "blk", axis=0)
    second_all = lax.all_gather(
        jnp.concatenate([w_up.T, w_down, *to_all_heads(wo)], 0), "blk", axis=0
    )
    token_pieces = to_all_heads(tokens_held)
    grad_held, tokens_far = lax.optimization_barrier((grad_out, token_pieces[2]))
    token_pieces = token_pieces[:2] + (tokens_far,) + token_pieces[3:]
    grad_pieces = to_all_heads(grad_held)
    token_pieces, grad_pieces = lax.optimization_barrier((token_pieces, grad_pieces))
    gain_pair = first_all[:, :, 6 * part, : 2 * part].reshape(
        blk_count, head_groups, 2, part
    ).transpose(2, 1, 0, 3).reshape(2, 1, width).astype(jnp.float32)
    gain_first, gain_second = gain_pair[0], gain_pair[1]
    weights = (
        first_all[:, :, : 6 * part]
        .reshape(blk_count, head_groups, 6, part, head_cols)
        .transpose(2, 1, 0, 3, 4)
        .reshape(6, width, head_cols)
    )
    wkv = jnp.concatenate([weights[0], weights[1]], 1)
    wo_held, wo_specs = wo_blocks(second_all, part, ff_part, head_groups)

    heads, normed, grouped, packed_mine = prepare(
        head, token_pieces, gain_first, weights, pad_rows
    )
    compressed = packed_mine[:, :comp_rows]
    recv_packed, recv_mem = passed_along(
        (packed_mine[seg_count - window :], heads[seg_count - 1 :, :, : 2 * head_cols]), "blk", 1
    )

    def all_columns(value):
        value = value.reshape(-1, head_cols)
        whole = jnp.zeros((value.shape[0], width), bf16)
        for bits, piece in enumerate(to_all_heads(value)):
            start = jnp.bitwise_xor(head_index, bits) * head_cols
            whole = lax.dynamic_update_slice(whole, piece, (0, start))
        return whole

    def comp_pairs(rows):
        return (
            jnp.dot(rows, wkv, preferred_element_type=jnp.float32)
            .astype(bf16)
            .reshape(-1, pad_rows, 2 * head_cols)
        )

    packed = all_columns(packed_mine)
    comp_ext = jnp.concatenate([comp_pairs(all_columns(recv_packed)), comp_pairs(packed)], 0)
    order = jnp.arange(lengths.shape[0], dtype=jnp.int32)
    starts = jnp.sum(jnp.where(order[None, :] < order[:, None], lengths[None, :], 0), axis=1)
    seg_ids = blk_index * seg_count + jnp.arange(seg_count, dtype=jnp.int32)
    seg_place = seg_ids - jnp.max(
        jnp.where(starts[None, :] <= seg_ids[:, None], starts[None, :], 0), axis=1
    )
    head_ids = head_index * local_heads + jnp.arange(local_heads, dtype=jnp.int32)
    slopes = jnp.exp2(-head_ids.astype(jnp.float32)) / 64.0 * LOG2E
    size = 2 if seg_count % 2 == 0 else seg_count
    firsts = range(0, seg_count, size)
    attention = [
        attend_fwd(first, size, seg_place, slopes, heads, recv_mem, comp_ext, head_cols)
        for first in firsts
    ]
    attended = [to_all_heads(attn_out) for attn_out, _ in attention]
    groups = len(firsts)
    first_grads = None
    f_keep, f_sent, hidden, far, summed = [], [], [], [], []
    grad_hidden, grad_branch, grad_gain_two, mixed_all = [], [], 0.0, []
    grad_query, grad_pair, grad_comp_parts = [], [], []
    held = jnp.zeros((seg_len, 2 * head_cols), jnp.float32)

    def run_middle(n):
        g_hidden, g_branch, g_gain, *mixed = middle(
            firsts[n], *summed[n], hidden[n], grad_out, gain_second, wo_held, wo_specs, head_cols
        )
        grad_hidden.append(g_hidden)
        grad_branch.append(g_branch)
        mixed_all.append(mixed[:1] + [head_swap(mixed[bits], bits) for bits in (1, 2, 3)])
        return mixed[0], g_gain[0]

    attended[0], attention = lax.optimization_barrier((attended[0], attention))
    for n in range(groups):
        pieces = attended[n]
        if n >= 1:
            pieces, far[n - 1] = lax.optimization_barrier((pieces, far[n - 1]))
            summed[n - 1] = summed[n - 1] + (head_swap(far[n - 1], 2),)
        if n >= 2:
            first_mixed, g_gain = run_middle(n - 2)
            grad_gain_two = grad_gain_two + g_gain
            pieces, first_mixed = lax.optimization_barrier((pieces, first_mixed))
            mixed_all[n - 2][0] = first_mixed
        keep, sent, n_keep, n_sent, hidden_part, first_grads = feed_forward(
            firsts[n], head, pieces, wo_held, wo_specs, token_pieces, grad_pieces, gain_second,
            second_all, ff_part, first_grads,
        )
        f_keep.append(keep)
        f_sent.append(sent)
        hidden.append(hidden_part)
        got = head_swap(n_sent, 1)
        far.append((n_keep[1].astype(jnp.float32) + got[1].astype(jnp.float32)).astype(bf16))
        summed.append((n_keep, got))
    first_sum = lax.psum_scatter(first_grads, "blk", scatter_dimension=0)
    summed[-1] = summed[-1] + (head_swap(far[-1], 2),)
    if groups == 2:
        first_mixed, g_gain = run_middle(0)
        grad_gain_two = grad_gain_two + g_gain
    early = -(-window // size)

    def comp_chunk(n):
        total = grad_comp_parts[n][:size] if n < groups else 0.0
        if n:
            over = jnp.pad(
                grad_comp_parts[n - 1][size:], ((0, max(size - CSEGS + 1, 0)), (0, 0), (0, 0))
            )
            total = total + over[:size]
        return total

    def comp_back():
        return jnp.concatenate([comp_chunk(n) for n in range(early)], 0)[:window].astype(bf16)

    for n in range(groups):
        if n + 1 < groups:
            first_mixed, g_gain = run_middle(n + 1)
        elif groups == 1:
            first_mixed, g_gain = run_middle(n)
        mixed = mixed_all[n]
        if n + 1 < groups or groups == 1:
            grad_gain_two = grad_gain_two + g_gain
            if n + 1 < groups:
                mixed, first_mixed, far[-1] = lax.optimization_barrier((mixed, first_mixed, far[-1]))
                mixed_all[n + 1][0] = first_mixed
        if n == early and n < groups:
            back, mixed = lax.optimization_barrier((comp_back(), mixed))
        attn_out, lse = attention[n]
        g_query, g_pair, held, g_comp = attend_bwd(
            firsts[n], head, seg_place, slopes, heads, recv_mem, comp_ext, mixed, attn_out, lse, held,
            head_cols,
        )
        grad_query.append(g_query)
        grad_pair.append(g_pair)
        grad_comp_parts.append(g_comp)
    f_sent, mixed = lax.optimization_barrier((jnp.concatenate(f_sent, 1), mixed))
    out_tokens = (
        jnp.concatenate(hidden, 0) + sum_over_heads(jnp.concatenate(f_keep, 1), f_sent)
    ).astype(bf16)
    grad_hidden = jnp.concatenate(grad_hidden, 0).reshape(token_count, width)
    grad_branch = jnp.concatenate(grad_branch, 0).reshape(token_count, width)
    grad_wo = [
        lax.dot_general(
            jnp.concatenate(
                [
                    lax.dynamic_slice_in_dim(pieces[bits], head_index * quarter, quarter, 1)
                    for pieces in attended
                ],
                0,
            ).reshape(token_count, head_cols),
            grad_branch,
            ROWS_IN,
            preferred_element_type=jnp.float32,
        ).astype(bf16)
        for bits in range(head_groups)
    ]
    if early >= groups:
        back = comp_back()
    grad_comp_parts = [comp_chunk(n) for n in range(groups + 1)]
    kept = jnp.concatenate(grad_comp_parts, 0)[window:]
    kept = jnp.pad(kept, ((0, seg_count - kept.shape[0]), (0, 0), (0, 0)))
    got_mem, got_comp = passed_along(
        (grad_pair[0][0], back), "blk", -1
    )
    last_pair = (held + got_mem.astype(jnp.float32)).astype(bf16)
    grad_pair = jnp.concatenate([grad_pair[0][1:], *grad_pair[1:], last_pair[None]], 0)
    grad_query = jnp.concatenate(grad_query, 0)
    comp_pair_grad = kept + jnp.pad(
        got_comp.astype(jnp.float32), ((seg_count - window, 0), (0, 0), (0, 0))
    )
    comp_grad_rows = comp_pair_grad.reshape(comp_count, 2 * head_cols).astype(bf16)
    grad_packed_part = lax.dot_general(
        comp_grad_rows, wkv, COLS_IN, preferred_element_type=jnp.float32
    ).astype(bf16)

    def columns_of(bits):
        start = jnp.bitwise_xor(head_index, bits) * head_cols
        return lax.dynamic_slice_in_dim(grad_packed_part, start, head_cols, 1)

    grad_packed = sum_over_heads(
        (columns_of(0), columns_of(2)), jnp.stack([columns_of(1), columns_of(3)])
    ).astype(bf16)
    keep, sent = g_normed_parts(
        head,
        grad_query,
        grad_pair,
        grad_packed.reshape(seg_count, pad_rows, head_cols),
        weights,
        quarter,
    )
    grad_normed = sum_over_heads(keep, sent).reshape(token_count, width)
    unit_one, spread_one = row_norm(tokens.reshape(token_count, width).astype(jnp.float32))
    grad_tokens = (
        (grad_hidden + norm_back(grad_normed, unit_one, spread_one, gain_first))
        .astype(bf16)
        .reshape(tokens.shape)
    )
    normed = normed.reshape(full_count, width)
    grad_kv = grad_pair.reshape(full_count, 2 * head_cols)
    grad_wq = lax.dot_general(
        normed, grad_query.reshape(full_count, head_cols), ROWS_IN, preferred_element_type=jnp.float32
    )
    grad_wkv = lax.dot_general(normed, grad_kv, ROWS_IN, preferred_element_type=jnp.float32)
    comp_term = lax.dot_general(packed, comp_grad_rows, ROWS_IN, preferred_element_type=jnp.float32)
    grad_comp = lax.dot_general(
        grouped.reshape(comp_count, RATE * width),
        grad_packed,
        ROWS_IN,
        preferred_element_type=jnp.float32,
    ).reshape(RATE, width, head_cols)
    grad_gain_one = (
        jnp.sum(grad_wq * weights[2].astype(jnp.float32), axis=1)
        + jnp.sum(grad_wkv * wkv.astype(jnp.float32), axis=1)
        + jnp.sum(grad_comp * weights[3:].astype(jnp.float32), axis=(0, 2))
    ) / gain_first[0]
    grad_wkv = grad_wkv + comp_term
    grad_wo = sum_over_heads((grad_wo[0], grad_wo[2]), jnp.stack([grad_wo[1], grad_wo[3]])).astype(bf16)

    def by_owner(value):
        return value.astype(bf16).reshape(
            head_groups, blk_count, part, value.shape[1]
        ).transpose(1, 0, 2, 3)

    gain_rows = (
        jnp.stack([grad_gain_one, grad_gain_two])
        .reshape(2, head_groups, blk_count, part)
        .transpose(2, 1, 0, 3)
        .astype(bf16)
    )
    second_grads = jnp.concatenate(
        [
            by_owner(grad_wq),
            by_owner(grad_wkv[:, :head_cols]),
            by_owner(grad_wkv[:, head_cols:]),
            by_owner(grad_comp[0]),
            by_owner(grad_comp[1]),
            by_owner(grad_comp[2]),
            jnp.pad(gain_rows, ((0, 0), (0, 0), (0, 14), (0, head_cols - part))),
            grad_wo.reshape(blk_count, part, head_groups, head_cols).transpose(0, 2, 1, 3),
        ],
        2,
    )
    second_grads, first_sum = lax.optimization_barrier((second_grads, first_sum))
    first_sum = first_sum.astype(jnp.float32)
    own_rows = 6 * part + 16
    second_part = lax.psum_scatter(
        second_grads.reshape(-1, head_cols), "blk", scatter_dimension=0, tiled=True
    ).reshape(head_groups, own_rows + part, head_cols)
    second_sum = lax.all_to_all(
        second_part[:, :own_rows], "head", split_axis=0, concat_axis=0, tiled=True
    ).astype(jnp.float32)
    gain_sum = jnp.sum(second_sum[:, 6 * part : 6 * part + 2, :part], axis=0)
    weight_sum = (
        second_sum[:, : 6 * part]
        .reshape(head_groups, 6, part, head_cols)
        .transpose(1, 2, 0, 3)
        .reshape(6, part, width)
    )
    wo_sum = second_part[:, own_rows:].astype(jnp.float32).transpose(1, 0, 2).reshape(part, width)
    return (
        out_tokens,
        compressed,
        grad_tokens,
        weight_sum[0],
        weight_sum[1],
        weight_sum[2],
        wo_sum,
        first_sum[:ff_part].T,
        first_sum[ff_part:],
        gain_sum[0],
        gain_sum[1],
        weight_sum[3:],
    )


def solution(mesh):
    return jax.shard_map(
        per_device,
        mesh=mesh,
        in_specs=(
            P("blk", "head", None),
            P(("head", "blk"), None),
            P(("head", "blk"), None),
            P(("head", "blk"), None),
            P(("head", "blk"), None),
            P(None, ("head", "blk")),
            P(("head", "blk"), None),
            P(("head", "blk")),
            P(("head", "blk")),
            P(None, ("head", "blk"), None),
            P(),
            P("blk", "head", None),
        ),
        out_specs=(
            P("blk", "head", None),
            P("blk", None, "head"),
            P("blk", "head", None),
            P(("head", "blk"), None),
            P(("head", "blk"), None),
            P(("head", "blk"), None),
            P(("head", "blk"), None),
            P(None, ("head", "blk")),
            P(("head", "blk"), None),
            P(("head", "blk")),
            P(("head", "blk")),
            P(None, ("head", "blk"), None),
        ),
        check_vma=False,
    )
```

```python
import functools

import jax
import jax.numpy as jnp
from jax import lax
from jax.experimental import pallas as pl
from jax.experimental.pallas import tpu as pltpu
from jax.sharding import PartitionSpec as P

HD = 128
RATE = 3
CSEGS = 3


EPS = 1e-05
NEG = -1e30
ROWS_IN = (((0,), (0,)), ((), ()))
COLS_IN = (((1,), (1,)), ((), ()))


def passed_along(value, axis, steps):
    count = lax.axis_size(axis)
    leading, last = (max(0, -steps), min(count, count - steps))
    return lax.ppermute(value, axis, [(source, source + steps) for source in range(leading, last)])


LOG2E = 1.4426950408889634
PAD_ROWS = 176
VMEM_LIMIT = 56 * 1024 * 1024


def key_bias(rows, base, step, valid_rows, open_, slope):
    row = lax.broadcasted_iota(jnp.int32, (rows, 1), 0)
    place = (base + step * row).astype(jnp.float32)
    return jnp.where((row < valid_rows) & open_, place * slope, NEG)


def fwd_kernel(first, shift, place_ref, slope_ref, q_ref, own_ref, prev_ref, recv_ref, comp_ref, out_ref, lse_ref):
    step = pl.program_id(0) + first
    place = place_ref[step]
    seg_len = q_ref.shape[1]
    half = seg_len // 2
    pad_rows = comp_ref.shape[1]
    local_heads = q_ref.shape[2] // HD
    values_at = local_heads * HD
    factor = HD ** (-0.5) * LOG2E
    lower = lax.broadcasted_iota(jnp.int32, (half, half), 0) <= lax.broadcasted_iota(
        jnp.int32, (half, half), 1
    )
    for h in range(local_heads):
        kc = slice(h * HD, (h + 1) * HD)
        vc = slice(values_at + h * HD, values_at + (h + 1) * HD)
        slope = slope_ref[h]
        parts = []
        for piece in range(CSEGS):
            lag = CSEGS + 1 - piece
            bias = key_bias(pad_rows, RATE // 2 - lag * seg_len, RATE, seg_len // RATE, place >= lag, slope)
            at = step + piece - shift
            parts.append((comp_ref[at, :, kc], comp_ref[at, :, vc], bias))
        bias = key_bias(seg_len, -seg_len, 1, seg_len, place >= 1, slope)
        if first:
            parts.append((prev_ref[0, :, kc], prev_ref[0, :, vc], bias))
        else:
            is_first = step == 0
            parts.append(
                (
                    jnp.where(is_first, recv_ref[0, :, kc], prev_ref[0, :, kc]),
                    jnp.where(is_first, recv_ref[0, :, vc], prev_ref[0, :, vc]),
                    bias,
                )
            )
        own_bias = [
            key_bias(half, n * half, 1, half, place >= 0, slope) for n in range(2)
        ]
        for n in range(2):
            query = q_ref[0, n * half : (n + 1) * half, kc]
            group = list(parts)
            for m in range(n + 1):
                rows = slice(m * half, (m + 1) * half)
                group.append((own_ref[0, rows, kc], own_ref[0, rows, vc], own_bias[m]))
            scores = []
            top = None
            for index, (k, v, bias) in enumerate(group):
                raw = lax.dot_general(k, query, COLS_IN, preferred_element_type=jnp.float32)
                raw = raw * factor + bias
                if index == len(group) - 1:
                    raw = jnp.where(lower, raw, NEG)
                scores.append(raw)
                peak = jnp.max(raw, axis=0, keepdims=True)
                top = peak if top is None else jnp.maximum(top, peak)
            total = jnp.zeros_like(top)
            result = jnp.zeros((HD, half), jnp.float32)
            for raw, (k, v, bias) in zip(scores, group):
                weight = jnp.exp2(raw - top)
                total = total + jnp.sum(weight, axis=0, keepdims=True)
                result = result + lax.dot_general(
                    v, weight.astype(jnp.bfloat16), ROWS_IN, preferred_element_type=jnp.float32
                )
            result = result * (1.0 / total)
            out_ref[0, n * half : (n + 1) * half, kc] = result.T.astype(jnp.bfloat16)
            lse_ref[0, h : h + 1, n * half : (n + 1) * half] = top + jnp.log(total) * LOG2E


def bwd_kernel(
    first, place_ref, slope_ref, q_ref, own_ref, prev_ref, recv_ref, comp_ref, head_ref, g0, g1, g2, g3, att_ref, lse_ref, held_ref,
    gq_ref, gkv_ref, tail_ref, gcomp_ref, grad_ref,
):
    step = pl.program_id(0) + first
    place = place_ref[step]
    seg_len = q_ref.shape[1]
    half = seg_len // 2
    pad_rows = comp_ref.shape[1]
    local_heads = q_ref.shape[2] // HD
    values_at = local_heads * HD
    scale = HD ** (-0.5)
    factor = scale * LOG2E
    is_first = step == 0
    lower = lax.broadcasted_iota(jnp.int32, (half, half), 0) <= lax.broadcasted_iota(
        jnp.int32, (half, half), 1
    )

    at_start = pl.program_id(0) == 0

    @pl.when(at_start)
    def _():
        tail_ref[...] = held_ref[...]
        gcomp_ref[...] = jnp.zeros_like(gcomp_ref)

    place_rows(head_ref[0], (g0, g1, g2, g3), grad_ref)
    for h in range(local_heads):
        kc = slice(h * HD, (h + 1) * HD)
        vc = slice(values_at + h * HD, values_at + (h + 1) * HD)
        slope = slope_ref[h]
        query = q_ref[0, :, kc]
        grad = grad_ref[:, kc]
        lse = lse_ref[0, h : h + 1, :]
        product = grad.astype(jnp.float32) * att_ref[0, :, kc].astype(jnp.float32)
        delta = jnp.sum(product.T, axis=0, keepdims=True)

        def part(k, v, bias, cols, masked):
            raw = lax.dot_general(k, query[cols], COLS_IN, preferred_element_type=jnp.float32)
            raw = raw * factor + bias
            if masked:
                raw = jnp.where(lower, raw, NEG)
            prob = jnp.exp2(raw - lse[:, cols])
            grad_prob = lax.dot_general(v, grad[cols], COLS_IN, preferred_element_type=jnp.float32)
            grad_score = (prob * (grad_prob - delta[:, cols])).astype(jnp.bfloat16)
            gk = jnp.dot(grad_score, query[cols], preferred_element_type=jnp.float32) * scale
            gv = jnp.dot(prob.astype(jnp.bfloat16), grad[cols], preferred_element_type=jnp.float32)
            gq = lax.dot_general(k, grad_score, ROWS_IN, preferred_element_type=jnp.float32)
            return gk, gv, gq

        every = slice(0, seg_len)
        total = jnp.zeros((HD, seg_len), jnp.float32)
        for piece in range(CSEGS):
            lag = CSEGS + 1 - piece
            bias = key_bias(pad_rows, RATE // 2 - lag * seg_len, RATE, seg_len // RATE, place >= lag, slope)
            gk, gv, gq = part(comp_ref[step + piece, :, kc], comp_ref[step + piece, :, vc], bias, every, False)
            gcomp_ref[step - first + piece, :, kc] += gk
            gcomp_ref[step - first + piece, :, vc] += gv
            total = total + gq
        for n in range(2):
            rows = slice(n * half, (n + 1) * half)
            bias = key_bias(half, n * half - seg_len, 1, half, place >= 1, slope)
            k = jnp.where(is_first, recv_ref[0, rows, kc], prev_ref[0, rows, kc])
            v = jnp.where(is_first, recv_ref[0, rows, vc], prev_ref[0, rows, vc])
            gk, gv, gq = part(k, v, bias, every, False)
            gkv_ref[0, rows, kc] = (tail_ref[rows, kc] + gk).astype(jnp.bfloat16)
            gkv_ref[0, rows, vc] = (tail_ref[rows, vc] + gv).astype(jnp.bfloat16)
            total = total + gq
        lo, hi = slice(0, half), slice(half, seg_len)
        bias_lo = key_bias(half, 0, 1, half, place >= 0, slope)
        bias_hi = key_bias(half, half, 1, half, place >= 0, slope)
        gk0, gv0, gq0 = part(own_ref[0, lo, kc], own_ref[0, lo, vc], bias_lo, lo, True)
        gk1, gv1, gq1 = part(own_ref[0, lo, kc], own_ref[0, lo, vc], bias_lo, hi, False)
        gk2, gv2, gq2 = part(own_ref[0, hi, kc], own_ref[0, hi, vc], bias_hi, hi, True)
        tail_ref[lo, kc] = gk0 + gk1
        tail_ref[lo, vc] = gv0 + gv1
        tail_ref[hi, kc] = gk2
        tail_ref[hi, vc] = gv2
        gq_ref[0, lo, kc] = ((total[:, lo] + gq0) * scale).T.astype(jnp.bfloat16)
        gq_ref[0, hi, kc] = ((total[:, hi] + gq1 + gq2) * scale).T.astype(jnp.bfloat16)


def attention_specs(first, seg_len, head_cols, comp_shape):
    pair = 2 * head_cols
    return [
        pl.BlockSpec(memory_space=pltpu.SMEM),
        pl.BlockSpec(memory_space=pltpu.SMEM),
        pl.BlockSpec((1, seg_len, head_cols), lambda s: (s + first, 0, 2)),
        pl.BlockSpec((1, seg_len, pair), lambda s: (s + first, 0, 0)),
        pl.BlockSpec((1, seg_len, pair), lambda s: (jnp.maximum(s + first - 1, 0), 0, 0)),
        fixed((1, seg_len, pair)),
        fixed(comp_shape),
    ]


def attend_fwd(first, shift, count, place, slope, heads, recv_mem, comp_ext, head_cols):
    seg_len = heads.shape[1]
    local_heads = head_cols // HD
    return pl.pallas_call(
        functools.partial(fwd_kernel, first, shift),
        grid=(count,),
        in_specs=attention_specs(first, seg_len, head_cols, comp_ext.shape),
        out_specs=[by_segment((seg_len, head_cols)), by_segment((local_heads, seg_len))],
        out_shape=[
            jax.ShapeDtypeStruct((count, seg_len, head_cols), jnp.bfloat16),
            jax.ShapeDtypeStruct((count, local_heads, seg_len), jnp.float32),
        ],
        compiler_params=pltpu.CompilerParams(vmem_limit_bytes=VMEM_LIMIT),
        cost_estimate=pl.CostEstimate(
            flops=count * 10**9, bytes_accessed=count * 3 * 10**6, transcendentals=count * 16 * 10**5
        ),
        name="attend_fwd",
    )(place, slope, heads, heads, heads, recv_mem, comp_ext)


def attend_bwd(
    first, count, head, place, slope, heads, recv_mem, comp_ext, grad_mixed, attn_out, lse, held, head_cols
):
    seg_len = attn_out.shape[1]
    local_heads = head_cols // HD
    pair = 2 * head_cols
    window = (count + CSEGS - 1,) + comp_ext.shape[1:]
    return pl.pallas_call(
        functools.partial(bwd_kernel, first),
        grid=(count,),
        in_specs=attention_specs(first, seg_len, head_cols, comp_ext.shape)
        + [pl.BlockSpec(memory_space=pltpu.SMEM)]
        + [by_segment(grad_mixed[0].shape[1:], first)] * 4
        + [
            by_segment((seg_len, head_cols), first),
            by_segment((local_heads, seg_len), first),
            fixed((seg_len, pair)),
        ],
        out_specs=[
            by_segment((seg_len, head_cols)),
            by_segment((seg_len, pair)),
            pl.BlockSpec((seg_len, pair), lambda s: (0, 0)),
            pl.BlockSpec(window, lambda s: (0, 0, 0)),
        ],
        out_shape=[
            jax.ShapeDtypeStruct((count, seg_len, head_cols), jnp.bfloat16),
            jax.ShapeDtypeStruct((count, seg_len, pair), jnp.bfloat16),
            jax.ShapeDtypeStruct((seg_len, pair), jnp.float32),
            jax.ShapeDtypeStruct(window, jnp.float32),
        ],
        scratch_shapes=[pltpu.VMEM((seg_len, head_cols), jnp.bfloat16)],
        compiler_params=pltpu.CompilerParams(vmem_limit_bytes=VMEM_LIMIT),
        cost_estimate=pl.CostEstimate(
            flops=count * 2 * 10**9, bytes_accessed=count * 4 * 10**6, transcendentals=count * 16 * 10**5
        ),
        name="attend_bwd",
    )(place, slope, heads, heads, heads, recv_mem, comp_ext, head, *grad_mixed, attn_out, lse, held)


def row_norm(values):
    average = jnp.mean(values, axis=-1, keepdims=True)
    center = values - average
    spread = lax.rsqrt(jnp.mean(center * center, axis=-1, keepdims=True) + EPS)
    return center * spread, spread


def norm_back(grad, unit, spread, gain):
    scaled = grad * gain
    along = jnp.mean(scaled * unit, axis=-1, keepdims=True)
    return spread * (scaled - jnp.mean(scaled, axis=-1, keepdims=True) - unit * along)


def place_rows(head, pieces, target):
    for bits, piece in enumerate(pieces):
        rows = piece.shape[1]
        at = pl.multiple_of(jnp.bitwise_xor(head, bits) * rows, rows)
        target[pl.ds(at, rows), :] = piece[0].astype(target.dtype)


def hand_out(head, source, keep_ref, sent_ref):
    rows = keep_ref.shape[2]
    for bits, (ref, slot) in enumerate(
        ((keep_ref, 0), (sent_ref, 0), (keep_ref, 1), (sent_ref, 1))
    ):
        at = pl.multiple_of(jnp.bitwise_xor(head, bits) * rows, rows)
        ref[slot, 0] = source[pl.ds(at, rows), :].astype(ref.dtype)


def prep_kernel(
    head_ref, t0, t1, t2, t3, gain_ref, w_ref, heads_ref, normed_ref, grouped_ref, packed_ref, spread
):
    head = head_ref[0]
    quarter, width = t0.shape[1:]
    seg_len = heads_ref.shape[1]
    head_cols = w_ref.shape[2]
    pad_rows = grouped_ref.shape[1]
    tiles = width // 128
    for bits, piece in enumerate((t0, t1, t2, t3)):
        unit, _ = row_norm(piece[0].astype(jnp.float32))
        normed = (unit * gain_ref[...]).astype(jnp.bfloat16)
        at = pl.multiple_of(jnp.bitwise_xor(head, bits) * quarter, quarter)
        normed_ref[0, pl.ds(at, quarter), :] = normed
        wide = normed.astype(jnp.float32)
        for c in range(tiles):
            spread[c, pl.ds(at, quarter), :] = wide[:, c * 128 : (c + 1) * 128]
    last = spread[:, seg_len - 8 : seg_len, :]
    row = lax.broadcasted_iota(jnp.int32, last.shape, 1)
    spread[:, seg_len - 8 : seg_len, :] = jnp.where(row < 8 - seg_len % RATE, last, 0.0)
    spread[:, seg_len:, :] = jnp.zeros((tiles, spread.shape[1] - seg_len, 128), jnp.float32)
    rows = normed_ref[0]
    for n in range(3):
        heads_ref[0, :, n * head_cols : (n + 1) * head_cols] = jnp.dot(
            rows, w_ref[n], preferred_element_type=jnp.float32
        ).astype(jnp.bfloat16)
    total = jnp.zeros((pad_rows, head_cols), jnp.float32)
    for tap in range(RATE):
        for c in range(tiles):
            at = tap * width + c * 128
            grouped_ref[0, :, at : at + 128] = spread[
                c, pl.ds(tap, pad_rows, stride=RATE), :
            ].astype(jnp.bfloat16)
        total = total + jnp.dot(
            grouped_ref[0, :, tap * width : (tap + 1) * width],
            w_ref[3 + tap],
            preferred_element_type=jnp.float32,
        )
    packed_ref[0] = total.astype(jnp.bfloat16)


def fixed(shape):
    return pl.BlockSpec(shape, lambda s: (0,) * len(shape), pipeline_mode=pl.Buffered(1))


def by_segment(shape, first=0):
    return pl.BlockSpec((1,) + shape, lambda s: (s + first,) + (0,) * len(shape))


def piece_specs(quarter, width):
    spec = pl.BlockSpec((2, 1, quarter, width), lambda s: (0, s, 0, 0))
    return [spec, spec]


def piece_shapes(seg_count, quarter, width):
    shape = jax.ShapeDtypeStruct((2, seg_count, quarter, width), jnp.bfloat16)
    return [shape, shape]


def prepare(head, tokens, gain, weights, pad_rows):
    seg_count, quarter, width = tokens[0].shape
    seg_len = quarter * len(tokens)
    head_cols = weights.shape[2]
    bf16 = jnp.bfloat16
    return pl.pallas_call(
        prep_kernel,
        grid=(seg_count,),
        in_specs=[pl.BlockSpec(memory_space=pltpu.SMEM)]
        + [by_segment((quarter, width))] * 4
        + [fixed((1, width)), fixed(weights.shape)],
        out_specs=[
            by_segment((seg_len, 3 * head_cols)),
            by_segment((seg_len, width)),
            by_segment((pad_rows, RATE * width)),
            by_segment((pad_rows, head_cols)),
        ],
        out_shape=[
            jax.ShapeDtypeStruct((seg_count, seg_len, 3 * head_cols), bf16),
            jax.ShapeDtypeStruct((seg_count, seg_len, width), bf16),
            jax.ShapeDtypeStruct((seg_count, pad_rows, RATE * width), bf16),
            jax.ShapeDtypeStruct((seg_count, pad_rows, head_cols), bf16),
        ],
        scratch_shapes=[pltpu.VMEM((width // 128, RATE * pad_rows, 128), jnp.float32)],
        compiler_params=pltpu.CompilerParams(vmem_limit_bytes=VMEM_LIMIT),
        cost_estimate=pl.CostEstimate(flops=7 * 10**9, bytes_accessed=30 * 10**6, transcendentals=3072),
        name="prepare",
    )(head, *tokens, gain, weights)


def ffn_kernel(
    head_ref, a0, a1, a2, a3, o0, o1, o2, o3, t0, t1, t2, t3, g0, g1, g2, g3, gain_ref,
    up_ref, down_ref, f_keep, f_sent, n_keep, n_sent, hidden_ref, pack_ref,
    rows, grads, acc_up, acc_down,
):
    step = pl.program_id(0)
    head = head_ref[0]
    quarter, width = t0.shape[1:]
    ff_part = up_ref.shape[1]
    parts = up_ref.shape[0] // 2
    block = parts * ff_part

    @pl.when(step == 0)
    def _():
        acc_up[...] = jnp.zeros_like(acc_up)
        acc_down[...] = jnp.zeros_like(acc_down)

    place_rows(head, (t0, t1, t2, t3), rows)
    place_rows(head, (g0, g1, g2, g3), grads)
    hidden = rows[...]
    for a, o in ((a0, o0), (a1, o1), (a2, o2), (a3, o3)):
        hidden = hidden + jnp.dot(
            a[0], o[...].reshape(a.shape[2], width), preferred_element_type=jnp.float32
        )
    rows[...] = hidden
    at = pl.multiple_of(head * quarter, quarter)
    hidden_ref[0] = rows[pl.ds(at, quarter), :]
    unit, _ = row_norm(hidden)
    normed = (unit * gain_ref[...]).astype(jnp.bfloat16)
    grad = grads[...]
    result = jnp.zeros(hidden.shape, jnp.float32)
    g_normed = jnp.zeros(hidden.shape, jnp.float32)
    for n in range(2):
        own = slice(n * parts, (n + 1) * parts)
        up = up_ref[own].reshape(block, width)
        down = down_ref[own].reshape(block, width)
        lifted = lax.dot_general(normed, up, COLS_IN, preferred_element_type=jnp.float32)
        sig = 0.5 * jnp.tanh(0.5 * lifted) + 0.5
        smooth = lifted * sig
        active = smooth.astype(jnp.bfloat16)
        g_active = lax.dot_general(grad, down, COLS_IN, preferred_element_type=jnp.float32)
        g_lifted = (g_active * (sig + smooth * (1.0 - sig))).astype(jnp.bfloat16)
        result = result + jnp.dot(active, down, preferred_element_type=jnp.float32)
        g_normed = g_normed + jnp.dot(g_lifted, up, preferred_element_type=jnp.float32)
        acc_down[n] += lax.dot_general(active, grad, ROWS_IN, preferred_element_type=jnp.float32)
        acc_up[n] += lax.dot_general(g_lifted, normed, ROWS_IN, preferred_element_type=jnp.float32)
    rows[...] = g_normed
    hand_out(head, rows, n_keep, n_sent)
    rows[...] = result
    hand_out(head, rows, f_keep, f_sent)

    @pl.when(step == pl.num_programs(0) - 1)
    def _():
        for n in range(2):
            own = slice(n * parts, (n + 1) * parts)
            shape = (parts, ff_part, width)
            pack_ref[own, :ff_part] = acc_up[n].astype(jnp.bfloat16).reshape(shape)
            pack_ref[own, ff_part:] = acc_down[n].astype(jnp.bfloat16).reshape(shape)


def wo_blocks(pack, part, ff_part, head_groups):
    blks, _, width = pack.shape
    start = 2 * ff_part
    if part % 16 == 0:
        specs = [
            pl.BlockSpec(
                (blks, part, width),
                functools.partial(lambda index, s: (0, index, 0), start // part + n),
                pipeline_mode=pl.Buffered(1),
            )
            for n in range(head_groups)
        ]
        return [pack] * head_groups, specs
    blocks = [
        pack[:, start + n * part : start + (n + 1) * part].reshape(blks * part, width)
        for n in range(head_groups)
    ]
    return blocks, [fixed((blks * part, width))] * head_groups


def feed_forward(head, attended, wo, wo_specs, tokens, grads, gain, pack, ff_part):
    quarter, width = tokens[0].shape[1:]
    count, seg_len, head_cols = attended[0].shape
    blks = pack.shape[0]
    half = blks // 2 * ff_part
    grad_shape = (blks, 2 * ff_part, width)
    pieces = piece_specs(quarter, width)
    shapes = piece_shapes(count, quarter, width)

    def weight(index):
        return pl.BlockSpec(
            (blks, ff_part, width), lambda s: (0, index, 0), pipeline_mode=pl.Buffered(1)
        )

    return pl.pallas_call(
        ffn_kernel,
        grid=(count,),
        in_specs=[pl.BlockSpec(memory_space=pltpu.SMEM)]
        + [by_segment((seg_len, head_cols))] * 4
        + wo_specs
        + [by_segment((quarter, width))] * 8
        + [fixed((1, width)), weight(0), weight(1)],
        out_specs=pieces + pieces
        + [by_segment((quarter, width)), pl.BlockSpec(grad_shape, lambda s: (0, 0, 0))],
        out_shape=shapes + shapes
        + [
            jax.ShapeDtypeStruct((count, quarter, width), jnp.float32),
            jax.ShapeDtypeStruct(grad_shape, jnp.bfloat16),
        ],
        scratch_shapes=[
            pltpu.VMEM((seg_len, width), jnp.float32),
            pltpu.VMEM((seg_len, width), jnp.bfloat16),
            pltpu.VMEM((2, half, width), jnp.float32),
            pltpu.VMEM((2, half, width), jnp.float32),
        ],
        compiler_params=pltpu.CompilerParams(vmem_limit_bytes=VMEM_LIMIT),
        cost_estimate=pl.CostEstimate(
            flops=count * 75 * 10**8, bytes_accessed=2 * 10**7 + count * 5 * 10**6, transcendentals=10**6
        ),
        name="feed_forward",
    )(head, *attended, *wo, *tokens, *grads, gain, pack, pack)


def middle_kernel(
    keep_ref, got_ref, far_ref, hidden_ref, grad_ref, gain_ref, o0, o1, o2, o3,
    g_hidden_ref, g_branch_ref, g_gain_ref, m0, m1, m2, m3,
):
    count, quarter, width = hidden_ref.shape
    flat = (count * quarter, width)
    gn = (
        keep_ref[0].astype(jnp.float32)
        + got_ref[0].astype(jnp.float32)
        + far_ref[...].astype(jnp.float32)
    ).reshape(flat)
    unit, spread = row_norm(hidden_ref[...].reshape(flat))
    gain_part = jnp.sum(gn * unit, axis=0, keepdims=True)

    @pl.when(pl.program_id(0) == 0)
    def _():
        g_gain_ref[...] = jnp.zeros_like(g_gain_ref)

    g_gain_ref[...] += gain_part
    g_hidden = grad_ref[...].astype(jnp.float32).reshape(flat) + norm_back(
        gn, unit, spread, gain_ref[...]
    )
    g_hidden_ref[...] = g_hidden.reshape(g_hidden_ref.shape)
    g_branch = g_hidden.astype(jnp.bfloat16)
    g_branch_ref[...] = g_branch.reshape(g_branch_ref.shape)
    for o, m in ((o0, m0), (o1, m1), (o2, m2), (o3, m3)):
        m[...] = (
            lax.dot_general(
                g_branch, o[...].reshape(m.shape[2], width), COLS_IN, preferred_element_type=jnp.float32
            )
            .astype(jnp.bfloat16)
            .reshape(m.shape)
        )


def middle(keep, got, far, hidden, grad, gain, wo, wo_specs, head_cols):
    count, quarter, width = hidden.shape
    size = 2 if count % 2 == 0 else 1
    piece = pl.BlockSpec((1, size, quarter, width), lambda s: (0, s, 0, 0))
    block = pl.BlockSpec((size, quarter, width), lambda s: (s, 0, 0))
    mixed = jax.ShapeDtypeStruct((count, quarter, head_cols), jnp.bfloat16)
    return pl.pallas_call(
        middle_kernel,
        grid=(count // size,),
        in_specs=[piece, piece, block, block, block, fixed((1, width))] + wo_specs,
        out_specs=[block, block, pl.BlockSpec((1, width), lambda s: (0, 0))]
        + [pl.BlockSpec((size, quarter, head_cols), lambda s: (s, 0, 0))] * 4,
        out_shape=[
            jax.ShapeDtypeStruct(hidden.shape, jnp.float32),
            jax.ShapeDtypeStruct(hidden.shape, jnp.bfloat16),
            jax.ShapeDtypeStruct((1, width), jnp.float32),
        ]
        + [mixed] * 4,
        compiler_params=pltpu.CompilerParams(vmem_limit_bytes=VMEM_LIMIT),
        cost_estimate=pl.CostEstimate(flops=count * 27 * 10**7, bytes_accessed=24 * 10**6, transcendentals=0),
        name="middle",
    )(keep, got, far, hidden, grad, gain, *wo)


def g_normed_kernel(head_ref, gq_ref, gkv_ref, gp_ref, w_ref, keep_ref, sent_ref, spread, rows):
    head = head_ref[0]
    seg_len, head_cols = gq_ref.shape[1:]
    pad_rows = gp_ref.shape[1]
    width = w_ref.shape[1]
    total = lax.dot_general(gq_ref[0], w_ref[2], COLS_IN, preferred_element_type=jnp.float32)
    for n in range(2):
        part = gkv_ref[0, :, n * head_cols : (n + 1) * head_cols]
        total = total + lax.dot_general(part, w_ref[n], COLS_IN, preferred_element_type=jnp.float32)
    for tap in range(RATE):
        sent = lax.dot_general(gp_ref[0], w_ref[3 + tap], COLS_IN, preferred_element_type=jnp.float32)
        for c in range(width // 128):
            spread[c, pl.ds(tap, pad_rows, stride=RATE), :] = sent[:, c * 128 : (c + 1) * 128]
    for c in range(width // 128):
        own = slice(c * 128, (c + 1) * 128)
        rows[:, own] = total[:, own] + spread[c, :seg_len, :]
    hand_out(head, rows, keep_ref, sent_ref)


def g_normed_parts(head, grad_query, grad_pair, grad_packed, weights, quarter):
    seg_count, seg_len, head_cols = grad_query.shape
    width = weights.shape[1]
    pad_rows = grad_packed.shape[1]
    return pl.pallas_call(
        g_normed_kernel,
        grid=(seg_count,),
        in_specs=[
            pl.BlockSpec(memory_space=pltpu.SMEM),
            by_segment((seg_len, head_cols)),
            by_segment((seg_len, 2 * head_cols)),
            by_segment((pad_rows, head_cols)),
            fixed(weights.shape),
        ],
        out_specs=piece_specs(quarter, width),
        out_shape=piece_shapes(seg_count, quarter, width),
        scratch_shapes=[
            pltpu.VMEM((width // 128, RATE * pad_rows, 128), jnp.float32),
            pltpu.VMEM((seg_len, width), jnp.float32),
        ],
        compiler_params=pltpu.CompilerParams(vmem_limit_bytes=VMEM_LIMIT),
        cost_estimate=pl.CostEstimate(flops=7 * 10**9, bytes_accessed=20 * 10**6, transcendentals=0),
        name="g_normed",
    )(head, grad_query, grad_pair, grad_packed, weights)


def head_swap(value, bit):
    count = lax.axis_size("head")
    return lax.ppermute(value, "head", [(source, source ^ bit) for source in range(count)])


def to_all_heads(value):
    far = head_swap(value, 2)
    return value, head_swap(value, 1), far, head_swap(far, 1)


def sum_over_heads(keep, sent):
    got = head_swap(sent, 1).astype(jnp.float32)
    far = (keep[1].astype(jnp.float32) + got[1]).astype(jnp.bfloat16)
    return keep[0].astype(jnp.float32) + got[0] + head_swap(far, 2).astype(jnp.float32)


def per_device(tokens, wq, wk, wv, wo, w_up, w_down, gain_one, gain_two, w_comp, lengths, grad_out):
    seg_count, quarter, width = tokens.shape
    head_groups = lax.axis_size("head")
    blk_count = lax.axis_size("blk")
    seg_len = quarter * head_groups
    head_cols = width // head_groups
    local_heads = head_cols // HD
    comp_rows = seg_len // RATE
    pad_rows = (comp_rows + 15) // 16 * 16
    window = CSEGS + 1
    head_index = lax.axis_index("head")
    blk_index = lax.axis_index("blk")
    token_count = seg_count * quarter
    full_count = seg_count * seg_len
    comp_count = seg_count * pad_rows
    part = wq.shape[0]
    ff_part = w_down.shape[0]
    bf16 = jnp.bfloat16
    head = head_index[None].astype(jnp.int32)

    columns = (
        jnp.concatenate([wk, wv, wq, w_comp.reshape(RATE * part, width)], 0)
        .reshape(6 * part, head_groups, head_cols)
        .transpose(1, 0, 2)
    )
    gains = jnp.pad(
        jnp.concatenate([gain_one, gain_two])[None], ((0, 15), (0, head_cols - 2 * part))
    )
    columns = jnp.concatenate(
        [columns, jnp.broadcast_to(gains, (head_groups, 16, head_cols))], 1
    )
    columns = lax.all_to_all(columns, "head", split_axis=0, concat_axis=0, tiled=True)
    columns, tokens_held = lax.optimization_barrier((columns, tokens))
    first_all = lax.all_gather(columns, "blk", axis=0)
    second_all = lax.all_gather(
        jnp.concatenate([w_up.T, w_down, *to_all_heads(wo)], 0), "blk", axis=0
    )
    token_pieces = to_all_heads(tokens_held)
    grad_held, tokens_far = lax.optimization_barrier((grad_out, token_pieces[2]))
    token_pieces = token_pieces[:2] + (tokens_far,) + token_pieces[3:]
    grad_far = head_swap(grad_held, 2)
    gain_pair = first_all[:, :, 6 * part, : 2 * part].reshape(
        blk_count, head_groups, 2, part
    ).transpose(2, 1, 0, 3).reshape(2, 1, width).astype(jnp.float32)
    gain_first, gain_second = gain_pair[0], gain_pair[1]
    weights = (
        first_all[:, :, : 6 * part]
        .reshape(blk_count, head_groups, 6, part, head_cols)
        .transpose(2, 1, 0, 3, 4)
        .reshape(6, width, head_cols)
    )
    wkv = jnp.concatenate([weights[0], weights[1]], 1)
    wo_held, wo_specs = wo_blocks(second_all, part, ff_part, head_groups)

    heads, normed, grouped, packed_mine = prepare(
        head, token_pieces, gain_first, weights, pad_rows
    )
    compressed = packed_mine[:, :comp_rows]
    recv_packed, recv_mem = passed_along(
        (packed_mine[seg_count - window :], heads[seg_count - 1 :, :, : 2 * head_cols]), "blk", 1
    )

    def all_columns(value):
        value = value.reshape(-1, head_cols)
        whole = jnp.zeros((value.shape[0], width), bf16)
        for bits, piece in enumerate(to_all_heads(value)):
            start = jnp.bitwise_xor(head_index, bits) * head_cols
            whole = lax.dynamic_update_slice(whole, piece, (0, start))
        return whole

    def comp_pairs(rows):
        return (
            jnp.dot(rows, wkv, preferred_element_type=jnp.float32)
            .astype(bf16)
            .reshape(-1, pad_rows, 2 * head_cols)
        )

    grad_far, grad_held, packed_mine = lax.optimization_barrier((grad_far, grad_held, packed_mine))
    grad_pieces = (grad_held, head_swap(grad_held, 1), grad_far, head_swap(grad_far, 1))
    packed = all_columns(packed_mine)
    comp_pair = comp_pairs(packed)
    comp_pair, grad_pieces = lax.optimization_barrier((comp_pair, grad_pieces))
    comp_ext = jnp.concatenate([comp_pairs(all_columns(recv_packed)), comp_pair], 0)
    order = jnp.arange(lengths.shape[0], dtype=jnp.int32)
    starts = jnp.sum(jnp.where(order[None, :] < order[:, None], lengths[None, :], 0), axis=1)
    seg_ids = blk_index * seg_count + jnp.arange(seg_count, dtype=jnp.int32)
    seg_place = seg_ids - jnp.max(
        jnp.where(starts[None, :] <= seg_ids[:, None], starts[None, :], 0), axis=1
    )
    head_ids = head_index * local_heads + jnp.arange(local_heads, dtype=jnp.int32)
    slopes = jnp.exp2(-head_ids.astype(jnp.float32)) / 64.0 * LOG2E
    late = attend_fwd(
        window, window, seg_count - window, seg_place, slopes, heads, heads[:1, :, : 2 * head_cols],
        comp_pair, head_cols,
    )
    comp_ext, late = lax.optimization_barrier((comp_ext, late))
    cuts = [0, window // 2, window]
    attention = [
        attend_fwd(a, 0, b - a, seg_place, slopes, heads, recv_mem, comp_ext, head_cols)
        for a, b in zip(cuts, cuts[1:])
    ] + [late]
    attn_out = jnp.concatenate([out for out, _ in attention], 0)
    lse = jnp.concatenate([total for _, total in attention], 0)
    far = jnp.concatenate([head_swap(out, 2) for out, _ in attention], 0)
    attended = (attn_out, head_swap(attn_out, 1), far, head_swap(far, 1))
    f_keep, f_sent, n_keep, n_sent, hidden, first_grads = feed_forward(
        head, attended, wo_held, wo_specs, token_pieces, grad_pieces, gain_second, second_all, ff_part
    )
    first_sum = lax.psum_scatter(first_grads, "blk", scatter_dimension=0)
    got = head_swap(n_sent, 1)
    far = (n_keep[1].astype(jnp.float32) + got[1].astype(jnp.float32)).astype(bf16)
    grad_hidden, grad_branch, grad_gain_two, *mixed = middle(
        n_keep, got, head_swap(far, 2), hidden, grad_out, gain_second, wo_held, wo_specs, head_cols
    )
    grad_gain_two = grad_gain_two[0]
    mixed = mixed[:1] + [head_swap(mixed[bits], bits) for bits in (1, 2, 3)]
    f_sent, mixed = lax.optimization_barrier((f_sent, mixed))

    def backward(a, b, held, mixed):
        return attend_bwd(
            a, b - a, head, seg_place, slopes, heads, recv_mem, comp_ext, mixed, attn_out, lse, held,
            head_cols,
        )

    held = jnp.zeros((seg_len, 2 * head_cols), jnp.float32)
    query_one, pair_one, held, comp_one = backward(0, window, held, mixed)
    mem_back, comp_back = pair_one[0], comp_one[:window].astype(bf16)
    mem_back, comp_back, mixed, held = lax.optimization_barrier((mem_back, comp_back, mixed, held))
    got_mem, got_comp = passed_along((mem_back, comp_back), "blk", -1)
    query_two, pair_two, held, comp_two = backward(window, seg_count, held, mixed)
    f_sum = sum_over_heads(f_keep, f_sent)
    query_two, f_sum, first_sum = lax.optimization_barrier((query_two, f_sum, first_sum))
    out_tokens = (hidden + f_sum).astype(bf16)
    grad_hidden = grad_hidden.reshape(token_count, width)
    grad_branch = grad_branch.reshape(token_count, width)
    over = comp_one.shape[0] - window
    kept = jnp.concatenate([comp_one[window:] + comp_two[:over], comp_two[over:]], 0)
    kept = jnp.pad(kept, ((0, seg_count - kept.shape[0]), (0, 0), (0, 0)))
    grad_pairs = [pair_one[1:], pair_two]
    last_pair = (held + got_mem.astype(jnp.float32)).astype(bf16)
    grad_pair = jnp.concatenate([*grad_pairs, last_pair[None]], 0)
    grad_query = jnp.concatenate([query_one, query_two], 0)
    comp_pair_grad = kept + jnp.pad(
        got_comp.astype(jnp.float32), ((seg_count - window, 0), (0, 0), (0, 0))
    )
    comp_grad_rows = comp_pair_grad.reshape(comp_count, 2 * head_cols).astype(bf16)
    grad_packed_part = lax.dot_general(
        comp_grad_rows, wkv, COLS_IN, preferred_element_type=jnp.float32
    ).astype(bf16)

    grad_packed_part, grad_query, grad_pair, grad_branch = lax.optimization_barrier(
        (grad_packed_part, grad_query, grad_pair, grad_branch)
    )
    grad_wo = [
        lax.dot_general(
            lax.dynamic_slice_in_dim(block, head_index * quarter, quarter, 1).reshape(
                token_count, head_cols
            ),
            grad_branch,
            ROWS_IN,
            preferred_element_type=jnp.float32,
        ).astype(bf16)
        for block in attended
    ]

    def columns_of(bits):
        start = jnp.bitwise_xor(head_index, bits) * head_cols
        return lax.dynamic_slice_in_dim(grad_packed_part, start, head_cols, 1)

    grad_packed = sum_over_heads(
        (columns_of(0), columns_of(2)), jnp.stack([columns_of(1), columns_of(3)])
    ).astype(bf16)
    keep, sent = g_normed_parts(
        head,
        grad_query,
        grad_pair,
        grad_packed.reshape(seg_count, pad_rows, head_cols),
        weights,
        quarter,
    )
    grad_normed = sum_over_heads(keep, sent).reshape(token_count, width)
    unit_one, spread_one = row_norm(tokens.reshape(token_count, width).astype(jnp.float32))
    grad_tokens = (
        (grad_hidden + norm_back(grad_normed, unit_one, spread_one, gain_first))
        .astype(bf16)
        .reshape(tokens.shape)
    )
    normed = normed.reshape(full_count, width)
    grad_kv = grad_pair.reshape(full_count, 2 * head_cols)
    grad_wq = lax.dot_general(
        normed, grad_query.reshape(full_count, head_cols), ROWS_IN, preferred_element_type=jnp.float32
    )
    grad_wkv = lax.dot_general(normed, grad_kv, ROWS_IN, preferred_element_type=jnp.float32)
    comp_term = lax.dot_general(packed, comp_grad_rows, ROWS_IN, preferred_element_type=jnp.float32)
    grad_comp = lax.dot_general(
        grouped.reshape(comp_count, RATE * width),
        grad_packed,
        ROWS_IN,
        preferred_element_type=jnp.float32,
    ).reshape(RATE, width, head_cols)
    grad_gain_one = (
        jnp.sum(grad_wq * weights[2].astype(jnp.float32), axis=1)
        + jnp.sum(grad_wkv * wkv.astype(jnp.float32), axis=1)
        + jnp.sum(grad_comp * weights[3:].astype(jnp.float32), axis=(0, 2))
    ) / gain_first[0]
    grad_wkv = grad_wkv + comp_term
    grad_wo = sum_over_heads((grad_wo[0], grad_wo[2]), jnp.stack([grad_wo[1], grad_wo[3]])).astype(bf16)

    def by_owner(value):
        return value.astype(bf16).reshape(
            head_groups, blk_count, part, value.shape[1]
        ).transpose(1, 0, 2, 3)

    gain_rows = (
        jnp.stack([grad_gain_one, grad_gain_two])
        .reshape(2, head_groups, blk_count, part)
        .transpose(2, 1, 0, 3)
        .astype(bf16)
    )
    second_grads = jnp.concatenate(
        [
            by_owner(grad_wq),
            by_owner(grad_wkv[:, :head_cols]),
            by_owner(grad_wkv[:, head_cols:]),
            by_owner(grad_comp[0]),
            by_owner(grad_comp[1]),
            by_owner(grad_comp[2]),
            jnp.pad(gain_rows, ((0, 0), (0, 0), (0, 14), (0, head_cols - part))),
            grad_wo.reshape(blk_count, part, head_groups, head_cols).transpose(0, 2, 1, 3),
        ],
        2,
    )
    second_grads, first_sum = lax.optimization_barrier((second_grads, first_sum))
    first_sum = first_sum.astype(jnp.float32)
    own_rows = 6 * part + 16
    second_part = lax.psum_scatter(
        second_grads.reshape(-1, head_cols), "blk", scatter_dimension=0, tiled=True
    ).reshape(head_groups, own_rows + part, head_cols)
    second_sum = lax.all_to_all(
        second_part[:, :own_rows], "head", split_axis=0, concat_axis=0, tiled=True
    ).astype(jnp.float32)
    gain_sum = jnp.sum(second_sum[:, 6 * part : 6 * part + 2, :part], axis=0)
    weight_sum = (
        second_sum[:, : 6 * part]
        .reshape(head_groups, 6, part, head_cols)
        .transpose(1, 2, 0, 3)
        .reshape(6, part, width)
    )
    wo_sum = second_part[:, own_rows:].astype(jnp.float32).transpose(1, 0, 2).reshape(part, width)
    return (
        out_tokens,
        compressed,
        grad_tokens,
        weight_sum[0],
        weight_sum[1],
        weight_sum[2],
        wo_sum,
        first_sum[:ff_part].T,
        first_sum[ff_part:],
        gain_sum[0],
        gain_sum[1],
        weight_sum[3:],
    )


def solution(mesh):
    return jax.shard_map(
        per_device,
        mesh=mesh,
        in_specs=(
            P("blk", "head", None),
            P(("head", "blk"), None),
            P(("head", "blk"), None),
            P(("head", "blk"), None),
            P(("head", "blk"), None),
            P(None, ("head", "blk")),
            P(("head", "blk"), None),
            P(("head", "blk")),
            P(("head", "blk")),
            P(None, ("head", "blk"), None),
            P(),
            P("blk", "head", None),
        ),
        out_specs=(
            P("blk", "head", None),
            P("blk", None, "head"),
            P("blk", "head", None),
            P(("head", "blk"), None),
            P(("head", "blk"), None),
            P(("head", "blk"), None),
            P(("head", "blk"), None),
            P(None, ("head", "blk")),
            P(("head", "blk"), None),
            P(("head", "blk")),
            P(("head", "blk")),
            P(None, ("head", "blk"), None),
        ),
        check_vma=False,
    )
```

```python
import functools

import jax
import jax.numpy as jnp
from jax import lax
from jax.experimental import pallas as pl
from jax.experimental.pallas import tpu as pltpu
from jax.sharding import PartitionSpec as P

HD = 128
RATE = 3
CSEGS = 3


EPS = 1e-05
NEG = -1e30
ROWS_IN = (((0,), (0,)), ((), ()))
COLS_IN = (((1,), (1,)), ((), ()))


def passed_along(value, axis, steps):
    count = lax.axis_size(axis)
    leading, last = (max(0, -steps), min(count, count - steps))
    return lax.ppermute(value, axis, [(source, source + steps) for source in range(leading, last)])


LOG2E = 1.4426950408889634
PAD_ROWS = 176
VMEM_LIMIT = 56 * 1024 * 1024


def key_bias(rows, base, step, valid_rows, open_, slope):
    row = lax.broadcasted_iota(jnp.int32, (rows, 1), 0)
    place = (base + step * row).astype(jnp.float32)
    return jnp.where((row < valid_rows) & open_, place * slope, NEG)


def fwd_kernel(first, shift, place_ref, slope_ref, q_ref, own_ref, prev_ref, recv_ref, comp_ref, out_ref, lse_ref):
    step = pl.program_id(0) + first
    place = place_ref[step]
    seg_len = q_ref.shape[1]
    half = seg_len // 2
    pad_rows = comp_ref.shape[1]
    local_heads = q_ref.shape[2] // HD
    values_at = local_heads * HD
    factor = HD ** (-0.5) * LOG2E
    lower = lax.broadcasted_iota(jnp.int32, (half, half), 0) <= lax.broadcasted_iota(
        jnp.int32, (half, half), 1
    )
    for h in range(local_heads):
        kc = slice(h * HD, (h + 1) * HD)
        vc = slice(values_at + h * HD, values_at + (h + 1) * HD)
        slope = slope_ref[h]
        parts = []
        for piece in range(CSEGS):
            lag = CSEGS + 1 - piece
            bias = key_bias(pad_rows, RATE // 2 - lag * seg_len, RATE, seg_len // RATE, place >= lag, slope)
            at = step + piece - shift
            parts.append((comp_ref[at, :, kc], comp_ref[at, :, vc], bias))
        bias = key_bias(seg_len, -seg_len, 1, seg_len, place >= 1, slope)
        if first:
            parts.append((prev_ref[0, :, kc], prev_ref[0, :, vc], bias))
        else:
            is_first = step == 0
            parts.append(
                (
                    jnp.where(is_first, recv_ref[0, :, kc], prev_ref[0, :, kc]),
                    jnp.where(is_first, recv_ref[0, :, vc], prev_ref[0, :, vc]),
                    bias,
                )
            )
        own_bias = [
            key_bias(half, n * half, 1, half, place >= 0, slope) for n in range(2)
        ]
        for n in range(2):
            query = q_ref[0, n * half : (n + 1) * half, kc]
            group = list(parts)
            for m in range(n + 1):
                rows = slice(m * half, (m + 1) * half)
                group.append((own_ref[0, rows, kc], own_ref[0, rows, vc], own_bias[m]))
            scores = []
            top = None
            for index, (k, v, bias) in enumerate(group):
                raw = lax.dot_general(k, query, COLS_IN, preferred_element_type=jnp.float32)
                raw = raw * factor + bias
                if index == len(group) - 1:
                    raw = jnp.where(lower, raw, NEG)
                scores.append(raw)
                peak = jnp.max(raw, axis=0, keepdims=True)
                top = peak if top is None else jnp.maximum(top, peak)
            total = jnp.zeros_like(top)
            result = jnp.zeros((HD, half), jnp.float32)
            for raw, (k, v, bias) in zip(scores, group):
                weight = jnp.exp2(raw - top)
                total = total + jnp.sum(weight, axis=0, keepdims=True)
                result = result + lax.dot_general(
                    v, weight.astype(jnp.bfloat16), ROWS_IN, preferred_element_type=jnp.float32
                )
            result = result * (1.0 / total)
            out_ref[0, n * half : (n + 1) * half, kc] = result.T.astype(jnp.bfloat16)
            lse_ref[0, h : h + 1, n * half : (n + 1) * half] = top + jnp.log(total) * LOG2E


def bwd_kernel(
    first, place_ref, slope_ref, q_ref, own_ref, prev_ref, recv_ref, comp_ref, head_ref, g0, g1, g2, g3,
    att_ref, lse_ref, held_ref, over_ref, gq_ref, gkv_ref, tail_ref, rest_ref, back_ref, grad_ref, gcomp_ref,
):
    opening = first == 0
    step = pl.program_id(0) + first
    place = place_ref[step]
    seg_len = q_ref.shape[1]
    half = seg_len // 2
    pad_rows = comp_ref.shape[1]
    local_heads = q_ref.shape[2] // HD
    values_at = local_heads * HD
    scale = HD ** (-0.5)
    factor = scale * LOG2E
    is_first = step == 0
    lower = lax.broadcasted_iota(jnp.int32, (half, half), 0) <= lax.broadcasted_iota(
        jnp.int32, (half, half), 1
    )

    at_start = pl.program_id(0) == 0

    @pl.when(at_start)
    def _():
        gcomp_ref[...] = jnp.zeros_like(gcomp_ref)
        if opening:
            tail_ref[...] = jnp.zeros_like(tail_ref)
        else:
            tail_ref[...] = held_ref[...]
            gcomp_ref[: CSEGS - 1] = over_ref[...]

    place_rows(head_ref[0], (g0, g1, g2, g3), grad_ref)
    for h in range(local_heads):
        kc = slice(h * HD, (h + 1) * HD)
        vc = slice(values_at + h * HD, values_at + (h + 1) * HD)
        slope = slope_ref[h]
        query = q_ref[0, :, kc]
        grad = grad_ref[:, kc]
        lse = lse_ref[0, h : h + 1, :]
        product = grad.astype(jnp.float32) * att_ref[0, :, kc].astype(jnp.float32)
        delta = jnp.sum(product.T, axis=0, keepdims=True)

        def part(k, v, bias, cols, masked):
            raw = lax.dot_general(k, query[cols], COLS_IN, preferred_element_type=jnp.float32)
            raw = raw * factor + bias
            if masked:
                raw = jnp.where(lower, raw, NEG)
            prob = jnp.exp2(raw - lse[:, cols])
            grad_prob = lax.dot_general(v, grad[cols], COLS_IN, preferred_element_type=jnp.float32)
            grad_score = (prob * (grad_prob - delta[:, cols])).astype(jnp.bfloat16)
            gk = jnp.dot(grad_score, query[cols], preferred_element_type=jnp.float32) * scale
            gv = jnp.dot(prob.astype(jnp.bfloat16), grad[cols], preferred_element_type=jnp.float32)
            gq = lax.dot_general(k, grad_score, ROWS_IN, preferred_element_type=jnp.float32)
            return gk, gv, gq

        every = slice(0, seg_len)
        total = jnp.zeros((HD, seg_len), jnp.float32)
        for piece in range(CSEGS):
            lag = CSEGS + 1 - piece
            bias = key_bias(pad_rows, RATE // 2 - lag * seg_len, RATE, seg_len // RATE, place >= lag, slope)
            gk, gv, gq = part(comp_ref[step + piece, :, kc], comp_ref[step + piece, :, vc], bias, every, False)
            gcomp_ref[step - first + piece, :, kc] += gk
            gcomp_ref[step - first + piece, :, vc] += gv
            total = total + gq
        for n in range(2):
            rows = slice(n * half, (n + 1) * half)
            bias = key_bias(half, n * half - seg_len, 1, half, place >= 1, slope)
            k, v = prev_ref[0, rows, kc], prev_ref[0, rows, vc]
            if opening:
                k = jnp.where(is_first, recv_ref[0, rows, kc], k)
                v = jnp.where(is_first, recv_ref[0, rows, vc], v)
            gk, gv, gq = part(k, v, bias, every, False)
            gk = (tail_ref[rows, kc] + gk).astype(jnp.bfloat16)
            gv = (tail_ref[rows, vc] + gv).astype(jnp.bfloat16)
            gkv_ref[0, rows, kc] = gk
            gkv_ref[0, rows, vc] = gv
            if opening:
                at = (CSEGS + 1) * pad_rows + n * half
                send = slice(at, at + half)

                @pl.when(is_first)
                def _(gk=gk, gv=gv, send=send):
                    back_ref[send, kc] = gk
                    back_ref[send, vc] = gv

            total = total + gq
        lo, hi = slice(0, half), slice(half, seg_len)
        bias_lo = key_bias(half, 0, 1, half, place >= 0, slope)
        bias_hi = key_bias(half, half, 1, half, place >= 0, slope)
        gk0, gv0, gq0 = part(own_ref[0, lo, kc], own_ref[0, lo, vc], bias_lo, lo, True)
        gk1, gv1, gq1 = part(own_ref[0, lo, kc], own_ref[0, lo, vc], bias_lo, hi, False)
        gk2, gv2, gq2 = part(own_ref[0, hi, kc], own_ref[0, hi, vc], bias_hi, hi, True)
        tail_ref[lo, kc] = gk0 + gk1
        tail_ref[lo, vc] = gv0 + gv1
        tail_ref[hi, kc] = gk2
        tail_ref[hi, vc] = gv2
        gq_ref[0, lo, kc] = ((total[:, lo] + gq0) * scale).T.astype(jnp.bfloat16)
        gq_ref[0, hi, kc] = ((total[:, hi] + gq1 + gq2) * scale).T.astype(jnp.bfloat16)

    @pl.when(pl.program_id(0) == pl.num_programs(0) - 1)
    def _():
        if opening:
            for entry in range(CSEGS + 1):
                rows = slice(entry * pad_rows, (entry + 1) * pad_rows)
                back_ref[rows, :] = gcomp_ref[entry].astype(jnp.bfloat16)
            rest_ref[...] = gcomp_ref[CSEGS + 1 :]
        else:
            rest_ref[...] = gcomp_ref[...]
            back_ref[...] = jnp.zeros_like(back_ref)


def attention_specs(first, seg_len, head_cols, comp_shape):
    pair = 2 * head_cols
    return [
        pl.BlockSpec(memory_space=pltpu.SMEM),
        pl.BlockSpec(memory_space=pltpu.SMEM),
        pl.BlockSpec((1, seg_len, head_cols), lambda s: (s + first, 0, 2)),
        pl.BlockSpec((1, seg_len, pair), lambda s: (s + first, 0, 0)),
        pl.BlockSpec((1, seg_len, pair), lambda s: (jnp.maximum(s + first - 1, 0), 0, 0)),
        fixed((1, seg_len, pair)),
        fixed(comp_shape),
    ]


def attend_fwd(first, shift, count, place, slope, heads, recv_mem, comp_ext, head_cols):
    seg_len = heads.shape[1]
    local_heads = head_cols // HD
    return pl.pallas_call(
        functools.partial(fwd_kernel, first, shift),
        grid=(count,),
        in_specs=attention_specs(first, seg_len, head_cols, comp_ext.shape),
        out_specs=[by_segment((seg_len, head_cols)), by_segment((local_heads, seg_len))],
        out_shape=[
            jax.ShapeDtypeStruct((count, seg_len, head_cols), jnp.bfloat16),
            jax.ShapeDtypeStruct((count, local_heads, seg_len), jnp.float32),
        ],
        compiler_params=pltpu.CompilerParams(vmem_limit_bytes=VMEM_LIMIT),
        cost_estimate=pl.CostEstimate(
            flops=count * 10**9, bytes_accessed=count * 3 * 10**6, transcendentals=count * 16 * 10**5
        ),
        name="attend_fwd",
    )(place, slope, heads, heads, heads, recv_mem, comp_ext)


def attend_bwd(
    first, count, head, place, slope, heads, recv_mem, comp_ext, grad_mixed, attn_out, lse, held, over, head_cols
):
    seg_len = attn_out.shape[1]
    local_heads = head_cols // HD
    pair = 2 * head_cols
    pad_rows = comp_ext.shape[1]
    entries = count + CSEGS - 1
    opening = first == 0
    done = count - 1 if opening else count
    rest = entries - CSEGS - 1 if opening else entries
    back = ((CSEGS + 1) * pad_rows + seg_len, pair) if opening else (16, pair)

    def pair_block(s):
        return (jnp.maximum(s - 1, 0) if opening else s, 0, 0)

    def stays(shape):
        return pl.BlockSpec(shape, lambda s: (0,) * len(shape))

    return pl.pallas_call(
        functools.partial(bwd_kernel, first),
        grid=(count,),
        in_specs=attention_specs(first, seg_len, head_cols, comp_ext.shape)
        + [pl.BlockSpec(memory_space=pltpu.SMEM)]
        + [by_segment(grad_mixed[0].shape[1:], first)] * 4
        + [
            by_segment((seg_len, head_cols), first),
            by_segment((local_heads, seg_len), first),
            fixed(held.shape),
            fixed(over.shape),
        ],
        out_specs=[
            by_segment((seg_len, head_cols)),
            pl.BlockSpec((1, seg_len, pair), pair_block),
            stays((seg_len, pair)),
            stays((rest, pad_rows, pair)),
            stays(back),
        ],
        out_shape=[
            jax.ShapeDtypeStruct((count, seg_len, head_cols), jnp.bfloat16),
            jax.ShapeDtypeStruct((done, seg_len, pair), jnp.bfloat16),
            jax.ShapeDtypeStruct((seg_len, pair), jnp.float32),
            jax.ShapeDtypeStruct((rest, pad_rows, pair), jnp.float32),
            jax.ShapeDtypeStruct(back, jnp.bfloat16),
        ],
        scratch_shapes=[
            pltpu.VMEM((seg_len, head_cols), jnp.bfloat16),
            pltpu.VMEM((entries, pad_rows, pair), jnp.float32),
        ],
        compiler_params=pltpu.CompilerParams(vmem_limit_bytes=VMEM_LIMIT),
        cost_estimate=pl.CostEstimate(
            flops=count * 2 * 10**9, bytes_accessed=count * 4 * 10**6, transcendentals=count * 16 * 10**5
        ),
        name="attend_bwd",
    )(place, slope, heads, heads, heads, recv_mem, comp_ext, head, *grad_mixed, attn_out, lse, held, over)


def row_norm(values):
    average = jnp.mean(values, axis=-1, keepdims=True)
    center = values - average
    spread = lax.rsqrt(jnp.mean(center * center, axis=-1, keepdims=True) + EPS)
    return center * spread, spread


def norm_back(grad, unit, spread, gain):
    scaled = grad * gain
    along = jnp.mean(scaled * unit, axis=-1, keepdims=True)
    return spread * (scaled - jnp.mean(scaled, axis=-1, keepdims=True) - unit * along)


def place_rows(head, pieces, target):
    for bits, piece in enumerate(pieces):
        rows = piece.shape[1]
        at = pl.multiple_of(jnp.bitwise_xor(head, bits) * rows, rows)
        target[pl.ds(at, rows), :] = piece[0].astype(target.dtype)


def hand_out(head, source, keep_ref, sent_ref):
    rows = keep_ref.shape[2]
    for bits, (ref, slot) in enumerate(
        ((keep_ref, 0), (sent_ref, 0), (keep_ref, 1), (sent_ref, 1))
    ):
        at = pl.multiple_of(jnp.bitwise_xor(head, bits) * rows, rows)
        ref[slot, 0] = source[pl.ds(at, rows), :].astype(ref.dtype)


def prep_kernel(
    head_ref, t0, t1, t2, t3, gain_ref, w_ref, heads_ref, normed_ref, grouped_ref, packed_ref, spread
):
    head = head_ref[0]
    quarter, width = t0.shape[1:]
    seg_len = heads_ref.shape[1]
    head_cols = w_ref.shape[2]
    pad_rows = grouped_ref.shape[1]
    tiles = width // 128
    for bits, piece in enumerate((t0, t1, t2, t3)):
        unit, _ = row_norm(piece[0].astype(jnp.float32))
        normed = (unit * gain_ref[...]).astype(jnp.bfloat16)
        at = pl.multiple_of(jnp.bitwise_xor(head, bits) * quarter, quarter)
        normed_ref[0, pl.ds(at, quarter), :] = normed
        wide = normed.astype(jnp.float32)
        for c in range(tiles):
            spread[c, pl.ds(at, quarter), :] = wide[:, c * 128 : (c + 1) * 128]
    last = spread[:, seg_len - 8 : seg_len, :]
    row = lax.broadcasted_iota(jnp.int32, last.shape, 1)
    spread[:, seg_len - 8 : seg_len, :] = jnp.where(row < 8 - seg_len % RATE, last, 0.0)
    spread[:, seg_len:, :] = jnp.zeros((tiles, spread.shape[1] - seg_len, 128), jnp.float32)
    rows = normed_ref[0]
    for n in range(3):
        heads_ref[0, :, n * head_cols : (n + 1) * head_cols] = jnp.dot(
            rows, w_ref[n], preferred_element_type=jnp.float32
        ).astype(jnp.bfloat16)
    total = jnp.zeros((pad_rows, head_cols), jnp.float32)
    for tap in range(RATE):
        for c in range(tiles):
            at = tap * width + c * 128
            grouped_ref[0, :, at : at + 128] = spread[
                c, pl.ds(tap, pad_rows, stride=RATE), :
            ].astype(jnp.bfloat16)
        total = total + jnp.dot(
            grouped_ref[0, :, tap * width : (tap + 1) * width],
            w_ref[3 + tap],
            preferred_element_type=jnp.float32,
        )
    packed_ref[0] = total.astype(jnp.bfloat16)


def fixed(shape):
    return pl.BlockSpec(shape, lambda s: (0,) * len(shape), pipeline_mode=pl.Buffered(1))


def by_segment(shape, first=0):
    return pl.BlockSpec((1,) + shape, lambda s: (s + first,) + (0,) * len(shape))


def piece_specs(quarter, width):
    spec = pl.BlockSpec((2, 1, quarter, width), lambda s: (0, s, 0, 0))
    return [spec, spec]


def piece_shapes(seg_count, quarter, width):
    shape = jax.ShapeDtypeStruct((2, seg_count, quarter, width), jnp.bfloat16)
    return [shape, shape]


def prepare(head, tokens, gain, weights, pad_rows):
    seg_count, quarter, width = tokens[0].shape
    seg_len = quarter * len(tokens)
    head_cols = weights.shape[2]
    bf16 = jnp.bfloat16
    return pl.pallas_call(
        prep_kernel,
        grid=(seg_count,),
        in_specs=[pl.BlockSpec(memory_space=pltpu.SMEM)]
        + [by_segment((quarter, width))] * 4
        + [fixed((1, width)), fixed(weights.shape)],
        out_specs=[
            by_segment((seg_len, 3 * head_cols)),
            by_segment((seg_len, width)),
            by_segment((pad_rows, RATE * width)),
            by_segment((pad_rows, head_cols)),
        ],
        out_shape=[
            jax.ShapeDtypeStruct((seg_count, seg_len, 3 * head_cols), bf16),
            jax.ShapeDtypeStruct((seg_count, seg_len, width), bf16),
            jax.ShapeDtypeStruct((seg_count, pad_rows, RATE * width), bf16),
            jax.ShapeDtypeStruct((seg_count, pad_rows, head_cols), bf16),
        ],
        scratch_shapes=[pltpu.VMEM((width // 128, RATE * pad_rows, 128), jnp.float32)],
        compiler_params=pltpu.CompilerParams(vmem_limit_bytes=VMEM_LIMIT),
        cost_estimate=pl.CostEstimate(flops=7 * 10**9, bytes_accessed=30 * 10**6, transcendentals=3072),
        name="prepare",
    )(head, *tokens, gain, weights)


def ffn_kernel(
    head_ref, a0, a1, a2, a3, o0, o1, o2, o3, t0, t1, t2, t3, g0, g1, g2, g3, gain_ref,
    up_ref, down_ref, f_keep, f_sent, n_keep, n_sent, hidden_ref, pack_ref,
    rows, grads, acc_up, acc_down,
):
    step = pl.program_id(0)
    head = head_ref[0]
    quarter, width = t0.shape[1:]
    ff_part = up_ref.shape[1]
    parts = up_ref.shape[0] // 2
    block = parts * ff_part

    @pl.when(step == 0)
    def _():
        acc_up[...] = jnp.zeros_like(acc_up)
        acc_down[...] = jnp.zeros_like(acc_down)

    place_rows(head, (t0, t1, t2, t3), rows)
    place_rows(head, (g0, g1, g2, g3), grads)
    hidden = rows[...]
    for a, o in ((a0, o0), (a1, o1), (a2, o2), (a3, o3)):
        hidden = hidden + jnp.dot(
            a[0], o[...].reshape(a.shape[2], width), preferred_element_type=jnp.float32
        )
    rows[...] = hidden
    at = pl.multiple_of(head * quarter, quarter)
    hidden_ref[0] = rows[pl.ds(at, quarter), :]
    unit, _ = row_norm(hidden)
    normed = (unit * gain_ref[...]).astype(jnp.bfloat16)
    grad = grads[...]
    result = jnp.zeros(hidden.shape, jnp.float32)
    g_normed = jnp.zeros(hidden.shape, jnp.float32)
    for n in range(2):
        own = slice(n * parts, (n + 1) * parts)
        up = up_ref[own].reshape(block, width)
        down = down_ref[own].reshape(block, width)
        lifted = lax.dot_general(normed, up, COLS_IN, preferred_element_type=jnp.float32)
        sig = 0.5 * jnp.tanh(0.5 * lifted) + 0.5
        smooth = lifted * sig
        active = smooth.astype(jnp.bfloat16)
        g_active = lax.dot_general(grad, down, COLS_IN, preferred_element_type=jnp.float32)
        g_lifted = (g_active * (sig + smooth * (1.0 - sig))).astype(jnp.bfloat16)
        result = result + jnp.dot(active, down, preferred_element_type=jnp.float32)
        g_normed = g_normed + jnp.dot(g_lifted, up, preferred_element_type=jnp.float32)
        acc_down[n] += lax.dot_general(active, grad, ROWS_IN, preferred_element_type=jnp.float32)
        acc_up[n] += lax.dot_general(g_lifted, normed, ROWS_IN, preferred_element_type=jnp.float32)
    rows[...] = g_normed
    hand_out(head, rows, n_keep, n_sent)
    rows[...] = result
    hand_out(head, rows, f_keep, f_sent)

    @pl.when(step == pl.num_programs(0) - 1)
    def _():
        for n in range(2):
            own = slice(n * parts, (n + 1) * parts)
            shape = (parts, ff_part, width)
            pack_ref[own, :ff_part] = acc_up[n].astype(jnp.bfloat16).reshape(shape)
            pack_ref[own, ff_part:] = acc_down[n].astype(jnp.bfloat16).reshape(shape)


def wo_blocks(pack, part, ff_part, head_groups):
    blks, _, width = pack.shape
    start = 2 * ff_part
    if part % 16 == 0:
        specs = [
            pl.BlockSpec(
                (blks, part, width),
                functools.partial(lambda index, s: (0, index, 0), start // part + n),
                pipeline_mode=pl.Buffered(1),
            )
            for n in range(head_groups)
        ]
        return [pack] * head_groups, specs
    blocks = [
        pack[:, start + n * part : start + (n + 1) * part].reshape(blks * part, width)
        for n in range(head_groups)
    ]
    return blocks, [fixed((blks * part, width))] * head_groups


def feed_forward(head, attended, wo, wo_specs, tokens, grads, gain, pack, ff_part):
    quarter, width = tokens[0].shape[1:]
    count, seg_len, head_cols = attended[0].shape
    blks = pack.shape[0]
    half = blks // 2 * ff_part
    grad_shape = (blks, 2 * ff_part, width)
    pieces = piece_specs(quarter, width)
    shapes = piece_shapes(count, quarter, width)

    def weight(index):
        return pl.BlockSpec(
            (blks, ff_part, width), lambda s: (0, index, 0), pipeline_mode=pl.Buffered(1)
        )

    return pl.pallas_call(
        ffn_kernel,
        grid=(count,),
        in_specs=[pl.BlockSpec(memory_space=pltpu.SMEM)]
        + [by_segment((seg_len, head_cols))] * 4
        + wo_specs
        + [by_segment((quarter, width))] * 8
        + [fixed((1, width)), weight(0), weight(1)],
        out_specs=pieces + pieces
        + [by_segment((quarter, width)), pl.BlockSpec(grad_shape, lambda s: (0, 0, 0))],
        out_shape=shapes + shapes
        + [
            jax.ShapeDtypeStruct((count, quarter, width), jnp.float32),
            jax.ShapeDtypeStruct(grad_shape, jnp.bfloat16),
        ],
        scratch_shapes=[
            pltpu.VMEM((seg_len, width), jnp.float32),
            pltpu.VMEM((seg_len, width), jnp.bfloat16),
            pltpu.VMEM((2, half, width), jnp.float32),
            pltpu.VMEM((2, half, width), jnp.float32),
        ],
        compiler_params=pltpu.CompilerParams(vmem_limit_bytes=VMEM_LIMIT),
        cost_estimate=pl.CostEstimate(
            flops=count * 75 * 10**8, bytes_accessed=2 * 10**7 + count * 5 * 10**6, transcendentals=10**6
        ),
        name="feed_forward",
    )(head, *attended, *wo, *tokens, *grads, gain, pack, pack)


def middle_kernel(
    keep_ref, got_ref, far_ref, hidden_ref, grad_ref, gain_ref, o0, o1, o2, o3,
    g_hidden_ref, g_branch_ref, g_gain_ref, m0, m1, m2, m3,
):
    count, quarter, width = hidden_ref.shape
    flat = (count * quarter, width)
    gn = (
        keep_ref[0].astype(jnp.float32)
        + got_ref[0].astype(jnp.float32)
        + far_ref[...].astype(jnp.float32)
    ).reshape(flat)
    unit, spread = row_norm(hidden_ref[...].reshape(flat))
    gain_part = jnp.sum(gn * unit, axis=0, keepdims=True)

    @pl.when(pl.program_id(0) == 0)
    def _():
        g_gain_ref[...] = jnp.zeros_like(g_gain_ref)

    g_gain_ref[...] += gain_part
    g_hidden = grad_ref[...].astype(jnp.float32).reshape(flat) + norm_back(
        gn, unit, spread, gain_ref[...]
    )
    g_hidden_ref[...] = g_hidden.reshape(g_hidden_ref.shape)
    g_branch = g_hidden.astype(jnp.bfloat16)
    g_branch_ref[...] = g_branch.reshape(g_branch_ref.shape)
    for o, m in ((o0, m0), (o1, m1), (o2, m2), (o3, m3)):
        m[...] = (
            lax.dot_general(
                g_branch, o[...].reshape(m.shape[2], width), COLS_IN, preferred_element_type=jnp.float32
            )
            .astype(jnp.bfloat16)
            .reshape(m.shape)
        )


def middle(keep, got, far, hidden, grad, gain, wo, wo_specs, head_cols):
    count, quarter, width = hidden.shape
    size = 2 if count % 2 == 0 else 1
    piece = pl.BlockSpec((1, size, quarter, width), lambda s: (0, s, 0, 0))
    block = pl.BlockSpec((size, quarter, width), lambda s: (s, 0, 0))
    mixed = jax.ShapeDtypeStruct((count, quarter, head_cols), jnp.bfloat16)
    return pl.pallas_call(
        middle_kernel,
        grid=(count // size,),
        in_specs=[piece, piece, block, block, block, fixed((1, width))] + wo_specs,
        out_specs=[block, block, pl.BlockSpec((1, width), lambda s: (0, 0))]
        + [pl.BlockSpec((size, quarter, head_cols), lambda s: (s, 0, 0))] * 4,
        out_shape=[
            jax.ShapeDtypeStruct(hidden.shape, jnp.float32),
            jax.ShapeDtypeStruct(hidden.shape, jnp.bfloat16),
            jax.ShapeDtypeStruct((1, width), jnp.float32),
        ]
        + [mixed] * 4,
        compiler_params=pltpu.CompilerParams(vmem_limit_bytes=VMEM_LIMIT),
        cost_estimate=pl.CostEstimate(flops=count * 27 * 10**7, bytes_accessed=24 * 10**6, transcendentals=0),
        name="middle",
    )(keep, got, far, hidden, grad, gain, *wo)


def g_normed_kernel(head_ref, gq_ref, gkv_ref, gp_ref, w_ref, keep_ref, sent_ref, spread, rows):
    head = head_ref[0]
    seg_len, head_cols = gq_ref.shape[1:]
    pad_rows = gp_ref.shape[1]
    width = w_ref.shape[1]
    total = lax.dot_general(gq_ref[0], w_ref[2], COLS_IN, preferred_element_type=jnp.float32)
    for n in range(2):
        part = gkv_ref[0, :, n * head_cols : (n + 1) * head_cols]
        total = total + lax.dot_general(part, w_ref[n], COLS_IN, preferred_element_type=jnp.float32)
    for tap in range(RATE):
        sent = lax.dot_general(gp_ref[0], w_ref[3 + tap], COLS_IN, preferred_element_type=jnp.float32)
        for c in range(width // 128):
            spread[c, pl.ds(tap, pad_rows, stride=RATE), :] = sent[:, c * 128 : (c + 1) * 128]
    for c in range(width // 128):
        own = slice(c * 128, (c + 1) * 128)
        rows[:, own] = total[:, own] + spread[c, :seg_len, :]
    hand_out(head, rows, keep_ref, sent_ref)


def g_normed_parts(head, grad_query, grad_pair, grad_packed, weights, quarter):
    seg_count, seg_len, head_cols = grad_query.shape
    width = weights.shape[1]
    pad_rows = grad_packed.shape[1]
    return pl.pallas_call(
        g_normed_kernel,
        grid=(seg_count,),
        in_specs=[
            pl.BlockSpec(memory_space=pltpu.SMEM),
            by_segment((seg_len, head_cols)),
            by_segment((seg_len, 2 * head_cols)),
            by_segment((pad_rows, head_cols)),
            fixed(weights.shape),
        ],
        out_specs=piece_specs(quarter, width),
        out_shape=piece_shapes(seg_count, quarter, width),
        scratch_shapes=[
            pltpu.VMEM((width // 128, RATE * pad_rows, 128), jnp.float32),
            pltpu.VMEM((seg_len, width), jnp.float32),
        ],
        compiler_params=pltpu.CompilerParams(vmem_limit_bytes=VMEM_LIMIT),
        cost_estimate=pl.CostEstimate(flops=7 * 10**9, bytes_accessed=20 * 10**6, transcendentals=0),
        name="g_normed",
    )(head, grad_query, grad_pair, grad_packed, weights)


def head_swap(value, bit):
    count = lax.axis_size("head")
    return lax.ppermute(value, "head", [(source, source ^ bit) for source in range(count)])


def to_all_heads(value):
    far = head_swap(value, 2)
    return value, head_swap(value, 1), far, head_swap(far, 1)


def sum_over_heads(keep, sent):
    got = head_swap(sent, 1).astype(jnp.float32)
    far = (keep[1].astype(jnp.float32) + got[1]).astype(jnp.bfloat16)
    return keep[0].astype(jnp.float32) + got[0] + head_swap(far, 2).astype(jnp.float32)


def per_device(tokens, wq, wk, wv, wo, w_up, w_down, gain_one, gain_two, w_comp, lengths, grad_out):
    seg_count, quarter, width = tokens.shape
    head_groups = lax.axis_size("head")
    blk_count = lax.axis_size("blk")
    seg_len = quarter * head_groups
    head_cols = width // head_groups
    local_heads = head_cols // HD
    comp_rows = seg_len // RATE
    pad_rows = (comp_rows + 15) // 16 * 16
    window = CSEGS + 1
    head_index = lax.axis_index("head")
    blk_index = lax.axis_index("blk")
    token_count = seg_count * quarter
    full_count = seg_count * seg_len
    comp_count = seg_count * pad_rows
    part = wq.shape[0]
    ff_part = w_down.shape[0]
    bf16 = jnp.bfloat16
    head = head_index[None].astype(jnp.int32)

    columns = (
        jnp.concatenate([wk, wv, wq, w_comp.reshape(RATE * part, width)], 0)
        .reshape(6 * part, head_groups, head_cols)
        .transpose(1, 0, 2)
    )
    gains = jnp.pad(
        jnp.concatenate([gain_one, gain_two])[None], ((0, 15), (0, head_cols - 2 * part))
    )
    columns = jnp.concatenate(
        [columns, jnp.broadcast_to(gains, (head_groups, 16, head_cols))], 1
    )
    columns = lax.all_to_all(columns, "head", split_axis=0, concat_axis=0, tiled=True)
    columns, tokens_held = lax.optimization_barrier((columns, tokens))
    first_all = lax.all_gather(columns, "blk", axis=0)
    second_all = lax.all_gather(
        jnp.concatenate([w_up.T, w_down, *to_all_heads(wo)], 0), "blk", axis=0
    )
    token_pieces = to_all_heads(tokens_held)
    grad_held, tokens_far = lax.optimization_barrier((grad_out, token_pieces[2]))
    token_pieces = token_pieces[:2] + (tokens_far,) + token_pieces[3:]
    grad_far = head_swap(grad_held, 2)
    gain_pair = first_all[:, :, 6 * part, : 2 * part].reshape(
        blk_count, head_groups, 2, part
    ).transpose(2, 1, 0, 3).reshape(2, 1, width).astype(jnp.float32)
    gain_first, gain_second = gain_pair[0], gain_pair[1]
    weights = (
        first_all[:, :, : 6 * part]
        .reshape(blk_count, head_groups, 6, part, head_cols)
        .transpose(2, 1, 0, 3, 4)
        .reshape(6, width, head_cols)
    )
    wkv = jnp.concatenate([weights[0], weights[1]], 1)
    wo_held, wo_specs = wo_blocks(second_all, part, ff_part, head_groups)

    heads, normed, grouped, packed_mine = prepare(
        head, token_pieces, gain_first, weights, pad_rows
    )
    compressed = packed_mine[:, :comp_rows]
    recv_packed, recv_mem = passed_along(
        (packed_mine[seg_count - window :], heads[seg_count - 1 :, :, : 2 * head_cols]), "blk", 1
    )

    def all_columns(value):
        value = value.reshape(-1, head_cols)
        whole = jnp.zeros((value.shape[0], width), bf16)
        for bits, piece in enumerate(to_all_heads(value)):
            start = jnp.bitwise_xor(head_index, bits) * head_cols
            whole = lax.dynamic_update_slice(whole, piece, (0, start))
        return whole

    def comp_pairs(rows):
        return (
            jnp.dot(rows, wkv, preferred_element_type=jnp.float32)
            .astype(bf16)
            .reshape(-1, pad_rows, 2 * head_cols)
        )

    grad_far, grad_held, packed_mine = lax.optimization_barrier((grad_far, grad_held, packed_mine))
    grad_pieces = (grad_held, head_swap(grad_held, 1), grad_far, head_swap(grad_far, 1))
    packed = all_columns(packed_mine)
    comp_pair = comp_pairs(packed)
    comp_pair, grad_pieces, recv_mem = lax.optimization_barrier((comp_pair, grad_pieces, recv_mem))
    comp_ext = jnp.concatenate([comp_pairs(all_columns(recv_packed)), comp_pair], 0)
    order = jnp.arange(lengths.shape[0], dtype=jnp.int32)
    starts = jnp.sum(jnp.where(order[None, :] < order[:, None], lengths[None, :], 0), axis=1)
    seg_ids = blk_index * seg_count + jnp.arange(seg_count, dtype=jnp.int32)
    seg_place = seg_ids - jnp.max(
        jnp.where(starts[None, :] <= seg_ids[:, None], starts[None, :], 0), axis=1
    )
    head_ids = head_index * local_heads + jnp.arange(local_heads, dtype=jnp.int32)
    slopes = jnp.exp2(-head_ids.astype(jnp.float32)) / 64.0 * LOG2E
    late = attend_fwd(
        window, window, seg_count - window, seg_place, slopes, heads, heads[:1, :, : 2 * head_cols],
        comp_pair, head_cols,
    )
    comp_ext, late = lax.optimization_barrier((comp_ext, late))
    middle_seg = window // 2

    def early(a, b, comp_ext):
        return attend_fwd(a, 0, b - a, seg_place, slopes, heads, recv_mem, comp_ext, head_cols)

    first = early(0, middle_seg, comp_ext)
    late_far = head_swap(late[0], 2)
    late_far, first, comp_ext = lax.optimization_barrier((late_far, first, comp_ext))
    attention = [first, early(middle_seg, window, comp_ext), late]
    attn_out = jnp.concatenate([out for out, _ in attention], 0)
    lse = jnp.concatenate([total for _, total in attention], 0)
    far = jnp.concatenate([head_swap(out, 2) for out, _ in attention[:2]] + [late_far], 0)
    attended = (attn_out, head_swap(attn_out, 1), far, head_swap(far, 1))
    f_keep, f_sent, n_keep, n_sent, hidden, first_grads = feed_forward(
        head, attended, wo_held, wo_specs, token_pieces, grad_pieces, gain_second, second_all, ff_part
    )
    first_sum = lax.psum_scatter(first_grads, "blk", scatter_dimension=0)
    got = head_swap(n_sent, 1)
    far = (n_keep[1].astype(jnp.float32) + got[1].astype(jnp.float32)).astype(bf16)
    grad_hidden, grad_branch, grad_gain_two, *mixed = middle(
        n_keep, got, head_swap(far, 2), hidden, grad_out, gain_second, wo_held, wo_specs, head_cols
    )
    grad_gain_two = grad_gain_two[0]
    mixed = mixed[:1] + [head_swap(mixed[bits], bits) for bits in (1, 2, 3)]
    grad_wo = [
        lax.dot_general(
            lax.dynamic_slice_in_dim(block, head_index * quarter, quarter, 1).reshape(
                token_count, head_cols
            ),
            grad_branch.reshape(token_count, width),
            ROWS_IN,
            preferred_element_type=jnp.float32,
        ).astype(bf16)
        for block in attended
    ]
    f_got = head_swap(f_sent, 1)
    f_far = (f_keep[1].astype(jnp.float32) + f_got[1].astype(jnp.float32)).astype(bf16)
    wo_sent = jnp.stack([grad_wo[1], grad_wo[3]])
    f_far, wo_sent, mixed = lax.optimization_barrier((f_far, wo_sent, mixed))

    def backward(a, b, held, over, mixed):
        return attend_bwd(
            a, b - a, head, seg_place, slopes, heads, recv_mem, comp_ext, mixed, attn_out, lse, held,
            over, head_cols,
        )

    held = jnp.zeros((16, 2 * head_cols), jnp.float32)
    query_one, pair_one, held, over, back = backward(0, window, held, held, mixed)
    wo_got = head_swap(wo_sent, 1).astype(jnp.float32)
    wo_far = (grad_wo[2].astype(jnp.float32) + wo_got[1]).astype(bf16)
    back, wo_far, held = lax.optimization_barrier((back, wo_far, held))
    got_back = passed_along(back, "blk", -1).astype(jnp.float32)
    query_two, pair_two, held, rest, _ = backward(window, seg_count, held, over, mixed)
    grad_hidden = grad_hidden.reshape(token_count, width)
    last_pair = (held + got_back[window * pad_rows :]).astype(bf16)
    grad_pair = jnp.concatenate([pair_one, pair_two, last_pair[None]], 0)
    grad_query = jnp.concatenate([query_one, query_two], 0)
    got_comp = got_back[: window * pad_rows].reshape(window, pad_rows, 2 * head_cols)
    comp_pair_grad = jnp.pad(rest, ((0, seg_count - rest.shape[0]), (0, 0), (0, 0))) + jnp.pad(
        got_comp, ((seg_count - window, 0), (0, 0), (0, 0))
    )
    comp_grad_rows = comp_pair_grad.reshape(comp_count, 2 * head_cols).astype(bf16)
    grad_packed_part = lax.dot_general(
        comp_grad_rows, wkv, COLS_IN, preferred_element_type=jnp.float32
    ).astype(bf16)

    grad_packed_part, grad_query, grad_pair = lax.optimization_barrier(
        (grad_packed_part, grad_query, grad_pair)
    )
    def columns_of(bits):
        start = jnp.bitwise_xor(head_index, bits) * head_cols
        return lax.dynamic_slice_in_dim(grad_packed_part, start, head_cols, 1)

    grad_packed = sum_over_heads(
        (columns_of(0), columns_of(2)), jnp.stack([columns_of(1), columns_of(3)])
    ).astype(bf16)
    f_far, wo_far = head_swap(f_far, 2), head_swap(wo_far, 2)
    grad_packed, f_far, first_sum, wo_far = lax.optimization_barrier(
        (grad_packed, f_far, first_sum, wo_far)
    )
    out_tokens = (
        hidden + f_keep[0].astype(jnp.float32) + f_got[0].astype(jnp.float32) + f_far.astype(jnp.float32)
    ).astype(bf16)
    grad_wo = (grad_wo[0].astype(jnp.float32) + wo_got[0] + wo_far.astype(jnp.float32)).astype(bf16)
    keep, sent = g_normed_parts(
        head,
        grad_query,
        grad_pair,
        grad_packed.reshape(seg_count, pad_rows, head_cols),
        weights,
        quarter,
    )
    grad_normed = sum_over_heads(keep, sent).reshape(token_count, width)
    unit_one, spread_one = row_norm(tokens.reshape(token_count, width).astype(jnp.float32))
    grad_tokens = (
        (grad_hidden + norm_back(grad_normed, unit_one, spread_one, gain_first))
        .astype(bf16)
        .reshape(tokens.shape)
    )
    normed = normed.reshape(full_count, width)
    grad_kv = grad_pair.reshape(full_count, 2 * head_cols)
    grad_wq = lax.dot_general(
        normed, grad_query.reshape(full_count, head_cols), ROWS_IN, preferred_element_type=jnp.float32
    )
    grad_wkv = lax.dot_general(normed, grad_kv, ROWS_IN, preferred_element_type=jnp.float32)
    comp_term = lax.dot_general(packed, comp_grad_rows, ROWS_IN, preferred_element_type=jnp.float32)
    grad_comp = lax.dot_general(
        grouped.reshape(comp_count, RATE * width),
        grad_packed,
        ROWS_IN,
        preferred_element_type=jnp.float32,
    ).reshape(RATE, width, head_cols)
    grad_gain_one = (
        jnp.sum(grad_wq * weights[2].astype(jnp.float32), axis=1)
        + jnp.sum(grad_wkv * wkv.astype(jnp.float32), axis=1)
        + jnp.sum(grad_comp * weights[3:].astype(jnp.float32), axis=(0, 2))
    ) / gain_first[0]
    grad_wkv = grad_wkv + comp_term

    def by_owner(value):
        return value.astype(bf16).reshape(
            head_groups, blk_count, part, value.shape[1]
        ).transpose(1, 0, 2, 3)

    gain_rows = (
        jnp.stack([grad_gain_one, grad_gain_two])
        .reshape(2, head_groups, blk_count, part)
        .transpose(2, 1, 0, 3)
        .astype(bf16)
    )
    second_grads = jnp.concatenate(
        [
            by_owner(grad_wq),
            by_owner(grad_wkv[:, :head_cols]),
            by_owner(grad_wkv[:, head_cols:]),
            by_owner(grad_comp[0]),
            by_owner(grad_comp[1]),
            by_owner(grad_comp[2]),
            jnp.pad(gain_rows, ((0, 0), (0, 0), (0, 14), (0, head_cols - part))),
            grad_wo.reshape(blk_count, part, head_groups, head_cols).transpose(0, 2, 1, 3),
        ],
        2,
    )
    second_grads, first_sum = lax.optimization_barrier((second_grads, first_sum))
    first_sum = first_sum.astype(jnp.float32)
    own_rows = 6 * part + 16
    second_part = lax.psum_scatter(
        second_grads.reshape(-1, head_cols), "blk", scatter_dimension=0, tiled=True
    ).reshape(head_groups, own_rows + part, head_cols)
    second_sum = lax.all_to_all(
        second_part[:, :own_rows], "head", split_axis=0, concat_axis=0, tiled=True
    ).astype(jnp.float32)
    gain_sum = jnp.sum(second_sum[:, 6 * part : 6 * part + 2, :part], axis=0)
    weight_sum = (
        second_sum[:, : 6 * part]
        .reshape(head_groups, 6, part, head_cols)
        .transpose(1, 2, 0, 3)
        .reshape(6, part, width)
    )
    wo_sum = second_part[:, own_rows:].astype(jnp.float32).transpose(1, 0, 2).reshape(part, width)
    return (
        out_tokens,
        compressed,
        grad_tokens,
        weight_sum[0],
        weight_sum[1],
        weight_sum[2],
        wo_sum,
        first_sum[:ff_part].T,
        first_sum[ff_part:],
        gain_sum[0],
        gain_sum[1],
        weight_sum[3:],
    )


def solution(mesh):
    return jax.shard_map(
        per_device,
        mesh=mesh,
        in_specs=(
            P("blk", "head", None),
            P(("head", "blk"), None),
            P(("head", "blk"), None),
            P(("head", "blk"), None),
            P(("head", "blk"), None),
            P(None, ("head", "blk")),
            P(("head", "blk"), None),
            P(("head", "blk")),
            P(("head", "blk")),
            P(None, ("head", "blk"), None),
            P(),
            P("blk", "head", None),
        ),
        out_specs=(
            P("blk", "head", None),
            P("blk", None, "head"),
            P("blk", "head", None),
            P(("head", "blk"), None),
            P(("head", "blk"), None),
            P(("head", "blk"), None),
            P(("head", "blk"), None),
            P(None, ("head", "blk")),
            P(("head", "blk"), None),
            P(("head", "blk")),
            P(("head", "blk")),
            P(None, ("head", "blk"), None),
        ),
        check_vma=False,
    )
```

```python
import functools

import jax
import jax.numpy as jnp
from jax import lax
from jax.experimental import pallas as pl
from jax.experimental.pallas import tpu as pltpu
from jax.sharding import PartitionSpec as P

HD = 128
RATE = 3
CSEGS = 3


EPS = 1e-05
NEG = -1e30
ROWS_IN = (((0,), (0,)), ((), ()))
COLS_IN = (((1,), (1,)), ((), ()))


def passed_along(value, axis, steps):
    count = lax.axis_size(axis)
    leading, last = (max(0, -steps), min(count, count - steps))
    return lax.ppermute(value, axis, [(source, source + steps) for source in range(leading, last)])


LOG2E = 1.4426950408889634
PAD_ROWS = 176
VMEM_LIMIT = 56 * 1024 * 1024


def key_bias(rows, base, step, valid_rows, open_, slope):
    row = lax.broadcasted_iota(jnp.int32, (rows, 1), 0)
    place = (base + step * row).astype(jnp.float32)
    return jnp.where((row < valid_rows) & open_, place * slope, NEG)


def fwd_kernel(first, shift, place_ref, slope_ref, q_ref, own_ref, prev_ref, recv_ref, comp_ref, out_ref, lse_ref):
    step = pl.program_id(0) + first
    place = place_ref[step]
    seg_len = q_ref.shape[1]
    half = seg_len // 2
    pad_rows = comp_ref.shape[1]
    local_heads = q_ref.shape[2] // HD
    values_at = local_heads * HD
    factor = HD ** (-0.5) * LOG2E
    lower = lax.broadcasted_iota(jnp.int32, (half, half), 0) <= lax.broadcasted_iota(
        jnp.int32, (half, half), 1
    )
    for h in range(local_heads):
        kc = slice(h * HD, (h + 1) * HD)
        vc = slice(values_at + h * HD, values_at + (h + 1) * HD)
        slope = slope_ref[h]
        parts = []
        for piece in range(CSEGS):
            lag = CSEGS + 1 - piece
            bias = key_bias(pad_rows, RATE // 2 - lag * seg_len, RATE, seg_len // RATE, place >= lag, slope)
            at = step + piece - shift
            parts.append((comp_ref[at, :, kc], comp_ref[at, :, vc], bias))
        bias = key_bias(seg_len, -seg_len, 1, seg_len, place >= 1, slope)
        if first:
            parts.append((prev_ref[0, :, kc], prev_ref[0, :, vc], bias))
        else:
            is_first = step == 0
            parts.append(
                (
                    jnp.where(is_first, recv_ref[0, :, kc], prev_ref[0, :, kc]),
                    jnp.where(is_first, recv_ref[0, :, vc], prev_ref[0, :, vc]),
                    bias,
                )
            )
        own_bias = [
            key_bias(half, n * half, 1, half, place >= 0, slope) for n in range(2)
        ]
        for n in range(2):
            query = q_ref[0, n * half : (n + 1) * half, kc]
            group = list(parts)
            for m in range(n + 1):
                rows = slice(m * half, (m + 1) * half)
                group.append((own_ref[0, rows, kc], own_ref[0, rows, vc], own_bias[m]))
            scores = []
            top = None
            for index, (k, v, bias) in enumerate(group):
                raw = lax.dot_general(k, query, COLS_IN, preferred_element_type=jnp.float32)
                raw = raw * factor + bias
                if index == len(group) - 1:
                    raw = jnp.where(lower, raw, NEG)
                scores.append(raw)
                peak = jnp.max(raw, axis=0, keepdims=True)
                top = peak if top is None else jnp.maximum(top, peak)
            total = jnp.zeros_like(top)
            result = jnp.zeros((HD, half), jnp.float32)
            for raw, (k, v, bias) in zip(scores, group):
                weight = jnp.exp2(raw - top)
                total = total + jnp.sum(weight, axis=0, keepdims=True)
                result = result + lax.dot_general(
                    v, weight.astype(jnp.bfloat16), ROWS_IN, preferred_element_type=jnp.float32
                )
            result = result * (1.0 / total)
            out_ref[0, n * half : (n + 1) * half, kc] = result.T.astype(jnp.bfloat16)
            lse_ref[0, h : h + 1, n * half : (n + 1) * half] = top + jnp.log(total) * LOG2E


def bwd_kernel(
    first, place_ref, slope_ref, q_ref, own_ref, prev_ref, recv_ref, comp_ref, head_ref, g0, g1, g2, g3,
    att_ref, lse_ref, held_ref, over_ref, gq_ref, gkv_ref, tail_ref, rest_ref, back_ref, grad_ref, gcomp_ref,
):
    opening = first == 0
    step = pl.program_id(0) + first
    place = place_ref[step]
    seg_len = q_ref.shape[1]
    half = seg_len // 2
    pad_rows = comp_ref.shape[1]
    local_heads = q_ref.shape[2] // HD
    values_at = local_heads * HD
    scale = HD ** (-0.5)
    factor = scale * LOG2E
    is_first = step == 0
    lower = lax.broadcasted_iota(jnp.int32, (half, half), 0) <= lax.broadcasted_iota(
        jnp.int32, (half, half), 1
    )

    at_start = pl.program_id(0) == 0

    @pl.when(at_start)
    def _():
        gcomp_ref[...] = jnp.zeros_like(gcomp_ref)
        if opening:
            tail_ref[...] = jnp.zeros_like(tail_ref)
        else:
            tail_ref[...] = held_ref[...]
            gcomp_ref[: CSEGS - 1] = over_ref[...]

    place_rows(head_ref[0], (g0, g1, g2, g3), grad_ref)
    for h in range(local_heads):
        kc = slice(h * HD, (h + 1) * HD)
        vc = slice(values_at + h * HD, values_at + (h + 1) * HD)
        slope = slope_ref[h]
        query = q_ref[0, :, kc]
        grad = grad_ref[:, kc]
        lse = lse_ref[0, h : h + 1, :]
        product = grad.astype(jnp.float32) * att_ref[0, :, kc].astype(jnp.float32)
        delta = jnp.sum(product.T, axis=0, keepdims=True)

        def part(k, v, bias, cols, masked):
            raw = lax.dot_general(k, query[cols], COLS_IN, preferred_element_type=jnp.float32)
            raw = raw * factor + bias
            if masked:
                raw = jnp.where(lower, raw, NEG)
            prob = jnp.exp2(raw - lse[:, cols])
            grad_prob = lax.dot_general(v, grad[cols], COLS_IN, preferred_element_type=jnp.float32)
            grad_score = (prob * (grad_prob - delta[:, cols])).astype(jnp.bfloat16)
            gk = jnp.dot(grad_score, query[cols], preferred_element_type=jnp.float32) * scale
            gv = jnp.dot(prob.astype(jnp.bfloat16), grad[cols], preferred_element_type=jnp.float32)
            gq = lax.dot_general(k, grad_score, ROWS_IN, preferred_element_type=jnp.float32)
            return gk, gv, gq

        every = slice(0, seg_len)
        total = jnp.zeros((HD, seg_len), jnp.float32)
        for piece in range(CSEGS):
            lag = CSEGS + 1 - piece
            bias = key_bias(pad_rows, RATE // 2 - lag * seg_len, RATE, seg_len // RATE, place >= lag, slope)
            gk, gv, gq = part(comp_ref[step + piece, :, kc], comp_ref[step + piece, :, vc], bias, every, False)
            gcomp_ref[step - first + piece, :, kc] += gk
            gcomp_ref[step - first + piece, :, vc] += gv
            total = total + gq
        for n in range(2):
            rows = slice(n * half, (n + 1) * half)
            bias = key_bias(half, n * half - seg_len, 1, half, place >= 1, slope)
            k, v = prev_ref[0, rows, kc], prev_ref[0, rows, vc]
            if opening:
                k = jnp.where(is_first, recv_ref[0, rows, kc], k)
                v = jnp.where(is_first, recv_ref[0, rows, vc], v)
            gk, gv, gq = part(k, v, bias, every, False)
            gk = (tail_ref[rows, kc] + gk).astype(jnp.bfloat16)
            gv = (tail_ref[rows, vc] + gv).astype(jnp.bfloat16)
            gkv_ref[0, rows, kc] = gk
            gkv_ref[0, rows, vc] = gv
            if opening:
                at = (CSEGS + 1) * pad_rows + n * half
                send = slice(at, at + half)

                @pl.when(is_first)
                def _(gk=gk, gv=gv, send=send):
                    back_ref[send, kc] = gk
                    back_ref[send, vc] = gv

            total = total + gq
        lo, hi = slice(0, half), slice(half, seg_len)
        bias_lo = key_bias(half, 0, 1, half, place >= 0, slope)
        bias_hi = key_bias(half, half, 1, half, place >= 0, slope)
        gk0, gv0, gq0 = part(own_ref[0, lo, kc], own_ref[0, lo, vc], bias_lo, lo, True)
        gk1, gv1, gq1 = part(own_ref[0, lo, kc], own_ref[0, lo, vc], bias_lo, hi, False)
        gk2, gv2, gq2 = part(own_ref[0, hi, kc], own_ref[0, hi, vc], bias_hi, hi, True)
        tail_ref[lo, kc] = gk0 + gk1
        tail_ref[lo, vc] = gv0 + gv1
        tail_ref[hi, kc] = gk2
        tail_ref[hi, vc] = gv2
        gq_ref[0, lo, kc] = ((total[:, lo] + gq0) * scale).T.astype(jnp.bfloat16)
        gq_ref[0, hi, kc] = ((total[:, hi] + gq1 + gq2) * scale).T.astype(jnp.bfloat16)

    @pl.when(pl.program_id(0) == pl.num_programs(0) - 1)
    def _():
        if opening:
            for entry in range(CSEGS + 1):
                rows = slice(entry * pad_rows, (entry + 1) * pad_rows)
                back_ref[rows, :] = gcomp_ref[entry].astype(jnp.bfloat16)
            rest_ref[...] = gcomp_ref[CSEGS + 1 :]
        else:
            rest_ref[...] = gcomp_ref[...]
            back_ref[...] = jnp.zeros_like(back_ref)


def attention_specs(first, seg_len, head_cols, comp_shape):
    pair = 2 * head_cols
    return [
        pl.BlockSpec(memory_space=pltpu.SMEM),
        pl.BlockSpec(memory_space=pltpu.SMEM),
        pl.BlockSpec((1, seg_len, head_cols), lambda s: (s + first, 0, 2)),
        pl.BlockSpec((1, seg_len, pair), lambda s: (s + first, 0, 0)),
        pl.BlockSpec((1, seg_len, pair), lambda s: (jnp.maximum(s + first - 1, 0), 0, 0)),
        fixed((1, seg_len, pair)),
        fixed(comp_shape),
    ]


def attend_fwd(first, shift, count, place, slope, heads, recv_mem, comp_ext, head_cols):
    seg_len = heads.shape[1]
    local_heads = head_cols // HD
    return pl.pallas_call(
        functools.partial(fwd_kernel, first, shift),
        grid=(count,),
        in_specs=attention_specs(first, seg_len, head_cols, comp_ext.shape),
        out_specs=[by_segment((seg_len, head_cols)), by_segment((local_heads, seg_len))],
        out_shape=[
            jax.ShapeDtypeStruct((count, seg_len, head_cols), jnp.bfloat16),
            jax.ShapeDtypeStruct((count, local_heads, seg_len), jnp.float32),
        ],
        compiler_params=pltpu.CompilerParams(vmem_limit_bytes=VMEM_LIMIT),
        cost_estimate=pl.CostEstimate(
            flops=count * 10**9, bytes_accessed=count * 3 * 10**6, transcendentals=count * 16 * 10**5
        ),
        name="attend_fwd",
    )(place, slope, heads, heads, heads, recv_mem, comp_ext)


def attend_bwd(
    first, count, head, place, slope, heads, recv_mem, comp_ext, grad_mixed, attn_out, lse, held, over, head_cols
):
    seg_len = attn_out.shape[1]
    local_heads = head_cols // HD
    pair = 2 * head_cols
    pad_rows = comp_ext.shape[1]
    entries = count + CSEGS - 1
    opening = first == 0
    done = count - 1 if opening else count
    rest = entries - CSEGS - 1 if opening else entries
    back = ((CSEGS + 1) * pad_rows + seg_len, pair) if opening else (16, pair)

    def pair_block(s):
        return (jnp.maximum(s - 1, 0) if opening else s, 0, 0)

    def stays(shape):
        return pl.BlockSpec(shape, lambda s: (0,) * len(shape))

    return pl.pallas_call(
        functools.partial(bwd_kernel, first),
        grid=(count,),
        in_specs=attention_specs(first, seg_len, head_cols, comp_ext.shape)
        + [pl.BlockSpec(memory_space=pltpu.SMEM)]
        + [by_segment(grad_mixed[0].shape[1:], first)] * 4
        + [
            by_segment((seg_len, head_cols), first),
            by_segment((local_heads, seg_len), first),
            fixed(held.shape),
            fixed(over.shape),
        ],
        out_specs=[
            by_segment((seg_len, head_cols)),
            pl.BlockSpec((1, seg_len, pair), pair_block),
            stays((seg_len, pair)),
            stays((rest, pad_rows, pair)),
            stays(back),
        ],
        out_shape=[
            jax.ShapeDtypeStruct((count, seg_len, head_cols), jnp.bfloat16),
            jax.ShapeDtypeStruct((done, seg_len, pair), jnp.bfloat16),
            jax.ShapeDtypeStruct((seg_len, pair), jnp.float32),
            jax.ShapeDtypeStruct((rest, pad_rows, pair), jnp.float32),
            jax.ShapeDtypeStruct(back, jnp.bfloat16),
        ],
        scratch_shapes=[
            pltpu.VMEM((seg_len, head_cols), jnp.bfloat16),
            pltpu.VMEM((entries, pad_rows, pair), jnp.float32),
        ],
        compiler_params=pltpu.CompilerParams(vmem_limit_bytes=VMEM_LIMIT),
        cost_estimate=pl.CostEstimate(
            flops=count * 2 * 10**9, bytes_accessed=count * 4 * 10**6, transcendentals=count * 16 * 10**5
        ),
        name="attend_bwd",
    )(place, slope, heads, heads, heads, recv_mem, comp_ext, head, *grad_mixed, attn_out, lse, held, over)


def row_norm(values):
    average = jnp.mean(values, axis=-1, keepdims=True)
    center = values - average
    spread = lax.rsqrt(jnp.mean(center * center, axis=-1, keepdims=True) + EPS)
    return center * spread, spread


def norm_back(grad, unit, spread, gain):
    scaled = grad * gain
    along = jnp.mean(scaled * unit, axis=-1, keepdims=True)
    return spread * (scaled - jnp.mean(scaled, axis=-1, keepdims=True) - unit * along)


def place_rows(head, pieces, target):
    for bits, piece in enumerate(pieces):
        rows = piece.shape[1]
        at = pl.multiple_of(jnp.bitwise_xor(head, bits) * rows, rows)
        target[pl.ds(at, rows), :] = piece[0].astype(target.dtype)


def hand_out(head, source, keep_ref, sent_ref):
    rows = keep_ref.shape[2]
    for bits, (ref, slot) in enumerate(
        ((keep_ref, 0), (sent_ref, 0), (keep_ref, 1), (sent_ref, 1))
    ):
        at = pl.multiple_of(jnp.bitwise_xor(head, bits) * rows, rows)
        ref[slot, 0] = source[pl.ds(at, rows), :].astype(ref.dtype)


def prep_kernel(
    head_ref, t0, t1, t2, t3, gain_ref, w_ref, heads_ref, normed_ref, grouped_ref, packed_ref, spread
):
    head = head_ref[0]
    quarter, width = t0.shape[1:]
    seg_len = heads_ref.shape[1]
    head_cols = w_ref.shape[2]
    pad_rows = grouped_ref.shape[1]
    tiles = width // 128
    for bits, piece in enumerate((t0, t1, t2, t3)):
        unit, _ = row_norm(piece[0].astype(jnp.float32))
        normed = (unit * gain_ref[...]).astype(jnp.bfloat16)
        at = pl.multiple_of(jnp.bitwise_xor(head, bits) * quarter, quarter)
        normed_ref[0, pl.ds(at, quarter), :] = normed
        wide = normed.astype(jnp.float32)
        for c in range(tiles):
            spread[c, pl.ds(at, quarter), :] = wide[:, c * 128 : (c + 1) * 128]
    last = spread[:, seg_len - 8 : seg_len, :]
    row = lax.broadcasted_iota(jnp.int32, last.shape, 1)
    spread[:, seg_len - 8 : seg_len, :] = jnp.where(row < 8 - seg_len % RATE, last, 0.0)
    spread[:, seg_len:, :] = jnp.zeros((tiles, spread.shape[1] - seg_len, 128), jnp.float32)
    rows = normed_ref[0]
    for n in range(3):
        heads_ref[0, :, n * head_cols : (n + 1) * head_cols] = jnp.dot(
            rows, w_ref[n], preferred_element_type=jnp.float32
        ).astype(jnp.bfloat16)
    total = jnp.zeros((pad_rows, head_cols), jnp.float32)
    for tap in range(RATE):
        for c in range(tiles):
            at = tap * width + c * 128
            grouped_ref[0, :, at : at + 128] = spread[
                c, pl.ds(tap, pad_rows, stride=RATE), :
            ].astype(jnp.bfloat16)
        total = total + jnp.dot(
            grouped_ref[0, :, tap * width : (tap + 1) * width],
            w_ref[3 + tap],
            preferred_element_type=jnp.float32,
        )
    packed_ref[0] = total.astype(jnp.bfloat16)


def fixed(shape):
    return pl.BlockSpec(shape, lambda s: (0,) * len(shape), pipeline_mode=pl.Buffered(1))


def by_segment(shape, first=0):
    return pl.BlockSpec((1,) + shape, lambda s: (s + first,) + (0,) * len(shape))


def piece_specs(quarter, width):
    spec = pl.BlockSpec((2, 1, quarter, width), lambda s: (0, s, 0, 0))
    return [spec, spec]


def piece_shapes(seg_count, quarter, width):
    shape = jax.ShapeDtypeStruct((2, seg_count, quarter, width), jnp.bfloat16)
    return [shape, shape]


def prepare(head, tokens, gain, weights, pad_rows):
    seg_count, quarter, width = tokens[0].shape
    seg_len = quarter * len(tokens)
    head_cols = weights.shape[2]
    bf16 = jnp.bfloat16
    return pl.pallas_call(
        prep_kernel,
        grid=(seg_count,),
        in_specs=[pl.BlockSpec(memory_space=pltpu.SMEM)]
        + [by_segment((quarter, width))] * 4
        + [fixed((1, width)), fixed(weights.shape)],
        out_specs=[
            by_segment((seg_len, 3 * head_cols)),
            by_segment((seg_len, width)),
            by_segment((pad_rows, RATE * width)),
            by_segment((pad_rows, head_cols)),
        ],
        out_shape=[
            jax.ShapeDtypeStruct((seg_count, seg_len, 3 * head_cols), bf16),
            jax.ShapeDtypeStruct((seg_count, seg_len, width), bf16),
            jax.ShapeDtypeStruct((seg_count, pad_rows, RATE * width), bf16),
            jax.ShapeDtypeStruct((seg_count, pad_rows, head_cols), bf16),
        ],
        scratch_shapes=[pltpu.VMEM((width // 128, RATE * pad_rows, 128), jnp.float32)],
        compiler_params=pltpu.CompilerParams(vmem_limit_bytes=VMEM_LIMIT),
        cost_estimate=pl.CostEstimate(flops=7 * 10**9, bytes_accessed=30 * 10**6, transcendentals=3072),
        name="prepare",
    )(head, *tokens, gain, weights)


def ffn_kernel(
    head_ref, a0, a1, a2, a3, o0, o1, o2, o3, t0, t1, t2, t3, g0, g1, g2, g3, gain_ref,
    up_ref, down_ref, f_keep, f_sent, n_keep, n_sent, hidden_ref, pack_ref,
    acc_up, acc_down,
):
    step = pl.program_id(0)
    head = head_ref[0]
    quarter, width = t0.shape[1:]
    ff_part = up_ref.shape[1]
    parts = up_ref.shape[0] // 2
    block = parts * ff_part

    @pl.when(step == 0)
    def _():
        acc_up[...] = jnp.zeros_like(acc_up)
        acc_down[...] = jnp.zeros_like(acc_down)

    starts = [
        pl.multiple_of(jnp.bitwise_xor(head, bits) * quarter, quarter) for bits in range(4)
    ]
    hidden = jnp.concatenate([t[0] for t in (t0, t1, t2, t3)], 0).astype(jnp.float32)
    for a, o in ((a0, o0), (a1, o1), (a2, o2), (a3, o3)):
        part = jnp.concatenate([a[0, pl.ds(at, quarter), :] for at in starts], 0)
        hidden = hidden + jnp.dot(
            part, o[...].reshape(a.shape[2], width), preferred_element_type=jnp.float32
        )
    hidden_ref[0] = hidden[:quarter]
    unit, _ = row_norm(hidden)
    normed = (unit * gain_ref[...]).astype(jnp.bfloat16)
    grad = jnp.concatenate([g[0] for g in (g0, g1, g2, g3)], 0)
    result = jnp.zeros(hidden.shape, jnp.float32)
    g_normed = jnp.zeros(hidden.shape, jnp.float32)
    for n in range(2):
        own = slice(n * parts, (n + 1) * parts)
        up = up_ref[own].reshape(block, width)
        down = down_ref[own].reshape(block, width)
        lifted = lax.dot_general(normed, up, COLS_IN, preferred_element_type=jnp.float32)
        sig = 0.5 * jnp.tanh(0.5 * lifted) + 0.5
        smooth = lifted * sig
        active = smooth.astype(jnp.bfloat16)
        g_active = lax.dot_general(grad, down, COLS_IN, preferred_element_type=jnp.float32)
        g_lifted = (g_active * (sig + smooth * (1.0 - sig))).astype(jnp.bfloat16)
        result = result + jnp.dot(active, down, preferred_element_type=jnp.float32)
        g_normed = g_normed + jnp.dot(g_lifted, up, preferred_element_type=jnp.float32)
        acc_down[n] += lax.dot_general(active, grad, ROWS_IN, preferred_element_type=jnp.float32)
        acc_up[n] += lax.dot_general(g_lifted, normed, ROWS_IN, preferred_element_type=jnp.float32)
    for value, keep, sent in ((g_normed, n_keep, n_sent), (result, f_keep, f_sent)):
        value = value.astype(jnp.bfloat16)
        for bits, (ref, slot) in enumerate(((keep, 0), (sent, 0), (keep, 1), (sent, 1))):
            ref[slot, 0] = value[bits * quarter : (bits + 1) * quarter]

    @pl.when(step == pl.num_programs(0) - 1)
    def _():
        for n in range(2):
            own = slice(n * parts, (n + 1) * parts)
            shape = (parts, ff_part, width)
            pack_ref[own, :ff_part] = acc_up[n].astype(jnp.bfloat16).reshape(shape)
            pack_ref[own, ff_part:] = acc_down[n].astype(jnp.bfloat16).reshape(shape)


def wo_blocks(pack, part, ff_part, head_groups):
    blks, _, width = pack.shape
    start = 2 * ff_part
    if part % 16 == 0:
        specs = [
            pl.BlockSpec(
                (blks, part, width),
                functools.partial(lambda index, s: (0, index, 0), start // part + n),
                pipeline_mode=pl.Buffered(1),
            )
            for n in range(head_groups)
        ]
        return [pack] * head_groups, specs
    blocks = [
        pack[:, start + n * part : start + (n + 1) * part].reshape(blks * part, width)
        for n in range(head_groups)
    ]
    return blocks, [fixed((blks * part, width))] * head_groups


def feed_forward(head, attended, wo, wo_specs, tokens, grads, gain, pack, ff_part):
    quarter, width = tokens[0].shape[1:]
    count, seg_len, head_cols = attended[0].shape
    blks = pack.shape[0]
    half = blks // 2 * ff_part
    grad_shape = (blks, 2 * ff_part, width)
    pieces = piece_specs(quarter, width)
    shapes = piece_shapes(count, quarter, width)

    def weight(index):
        return pl.BlockSpec(
            (blks, ff_part, width), lambda s: (0, index, 0), pipeline_mode=pl.Buffered(1)
        )

    return pl.pallas_call(
        ffn_kernel,
        grid=(count,),
        in_specs=[pl.BlockSpec(memory_space=pltpu.SMEM)]
        + [by_segment((seg_len, head_cols))] * 4
        + wo_specs
        + [by_segment((quarter, width))] * 8
        + [fixed((1, width)), weight(0), weight(1)],
        out_specs=pieces + pieces
        + [by_segment((quarter, width)), pl.BlockSpec(grad_shape, lambda s: (0, 0, 0))],
        out_shape=shapes + shapes
        + [
            jax.ShapeDtypeStruct((count, quarter, width), jnp.float32),
            jax.ShapeDtypeStruct(grad_shape, jnp.bfloat16),
        ],
        scratch_shapes=[
            pltpu.VMEM((2, half, width), jnp.float32),
            pltpu.VMEM((2, half, width), jnp.float32),
        ],
        compiler_params=pltpu.CompilerParams(vmem_limit_bytes=VMEM_LIMIT),
        cost_estimate=pl.CostEstimate(
            flops=count * 75 * 10**8, bytes_accessed=2 * 10**7 + count * 5 * 10**6, transcendentals=10**6
        ),
        name="feed_forward",
    )(head, *attended, *wo, *tokens, *grads, gain, pack, pack)


def middle_kernel(
    keep_ref, got_ref, far_ref, hidden_ref, grad_ref, gain_ref, o0, o1, o2, o3,
    g_hidden_ref, g_branch_ref, g_gain_ref, m0, m1, m2, m3,
):
    count, quarter, width = hidden_ref.shape
    flat = (count * quarter, width)
    gn = (
        keep_ref[0].astype(jnp.float32)
        + got_ref[0].astype(jnp.float32)
        + far_ref[...].astype(jnp.float32)
    ).reshape(flat)
    unit, spread = row_norm(hidden_ref[...].reshape(flat))
    gain_part = jnp.sum(gn * unit, axis=0, keepdims=True)

    @pl.when(pl.program_id(0) == 0)
    def _():
        g_gain_ref[...] = jnp.zeros_like(g_gain_ref)

    g_gain_ref[...] += gain_part
    g_hidden = grad_ref[...].astype(jnp.float32).reshape(flat) + norm_back(
        gn, unit, spread, gain_ref[...]
    )
    g_hidden_ref[...] = g_hidden.reshape(g_hidden_ref.shape)
    g_branch = g_hidden.astype(jnp.bfloat16)
    g_branch_ref[...] = g_branch.reshape(g_branch_ref.shape)
    for o, m in ((o0, m0), (o1, m1), (o2, m2), (o3, m3)):
        m[...] = (
            lax.dot_general(
                g_branch, o[...].reshape(m.shape[2], width), COLS_IN, preferred_element_type=jnp.float32
            )
            .astype(jnp.bfloat16)
            .reshape(m.shape)
        )


def middle(keep, got, far, hidden, grad, gain, wo, wo_specs, head_cols):
    count, quarter, width = hidden.shape
    size = 2 if count % 2 == 0 else 1
    piece = pl.BlockSpec((1, size, quarter, width), lambda s: (0, s, 0, 0))
    block = pl.BlockSpec((size, quarter, width), lambda s: (s, 0, 0))
    mixed = jax.ShapeDtypeStruct((count, quarter, head_cols), jnp.bfloat16)
    return pl.pallas_call(
        middle_kernel,
        grid=(count // size,),
        in_specs=[piece, piece, block, block, block, fixed((1, width))] + wo_specs,
        out_specs=[block, block, pl.BlockSpec((1, width), lambda s: (0, 0))]
        + [pl.BlockSpec((size, quarter, head_cols), lambda s: (s, 0, 0))] * 4,
        out_shape=[
            jax.ShapeDtypeStruct(hidden.shape, jnp.float32),
            jax.ShapeDtypeStruct(hidden.shape, jnp.bfloat16),
            jax.ShapeDtypeStruct((1, width), jnp.float32),
        ]
        + [mixed] * 4,
        compiler_params=pltpu.CompilerParams(vmem_limit_bytes=VMEM_LIMIT),
        cost_estimate=pl.CostEstimate(flops=count * 27 * 10**7, bytes_accessed=24 * 10**6, transcendentals=0),
        name="middle",
    )(keep, got, far, hidden, grad, gain, *wo)


def g_normed_kernel(head_ref, gq_ref, gkv_ref, gp_ref, w_ref, keep_ref, sent_ref, spread, rows):
    head = head_ref[0]
    seg_len, head_cols = gq_ref.shape[1:]
    pad_rows = gp_ref.shape[1]
    width = w_ref.shape[1]
    total = lax.dot_general(gq_ref[0], w_ref[2], COLS_IN, preferred_element_type=jnp.float32)
    for n in range(2):
        part = gkv_ref[0, :, n * head_cols : (n + 1) * head_cols]
        total = total + lax.dot_general(part, w_ref[n], COLS_IN, preferred_element_type=jnp.float32)
    for tap in range(RATE):
        sent = lax.dot_general(gp_ref[0], w_ref[3 + tap], COLS_IN, preferred_element_type=jnp.float32)
        for c in range(width // 128):
            spread[c, pl.ds(tap, pad_rows, stride=RATE), :] = sent[:, c * 128 : (c + 1) * 128]
    for c in range(width // 128):
        own = slice(c * 128, (c + 1) * 128)
        rows[:, own] = total[:, own] + spread[c, :seg_len, :]
    hand_out(head, rows, keep_ref, sent_ref)


def g_normed_parts(head, grad_query, grad_pair, grad_packed, weights, quarter):
    seg_count, seg_len, head_cols = grad_query.shape
    width = weights.shape[1]
    pad_rows = grad_packed.shape[1]
    return pl.pallas_call(
        g_normed_kernel,
        grid=(seg_count,),
        in_specs=[
            pl.BlockSpec(memory_space=pltpu.SMEM),
            by_segment((seg_len, head_cols)),
            by_segment((seg_len, 2 * head_cols)),
            by_segment((pad_rows, head_cols)),
            fixed(weights.shape),
        ],
        out_specs=piece_specs(quarter, width),
        out_shape=piece_shapes(seg_count, quarter, width),
        scratch_shapes=[
            pltpu.VMEM((width // 128, RATE * pad_rows, 128), jnp.float32),
            pltpu.VMEM((seg_len, width), jnp.float32),
        ],
        compiler_params=pltpu.CompilerParams(vmem_limit_bytes=VMEM_LIMIT),
        cost_estimate=pl.CostEstimate(flops=7 * 10**9, bytes_accessed=20 * 10**6, transcendentals=0),
        name="g_normed",
    )(head, grad_query, grad_pair, grad_packed, weights)


def head_swap(value, bit):
    count = lax.axis_size("head")
    return lax.ppermute(value, "head", [(source, source ^ bit) for source in range(count)])


def to_all_heads(value):
    far = head_swap(value, 2)
    return value, head_swap(value, 1), far, head_swap(far, 1)


def sum_over_heads(keep, sent):
    got = head_swap(sent, 1).astype(jnp.float32)
    far = (keep[1].astype(jnp.float32) + got[1]).astype(jnp.bfloat16)
    return keep[0].astype(jnp.float32) + got[0] + head_swap(far, 2).astype(jnp.float32)


def per_device(tokens, wq, wk, wv, wo, w_up, w_down, gain_one, gain_two, w_comp, lengths, grad_out):
    seg_count, quarter, width = tokens.shape
    head_groups = lax.axis_size("head")
    blk_count = lax.axis_size("blk")
    seg_len = quarter * head_groups
    head_cols = width // head_groups
    local_heads = head_cols // HD
    comp_rows = seg_len // RATE
    pad_rows = (comp_rows + 15) // 16 * 16
    window = CSEGS + 1
    head_index = lax.axis_index("head")
    blk_index = lax.axis_index("blk")
    token_count = seg_count * quarter
    full_count = seg_count * seg_len
    comp_count = seg_count * pad_rows
    part = wq.shape[0]
    ff_part = w_down.shape[0]
    bf16 = jnp.bfloat16
    head = head_index[None].astype(jnp.int32)

    columns = (
        jnp.concatenate([wk, wv, wq, w_comp.reshape(RATE * part, width)], 0)
        .reshape(6 * part, head_groups, head_cols)
        .transpose(1, 0, 2)
    )
    gains = jnp.pad(
        jnp.concatenate([gain_one, gain_two])[None], ((0, 15), (0, head_cols - 2 * part))
    )
    columns = jnp.concatenate(
        [columns, jnp.broadcast_to(gains, (head_groups, 16, head_cols))], 1
    )
    columns = lax.all_to_all(columns, "head", split_axis=0, concat_axis=0, tiled=True)
    columns, tokens_held = lax.optimization_barrier((columns, tokens))
    first_all = lax.all_gather(columns, "blk", axis=0)
    second_all = lax.all_gather(
        jnp.concatenate([w_up.T, w_down, *to_all_heads(wo)], 0), "blk", axis=0
    )
    token_pieces = to_all_heads(tokens_held)
    grad_held, tokens_far = lax.optimization_barrier((grad_out, token_pieces[2]))
    token_pieces = token_pieces[:2] + (tokens_far,) + token_pieces[3:]
    grad_far = head_swap(grad_held, 2)
    gain_pair = first_all[:, :, 6 * part, : 2 * part].reshape(
        blk_count, head_groups, 2, part
    ).transpose(2, 1, 0, 3).reshape(2, 1, width).astype(jnp.float32)
    gain_first, gain_second = gain_pair[0], gain_pair[1]
    weights = (
        first_all[:, :, : 6 * part]
        .reshape(blk_count, head_groups, 6, part, head_cols)
        .transpose(2, 1, 0, 3, 4)
        .reshape(6, width, head_cols)
    )
    wkv = jnp.concatenate([weights[0], weights[1]], 1)
    wo_held, wo_specs = wo_blocks(second_all, part, ff_part, head_groups)

    heads, normed, grouped, packed_mine = prepare(
        head, token_pieces, gain_first, weights, pad_rows
    )
    compressed = packed_mine[:, :comp_rows]
    pair = 2 * head_cols
    tail_rows = packed_mine[seg_count - window :].reshape(window * pad_rows, head_cols)
    half_rows = window * pad_rows // 2
    onward = jnp.concatenate(
        [
            heads[seg_count - 1, :, :pair],
            jnp.concatenate([tail_rows[:half_rows], tail_rows[half_rows:]], 1),
        ],
        0,
    )
    recv = passed_along(onward, "blk", 1)
    recv_mem = recv[None, :seg_len]
    recv_packed = jnp.concatenate([recv[seg_len:, :head_cols], recv[seg_len:, head_cols:]], 0)

    def all_columns(value):
        value = value.reshape(-1, head_cols)
        whole = jnp.zeros((value.shape[0], width), bf16)
        for bits, piece in enumerate(to_all_heads(value)):
            start = jnp.bitwise_xor(head_index, bits) * head_cols
            whole = lax.dynamic_update_slice(whole, piece, (0, start))
        return whole

    def comp_pairs(rows):
        return (
            jnp.dot(rows, wkv, preferred_element_type=jnp.float32)
            .astype(bf16)
            .reshape(-1, pad_rows, 2 * head_cols)
        )

    grad_far, grad_held, packed_mine = lax.optimization_barrier((grad_far, grad_held, packed_mine))
    grad_pieces = (grad_held, head_swap(grad_held, 1), grad_far, head_swap(grad_far, 1))
    packed = all_columns(packed_mine)
    comp_pair = comp_pairs(packed)
    comp_pair, grad_pieces = lax.optimization_barrier((comp_pair, grad_pieces))
    comp_ext = jnp.concatenate([comp_pairs(all_columns(recv_packed)), comp_pair], 0)
    order = jnp.arange(lengths.shape[0], dtype=jnp.int32)
    starts = jnp.sum(jnp.where(order[None, :] < order[:, None], lengths[None, :], 0), axis=1)
    seg_ids = blk_index * seg_count + jnp.arange(seg_count, dtype=jnp.int32)
    seg_place = seg_ids - jnp.max(
        jnp.where(starts[None, :] <= seg_ids[:, None], starts[None, :], 0), axis=1
    )
    head_ids = head_index * local_heads + jnp.arange(local_heads, dtype=jnp.int32)
    slopes = jnp.exp2(-head_ids.astype(jnp.float32)) / 64.0 * LOG2E
    late = attend_fwd(
        window, window, seg_count - window, seg_place, slopes, heads, heads[:1, :, : 2 * head_cols],
        comp_pair, head_cols,
    )
    comp_ext, late = lax.optimization_barrier((comp_ext, late))
    middle_seg = window // 2

    def early(a, b, comp_ext):
        return attend_fwd(a, 0, b - a, seg_place, slopes, heads, recv_mem, comp_ext, head_cols)

    first = early(0, middle_seg, comp_ext)
    late_far = head_swap(late[0], 2)
    late_far, first, comp_ext = lax.optimization_barrier((late_far, first, comp_ext))
    attention = [first, early(middle_seg, window, comp_ext), late]
    attn_out = jnp.concatenate([out for out, _ in attention], 0)
    lse = jnp.concatenate([total for _, total in attention], 0)
    far = jnp.concatenate([head_swap(out, 2) for out, _ in attention[:2]] + [late_far], 0)
    attended = (attn_out, head_swap(attn_out, 1), far, head_swap(far, 1))
    f_keep, f_sent, n_keep, n_sent, hidden, first_grads = feed_forward(
        head, attended, wo_held, wo_specs, token_pieces, grad_pieces, gain_second, second_all, ff_part
    )
    first_sum = lax.psum_scatter(first_grads, "blk", scatter_dimension=0)
    got = head_swap(n_sent, 1)
    far = (n_keep[1].astype(jnp.float32) + got[1].astype(jnp.float32)).astype(bf16)
    grad_hidden, grad_branch, grad_gain_two, *mixed = middle(
        n_keep, got, head_swap(far, 2), hidden, grad_out, gain_second, wo_held, wo_specs, head_cols
    )
    grad_gain_two = grad_gain_two[0]
    mixed = mixed[:1] + [head_swap(mixed[bits], bits) for bits in (1, 2, 3)]
    grad_wo = [
        lax.dot_general(
            lax.dynamic_slice_in_dim(block, head_index * quarter, quarter, 1).reshape(
                token_count, head_cols
            ),
            grad_branch.reshape(token_count, width),
            ROWS_IN,
            preferred_element_type=jnp.float32,
        ).astype(bf16)
        for block in attended
    ]
    f_got = head_swap(f_sent, 1)
    f_far = (f_keep[1].astype(jnp.float32) + f_got[1].astype(jnp.float32)).astype(bf16)
    wo_sent = jnp.stack([grad_wo[1], grad_wo[3]])
    f_far, wo_sent, mixed = lax.optimization_barrier((f_far, wo_sent, mixed))

    def backward(a, b, held, over, mixed):
        return attend_bwd(
            a, b - a, head, seg_place, slopes, heads, recv_mem, comp_ext, mixed, attn_out, lse, held,
            over, head_cols,
        )

    held = jnp.zeros((16, 2 * head_cols), jnp.float32)
    query_one, pair_one, held, over, back = backward(0, window, held, held, mixed)
    wo_got = head_swap(wo_sent, 1).astype(jnp.float32)
    wo_far = (grad_wo[2].astype(jnp.float32) + wo_got[1]).astype(bf16)
    back, wo_far, held = lax.optimization_barrier((back, wo_far, held))
    got_back = passed_along(back, "blk", -1)
    query_two, pair_two, held, rest, _ = backward(window, seg_count, held, over, mixed)
    grad_hidden = grad_hidden.reshape(token_count, width)
    grad_query = jnp.concatenate([query_one, query_two], 0)
    normed = normed.reshape(full_count, width)
    grad_wq = lax.dot_general(
        normed, grad_query.reshape(full_count, head_cols), ROWS_IN, preferred_element_type=jnp.float32
    )
    wo_far = head_swap(wo_far, 2).astype(jnp.float32)
    grad_wo = (grad_wo[0].astype(jnp.float32) + wo_got[0] + wo_far).astype(bf16)

    def by_owner(value):
        return value.astype(bf16).reshape(
            head_groups, blk_count, part, value.shape[1]
        ).transpose(1, 0, 2, 3)

    query_grads = jnp.concatenate(
        [
            by_owner(grad_wq),
            grad_wo.reshape(blk_count, part, head_groups, head_cols).transpose(0, 2, 1, 3),
        ],
        2,
    )
    query_grads, first_sum, got_back = lax.optimization_barrier((query_grads, first_sum, got_back))
    got_back = got_back.astype(jnp.float32)
    query_part = lax.psum_scatter(
        query_grads.reshape(-1, head_cols), "blk", scatter_dimension=0, tiled=True
    ).reshape(head_groups, 2 * part, head_cols)
    last_pair = (held + got_back[window * pad_rows :]).astype(bf16)
    grad_pair = jnp.concatenate([pair_one, pair_two, last_pair[None]], 0)
    got_comp = got_back[: window * pad_rows].reshape(window, pad_rows, 2 * head_cols)
    comp_pair_grad = jnp.pad(rest, ((0, seg_count - rest.shape[0]), (0, 0), (0, 0))) + jnp.pad(
        got_comp, ((seg_count - window, 0), (0, 0), (0, 0))
    )
    comp_grad_rows = comp_pair_grad.reshape(comp_count, 2 * head_cols).astype(bf16)
    grad_packed_part = lax.dot_general(
        comp_grad_rows, wkv, COLS_IN, preferred_element_type=jnp.float32
    ).astype(bf16)

    grad_packed_part, grad_pair = lax.optimization_barrier((grad_packed_part, grad_pair))

    def columns_of(bits):
        start = jnp.bitwise_xor(head_index, bits) * head_cols
        return lax.dynamic_slice_in_dim(grad_packed_part, start, head_cols, 1)

    grad_packed = sum_over_heads(
        (columns_of(0), columns_of(2)), jnp.stack([columns_of(1), columns_of(3)])
    ).astype(bf16)
    f_far = head_swap(f_far, 2)
    grad_packed, f_far = lax.optimization_barrier((grad_packed, f_far))
    out_tokens = (
        hidden + f_keep[0].astype(jnp.float32) + f_got[0].astype(jnp.float32) + f_far.astype(jnp.float32)
    ).astype(bf16)
    keep, sent = g_normed_parts(
        head,
        grad_query,
        grad_pair,
        grad_packed.reshape(seg_count, pad_rows, head_cols),
        weights,
        quarter,
    )
    grad_normed = sum_over_heads(keep, sent).reshape(token_count, width)
    unit_one, spread_one = row_norm(tokens.reshape(token_count, width).astype(jnp.float32))
    grad_tokens = (
        (grad_hidden + norm_back(grad_normed, unit_one, spread_one, gain_first))
        .astype(bf16)
        .reshape(tokens.shape)
    )
    grad_kv = grad_pair.reshape(full_count, 2 * head_cols)
    grad_wkv = lax.dot_general(normed, grad_kv, ROWS_IN, preferred_element_type=jnp.float32)
    comp_term = lax.dot_general(packed, comp_grad_rows, ROWS_IN, preferred_element_type=jnp.float32)
    grad_comp = lax.dot_general(
        grouped.reshape(comp_count, RATE * width),
        grad_packed,
        ROWS_IN,
        preferred_element_type=jnp.float32,
    ).reshape(RATE, width, head_cols)
    grad_gain_one = (
        jnp.sum(grad_wq * weights[2].astype(jnp.float32), axis=1)
        + jnp.sum(grad_wkv * wkv.astype(jnp.float32), axis=1)
        + jnp.sum(grad_comp * weights[3:].astype(jnp.float32), axis=(0, 2))
    ) / gain_first[0]
    grad_wkv = grad_wkv + comp_term

    gain_rows = (
        jnp.stack([grad_gain_one, grad_gain_two])
        .reshape(2, head_groups, blk_count, part)
        .transpose(2, 1, 0, 3)
        .astype(bf16)
    )
    second_grads = jnp.concatenate(
        [
            by_owner(grad_wkv[:, :head_cols]),
            by_owner(grad_wkv[:, head_cols:]),
            by_owner(grad_comp[0]),
            by_owner(grad_comp[1]),
            by_owner(grad_comp[2]),
            jnp.pad(gain_rows, ((0, 0), (0, 0), (0, 14), (0, head_cols - part))),
        ],
        2,
    )
    second_grads, query_part = lax.optimization_barrier((second_grads, query_part))
    first_sum = first_sum.astype(jnp.float32)
    own_rows = 5 * part + 16
    second_part = lax.psum_scatter(
        second_grads.reshape(-1, head_cols), "blk", scatter_dimension=0, tiled=True
    ).reshape(head_groups, own_rows, head_cols)
    second_sum = lax.all_to_all(
        second_part, "head", split_axis=0, concat_axis=0, tiled=True
    ).astype(jnp.float32)
    query_sum = lax.all_to_all(
        query_part[:, :part], "head", split_axis=0, concat_axis=0, tiled=True
    ).astype(jnp.float32)
    gain_sum = jnp.sum(second_sum[:, 5 * part : 5 * part + 2, :part], axis=0)
    weight_sum = (
        second_sum[:, : 5 * part]
        .reshape(head_groups, 5, part, head_cols)
        .transpose(1, 2, 0, 3)
        .reshape(5, part, width)
    )
    wo_sum = query_part[:, part:].astype(jnp.float32).transpose(1, 0, 2).reshape(part, width)
    return (
        out_tokens,
        compressed,
        grad_tokens,
        query_sum.transpose(1, 0, 2).reshape(part, width),
        weight_sum[0],
        weight_sum[1],
        wo_sum,
        first_sum[:ff_part].T,
        first_sum[ff_part:],
        gain_sum[0],
        gain_sum[1],
        weight_sum[2:],
    )


def solution(mesh):
    return jax.shard_map(
        per_device,
        mesh=mesh,
        in_specs=(
            P("blk", "head", None),
            P(("head", "blk"), None),
            P(("head", "blk"), None),
            P(("head", "blk"), None),
            P(("head", "blk"), None),
            P(None, ("head", "blk")),
            P(("head", "blk"), None),
            P(("head", "blk")),
            P(("head", "blk")),
            P(None, ("head", "blk"), None),
            P(),
            P("blk", "head", None),
        ),
        out_specs=(
            P("blk", "head", None),
            P("blk", None, "head"),
            P("blk", "head", None),
            P(("head", "blk"), None),
            P(("head", "blk"), None),
            P(("head", "blk"), None),
            P(("head", "blk"), None),
            P(None, ("head", "blk")),
            P(("head", "blk"), None),
            P(("head", "blk")),
            P(("head", "blk")),
            P(None, ("head", "blk"), None),
        ),
        check_vma=False,
    )
```

```python
import functools

import jax
import jax.numpy as jnp
from jax import lax
from jax.experimental import pallas as pl
from jax.experimental.pallas import tpu as pltpu
from jax.sharding import PartitionSpec as P

HD = 128
RATE = 3
CSEGS = 3


EPS = 1e-05
NEG = -1e30
ROWS_IN = (((0,), (0,)), ((), ()))
COLS_IN = (((1,), (1,)), ((), ()))


def passed_along(value, axis, steps):
    count = lax.axis_size(axis)
    leading, last = (max(0, -steps), min(count, count - steps))
    return lax.ppermute(value, axis, [(source, source + steps) for source in range(leading, last)])


LOG2E = 1.4426950408889634
PAD_ROWS = 176
VMEM_LIMIT = 56 * 1024 * 1024


def key_bias(rows, base, step, valid_rows, open_, slope):
    row = lax.broadcasted_iota(jnp.int32, (rows, 1), 0)
    place = (base + step * row).astype(jnp.float32)
    return jnp.where((row < valid_rows) & open_, place * slope, NEG)


def fwd_kernel(first, shift, place_ref, slope_ref, q_ref, own_ref, prev_ref, recv_ref, comp_ref, out_ref, lse_ref):
    step = pl.program_id(0) + first
    place = place_ref[step]
    seg_len = q_ref.shape[1]
    half = seg_len // 2
    pad_rows = comp_ref.shape[1]
    local_heads = q_ref.shape[2] // HD
    values_at = local_heads * HD
    factor = HD ** (-0.5) * LOG2E
    lower = lax.broadcasted_iota(jnp.int32, (half, half), 0) <= lax.broadcasted_iota(
        jnp.int32, (half, half), 1
    )
    for h in range(local_heads):
        kc = slice(h * HD, (h + 1) * HD)
        vc = slice(values_at + h * HD, values_at + (h + 1) * HD)
        slope = slope_ref[h]
        parts = []
        for piece in range(CSEGS):
            lag = CSEGS + 1 - piece
            bias = key_bias(pad_rows, RATE // 2 - lag * seg_len, RATE, seg_len // RATE, place >= lag, slope)
            at = step + piece - shift
            parts.append((comp_ref[at, :, kc], comp_ref[at, :, vc], bias))
        bias = key_bias(seg_len, -seg_len, 1, seg_len, place >= 1, slope)
        if first:
            parts.append((prev_ref[0, :, kc], prev_ref[0, :, vc], bias))
        else:
            is_first = step == 0
            parts.append(
                (
                    jnp.where(is_first, recv_ref[0, :, kc], prev_ref[0, :, kc]),
                    jnp.where(is_first, recv_ref[0, :, vc], prev_ref[0, :, vc]),
                    bias,
                )
            )
        own_bias = [
            key_bias(half, n * half, 1, half, place >= 0, slope) for n in range(2)
        ]
        for n in range(2):
            query = q_ref[0, n * half : (n + 1) * half, kc]
            group = list(parts)
            for m in range(n + 1):
                rows = slice(m * half, (m + 1) * half)
                group.append((own_ref[0, rows, kc], own_ref[0, rows, vc], own_bias[m]))
            scores = []
            top = None
            for index, (k, v, bias) in enumerate(group):
                raw = lax.dot_general(k, query, COLS_IN, preferred_element_type=jnp.float32)
                raw = raw * factor + bias
                if index == len(group) - 1:
                    raw = jnp.where(lower, raw, NEG)
                scores.append(raw)
                peak = jnp.max(raw, axis=0, keepdims=True)
                top = peak if top is None else jnp.maximum(top, peak)
            total = jnp.zeros_like(top)
            result = jnp.zeros((HD, half), jnp.float32)
            for raw, (k, v, bias) in zip(scores, group):
                weight = jnp.exp2(raw - top)
                total = total + jnp.sum(weight, axis=0, keepdims=True)
                result = result + lax.dot_general(
                    v, weight.astype(jnp.bfloat16), ROWS_IN, preferred_element_type=jnp.float32
                )
            result = result * (1.0 / total)
            out_ref[0, n * half : (n + 1) * half, kc] = result.T.astype(jnp.bfloat16)
            lse_ref[0, h : h + 1, n * half : (n + 1) * half] = top + jnp.log(total) * LOG2E


def bwd_kernel(
    first, place_ref, slope_ref, q_ref, own_ref, prev_ref, recv_ref, comp_ref, head_ref, g0, g1, g2, g3,
    att_ref, lse_ref, held_ref, over_ref, gq_ref, gkv_ref, tail_ref, rest_ref, back_ref, grad_ref, gcomp_ref,
):
    opening = first == 0
    step = pl.program_id(0) + first
    place = place_ref[step]
    seg_len = q_ref.shape[1]
    half = seg_len // 2
    pad_rows = comp_ref.shape[1]
    local_heads = q_ref.shape[2] // HD
    values_at = local_heads * HD
    scale = HD ** (-0.5)
    factor = scale * LOG2E
    is_first = step == 0
    lower = lax.broadcasted_iota(jnp.int32, (half, half), 0) <= lax.broadcasted_iota(
        jnp.int32, (half, half), 1
    )

    at_start = pl.program_id(0) == 0

    @pl.when(at_start)
    def _():
        gcomp_ref[...] = jnp.zeros_like(gcomp_ref)
        if opening:
            tail_ref[...] = jnp.zeros_like(tail_ref)
        else:
            tail_ref[...] = held_ref[...]
            gcomp_ref[: CSEGS - 1] = over_ref[...]

    place_rows(head_ref[0], (g0, g1, g2, g3), grad_ref)
    for h in range(local_heads):
        kc = slice(h * HD, (h + 1) * HD)
        vc = slice(values_at + h * HD, values_at + (h + 1) * HD)
        slope = slope_ref[h]
        query = q_ref[0, :, kc]
        grad = grad_ref[:, kc]
        lse = lse_ref[0, h : h + 1, :]
        product = grad.astype(jnp.float32) * att_ref[0, :, kc].astype(jnp.float32)
        delta = jnp.sum(product.T, axis=0, keepdims=True)

        def part(k, v, bias, cols, masked):
            raw = lax.dot_general(k, query[cols], COLS_IN, preferred_element_type=jnp.float32)
            raw = raw * factor + bias
            if masked:
                raw = jnp.where(lower, raw, NEG)
            prob = jnp.exp2(raw - lse[:, cols])
            grad_prob = lax.dot_general(v, grad[cols], COLS_IN, preferred_element_type=jnp.float32)
            grad_score = (prob * (grad_prob - delta[:, cols])).astype(jnp.bfloat16)
            gk = jnp.dot(grad_score, query[cols], preferred_element_type=jnp.float32) * scale
            gv = jnp.dot(prob.astype(jnp.bfloat16), grad[cols], preferred_element_type=jnp.float32)
            gq = lax.dot_general(k, grad_score, ROWS_IN, preferred_element_type=jnp.float32)
            return gk, gv, gq

        every = slice(0, seg_len)
        total = jnp.zeros((HD, seg_len), jnp.float32)
        for piece in range(CSEGS):
            lag = CSEGS + 1 - piece
            bias = key_bias(pad_rows, RATE // 2 - lag * seg_len, RATE, seg_len // RATE, place >= lag, slope)
            gk, gv, gq = part(comp_ref[step + piece, :, kc], comp_ref[step + piece, :, vc], bias, every, False)
            gcomp_ref[step - first + piece, :, kc] += gk
            gcomp_ref[step - first + piece, :, vc] += gv
            total = total + gq
        for n in range(2):
            rows = slice(n * half, (n + 1) * half)
            bias = key_bias(half, n * half - seg_len, 1, half, place >= 1, slope)
            k, v = prev_ref[0, rows, kc], prev_ref[0, rows, vc]
            if opening:
                k = jnp.where(is_first, recv_ref[0, rows, kc], k)
                v = jnp.where(is_first, recv_ref[0, rows, vc], v)
            gk, gv, gq = part(k, v, bias, every, False)
            gk = (tail_ref[rows, kc] + gk).astype(jnp.bfloat16)
            gv = (tail_ref[rows, vc] + gv).astype(jnp.bfloat16)
            gkv_ref[0, rows, kc] = gk
            gkv_ref[0, rows, vc] = gv
            if opening:
                at = (CSEGS + 1) * pad_rows + n * half
                send = slice(at, at + half)

                @pl.when(is_first)
                def _(gk=gk, gv=gv, send=send):
                    back_ref[send, kc] = gk
                    back_ref[send, vc] = gv

            total = total + gq
        lo, hi = slice(0, half), slice(half, seg_len)
        bias_lo = key_bias(half, 0, 1, half, place >= 0, slope)
        bias_hi = key_bias(half, half, 1, half, place >= 0, slope)
        gk0, gv0, gq0 = part(own_ref[0, lo, kc], own_ref[0, lo, vc], bias_lo, lo, True)
        gk1, gv1, gq1 = part(own_ref[0, lo, kc], own_ref[0, lo, vc], bias_lo, hi, False)
        gk2, gv2, gq2 = part(own_ref[0, hi, kc], own_ref[0, hi, vc], bias_hi, hi, True)
        tail_ref[lo, kc] = gk0 + gk1
        tail_ref[lo, vc] = gv0 + gv1
        tail_ref[hi, kc] = gk2
        tail_ref[hi, vc] = gv2
        gq_ref[0, lo, kc] = ((total[:, lo] + gq0) * scale).T.astype(jnp.bfloat16)
        gq_ref[0, hi, kc] = ((total[:, hi] + gq1 + gq2) * scale).T.astype(jnp.bfloat16)

    @pl.when(pl.program_id(0) == pl.num_programs(0) - 1)
    def _():
        if opening:
            for entry in range(CSEGS + 1):
                rows = slice(entry * pad_rows, (entry + 1) * pad_rows)
                back_ref[rows, :] = gcomp_ref[entry].astype(jnp.bfloat16)
            rest_ref[...] = gcomp_ref[CSEGS + 1 :]
        else:
            rest_ref[...] = gcomp_ref[...]
            back_ref[...] = jnp.zeros_like(back_ref)


def attention_specs(first, seg_len, head_cols, comp_shape):
    pair = 2 * head_cols
    return [
        pl.BlockSpec(memory_space=pltpu.SMEM),
        pl.BlockSpec(memory_space=pltpu.SMEM),
        pl.BlockSpec((1, seg_len, head_cols), lambda s: (s + first, 0, 2)),
        pl.BlockSpec((1, seg_len, pair), lambda s: (s + first, 0, 0)),
        pl.BlockSpec((1, seg_len, pair), lambda s: (jnp.maximum(s + first - 1, 0), 0, 0)),
        fixed((1, seg_len, pair)),
        fixed(comp_shape),
    ]


def attend_fwd(first, shift, count, place, slope, heads, recv_mem, comp_ext, head_cols):
    seg_len = heads.shape[1]
    local_heads = head_cols // HD
    return pl.pallas_call(
        functools.partial(fwd_kernel, first, shift),
        grid=(count,),
        in_specs=attention_specs(first, seg_len, head_cols, comp_ext.shape),
        out_specs=[by_segment((seg_len, head_cols)), by_segment((local_heads, seg_len))],
        out_shape=[
            jax.ShapeDtypeStruct((count, seg_len, head_cols), jnp.bfloat16),
            jax.ShapeDtypeStruct((count, local_heads, seg_len), jnp.float32),
        ],
        compiler_params=pltpu.CompilerParams(vmem_limit_bytes=VMEM_LIMIT),
        cost_estimate=pl.CostEstimate(
            flops=count * 10**9, bytes_accessed=count * 3 * 10**6, transcendentals=count * 16 * 10**5
        ),
        name="attend_fwd",
    )(place, slope, heads, heads, heads, recv_mem, comp_ext)


def attend_bwd(
    first, count, head, place, slope, heads, recv_mem, comp_ext, grad_mixed, attn_out, lse, held, over, head_cols
):
    seg_len = attn_out.shape[1]
    local_heads = head_cols // HD
    pair = 2 * head_cols
    pad_rows = comp_ext.shape[1]
    entries = count + CSEGS - 1
    opening = first == 0
    done = count - 1 if opening else count
    rest = entries - CSEGS - 1 if opening else entries
    back = ((CSEGS + 1) * pad_rows + seg_len, pair) if opening else (16, pair)

    def pair_block(s):
        return (jnp.maximum(s - 1, 0) if opening else s, 0, 0)

    def stays(shape):
        return pl.BlockSpec(shape, lambda s: (0,) * len(shape))

    return pl.pallas_call(
        functools.partial(bwd_kernel, first),
        grid=(count,),
        in_specs=attention_specs(first, seg_len, head_cols, comp_ext.shape)
        + [pl.BlockSpec(memory_space=pltpu.SMEM)]
        + [by_segment(grad_mixed[0].shape[1:], first)] * 4
        + [
            by_segment((seg_len, head_cols), first),
            by_segment((local_heads, seg_len), first),
            fixed(held.shape),
            fixed(over.shape),
        ],
        out_specs=[
            by_segment((seg_len, head_cols)),
            pl.BlockSpec((1, seg_len, pair), pair_block),
            stays((seg_len, pair)),
            stays((rest, pad_rows, pair)),
            stays(back),
        ],
        out_shape=[
            jax.ShapeDtypeStruct((count, seg_len, head_cols), jnp.bfloat16),
            jax.ShapeDtypeStruct((done, seg_len, pair), jnp.bfloat16),
            jax.ShapeDtypeStruct((seg_len, pair), jnp.float32),
            jax.ShapeDtypeStruct((rest, pad_rows, pair), jnp.float32),
            jax.ShapeDtypeStruct(back, jnp.bfloat16),
        ],
        scratch_shapes=[
            pltpu.VMEM((seg_len, head_cols), jnp.bfloat16),
            pltpu.VMEM((entries, pad_rows, pair), jnp.float32),
        ],
        compiler_params=pltpu.CompilerParams(vmem_limit_bytes=VMEM_LIMIT),
        cost_estimate=pl.CostEstimate(
            flops=count * 2 * 10**9, bytes_accessed=count * 4 * 10**6, transcendentals=count * 16 * 10**5
        ),
        name="attend_bwd",
    )(place, slope, heads, heads, heads, recv_mem, comp_ext, head, *grad_mixed, attn_out, lse, held, over)


def row_norm(values):
    average = jnp.mean(values, axis=-1, keepdims=True)
    center = values - average
    spread = lax.rsqrt(jnp.mean(center * center, axis=-1, keepdims=True) + EPS)
    return center * spread, spread


def norm_back(grad, unit, spread, gain):
    scaled = grad * gain
    along = jnp.mean(scaled * unit, axis=-1, keepdims=True)
    return spread * (scaled - jnp.mean(scaled, axis=-1, keepdims=True) - unit * along)


def place_rows(head, pieces, target):
    for bits, piece in enumerate(pieces):
        rows = piece.shape[1]
        at = pl.multiple_of(jnp.bitwise_xor(head, bits) * rows, rows)
        target[pl.ds(at, rows), :] = piece[0].astype(target.dtype)


def hand_out(head, source, keep_ref, sent_ref):
    rows = keep_ref.shape[2]
    for bits, (ref, slot) in enumerate(
        ((keep_ref, 0), (sent_ref, 0), (keep_ref, 1), (sent_ref, 1))
    ):
        at = pl.multiple_of(jnp.bitwise_xor(head, bits) * rows, rows)
        ref[slot, 0] = source[pl.ds(at, rows), :].astype(ref.dtype)


def prep_kernel(
    head_ref, t0, t1, t2, t3, gain_ref, w_ref, heads_ref, normed_ref, grouped_ref, packed_ref, spread
):
    head = head_ref[0]
    quarter, width = t0.shape[1:]
    seg_len = heads_ref.shape[1]
    head_cols = w_ref.shape[2]
    pad_rows = grouped_ref.shape[1]
    tiles = width // 128
    for bits, piece in enumerate((t0, t1, t2, t3)):
        unit, _ = row_norm(piece[0].astype(jnp.float32))
        normed = (unit * gain_ref[...]).astype(jnp.bfloat16)
        at = pl.multiple_of(jnp.bitwise_xor(head, bits) * quarter, quarter)
        normed_ref[0, pl.ds(at, quarter), :] = normed
        wide = normed.astype(jnp.float32)
        for c in range(tiles):
            spread[c, pl.ds(at, quarter), :] = wide[:, c * 128 : (c + 1) * 128]
    last = spread[:, seg_len - 8 : seg_len, :]
    row = lax.broadcasted_iota(jnp.int32, last.shape, 1)
    spread[:, seg_len - 8 : seg_len, :] = jnp.where(row < 8 - seg_len % RATE, last, 0.0)
    spread[:, seg_len:, :] = jnp.zeros((tiles, spread.shape[1] - seg_len, 128), jnp.float32)
    rows = normed_ref[0]
    for n in range(3):
        heads_ref[0, :, n * head_cols : (n + 1) * head_cols] = jnp.dot(
            rows, w_ref[n], preferred_element_type=jnp.float32
        ).astype(jnp.bfloat16)
    total = jnp.zeros((pad_rows, head_cols), jnp.float32)
    for tap in range(RATE):
        for c in range(tiles):
            at = tap * width + c * 128
            grouped_ref[0, :, at : at + 128] = spread[
                c, pl.ds(tap, pad_rows, stride=RATE), :
            ].astype(jnp.bfloat16)
        total = total + jnp.dot(
            grouped_ref[0, :, tap * width : (tap + 1) * width],
            w_ref[3 + tap],
            preferred_element_type=jnp.float32,
        )
    packed_ref[0] = total.astype(jnp.bfloat16)


def fixed(shape):
    return pl.BlockSpec(shape, lambda s: (0,) * len(shape), pipeline_mode=pl.Buffered(1))


def by_segment(shape, first=0):
    return pl.BlockSpec((1,) + shape, lambda s: (s + first,) + (0,) * len(shape))


def piece_specs(quarter, width):
    spec = pl.BlockSpec((2, 1, quarter, width), lambda s: (0, s, 0, 0))
    return [spec, spec]


def piece_shapes(seg_count, quarter, width):
    shape = jax.ShapeDtypeStruct((2, seg_count, quarter, width), jnp.bfloat16)
    return [shape, shape]


def prepare(head, tokens, gain, weights, pad_rows):
    seg_count, quarter, width = tokens[0].shape
    seg_len = quarter * len(tokens)
    head_cols = weights.shape[2]
    bf16 = jnp.bfloat16
    return pl.pallas_call(
        prep_kernel,
        grid=(seg_count,),
        in_specs=[pl.BlockSpec(memory_space=pltpu.SMEM)]
        + [by_segment((quarter, width))] * 4
        + [fixed((1, width)), fixed(weights.shape)],
        out_specs=[
            by_segment((seg_len, 3 * head_cols)),
            by_segment((seg_len, width)),
            by_segment((pad_rows, RATE * width)),
            by_segment((pad_rows, head_cols)),
        ],
        out_shape=[
            jax.ShapeDtypeStruct((seg_count, seg_len, 3 * head_cols), bf16),
            jax.ShapeDtypeStruct((seg_count, seg_len, width), bf16),
            jax.ShapeDtypeStruct((seg_count, pad_rows, RATE * width), bf16),
            jax.ShapeDtypeStruct((seg_count, pad_rows, head_cols), bf16),
        ],
        scratch_shapes=[pltpu.VMEM((width // 128, RATE * pad_rows, 128), jnp.float32)],
        compiler_params=pltpu.CompilerParams(vmem_limit_bytes=VMEM_LIMIT),
        cost_estimate=pl.CostEstimate(flops=7 * 10**9, bytes_accessed=30 * 10**6, transcendentals=3072),
        name="prepare",
    )(head, *tokens, gain, weights)


def ffn_kernel(
    head_ref, a0, a1, a2, a3, o0, o1, o2, o3, t0, t1, t2, t3, g0, g1, g2, g3, gain_ref,
    up_ref, down_ref, f_keep, f_sent, n_keep, n_sent, hidden_ref, pack_ref,
    acc_up, acc_down,
):
    step = pl.program_id(0)
    head = head_ref[0]
    quarter, width = t0.shape[1:]
    ff_part = up_ref.shape[1]
    parts = up_ref.shape[0] // 2
    block = parts * ff_part

    @pl.when(step == 0)
    def _():
        acc_up[...] = jnp.zeros_like(acc_up)
        acc_down[...] = jnp.zeros_like(acc_down)

    starts = [
        pl.multiple_of(jnp.bitwise_xor(head, bits) * quarter, quarter) for bits in range(4)
    ]
    hidden = jnp.concatenate([t[0] for t in (t0, t1, t2, t3)], 0).astype(jnp.float32)
    for a, o in ((a0, o0), (a1, o1), (a2, o2), (a3, o3)):
        part = jnp.concatenate([a[0, pl.ds(at, quarter), :] for at in starts], 0)
        hidden = hidden + jnp.dot(
            part, o[...].reshape(a.shape[2], width), preferred_element_type=jnp.float32
        )
    hidden_ref[0] = hidden[:quarter]
    unit, _ = row_norm(hidden)
    normed = (unit * gain_ref[...]).astype(jnp.bfloat16)
    grad = jnp.concatenate([g[0] for g in (g0, g1, g2, g3)], 0)
    result = jnp.zeros(hidden.shape, jnp.float32)
    g_normed = jnp.zeros(hidden.shape, jnp.float32)
    for n in range(2):
        own = slice(n * parts, (n + 1) * parts)
        up = up_ref[own].reshape(block, width)
        down = down_ref[own].reshape(block, width)
        lifted = lax.dot_general(normed, up, COLS_IN, preferred_element_type=jnp.float32)
        sig = 0.5 * jnp.tanh(0.5 * lifted) + 0.5
        smooth = lifted * sig
        active = smooth.astype(jnp.bfloat16)
        g_active = lax.dot_general(grad, down, COLS_IN, preferred_element_type=jnp.float32)
        g_lifted = (g_active * (sig + smooth * (1.0 - sig))).astype(jnp.bfloat16)
        result = result + jnp.dot(active, down, preferred_element_type=jnp.float32)
        g_normed = g_normed + jnp.dot(g_lifted, up, preferred_element_type=jnp.float32)
        acc_down[n] += lax.dot_general(active, grad, ROWS_IN, preferred_element_type=jnp.float32)
        acc_up[n] += lax.dot_general(g_lifted, normed, ROWS_IN, preferred_element_type=jnp.float32)
    for value, keep, sent in ((g_normed, n_keep, n_sent), (result, f_keep, f_sent)):
        value = value.astype(jnp.bfloat16)
        for bits, (ref, slot) in enumerate(((keep, 0), (sent, 0), (keep, 1), (sent, 1))):
            ref[slot, 0] = value[bits * quarter : (bits + 1) * quarter]

    @pl.when(step == pl.num_programs(0) - 1)
    def _():
        for n in range(2):
            own = slice(n * parts, (n + 1) * parts)
            shape = (parts, ff_part, width)
            pack_ref[own, :ff_part] = acc_up[n].astype(jnp.bfloat16).reshape(shape)
            pack_ref[own, ff_part:] = acc_down[n].astype(jnp.bfloat16).reshape(shape)


def wo_blocks(pack, part, ff_part, head_groups):
    blks, _, width = pack.shape
    start = 2 * ff_part
    if part % 16 == 0:
        specs = [
            pl.BlockSpec(
                (blks, part, width),
                functools.partial(lambda index, s: (0, index, 0), start // part + n),
                pipeline_mode=pl.Buffered(1),
            )
            for n in range(head_groups)
        ]
        return [pack] * head_groups, specs
    blocks = [
        pack[:, start + n * part : start + (n + 1) * part].reshape(blks * part, width)
        for n in range(head_groups)
    ]
    return blocks, [fixed((blks * part, width))] * head_groups


def feed_forward(head, attended, wo, wo_specs, tokens, grads, gain, pack, ff_part):
    quarter, width = tokens[0].shape[1:]
    count, seg_len, head_cols = attended[0].shape
    blks = pack.shape[0]
    half = blks // 2 * ff_part
    grad_shape = (blks, 2 * ff_part, width)
    pieces = piece_specs(quarter, width)
    shapes = piece_shapes(count, quarter, width)

    def weight(index):
        return pl.BlockSpec(
            (blks, ff_part, width), lambda s: (0, index, 0), pipeline_mode=pl.Buffered(1)
        )

    return pl.pallas_call(
        ffn_kernel,
        grid=(count,),
        in_specs=[pl.BlockSpec(memory_space=pltpu.SMEM)]
        + [by_segment((seg_len, head_cols))] * 4
        + wo_specs
        + [by_segment((quarter, width))] * 8
        + [fixed((1, width)), weight(0), weight(1)],
        out_specs=pieces + pieces
        + [by_segment((quarter, width)), pl.BlockSpec(grad_shape, lambda s: (0, 0, 0))],
        out_shape=shapes + shapes
        + [
            jax.ShapeDtypeStruct((count, quarter, width), jnp.float32),
            jax.ShapeDtypeStruct(grad_shape, jnp.bfloat16),
        ],
        scratch_shapes=[
            pltpu.VMEM((2, half, width), jnp.float32),
            pltpu.VMEM((2, half, width), jnp.float32),
        ],
        compiler_params=pltpu.CompilerParams(vmem_limit_bytes=VMEM_LIMIT),
        cost_estimate=pl.CostEstimate(
            flops=count * 75 * 10**8, bytes_accessed=2 * 10**7 + count * 5 * 10**6, transcendentals=10**6
        ),
        name="feed_forward",
    )(head, *attended, *wo, *tokens, *grads, gain, pack, pack)


def middle_kernel(
    keep_ref, got_ref, far_ref, hidden_ref, grad_ref, gain_ref, o0, o1, o2, o3,
    g_hidden_ref, g_branch_ref, g_gain_ref, m0, m1, m2, m3,
):
    count, quarter, width = hidden_ref.shape
    flat = (count * quarter, width)
    gn = (
        keep_ref[0].astype(jnp.float32)
        + got_ref[0].astype(jnp.float32)
        + far_ref[...].astype(jnp.float32)
    ).reshape(flat)
    unit, spread = row_norm(hidden_ref[...].reshape(flat))
    gain_part = jnp.sum(gn * unit, axis=0, keepdims=True)

    @pl.when(pl.program_id(0) == 0)
    def _():
        g_gain_ref[...] = jnp.zeros_like(g_gain_ref)

    g_gain_ref[...] += gain_part
    g_hidden = grad_ref[...].astype(jnp.float32).reshape(flat) + norm_back(
        gn, unit, spread, gain_ref[...]
    )
    g_hidden_ref[...] = g_hidden.reshape(g_hidden_ref.shape)
    g_branch = g_hidden.astype(jnp.bfloat16)
    g_branch_ref[...] = g_branch.reshape(g_branch_ref.shape)
    for o, m in ((o0, m0), (o1, m1), (o2, m2), (o3, m3)):
        m[...] = (
            lax.dot_general(
                g_branch, o[...].reshape(m.shape[2], width), COLS_IN, preferred_element_type=jnp.float32
            )
            .astype(jnp.bfloat16)
            .reshape(m.shape)
        )


def middle(keep, got, far, hidden, grad, gain, wo, wo_specs, head_cols):
    count, quarter, width = hidden.shape
    size = 2 if count % 2 == 0 else 1
    piece = pl.BlockSpec((1, size, quarter, width), lambda s: (0, s, 0, 0))
    block = pl.BlockSpec((size, quarter, width), lambda s: (s, 0, 0))
    mixed = jax.ShapeDtypeStruct((count, quarter, head_cols), jnp.bfloat16)
    return pl.pallas_call(
        middle_kernel,
        grid=(count // size,),
        in_specs=[piece, piece, block, block, block, fixed((1, width))] + wo_specs,
        out_specs=[block, block, pl.BlockSpec((1, width), lambda s: (0, 0))]
        + [pl.BlockSpec((size, quarter, head_cols), lambda s: (s, 0, 0))] * 4,
        out_shape=[
            jax.ShapeDtypeStruct(hidden.shape, jnp.float32),
            jax.ShapeDtypeStruct(hidden.shape, jnp.bfloat16),
            jax.ShapeDtypeStruct((1, width), jnp.float32),
        ]
        + [mixed] * 4,
        compiler_params=pltpu.CompilerParams(vmem_limit_bytes=VMEM_LIMIT),
        cost_estimate=pl.CostEstimate(flops=count * 27 * 10**7, bytes_accessed=24 * 10**6, transcendentals=0),
        name="middle",
    )(keep, got, far, hidden, grad, gain, *wo)


def g_normed_kernel(head_ref, gq_ref, gkv_ref, gp_ref, w_ref, keep_ref, sent_ref, spread, rows):
    head = head_ref[0]
    seg_len, head_cols = gq_ref.shape[1:]
    pad_rows = gp_ref.shape[1]
    width = w_ref.shape[1]
    total = lax.dot_general(gq_ref[0], w_ref[2], COLS_IN, preferred_element_type=jnp.float32)
    for n in range(2):
        part = gkv_ref[0, :, n * head_cols : (n + 1) * head_cols]
        total = total + lax.dot_general(part, w_ref[n], COLS_IN, preferred_element_type=jnp.float32)
    for tap in range(RATE):
        sent = lax.dot_general(gp_ref[0], w_ref[3 + tap], COLS_IN, preferred_element_type=jnp.float32)
        for c in range(width // 128):
            spread[c, pl.ds(tap, pad_rows, stride=RATE), :] = sent[:, c * 128 : (c + 1) * 128]
    for c in range(width // 128):
        own = slice(c * 128, (c + 1) * 128)
        rows[:, own] = total[:, own] + spread[c, :seg_len, :]
    hand_out(head, rows, keep_ref, sent_ref)


def g_normed_parts(head, grad_query, grad_pair, grad_packed, weights, quarter):
    seg_count, seg_len, head_cols = grad_query.shape
    width = weights.shape[1]
    pad_rows = grad_packed.shape[1]
    return pl.pallas_call(
        g_normed_kernel,
        grid=(seg_count,),
        in_specs=[
            pl.BlockSpec(memory_space=pltpu.SMEM),
            by_segment((seg_len, head_cols)),
            by_segment((seg_len, 2 * head_cols)),
            by_segment((pad_rows, head_cols)),
            fixed(weights.shape),
        ],
        out_specs=piece_specs(quarter, width),
        out_shape=piece_shapes(seg_count, quarter, width),
        scratch_shapes=[
            pltpu.VMEM((width // 128, RATE * pad_rows, 128), jnp.float32),
            pltpu.VMEM((seg_len, width), jnp.float32),
        ],
        compiler_params=pltpu.CompilerParams(vmem_limit_bytes=VMEM_LIMIT),
        cost_estimate=pl.CostEstimate(flops=7 * 10**9, bytes_accessed=20 * 10**6, transcendentals=0),
        name="g_normed",
    )(head, grad_query, grad_pair, grad_packed, weights)


def head_swap(value, bit):
    count = lax.axis_size("head")
    return lax.ppermute(value, "head", [(source, source ^ bit) for source in range(count)])


def to_all_heads(value):
    far = head_swap(value, 2)
    return value, head_swap(value, 1), far, head_swap(far, 1)


def sum_over_heads(keep, sent):
    got = head_swap(sent, 1).astype(jnp.float32)
    far = (keep[1].astype(jnp.float32) + got[1]).astype(jnp.bfloat16)
    return keep[0].astype(jnp.float32) + got[0] + head_swap(far, 2).astype(jnp.float32)


def per_device(tokens, wq, wk, wv, wo, w_up, w_down, gain_one, gain_two, w_comp, lengths, grad_out):
    seg_count, quarter, width = tokens.shape
    head_groups = lax.axis_size("head")
    blk_count = lax.axis_size("blk")
    seg_len = quarter * head_groups
    head_cols = width // head_groups
    local_heads = head_cols // HD
    comp_rows = seg_len // RATE
    pad_rows = (comp_rows + 15) // 16 * 16
    window = CSEGS + 1
    head_index = lax.axis_index("head")
    blk_index = lax.axis_index("blk")
    token_count = seg_count * quarter
    full_count = seg_count * seg_len
    comp_count = seg_count * pad_rows
    part = wq.shape[0]
    ff_part = w_down.shape[0]
    bf16 = jnp.bfloat16
    head = head_index[None].astype(jnp.int32)

    columns = (
        jnp.concatenate([wk, wv, wq, w_comp.reshape(RATE * part, width)], 0)
        .reshape(6 * part, head_groups, head_cols)
        .transpose(1, 0, 2)
    )
    gains = jnp.pad(
        jnp.concatenate([gain_one, gain_two])[None], ((0, 15), (0, head_cols - 2 * part))
    )
    columns = jnp.concatenate(
        [columns, jnp.broadcast_to(gains, (head_groups, 16, head_cols))], 1
    )
    columns = lax.all_to_all(columns, "head", split_axis=0, concat_axis=0, tiled=True)
    columns, tokens_held = lax.optimization_barrier((columns, tokens))
    first_all = lax.all_gather(columns, "blk", axis=0)
    second_all = lax.all_gather(
        jnp.concatenate([w_up.T, w_down, *to_all_heads(wo)], 0), "blk", axis=0
    )
    token_pieces = to_all_heads(tokens_held)
    grad_held, tokens_far = lax.optimization_barrier((grad_out, token_pieces[2]))
    token_pieces = token_pieces[:2] + (tokens_far,) + token_pieces[3:]
    grad_far = head_swap(grad_held, 2)
    gain_pair = first_all[:, :, 6 * part, : 2 * part].reshape(
        blk_count, head_groups, 2, part
    ).transpose(2, 1, 0, 3).reshape(2, 1, width).astype(jnp.float32)
    gain_first, gain_second = gain_pair[0], gain_pair[1]
    weights = (
        first_all[:, :, : 6 * part]
        .reshape(blk_count, head_groups, 6, part, head_cols)
        .transpose(2, 1, 0, 3, 4)
        .reshape(6, width, head_cols)
    )
    wkv = jnp.concatenate([weights[0], weights[1]], 1)
    wo_held, wo_specs = wo_blocks(second_all, part, ff_part, head_groups)

    heads, normed, grouped, packed_mine = prepare(
        head, token_pieces, gain_first, weights, pad_rows
    )
    compressed = packed_mine[:, :comp_rows]
    pair = 2 * head_cols
    tail_rows = packed_mine[seg_count - window :].reshape(window * pad_rows, head_cols)
    half_rows = window * pad_rows // 2
    onward = jnp.concatenate(
        [
            heads[seg_count - 1, :, :pair],
            jnp.concatenate([tail_rows[:half_rows], tail_rows[half_rows:]], 1),
        ],
        0,
    )
    recv = passed_along(onward, "blk", 1)
    def all_columns(value):
        value = value.reshape(-1, head_cols)
        whole = jnp.zeros((value.shape[0], width), bf16)
        for bits, piece in enumerate(to_all_heads(value)):
            start = jnp.bitwise_xor(head_index, bits) * head_cols
            whole = lax.dynamic_update_slice(whole, piece, (0, start))
        return whole

    def comp_pairs(rows):
        return (
            jnp.dot(rows, wkv, preferred_element_type=jnp.float32)
            .astype(bf16)
            .reshape(-1, pad_rows, 2 * head_cols)
        )

    grad_far, grad_held, packed_mine = lax.optimization_barrier((grad_far, grad_held, packed_mine))
    grad_pieces = (grad_held, head_swap(grad_held, 1), grad_far, head_swap(grad_far, 1))
    packed = all_columns(packed_mine)
    comp_pair = comp_pairs(packed)
    comp_pair, grad_pieces = lax.optimization_barrier((comp_pair, grad_pieces))
    order = jnp.arange(lengths.shape[0], dtype=jnp.int32)
    starts = jnp.sum(jnp.where(order[None, :] < order[:, None], lengths[None, :], 0), axis=1)
    seg_ids = blk_index * seg_count + jnp.arange(seg_count, dtype=jnp.int32)
    seg_place = seg_ids - jnp.max(
        jnp.where(starts[None, :] <= seg_ids[:, None], starts[None, :], 0), axis=1
    )
    head_ids = head_index * local_heads + jnp.arange(local_heads, dtype=jnp.int32)
    slopes = jnp.exp2(-head_ids.astype(jnp.float32)) / 64.0 * LOG2E
    late = attend_fwd(
        window, window, seg_count - window, seg_place, slopes, heads, heads[:1, :, : 2 * head_cols],
        comp_pair, head_cols,
    )
    recv, late = lax.optimization_barrier((recv, late))
    recv_mem = recv[None, :seg_len]
    recv_packed = jnp.concatenate([recv[seg_len:, :head_cols], recv[seg_len:, head_cols:]], 0)
    comp_ext = jnp.concatenate([comp_pairs(all_columns(recv_packed)), comp_pair], 0)
    middle_seg = window // 2

    def early(a, b, comp_ext):
        return attend_fwd(a, 0, b - a, seg_place, slopes, heads, recv_mem, comp_ext, head_cols)

    first = early(0, middle_seg, comp_ext)
    late_far = head_swap(late[0], 2)
    late_far, first, comp_ext = lax.optimization_barrier((late_far, first, comp_ext))
    attention = [first, early(middle_seg, window, comp_ext), late]
    attn_out = jnp.concatenate([out for out, _ in attention], 0)
    lse = jnp.concatenate([total for _, total in attention], 0)
    far = jnp.concatenate([head_swap(out, 2) for out, _ in attention[:2]] + [late_far], 0)
    attended = (attn_out, head_swap(attn_out, 1), far, head_swap(far, 1))
    f_keep, f_sent, n_keep, n_sent, hidden, first_grads = feed_forward(
        head, attended, wo_held, wo_specs, token_pieces, grad_pieces, gain_second, second_all, ff_part
    )
    first_sum = lax.psum_scatter(first_grads, "blk", scatter_dimension=0)
    got = head_swap(n_sent, 1)
    far = (n_keep[1].astype(jnp.float32) + got[1].astype(jnp.float32)).astype(bf16)
    grad_hidden, grad_branch, grad_gain_two, *mixed = middle(
        n_keep, got, head_swap(far, 2), hidden, grad_out, gain_second, wo_held, wo_specs, head_cols
    )
    grad_gain_two = grad_gain_two[0]
    mixed = mixed[:1] + [head_swap(mixed[bits], bits) for bits in (1, 2, 3)]
    grad_wo = [
        lax.dot_general(
            lax.dynamic_slice_in_dim(block, head_index * quarter, quarter, 1).reshape(
                token_count, head_cols
            ),
            grad_branch.reshape(token_count, width),
            ROWS_IN,
            preferred_element_type=jnp.float32,
        ).astype(bf16)
        for block in attended
    ]
    f_got = head_swap(f_sent, 1)
    f_far = (f_keep[1].astype(jnp.float32) + f_got[1].astype(jnp.float32)).astype(bf16)
    wo_sent = jnp.stack([grad_wo[1], grad_wo[3]])
    wo_got = head_swap(wo_sent, 1).astype(jnp.float32)
    wo_far = (grad_wo[2].astype(jnp.float32) + wo_got[1]).astype(bf16)
    f_far, wo_far, mixed = lax.optimization_barrier((f_far, wo_far, mixed))
    wo_far = head_swap(wo_far, 2).astype(jnp.float32)

    none = jnp.zeros((16, 2 * head_cols), jnp.float32)
    grad_query, pair_done, held, rest, back = attend_bwd(
        0, seg_count, head, seg_place, slopes, heads, recv_mem, comp_ext, mixed, attn_out, lse, none,
        none, head_cols,
    )
    back, f_far = lax.optimization_barrier((back, f_far))
    got_back = passed_along(back, "blk", -1)
    f_far = head_swap(f_far, 2)
    grad_hidden = grad_hidden.reshape(token_count, width)
    normed = normed.reshape(full_count, width)
    grad_wq = lax.dot_general(
        normed, grad_query.reshape(full_count, head_cols), ROWS_IN, preferred_element_type=jnp.float32
    )
    grad_wo = (grad_wo[0].astype(jnp.float32) + wo_got[0] + wo_far).astype(bf16)

    def by_owner(value):
        return value.astype(bf16).reshape(
            head_groups, blk_count, part, value.shape[1]
        ).transpose(1, 0, 2, 3)

    wq_rows = by_owner(grad_wq)
    wo_rows = grad_wo.reshape(blk_count, part, head_groups, head_cols).transpose(0, 2, 1, 3)
    wq_rows, wo_rows, got_back = lax.optimization_barrier((wq_rows, wo_rows, got_back))
    got_back = got_back.astype(jnp.float32)
    last_pair = (held + got_back[window * pad_rows :]).astype(bf16)
    grad_pair = jnp.concatenate([pair_done, last_pair[None]], 0)
    got_comp = got_back[: window * pad_rows].reshape(window, pad_rows, 2 * head_cols)
    comp_pair_grad = jnp.pad(rest, ((0, seg_count - rest.shape[0]), (0, 0), (0, 0))) + jnp.pad(
        got_comp, ((seg_count - window, 0), (0, 0), (0, 0))
    )
    comp_grad_rows = comp_pair_grad.reshape(comp_count, 2 * head_cols).astype(bf16)
    grad_packed_part = lax.dot_general(
        comp_grad_rows, wkv, COLS_IN, preferred_element_type=jnp.float32
    ).astype(bf16)

    grad_packed_part, grad_pair = lax.optimization_barrier((grad_packed_part, grad_pair))

    def columns_of(bits):
        start = jnp.bitwise_xor(head_index, bits) * head_cols
        return lax.dynamic_slice_in_dim(grad_packed_part, start, head_cols, 1)

    grad_packed = sum_over_heads(
        (columns_of(0), columns_of(2)), jnp.stack([columns_of(1), columns_of(3)])
    ).astype(bf16)
    grad_packed, f_far = lax.optimization_barrier((grad_packed, f_far))
    out_tokens = (
        hidden + f_keep[0].astype(jnp.float32) + f_got[0].astype(jnp.float32) + f_far.astype(jnp.float32)
    ).astype(bf16)
    keep, sent = g_normed_parts(
        head,
        grad_query,
        grad_pair,
        grad_packed.reshape(seg_count, pad_rows, head_cols),
        weights,
        quarter,
    )
    grad_normed = sum_over_heads(keep, sent).reshape(token_count, width)
    unit_one, spread_one = row_norm(tokens.reshape(token_count, width).astype(jnp.float32))
    grad_tokens = (
        (grad_hidden + norm_back(grad_normed, unit_one, spread_one, gain_first))
        .astype(bf16)
        .reshape(tokens.shape)
    )
    grad_kv = grad_pair.reshape(full_count, 2 * head_cols)
    grad_wkv = lax.dot_general(normed, grad_kv, ROWS_IN, preferred_element_type=jnp.float32)
    comp_term = lax.dot_general(packed, comp_grad_rows, ROWS_IN, preferred_element_type=jnp.float32)
    grad_comp = lax.dot_general(
        grouped.reshape(comp_count, RATE * width),
        grad_packed,
        ROWS_IN,
        preferred_element_type=jnp.float32,
    ).reshape(RATE, width, head_cols)
    grad_gain_one = (
        jnp.sum(grad_wq * weights[2].astype(jnp.float32), axis=1)
        + jnp.sum(grad_wkv * wkv.astype(jnp.float32), axis=1)
        + jnp.sum(grad_comp * weights[3:].astype(jnp.float32), axis=(0, 2))
    ) / gain_first[0]
    grad_wkv = grad_wkv + comp_term

    gain_rows = (
        jnp.stack([grad_gain_one, grad_gain_two])
        .reshape(2, head_groups, blk_count, part)
        .transpose(2, 1, 0, 3)
        .astype(bf16)
    )
    second_grads = jnp.concatenate(
        [
            wq_rows,
            by_owner(grad_wkv[:, :head_cols]),
            by_owner(grad_wkv[:, head_cols:]),
            by_owner(grad_comp[0]),
            by_owner(grad_comp[1]),
            by_owner(grad_comp[2]),
            jnp.pad(gain_rows, ((0, 0), (0, 0), (0, 14), (0, head_cols - part))),
            wo_rows,
        ],
        2,
    )
    second_grads, first_sum = lax.optimization_barrier((second_grads, first_sum))
    first_sum = first_sum.astype(jnp.float32)
    own_rows = 6 * part + 16
    second_part = lax.psum_scatter(
        second_grads.reshape(-1, head_cols), "blk", scatter_dimension=0, tiled=True
    ).reshape(head_groups, own_rows + part, head_cols)
    second_sum = lax.all_to_all(
        second_part[:, :own_rows], "head", split_axis=0, concat_axis=0, tiled=True
    ).astype(jnp.float32)
    gain_sum = jnp.sum(second_sum[:, 6 * part : 6 * part + 2, :part], axis=0)
    weight_sum = (
        second_sum[:, : 6 * part]
        .reshape(head_groups, 6, part, head_cols)
        .transpose(1, 2, 0, 3)
        .reshape(6, part, width)
    )
    wo_sum = second_part[:, own_rows:].astype(jnp.float32).transpose(1, 0, 2).reshape(part, width)
    return (
        out_tokens,
        compressed,
        grad_tokens,
        weight_sum[0],
        weight_sum[1],
        weight_sum[2],
        wo_sum,
        first_sum[:ff_part].T,
        first_sum[ff_part:],
        gain_sum[0],
        gain_sum[1],
        weight_sum[3:],
    )


def solution(mesh):
    return jax.shard_map(
        per_device,
        mesh=mesh,
        in_specs=(
            P("blk", "head", None),
            P(("head", "blk"), None),
            P(("head", "blk"), None),
            P(("head", "blk"), None),
            P(("head", "blk"), None),
            P(None, ("head", "blk")),
            P(("head", "blk"), None),
            P(("head", "blk")),
            P(("head", "blk")),
            P(None, ("head", "blk"), None),
            P(),
            P("blk", "head", None),
        ),
        out_specs=(
            P("blk", "head", None),
            P("blk", None, "head"),
            P("blk", "head", None),
            P(("head", "blk"), None),
            P(("head", "blk"), None),
            P(("head", "blk"), None),
            P(("head", "blk"), None),
            P(None, ("head", "blk")),
            P(("head", "blk"), None),
            P(("head", "blk")),
            P(("head", "blk")),
            P(None, ("head", "blk"), None),
        ),
        check_vma=False,
    )
```

```python
import functools

import jax
import jax.numpy as jnp
from jax import lax
from jax.experimental import pallas as pl
from jax.experimental.pallas import tpu as pltpu
from jax.sharding import PartitionSpec as P

HD = 128
RATE = 3
CSEGS = 3


EPS = 1e-05
NEG = -1e30
ROWS_IN = (((0,), (0,)), ((), ()))
COLS_IN = (((1,), (1,)), ((), ()))


def passed_along(value, axis, steps):
    count = lax.axis_size(axis)
    leading, last = (max(0, -steps), min(count, count - steps))
    return lax.ppermute(value, axis, [(source, source + steps) for source in range(leading, last)])


LOG2E = 1.4426950408889634
PAD_ROWS = 176
VMEM_LIMIT = 56 * 1024 * 1024


def key_bias(rows, base, step, valid_rows, open_, slope):
    row = lax.broadcasted_iota(jnp.int32, (rows, 1), 0)
    place = (base + step * row).astype(jnp.float32)
    return jnp.where((row < valid_rows) & open_, place * slope, NEG)


def fwd_kernel(first, shift, place_ref, slope_ref, q_ref, own_ref, prev_ref, recv_ref, comp_ref, out_ref, lse_ref):
    step = pl.program_id(0) + first
    place = place_ref[step]
    seg_len = q_ref.shape[1]
    half = seg_len // 2
    pad_rows = comp_ref.shape[1]
    local_heads = q_ref.shape[2] // HD
    values_at = local_heads * HD
    factor = HD ** (-0.5) * LOG2E
    lower = lax.broadcasted_iota(jnp.int32, (half, half), 0) <= lax.broadcasted_iota(
        jnp.int32, (half, half), 1
    )
    for h in range(local_heads):
        kc = slice(h * HD, (h + 1) * HD)
        vc = slice(values_at + h * HD, values_at + (h + 1) * HD)
        slope = slope_ref[h]
        parts = []
        for piece in range(CSEGS):
            lag = CSEGS + 1 - piece
            bias = key_bias(pad_rows, RATE // 2 - lag * seg_len, RATE, seg_len // RATE, place >= lag, slope)
            at = step + piece - shift
            parts.append((comp_ref[at, :, kc], comp_ref[at, :, vc], bias))
        bias = key_bias(seg_len, -seg_len, 1, seg_len, place >= 1, slope)
        if first:
            parts.append((prev_ref[0, :, kc], prev_ref[0, :, vc], bias))
        else:
            is_first = step == 0
            parts.append(
                (
                    jnp.where(is_first, recv_ref[0, :, kc], prev_ref[0, :, kc]),
                    jnp.where(is_first, recv_ref[0, :, vc], prev_ref[0, :, vc]),
                    bias,
                )
            )
        own_bias = [
            key_bias(half, n * half, 1, half, place >= 0, slope) for n in range(2)
        ]
        for n in range(2):
            query = q_ref[0, n * half : (n + 1) * half, kc]
            group = list(parts)
            for m in range(n + 1):
                rows = slice(m * half, (m + 1) * half)
                group.append((own_ref[0, rows, kc], own_ref[0, rows, vc], own_bias[m]))
            scores = []
            top = None
            for index, (k, v, bias) in enumerate(group):
                raw = lax.dot_general(k, query, COLS_IN, preferred_element_type=jnp.float32)
                raw = raw * factor + bias
                if index == len(group) - 1:
                    raw = jnp.where(lower, raw, NEG)
                scores.append(raw)
                peak = jnp.max(raw, axis=0, keepdims=True)
                top = peak if top is None else jnp.maximum(top, peak)
            total = jnp.zeros_like(top)
            result = jnp.zeros((HD, half), jnp.float32)
            for raw, (k, v, bias) in zip(scores, group):
                weight = jnp.exp2(raw - top)
                total = total + jnp.sum(weight, axis=0, keepdims=True)
                result = result + lax.dot_general(
                    v, weight.astype(jnp.bfloat16), ROWS_IN, preferred_element_type=jnp.float32
                )
            result = result * (1.0 / total)
            out_ref[0, n * half : (n + 1) * half, kc] = result.T.astype(jnp.bfloat16)
            lse_ref[0, h : h + 1, n * half : (n + 1) * half] = top + jnp.log(total) * LOG2E


def bwd_kernel(
    first, place_ref, slope_ref, q_ref, own_ref, prev_ref, recv_ref, comp_ref, head_ref, g0, g1, g2, g3,
    att_ref, lse_ref, held_ref, over_ref, gq_ref, gkv_ref, tail_ref, rest_ref, back_ref, grad_ref, gcomp_ref,
):
    opening = first == 0
    step = pl.program_id(0) + first
    place = place_ref[step]
    seg_len = q_ref.shape[1]
    half = seg_len // 2
    pad_rows = comp_ref.shape[1]
    local_heads = q_ref.shape[2] // HD
    values_at = local_heads * HD
    scale = HD ** (-0.5)
    factor = scale * LOG2E
    is_first = step == 0
    lower = lax.broadcasted_iota(jnp.int32, (half, half), 0) <= lax.broadcasted_iota(
        jnp.int32, (half, half), 1
    )

    at_start = pl.program_id(0) == 0

    @pl.when(at_start)
    def _():
        gcomp_ref[...] = jnp.zeros_like(gcomp_ref)
        if opening:
            tail_ref[...] = jnp.zeros_like(tail_ref)
        else:
            tail_ref[...] = held_ref[...]
            gcomp_ref[: CSEGS - 1] = over_ref[...]

    place_rows(head_ref[0], (g0, g1, g2, g3), grad_ref)
    for h in range(local_heads):
        kc = slice(h * HD, (h + 1) * HD)
        vc = slice(values_at + h * HD, values_at + (h + 1) * HD)
        slope = slope_ref[h]
        query = q_ref[0, :, kc]
        grad = grad_ref[:, kc]
        lse = lse_ref[0, h : h + 1, :]
        product = grad.astype(jnp.float32) * att_ref[0, :, kc].astype(jnp.float32)
        delta = jnp.sum(product.T, axis=0, keepdims=True)

        def part(k, v, bias, cols, masked):
            raw = lax.dot_general(k, query[cols], COLS_IN, preferred_element_type=jnp.float32)
            raw = raw * factor + bias
            if masked:
                raw = jnp.where(lower, raw, NEG)
            prob = jnp.exp2(raw - lse[:, cols])
            grad_prob = lax.dot_general(v, grad[cols], COLS_IN, preferred_element_type=jnp.float32)
            grad_score = (prob * (grad_prob - delta[:, cols])).astype(jnp.bfloat16)
            gk = jnp.dot(grad_score, query[cols], preferred_element_type=jnp.float32) * scale
            gv = jnp.dot(prob.astype(jnp.bfloat16), grad[cols], preferred_element_type=jnp.float32)
            gq = lax.dot_general(k, grad_score, ROWS_IN, preferred_element_type=jnp.float32)
            return gk, gv, gq

        every = slice(0, seg_len)
        total = jnp.zeros((HD, seg_len), jnp.float32)
        for piece in range(CSEGS):
            lag = CSEGS + 1 - piece
            bias = key_bias(pad_rows, RATE // 2 - lag * seg_len, RATE, seg_len // RATE, place >= lag, slope)
            gk, gv, gq = part(comp_ref[step + piece, :, kc], comp_ref[step + piece, :, vc], bias, every, False)
            gcomp_ref[step - first + piece, :, kc] += gk
            gcomp_ref[step - first + piece, :, vc] += gv
            total = total + gq
        for n in range(2):
            rows = slice(n * half, (n + 1) * half)
            bias = key_bias(half, n * half - seg_len, 1, half, place >= 1, slope)
            k, v = prev_ref[0, rows, kc], prev_ref[0, rows, vc]
            if opening:
                k = jnp.where(is_first, recv_ref[0, rows, kc], k)
                v = jnp.where(is_first, recv_ref[0, rows, vc], v)
            gk, gv, gq = part(k, v, bias, every, False)
            gk = (tail_ref[rows, kc] + gk).astype(jnp.bfloat16)
            gv = (tail_ref[rows, vc] + gv).astype(jnp.bfloat16)
            gkv_ref[0, rows, kc] = gk
            gkv_ref[0, rows, vc] = gv
            if opening:
                at = (CSEGS + 1) * pad_rows + n * half
                send = slice(at, at + half)

                @pl.when(is_first)
                def _(gk=gk, gv=gv, send=send):
                    back_ref[send, kc] = gk
                    back_ref[send, vc] = gv

            total = total + gq
        lo, hi = slice(0, half), slice(half, seg_len)
        bias_lo = key_bias(half, 0, 1, half, place >= 0, slope)
        bias_hi = key_bias(half, half, 1, half, place >= 0, slope)
        gk0, gv0, gq0 = part(own_ref[0, lo, kc], own_ref[0, lo, vc], bias_lo, lo, True)
        gk1, gv1, gq1 = part(own_ref[0, lo, kc], own_ref[0, lo, vc], bias_lo, hi, False)
        gk2, gv2, gq2 = part(own_ref[0, hi, kc], own_ref[0, hi, vc], bias_hi, hi, True)
        tail_ref[lo, kc] = gk0 + gk1
        tail_ref[lo, vc] = gv0 + gv1
        tail_ref[hi, kc] = gk2
        tail_ref[hi, vc] = gv2
        gq_ref[0, lo, kc] = ((total[:, lo] + gq0) * scale).T.astype(jnp.bfloat16)
        gq_ref[0, hi, kc] = ((total[:, hi] + gq1 + gq2) * scale).T.astype(jnp.bfloat16)

    @pl.when(pl.program_id(0) == pl.num_programs(0) - 1)
    def _():
        if opening:
            for entry in range(CSEGS + 1):
                rows = slice(entry * pad_rows, (entry + 1) * pad_rows)
                back_ref[rows, :] = gcomp_ref[entry].astype(jnp.bfloat16)
            rest_ref[...] = gcomp_ref[CSEGS + 1 :]
        else:
            rest_ref[...] = gcomp_ref[...]
            back_ref[...] = jnp.zeros_like(back_ref)


def attention_specs(first, seg_len, head_cols, comp_shape):
    pair = 2 * head_cols
    return [
        pl.BlockSpec(memory_space=pltpu.SMEM),
        pl.BlockSpec(memory_space=pltpu.SMEM),
        pl.BlockSpec((1, seg_len, head_cols), lambda s: (s + first, 0, 2)),
        pl.BlockSpec((1, seg_len, pair), lambda s: (s + first, 0, 0)),
        pl.BlockSpec((1, seg_len, pair), lambda s: (jnp.maximum(s + first - 1, 0), 0, 0)),
        fixed((1, seg_len, pair)),
        fixed(comp_shape),
    ]


def attend_fwd(first, shift, count, place, slope, heads, recv_mem, comp_ext, head_cols):
    seg_len = heads.shape[1]
    local_heads = head_cols // HD
    return pl.pallas_call(
        functools.partial(fwd_kernel, first, shift),
        grid=(count,),
        in_specs=attention_specs(first, seg_len, head_cols, comp_ext.shape),
        out_specs=[by_segment((seg_len, head_cols)), by_segment((local_heads, seg_len))],
        out_shape=[
            jax.ShapeDtypeStruct((count, seg_len, head_cols), jnp.bfloat16),
            jax.ShapeDtypeStruct((count, local_heads, seg_len), jnp.float32),
        ],
        compiler_params=pltpu.CompilerParams(vmem_limit_bytes=VMEM_LIMIT),
        cost_estimate=pl.CostEstimate(
            flops=count * 10**9, bytes_accessed=count * 3 * 10**6, transcendentals=count * 16 * 10**5
        ),
        name="attend_fwd",
    )(place, slope, heads, heads, heads, recv_mem, comp_ext)


def attend_bwd(
    first, count, head, place, slope, heads, recv_mem, comp_ext, grad_mixed, attn_out, lse, held, over, head_cols
):
    seg_len = attn_out.shape[1]
    local_heads = head_cols // HD
    pair = 2 * head_cols
    pad_rows = comp_ext.shape[1]
    entries = count + CSEGS - 1
    opening = first == 0
    done = count - 1 if opening else count
    rest = entries - CSEGS - 1 if opening else entries
    back = ((CSEGS + 1) * pad_rows + seg_len, pair) if opening else (16, pair)

    def pair_block(s):
        return (jnp.maximum(s - 1, 0) if opening else s, 0, 0)

    def stays(shape):
        return pl.BlockSpec(shape, lambda s: (0,) * len(shape))

    return pl.pallas_call(
        functools.partial(bwd_kernel, first),
        grid=(count,),
        in_specs=attention_specs(first, seg_len, head_cols, comp_ext.shape)
        + [pl.BlockSpec(memory_space=pltpu.SMEM)]
        + [by_segment(grad_mixed[0].shape[1:], first)] * 4
        + [
            by_segment((seg_len, head_cols), first),
            by_segment((local_heads, seg_len), first),
            fixed(held.shape),
            fixed(over.shape),
        ],
        out_specs=[
            by_segment((seg_len, head_cols)),
            pl.BlockSpec((1, seg_len, pair), pair_block),
            stays((seg_len, pair)),
            stays((rest, pad_rows, pair)),
            stays(back),
        ],
        out_shape=[
            jax.ShapeDtypeStruct((count, seg_len, head_cols), jnp.bfloat16),
            jax.ShapeDtypeStruct((done, seg_len, pair), jnp.bfloat16),
            jax.ShapeDtypeStruct((seg_len, pair), jnp.float32),
            jax.ShapeDtypeStruct((rest, pad_rows, pair), jnp.float32),
            jax.ShapeDtypeStruct(back, jnp.bfloat16),
        ],
        scratch_shapes=[
            pltpu.VMEM((seg_len, head_cols), jnp.bfloat16),
            pltpu.VMEM((entries, pad_rows, pair), jnp.float32),
        ],
        compiler_params=pltpu.CompilerParams(vmem_limit_bytes=VMEM_LIMIT),
        cost_estimate=pl.CostEstimate(
            flops=count * 2 * 10**9, bytes_accessed=count * 4 * 10**6, transcendentals=count * 16 * 10**5
        ),
        name="attend_bwd",
    )(place, slope, heads, heads, heads, recv_mem, comp_ext, head, *grad_mixed, attn_out, lse, held, over)


def row_norm(values):
    average = jnp.mean(values, axis=-1, keepdims=True)
    center = values - average
    spread = lax.rsqrt(jnp.mean(center * center, axis=-1, keepdims=True) + EPS)
    return center * spread, spread


def norm_back(grad, unit, spread, gain):
    scaled = grad * gain
    along = jnp.mean(scaled * unit, axis=-1, keepdims=True)
    return spread * (scaled - jnp.mean(scaled, axis=-1, keepdims=True) - unit * along)


def place_rows(head, pieces, target):
    for bits, piece in enumerate(pieces):
        rows = piece.shape[1]
        at = pl.multiple_of(jnp.bitwise_xor(head, bits) * rows, rows)
        target[pl.ds(at, rows), :] = piece[0].astype(target.dtype)


def hand_out(head, source, keep_ref, sent_ref):
    rows = keep_ref.shape[2]
    for bits, (ref, slot) in enumerate(
        ((keep_ref, 0), (sent_ref, 0), (keep_ref, 1), (sent_ref, 1))
    ):
        at = pl.multiple_of(jnp.bitwise_xor(head, bits) * rows, rows)
        ref[slot, 0] = source[pl.ds(at, rows), :].astype(ref.dtype)


def prep_kernel(
    head_ref, t0, t1, t2, t3, gain_ref, w_ref, heads_ref, normed_ref, grouped_ref, packed_ref, spread
):
    head = head_ref[0]
    quarter, width = t0.shape[1:]
    seg_len = heads_ref.shape[1]
    head_cols = w_ref.shape[2]
    pad_rows = grouped_ref.shape[1]
    tiles = width // 128
    for bits, piece in enumerate((t0, t1, t2, t3)):
        unit, _ = row_norm(piece[0].astype(jnp.float32))
        normed = (unit * gain_ref[...]).astype(jnp.bfloat16)
        at = pl.multiple_of(jnp.bitwise_xor(head, bits) * quarter, quarter)
        normed_ref[0, pl.ds(at, quarter), :] = normed
        wide = normed.astype(jnp.float32)
        for c in range(tiles):
            spread[c, pl.ds(at, quarter), :] = wide[:, c * 128 : (c + 1) * 128]
    last = spread[:, seg_len - 8 : seg_len, :]
    row = lax.broadcasted_iota(jnp.int32, last.shape, 1)
    spread[:, seg_len - 8 : seg_len, :] = jnp.where(row < 8 - seg_len % RATE, last, 0.0)
    spread[:, seg_len:, :] = jnp.zeros((tiles, spread.shape[1] - seg_len, 128), jnp.float32)
    rows = normed_ref[0]
    for n in range(3):
        heads_ref[0, :, n * head_cols : (n + 1) * head_cols] = jnp.dot(
            rows, w_ref[n], preferred_element_type=jnp.float32
        ).astype(jnp.bfloat16)
    total = jnp.zeros((pad_rows, head_cols), jnp.float32)
    for tap in range(RATE):
        for c in range(tiles):
            at = tap * width + c * 128
            grouped_ref[0, :, at : at + 128] = spread[
                c, pl.ds(tap, pad_rows, stride=RATE), :
            ].astype(jnp.bfloat16)
        total = total + jnp.dot(
            grouped_ref[0, :, tap * width : (tap + 1) * width],
            w_ref[3 + tap],
            preferred_element_type=jnp.float32,
        )
    packed_ref[0] = total.astype(jnp.bfloat16)


def fixed(shape):
    return pl.BlockSpec(shape, lambda s: (0,) * len(shape), pipeline_mode=pl.Buffered(1))


def by_segment(shape, first=0):
    return pl.BlockSpec((1,) + shape, lambda s: (s + first,) + (0,) * len(shape))


def piece_specs(quarter, width):
    spec = pl.BlockSpec((2, 1, quarter, width), lambda s: (0, s, 0, 0))
    return [spec, spec]


def piece_shapes(seg_count, quarter, width):
    shape = jax.ShapeDtypeStruct((2, seg_count, quarter, width), jnp.bfloat16)
    return [shape, shape]


def prepare(head, tokens, gain, weights, pad_rows):
    seg_count, quarter, width = tokens[0].shape
    seg_len = quarter * len(tokens)
    head_cols = weights.shape[2]
    bf16 = jnp.bfloat16
    return pl.pallas_call(
        prep_kernel,
        grid=(seg_count,),
        in_specs=[pl.BlockSpec(memory_space=pltpu.SMEM)]
        + [by_segment((quarter, width))] * 4
        + [fixed((1, width)), fixed(weights.shape)],
        out_specs=[
            by_segment((seg_len, 3 * head_cols)),
            by_segment((seg_len, width)),
            by_segment((pad_rows, RATE * width)),
            by_segment((pad_rows, head_cols)),
        ],
        out_shape=[
            jax.ShapeDtypeStruct((seg_count, seg_len, 3 * head_cols), bf16),
            jax.ShapeDtypeStruct((seg_count, seg_len, width), bf16),
            jax.ShapeDtypeStruct((seg_count, pad_rows, RATE * width), bf16),
            jax.ShapeDtypeStruct((seg_count, pad_rows, head_cols), bf16),
        ],
        scratch_shapes=[pltpu.VMEM((width // 128, RATE * pad_rows, 128), jnp.float32)],
        compiler_params=pltpu.CompilerParams(vmem_limit_bytes=VMEM_LIMIT),
        cost_estimate=pl.CostEstimate(flops=7 * 10**9, bytes_accessed=30 * 10**6, transcendentals=3072),
        name="prepare",
    )(head, *tokens, gain, weights)


def ffn_kernel(
    head_ref, a0, a1, a2, a3, o0, o1, o2, o3, t0, t1, t2, t3, g0, g1, g2, g3, gain_ref,
    up_ref, down_ref, f_keep, f_sent, n_keep, n_sent, hidden_ref, pack_ref,
    acc_up, acc_down,
):
    step = pl.program_id(0)
    head = head_ref[0]
    quarter, width = t0.shape[1:]
    ff_part = up_ref.shape[1]
    parts = up_ref.shape[0] // 2
    block = parts * ff_part

    @pl.when(step == 0)
    def _():
        acc_up[...] = jnp.zeros_like(acc_up)
        acc_down[...] = jnp.zeros_like(acc_down)

    starts = [
        pl.multiple_of(jnp.bitwise_xor(head, bits) * quarter, quarter) for bits in range(4)
    ]
    hidden = jnp.concatenate([t[0] for t in (t0, t1, t2, t3)], 0).astype(jnp.float32)
    for a, o in ((a0, o0), (a1, o1), (a2, o2), (a3, o3)):
        part = jnp.concatenate([a[0, pl.ds(at, quarter), :] for at in starts], 0)
        hidden = hidden + jnp.dot(
            part, o[...].reshape(a.shape[2], width), preferred_element_type=jnp.float32
        )
    hidden_ref[0] = hidden[:quarter]
    unit, _ = row_norm(hidden)
    normed = (unit * gain_ref[...]).astype(jnp.bfloat16)
    grad = jnp.concatenate([g[0] for g in (g0, g1, g2, g3)], 0)
    result = jnp.zeros(hidden.shape, jnp.float32)
    g_normed = jnp.zeros(hidden.shape, jnp.float32)
    for n in range(2):
        own = slice(n * parts, (n + 1) * parts)
        up = up_ref[own].reshape(block, width)
        down = down_ref[own].reshape(block, width)
        lifted = lax.dot_general(normed, up, COLS_IN, preferred_element_type=jnp.float32)
        sig = 0.5 * jnp.tanh(0.5 * lifted) + 0.5
        smooth = lifted * sig
        active = smooth.astype(jnp.bfloat16)
        g_active = lax.dot_general(grad, down, COLS_IN, preferred_element_type=jnp.float32)
        g_lifted = (g_active * (sig + smooth * (1.0 - sig))).astype(jnp.bfloat16)
        result = result + jnp.dot(active, down, preferred_element_type=jnp.float32)
        g_normed = g_normed + jnp.dot(g_lifted, up, preferred_element_type=jnp.float32)
        acc_down[n] += lax.dot_general(active, grad, ROWS_IN, preferred_element_type=jnp.float32)
        acc_up[n] += lax.dot_general(g_lifted, normed, ROWS_IN, preferred_element_type=jnp.float32)
    for value, keep, sent in ((g_normed, n_keep, n_sent), (result, f_keep, f_sent)):
        value = value.astype(jnp.bfloat16)
        for bits, (ref, slot) in enumerate(((keep, 0), (sent, 0), (keep, 1), (sent, 1))):
            ref[slot, 0] = value[bits * quarter : (bits + 1) * quarter]

    @pl.when(step == pl.num_programs(0) - 1)
    def _():
        for n in range(2):
            own = slice(n * parts, (n + 1) * parts)
            shape = (parts, ff_part, width)
            pack_ref[own, :ff_part] = acc_up[n].astype(jnp.bfloat16).reshape(shape)
            pack_ref[own, ff_part:] = acc_down[n].astype(jnp.bfloat16).reshape(shape)


def wo_blocks(pack, part, ff_part, head_groups):
    blks, _, width = pack.shape
    start = 2 * ff_part
    if part % 16 == 0:
        specs = [
            pl.BlockSpec(
                (blks, part, width),
                functools.partial(lambda index, s: (0, index, 0), start // part + n),
                pipeline_mode=pl.Buffered(1),
            )
            for n in range(head_groups)
        ]
        return [pack] * head_groups, specs
    blocks = [
        pack[:, start + n * part : start + (n + 1) * part].reshape(blks * part, width)
        for n in range(head_groups)
    ]
    return blocks, [fixed((blks * part, width))] * head_groups


def feed_forward(head, attended, wo, wo_specs, tokens, grads, gain, pack, ff_part):
    quarter, width = tokens[0].shape[1:]
    count, seg_len, head_cols = attended[0].shape
    blks = pack.shape[0]
    half = blks // 2 * ff_part
    grad_shape = (blks, 2 * ff_part, width)
    pieces = piece_specs(quarter, width)
    shapes = piece_shapes(count, quarter, width)

    def weight(index):
        return pl.BlockSpec(
            (blks, ff_part, width), lambda s: (0, index, 0), pipeline_mode=pl.Buffered(1)
        )

    return pl.pallas_call(
        ffn_kernel,
        grid=(count,),
        in_specs=[pl.BlockSpec(memory_space=pltpu.SMEM)]
        + [by_segment((seg_len, head_cols))] * 4
        + wo_specs
        + [by_segment((quarter, width))] * 8
        + [fixed((1, width)), weight(0), weight(1)],
        out_specs=pieces + pieces
        + [by_segment((quarter, width)), pl.BlockSpec(grad_shape, lambda s: (0, 0, 0))],
        out_shape=shapes + shapes
        + [
            jax.ShapeDtypeStruct((count, quarter, width), jnp.float32),
            jax.ShapeDtypeStruct(grad_shape, jnp.bfloat16),
        ],
        scratch_shapes=[
            pltpu.VMEM((2, half, width), jnp.float32),
            pltpu.VMEM((2, half, width), jnp.float32),
        ],
        compiler_params=pltpu.CompilerParams(vmem_limit_bytes=VMEM_LIMIT),
        cost_estimate=pl.CostEstimate(
            flops=count * 75 * 10**8, bytes_accessed=2 * 10**7 + count * 5 * 10**6, transcendentals=10**6
        ),
        name="feed_forward",
    )(head, *attended, *wo, *tokens, *grads, gain, pack, pack)


def middle_kernel(
    keep_ref, got_ref, far_ref, hidden_ref, grad_ref, gain_ref, o0, o1, o2, o3,
    g_hidden_ref, g_branch_ref, g_gain_ref, m0, m1, m2, m3,
):
    count, quarter, width = hidden_ref.shape
    flat = (count * quarter, width)
    gn = (
        keep_ref[0].astype(jnp.float32)
        + got_ref[0].astype(jnp.float32)
        + far_ref[...].astype(jnp.float32)
    ).reshape(flat)
    unit, spread = row_norm(hidden_ref[...].reshape(flat))
    gain_part = jnp.sum(gn * unit, axis=0, keepdims=True)

    @pl.when(pl.program_id(0) == 0)
    def _():
        g_gain_ref[...] = jnp.zeros_like(g_gain_ref)

    g_gain_ref[...] += gain_part
    g_hidden = grad_ref[...].astype(jnp.float32).reshape(flat) + norm_back(
        gn, unit, spread, gain_ref[...]
    )
    g_hidden_ref[...] = g_hidden.reshape(g_hidden_ref.shape)
    g_branch = g_hidden.astype(jnp.bfloat16)
    g_branch_ref[...] = g_branch.reshape(g_branch_ref.shape)
    for o, m in ((o0, m0), (o1, m1), (o2, m2), (o3, m3)):
        m[...] = (
            lax.dot_general(
                g_branch, o[...].reshape(m.shape[2], width), COLS_IN, preferred_element_type=jnp.float32
            )
            .astype(jnp.bfloat16)
            .reshape(m.shape)
        )


def middle(keep, got, far, hidden, grad, gain, wo, wo_specs, head_cols):
    count, quarter, width = hidden.shape
    size = 2 if count % 2 == 0 else 1
    piece = pl.BlockSpec((1, size, quarter, width), lambda s: (0, s, 0, 0))
    block = pl.BlockSpec((size, quarter, width), lambda s: (s, 0, 0))
    mixed = jax.ShapeDtypeStruct((count, quarter, head_cols), jnp.bfloat16)
    return pl.pallas_call(
        middle_kernel,
        grid=(count // size,),
        in_specs=[piece, piece, block, block, block, fixed((1, width))] + wo_specs,
        out_specs=[block, block, pl.BlockSpec((1, width), lambda s: (0, 0))]
        + [pl.BlockSpec((size, quarter, head_cols), lambda s: (s, 0, 0))] * 4,
        out_shape=[
            jax.ShapeDtypeStruct(hidden.shape, jnp.float32),
            jax.ShapeDtypeStruct(hidden.shape, jnp.bfloat16),
            jax.ShapeDtypeStruct((1, width), jnp.float32),
        ]
        + [mixed] * 4,
        compiler_params=pltpu.CompilerParams(vmem_limit_bytes=VMEM_LIMIT),
        cost_estimate=pl.CostEstimate(flops=count * 27 * 10**7, bytes_accessed=24 * 10**6, transcendentals=0),
        name="middle",
    )(keep, got, far, hidden, grad, gain, *wo)


def g_normed_kernel(head_ref, gq_ref, gkv_ref, gp_ref, w_ref, keep_ref, sent_ref, spread, rows):
    head = head_ref[0]
    seg_len, head_cols = gq_ref.shape[1:]
    pad_rows = gp_ref.shape[1]
    width = w_ref.shape[1]
    total = lax.dot_general(gq_ref[0], w_ref[2], COLS_IN, preferred_element_type=jnp.float32)
    for n in range(2):
        part = gkv_ref[0, :, n * head_cols : (n + 1) * head_cols]
        total = total + lax.dot_general(part, w_ref[n], COLS_IN, preferred_element_type=jnp.float32)
    for tap in range(RATE):
        sent = lax.dot_general(gp_ref[0], w_ref[3 + tap], COLS_IN, preferred_element_type=jnp.float32)
        for c in range(width // 128):
            spread[c, pl.ds(tap, pad_rows, stride=RATE), :] = sent[:, c * 128 : (c + 1) * 128]
    for c in range(width // 128):
        own = slice(c * 128, (c + 1) * 128)
        rows[:, own] = total[:, own] + spread[c, :seg_len, :]
    hand_out(head, rows, keep_ref, sent_ref)


def g_normed_parts(head, grad_query, grad_pair, grad_packed, weights, quarter):
    seg_count, seg_len, head_cols = grad_query.shape
    width = weights.shape[1]
    pad_rows = grad_packed.shape[1]
    return pl.pallas_call(
        g_normed_kernel,
        grid=(seg_count,),
        in_specs=[
            pl.BlockSpec(memory_space=pltpu.SMEM),
            by_segment((seg_len, head_cols)),
            by_segment((seg_len, 2 * head_cols)),
            by_segment((pad_rows, head_cols)),
            fixed(weights.shape),
        ],
        out_specs=piece_specs(quarter, width),
        out_shape=piece_shapes(seg_count, quarter, width),
        scratch_shapes=[
            pltpu.VMEM((width // 128, RATE * pad_rows, 128), jnp.float32),
            pltpu.VMEM((seg_len, width), jnp.float32),
        ],
        compiler_params=pltpu.CompilerParams(vmem_limit_bytes=VMEM_LIMIT),
        cost_estimate=pl.CostEstimate(flops=7 * 10**9, bytes_accessed=20 * 10**6, transcendentals=0),
        name="g_normed",
    )(head, grad_query, grad_pair, grad_packed, weights)


def head_swap(value, bit):
    count = lax.axis_size("head")
    return lax.ppermute(value, "head", [(source, source ^ bit) for source in range(count)])


def to_all_heads(value):
    far = head_swap(value, 2)
    return value, head_swap(value, 1), far, head_swap(far, 1)


def sum_over_heads(keep, sent):
    got = head_swap(sent, 1).astype(jnp.float32)
    far = (keep[1].astype(jnp.float32) + got[1]).astype(jnp.bfloat16)
    return keep[0].astype(jnp.float32) + got[0] + head_swap(far, 2).astype(jnp.float32)


def per_device(tokens, wq, wk, wv, wo, w_up, w_down, gain_one, gain_two, w_comp, lengths, grad_out):
    seg_count, quarter, width = tokens.shape
    head_groups = lax.axis_size("head")
    blk_count = lax.axis_size("blk")
    seg_len = quarter * head_groups
    head_cols = width // head_groups
    local_heads = head_cols // HD
    comp_rows = seg_len // RATE
    pad_rows = (comp_rows + 15) // 16 * 16
    window = CSEGS + 1
    head_index = lax.axis_index("head")
    blk_index = lax.axis_index("blk")
    token_count = seg_count * quarter
    full_count = seg_count * seg_len
    comp_count = seg_count * pad_rows
    part = wq.shape[0]
    ff_part = w_down.shape[0]
    bf16 = jnp.bfloat16
    head = head_index[None].astype(jnp.int32)

    columns = (
        jnp.concatenate([wk, wv, wq, w_comp.reshape(RATE * part, width)], 0)
        .reshape(6 * part, head_groups, head_cols)
        .transpose(1, 0, 2)
    )
    gains = jnp.pad(
        jnp.concatenate([gain_one, gain_two])[None], ((0, 15), (0, head_cols - 2 * part))
    )
    columns = jnp.concatenate(
        [columns, jnp.broadcast_to(gains, (head_groups, 16, head_cols))], 1
    )
    columns = lax.all_to_all(columns, "head", split_axis=0, concat_axis=0, tiled=True)
    columns, tokens_held = lax.optimization_barrier((columns, tokens))
    first_all = lax.all_gather(columns, "blk", axis=0)
    second_all = lax.all_gather(
        jnp.concatenate([w_up.T, w_down, *to_all_heads(wo)], 0), "blk", axis=0
    )
    token_pieces = to_all_heads(tokens_held)
    grad_held, tokens_far = lax.optimization_barrier((grad_out, token_pieces[2]))
    token_pieces = token_pieces[:2] + (tokens_far,) + token_pieces[3:]
    grad_far = head_swap(grad_held, 2)
    gain_pair = first_all[:, :, 6 * part, : 2 * part].reshape(
        blk_count, head_groups, 2, part
    ).transpose(2, 1, 0, 3).reshape(2, 1, width).astype(jnp.float32)
    gain_first, gain_second = gain_pair[0], gain_pair[1]
    weights = (
        first_all[:, :, : 6 * part]
        .reshape(blk_count, head_groups, 6, part, head_cols)
        .transpose(2, 1, 0, 3, 4)
        .reshape(6, width, head_cols)
    )
    wkv = jnp.concatenate([weights[0], weights[1]], 1)
    wo_held, wo_specs = wo_blocks(second_all, part, ff_part, head_groups)

    heads, normed, grouped, packed_mine = prepare(
        head, token_pieces, gain_first, weights, pad_rows
    )
    compressed = packed_mine[:, :comp_rows]
    pair = 2 * head_cols
    tail_rows = packed_mine[seg_count - window :].reshape(window * pad_rows, head_cols)
    half_rows = window * pad_rows // 2
    onward = jnp.concatenate(
        [
            heads[seg_count - 1, :, :pair],
            jnp.concatenate([tail_rows[:half_rows], tail_rows[half_rows:]], 1),
        ],
        0,
    )
    recv = passed_along(onward, "blk", 1)
    def all_columns(value):
        value = value.reshape(-1, head_cols)
        whole = jnp.zeros((value.shape[0], width), bf16)
        for bits, piece in enumerate(to_all_heads(value)):
            start = jnp.bitwise_xor(head_index, bits) * head_cols
            whole = lax.dynamic_update_slice(whole, piece, (0, start))
        return whole

    def comp_pairs(rows):
        return (
            jnp.dot(rows, wkv, preferred_element_type=jnp.float32)
            .astype(bf16)
            .reshape(-1, pad_rows, 2 * head_cols)
        )

    grad_far, grad_held, packed_mine = lax.optimization_barrier((grad_far, grad_held, packed_mine))
    grad_pieces = (grad_held, head_swap(grad_held, 1), grad_far, head_swap(grad_far, 1))
    packed = all_columns(packed_mine)
    comp_pair = comp_pairs(packed)
    comp_pair, grad_pieces = lax.optimization_barrier((comp_pair, grad_pieces))
    order = jnp.arange(lengths.shape[0], dtype=jnp.int32)
    starts = jnp.sum(jnp.where(order[None, :] < order[:, None], lengths[None, :], 0), axis=1)
    seg_ids = blk_index * seg_count + jnp.arange(seg_count, dtype=jnp.int32)
    seg_place = seg_ids - jnp.max(
        jnp.where(starts[None, :] <= seg_ids[:, None], starts[None, :], 0), axis=1
    )
    head_ids = head_index * local_heads + jnp.arange(local_heads, dtype=jnp.int32)
    slopes = jnp.exp2(-head_ids.astype(jnp.float32)) / 64.0 * LOG2E
    late = attend_fwd(
        window, window, seg_count - window, seg_place, slopes, heads, heads[:1, :, : 2 * head_cols],
        comp_pair, head_cols,
    )
    recv, late = lax.optimization_barrier((recv, late))
    recv_mem = recv[None, :seg_len]
    recv_packed = jnp.concatenate([recv[seg_len:, :head_cols], recv[seg_len:, head_cols:]], 0)
    comp_ext = jnp.concatenate([comp_pairs(all_columns(recv_packed)), comp_pair], 0)
    middle_seg = window // 2

    def early(a, b, comp_ext):
        return attend_fwd(a, 0, b - a, seg_place, slopes, heads, recv_mem, comp_ext, head_cols)

    first = early(0, middle_seg, comp_ext)
    late_far = head_swap(late[0], 2)
    late_far, first, comp_ext = lax.optimization_barrier((late_far, first, comp_ext))
    attention = [first, early(middle_seg, window, comp_ext), late]
    attn_out = jnp.concatenate([out for out, _ in attention], 0)
    lse = jnp.concatenate([total for _, total in attention], 0)
    far = jnp.concatenate([head_swap(out, 2) for out, _ in attention[:2]] + [late_far], 0)
    attended = (attn_out, head_swap(attn_out, 1), far, head_swap(far, 1))
    f_keep, f_sent, n_keep, n_sent, hidden, first_grads = feed_forward(
        head, attended, wo_held, wo_specs, token_pieces, grad_pieces, gain_second, second_all, ff_part
    )
    first_sum = lax.psum_scatter(first_grads, "blk", scatter_dimension=0)
    got = head_swap(n_sent, 1)
    far = (n_keep[1].astype(jnp.float32) + got[1].astype(jnp.float32)).astype(bf16)
    grad_hidden, grad_branch, grad_gain_two, *mixed = middle(
        n_keep, got, head_swap(far, 2), hidden, grad_out, gain_second, wo_held, wo_specs, head_cols
    )
    grad_gain_two = grad_gain_two[0]
    mixed = mixed[:1] + [head_swap(mixed[bits], bits) for bits in (1, 2, 3)]
    grad_wo = [
        lax.dot_general(
            lax.dynamic_slice_in_dim(block, head_index * quarter, quarter, 1).reshape(
                token_count, head_cols
            ),
            grad_branch.reshape(token_count, width),
            ROWS_IN,
            preferred_element_type=jnp.float32,
        ).astype(bf16)
        for block in attended
    ]
    f_got = head_swap(f_sent, 1)
    f_far = (f_keep[1].astype(jnp.float32) + f_got[1].astype(jnp.float32)).astype(bf16)
    wo_sent = jnp.stack([grad_wo[1], grad_wo[3]])
    wo_got = head_swap(wo_sent, 1).astype(jnp.float32)
    wo_far = (grad_wo[2].astype(jnp.float32) + wo_got[1]).astype(bf16)
    f_far, wo_far, mixed = lax.optimization_barrier((f_far, wo_far, mixed))
    wo_far = head_swap(wo_far, 2).astype(jnp.float32)

    none = jnp.zeros((16, 2 * head_cols), jnp.float32)
    grad_query, pair_done, held, rest, back = attend_bwd(
        0, seg_count, head, seg_place, slopes, heads, recv_mem, comp_ext, mixed, attn_out, lse, none,
        none, head_cols,
    )
    back, f_far = lax.optimization_barrier((back, f_far))
    got_back = passed_along(back, "blk", -1)
    f_far = head_swap(f_far, 2)
    grad_hidden = grad_hidden.reshape(token_count, width)
    normed = normed.reshape(full_count, width)
    grad_wq = lax.dot_general(
        normed, grad_query.reshape(full_count, head_cols), ROWS_IN, preferred_element_type=jnp.float32
    )
    grad_wo = (grad_wo[0].astype(jnp.float32) + wo_got[0] + wo_far).astype(bf16)

    def by_owner(value):
        return value.astype(bf16).reshape(
            head_groups, blk_count, part, value.shape[1]
        ).transpose(1, 0, 2, 3)

    wq_rows = by_owner(grad_wq)
    wo_rows = grad_wo.reshape(blk_count, part, head_groups, head_cols).transpose(0, 2, 1, 3)
    wq_rows, wo_rows, got_back, first_sum = lax.optimization_barrier(
        (wq_rows, wo_rows, got_back, first_sum)
    )
    got_back = got_back.astype(jnp.float32)
    last_pair = (held + got_back[window * pad_rows :]).astype(bf16)
    grad_pair = jnp.concatenate([pair_done, last_pair[None]], 0)
    got_comp = got_back[: window * pad_rows].reshape(window, pad_rows, 2 * head_cols)
    comp_pair_grad = jnp.pad(rest, ((0, seg_count - rest.shape[0]), (0, 0), (0, 0))) + jnp.pad(
        got_comp, ((seg_count - window, 0), (0, 0), (0, 0))
    )
    comp_grad_rows = comp_pair_grad.reshape(comp_count, 2 * head_cols).astype(bf16)
    grad_packed_part = lax.dot_general(
        comp_grad_rows, wkv, COLS_IN, preferred_element_type=jnp.float32
    ).astype(bf16)

    grad_packed_part, grad_pair = lax.optimization_barrier((grad_packed_part, grad_pair))

    def columns_of(bits):
        start = jnp.bitwise_xor(head_index, bits) * head_cols
        return lax.dynamic_slice_in_dim(grad_packed_part, start, head_cols, 1)

    grad_packed = sum_over_heads(
        (columns_of(0), columns_of(2)), jnp.stack([columns_of(1), columns_of(3)])
    ).astype(bf16)
    grad_packed, f_far = lax.optimization_barrier((grad_packed, f_far))
    out_tokens = (
        hidden + f_keep[0].astype(jnp.float32) + f_got[0].astype(jnp.float32) + f_far.astype(jnp.float32)
    ).astype(bf16)
    keep, sent = g_normed_parts(
        head,
        grad_query,
        grad_pair,
        grad_packed.reshape(seg_count, pad_rows, head_cols),
        weights,
        quarter,
    )
    grad_normed = sum_over_heads(keep, sent).reshape(token_count, width)
    unit_one, spread_one = row_norm(tokens.reshape(token_count, width).astype(jnp.float32))
    grad_tokens = (
        (grad_hidden + norm_back(grad_normed, unit_one, spread_one, gain_first))
        .astype(bf16)
        .reshape(tokens.shape)
    )
    grad_kv = grad_pair.reshape(full_count, 2 * head_cols)
    grad_wkv = lax.dot_general(normed, grad_kv, ROWS_IN, preferred_element_type=jnp.float32)
    comp_term = lax.dot_general(packed, comp_grad_rows, ROWS_IN, preferred_element_type=jnp.float32)
    grad_comp = lax.dot_general(
        grouped.reshape(comp_count, RATE * width),
        grad_packed,
        ROWS_IN,
        preferred_element_type=jnp.float32,
    ).reshape(RATE, width, head_cols)
    grad_gain_one = (
        jnp.sum(grad_wq * weights[2].astype(jnp.float32), axis=1)
        + jnp.sum(grad_wkv * wkv.astype(jnp.float32), axis=1)
        + jnp.sum(grad_comp * weights[3:].astype(jnp.float32), axis=(0, 2))
    ) / gain_first[0]
    grad_wkv = grad_wkv + comp_term

    gain_rows = (
        jnp.stack([grad_gain_one, grad_gain_two])
        .reshape(2, head_groups, blk_count, part)
        .transpose(2, 1, 0, 3)
        .astype(bf16)
    )
    second_grads = jnp.concatenate(
        [
            wq_rows,
            by_owner(grad_wkv[:, :head_cols]),
            by_owner(grad_wkv[:, head_cols:]),
            by_owner(grad_comp[0]),
            by_owner(grad_comp[1]),
            by_owner(grad_comp[2]),
            jnp.pad(gain_rows, ((0, 0), (0, 0), (0, 14), (0, head_cols - part))),
            wo_rows,
        ],
        2,
    )
    first_sum = first_sum.astype(jnp.float32)
    own_rows = 6 * part + 16
    second_part = lax.psum_scatter(
        second_grads.reshape(-1, head_cols), "blk", scatter_dimension=0, tiled=True
    ).reshape(head_groups, own_rows + part, head_cols)
    second_sum = lax.all_to_all(
        second_part[:, :own_rows], "head", split_axis=0, concat_axis=0, tiled=True
    ).astype(jnp.float32)
    gain_sum = jnp.sum(second_sum[:, 6 * part : 6 * part + 2, :part], axis=0)
    weight_sum = (
        second_sum[:, : 6 * part]
        .reshape(head_groups, 6, part, head_cols)
        .transpose(1, 2, 0, 3)
        .reshape(6, part, width)
    )
    wo_sum = second_part[:, own_rows:].astype(jnp.float32).transpose(1, 0, 2).reshape(part, width)
    return (
        out_tokens,
        compressed,
        grad_tokens,
        weight_sum[0],
        weight_sum[1],
        weight_sum[2],
        wo_sum,
        first_sum[:ff_part].T,
        first_sum[ff_part:],
        gain_sum[0],
        gain_sum[1],
        weight_sum[3:],
    )


def solution(mesh):
    return jax.shard_map(
        per_device,
        mesh=mesh,
        in_specs=(
            P("blk", "head", None),
            P(("head", "blk"), None),
            P(("head", "blk"), None),
            P(("head", "blk"), None),
            P(("head", "blk"), None),
            P(None, ("head", "blk")),
            P(("head", "blk"), None),
            P(("head", "blk")),
            P(("head", "blk")),
            P(None, ("head", "blk"), None),
            P(),
            P("blk", "head", None),
        ),
        out_specs=(
            P("blk", "head", None),
            P("blk", None, "head"),
            P("blk", "head", None),
            P(("head", "blk"), None),
            P(("head", "blk"), None),
            P(("head", "blk"), None),
            P(("head", "blk"), None),
            P(None, ("head", "blk")),
            P(("head", "blk"), None),
            P(("head", "blk")),
            P(("head", "blk")),
            P(None, ("head", "blk"), None),
        ),
        check_vma=False,
    )
```

```python
import functools

import jax
import jax.numpy as jnp
from jax import lax
from jax.experimental import pallas as pl
from jax.experimental.pallas import tpu as pltpu
from jax.sharding import PartitionSpec as P

HD = 128
RATE = 3
CSEGS = 3


EPS = 1e-05
NEG = -1e30
ROWS_IN = (((0,), (0,)), ((), ()))
COLS_IN = (((1,), (1,)), ((), ()))


def passed_along(value, axis, steps):
    count = lax.axis_size(axis)
    leading, last = (max(0, -steps), min(count, count - steps))
    return lax.ppermute(value, axis, [(source, source + steps) for source in range(leading, last)])


LOG2E = 1.4426950408889634
PAD_ROWS = 176
VMEM_LIMIT = 56 * 1024 * 1024


def key_bias(rows, base, step, valid_rows, open_, slope):
    row = lax.broadcasted_iota(jnp.int32, (rows, 1), 0)
    place = (base + step * row).astype(jnp.float32)
    return jnp.where((row < valid_rows) & open_, place * slope, NEG)


def fwd_kernel(first, shift, place_ref, slope_ref, q_ref, own_ref, prev_ref, recv_ref, comp_ref, out_ref, lse_ref):
    step = pl.program_id(0) + first
    place = place_ref[step]
    seg_len = q_ref.shape[1]
    half = seg_len // 2
    pad_rows = comp_ref.shape[1]
    local_heads = q_ref.shape[2] // HD
    values_at = local_heads * HD
    factor = HD ** (-0.5) * LOG2E
    lower = lax.broadcasted_iota(jnp.int32, (half, half), 0) <= lax.broadcasted_iota(
        jnp.int32, (half, half), 1
    )
    for h in range(local_heads):
        kc = slice(h * HD, (h + 1) * HD)
        vc = slice(values_at + h * HD, values_at + (h + 1) * HD)
        slope = slope_ref[h]
        parts = []
        for piece in range(CSEGS):
            lag = CSEGS + 1 - piece
            bias = key_bias(pad_rows, RATE // 2 - lag * seg_len, RATE, seg_len // RATE, place >= lag, slope)
            at = step + piece - shift
            parts.append((comp_ref[at, :, kc], comp_ref[at, :, vc], bias))
        bias = key_bias(seg_len, -seg_len, 1, seg_len, place >= 1, slope)
        if first:
            parts.append((prev_ref[0, :, kc], prev_ref[0, :, vc], bias))
        else:
            is_first = step == 0
            parts.append(
                (
                    jnp.where(is_first, recv_ref[0, :, kc], prev_ref[0, :, kc]),
                    jnp.where(is_first, recv_ref[0, :, vc], prev_ref[0, :, vc]),
                    bias,
                )
            )
        own_bias = [
            key_bias(half, n * half, 1, half, place >= 0, slope) for n in range(2)
        ]
        for n in range(2):
            query = q_ref[0, n * half : (n + 1) * half, kc]
            group = list(parts)
            for m in range(n + 1):
                rows = slice(m * half, (m + 1) * half)
                group.append((own_ref[0, rows, kc], own_ref[0, rows, vc], own_bias[m]))
            scores = []
            top = None
            for index, (k, v, bias) in enumerate(group):
                raw = lax.dot_general(k, query, COLS_IN, preferred_element_type=jnp.float32)
                raw = raw * factor + bias
                if index == len(group) - 1:
                    raw = jnp.where(lower, raw, NEG)
                scores.append(raw)
                peak = jnp.max(raw, axis=0, keepdims=True)
                top = peak if top is None else jnp.maximum(top, peak)
            total = jnp.zeros_like(top)
            result = jnp.zeros((HD, half), jnp.float32)
            for raw, (k, v, bias) in zip(scores, group):
                weight = jnp.exp2(raw - top)
                total = total + jnp.sum(weight, axis=0, keepdims=True)
                result = result + lax.dot_general(
                    v, weight.astype(jnp.bfloat16), ROWS_IN, preferred_element_type=jnp.float32
                )
            result = result * (1.0 / total)
            out_ref[0, n * half : (n + 1) * half, kc] = result.T.astype(jnp.bfloat16)
            lse_ref[0, h : h + 1, n * half : (n + 1) * half] = top + jnp.log(total) * LOG2E


def bwd_kernel(
    first, place_ref, slope_ref, q_ref, own_ref, prev_ref, recv_ref, comp_ref, head_ref, g0, g1, g2, g3,
    att_ref, lse_ref, held_ref, over_ref, gq_ref, gkv_ref, tail_ref, rest_ref, back_ref, grad_ref, gcomp_ref,
):
    opening = first == 0
    step = pl.program_id(0) + first
    place = place_ref[step]
    seg_len = q_ref.shape[1]
    half = seg_len // 2
    pad_rows = comp_ref.shape[1]
    local_heads = q_ref.shape[2] // HD
    values_at = local_heads * HD
    scale = HD ** (-0.5)
    factor = scale * LOG2E
    is_first = step == 0
    lower = lax.broadcasted_iota(jnp.int32, (half, half), 0) <= lax.broadcasted_iota(
        jnp.int32, (half, half), 1
    )

    at_start = pl.program_id(0) == 0

    @pl.when(at_start)
    def _():
        gcomp_ref[...] = jnp.zeros_like(gcomp_ref)
        if opening:
            tail_ref[...] = jnp.zeros_like(tail_ref)
        else:
            tail_ref[...] = held_ref[...]
            gcomp_ref[: CSEGS - 1] = over_ref[...]

    place_rows(head_ref[0], (g0, g1, g2, g3), grad_ref)
    for h in range(local_heads):
        kc = slice(h * HD, (h + 1) * HD)
        vc = slice(values_at + h * HD, values_at + (h + 1) * HD)
        slope = slope_ref[h]
        query = q_ref[0, :, kc]
        grad = grad_ref[:, kc]
        lse = lse_ref[0, h : h + 1, :]
        product = grad.astype(jnp.float32) * att_ref[0, :, kc].astype(jnp.float32)
        delta = jnp.sum(product.T, axis=0, keepdims=True)

        def part(k, v, bias, cols, masked):
            raw = lax.dot_general(k, query[cols], COLS_IN, preferred_element_type=jnp.float32)
            raw = raw * factor + bias
            if masked:
                raw = jnp.where(lower, raw, NEG)
            prob = jnp.exp2(raw - lse[:, cols])
            grad_prob = lax.dot_general(v, grad[cols], COLS_IN, preferred_element_type=jnp.float32)
            grad_score = (prob * (grad_prob - delta[:, cols])).astype(jnp.bfloat16)
            gk = jnp.dot(grad_score, query[cols], preferred_element_type=jnp.float32) * scale
            gv = jnp.dot(prob.astype(jnp.bfloat16), grad[cols], preferred_element_type=jnp.float32)
            gq = lax.dot_general(k, grad_score, ROWS_IN, preferred_element_type=jnp.float32)
            return gk, gv, gq

        every = slice(0, seg_len)
        total = jnp.zeros((HD, seg_len), jnp.float32)
        for piece in range(CSEGS):
            lag = CSEGS + 1 - piece
            bias = key_bias(pad_rows, RATE // 2 - lag * seg_len, RATE, seg_len // RATE, place >= lag, slope)
            gk, gv, gq = part(comp_ref[step + piece, :, kc], comp_ref[step + piece, :, vc], bias, every, False)
            gcomp_ref[step - first + piece, :, kc] += gk
            gcomp_ref[step - first + piece, :, vc] += gv
            total = total + gq
        for n in range(2):
            rows = slice(n * half, (n + 1) * half)
            bias = key_bias(half, n * half - seg_len, 1, half, place >= 1, slope)
            k, v = prev_ref[0, rows, kc], prev_ref[0, rows, vc]
            if opening:
                k = jnp.where(is_first, recv_ref[0, rows, kc], k)
                v = jnp.where(is_first, recv_ref[0, rows, vc], v)
            gk, gv, gq = part(k, v, bias, every, False)
            gk = (tail_ref[rows, kc] + gk).astype(jnp.bfloat16)
            gv = (tail_ref[rows, vc] + gv).astype(jnp.bfloat16)
            gkv_ref[0, rows, kc] = gk
            gkv_ref[0, rows, vc] = gv
            if opening:
                at = (CSEGS + 1) * pad_rows + n * half
                send = slice(at, at + half)

                @pl.when(is_first)
                def _(gk=gk, gv=gv, send=send):
                    back_ref[send, kc] = gk
                    back_ref[send, vc] = gv

            total = total + gq
        lo, hi = slice(0, half), slice(half, seg_len)
        bias_lo = key_bias(half, 0, 1, half, place >= 0, slope)
        bias_hi = key_bias(half, half, 1, half, place >= 0, slope)
        gk0, gv0, gq0 = part(own_ref[0, lo, kc], own_ref[0, lo, vc], bias_lo, lo, True)
        gk1, gv1, gq1 = part(own_ref[0, lo, kc], own_ref[0, lo, vc], bias_lo, hi, False)
        gk2, gv2, gq2 = part(own_ref[0, hi, kc], own_ref[0, hi, vc], bias_hi, hi, True)
        tail_ref[lo, kc] = gk0 + gk1
        tail_ref[lo, vc] = gv0 + gv1
        tail_ref[hi, kc] = gk2
        tail_ref[hi, vc] = gv2
        gq_ref[0, lo, kc] = ((total[:, lo] + gq0) * scale).T.astype(jnp.bfloat16)
        gq_ref[0, hi, kc] = ((total[:, hi] + gq1 + gq2) * scale).T.astype(jnp.bfloat16)

    @pl.when(pl.program_id(0) == pl.num_programs(0) - 1)
    def _():
        if opening:
            for entry in range(CSEGS + 1):
                rows = slice(entry * pad_rows, (entry + 1) * pad_rows)
                back_ref[rows, :] = gcomp_ref[entry].astype(jnp.bfloat16)
            rest_ref[...] = gcomp_ref[CSEGS + 1 :]
        else:
            rest_ref[...] = gcomp_ref[...]
            back_ref[...] = jnp.zeros_like(back_ref)


def attention_specs(first, seg_len, head_cols, comp_shape):
    pair = 2 * head_cols
    return [
        pl.BlockSpec(memory_space=pltpu.SMEM),
        pl.BlockSpec(memory_space=pltpu.SMEM),
        pl.BlockSpec((1, seg_len, head_cols), lambda s: (s + first, 0, 2)),
        pl.BlockSpec((1, seg_len, pair), lambda s: (s + first, 0, 0)),
        pl.BlockSpec((1, seg_len, pair), lambda s: (jnp.maximum(s + first - 1, 0), 0, 0)),
        fixed((1, seg_len, pair)),
        fixed(comp_shape),
    ]


def attend_fwd(first, shift, count, place, slope, heads, recv_mem, comp_ext, head_cols):
    seg_len = heads.shape[1]
    local_heads = head_cols // HD
    return pl.pallas_call(
        functools.partial(fwd_kernel, first, shift),
        grid=(count,),
        in_specs=attention_specs(first, seg_len, head_cols, comp_ext.shape),
        out_specs=[by_segment((seg_len, head_cols)), by_segment((local_heads, seg_len))],
        out_shape=[
            jax.ShapeDtypeStruct((count, seg_len, head_cols), jnp.bfloat16),
            jax.ShapeDtypeStruct((count, local_heads, seg_len), jnp.float32),
        ],
        compiler_params=pltpu.CompilerParams(vmem_limit_bytes=VMEM_LIMIT),
        cost_estimate=pl.CostEstimate(
            flops=count * 10**9, bytes_accessed=count * 3 * 10**6, transcendentals=count * 16 * 10**5
        ),
        name="attend_fwd",
    )(place, slope, heads, heads, heads, recv_mem, comp_ext)


def attend_bwd(
    first, count, head, place, slope, heads, recv_mem, comp_ext, grad_mixed, attn_out, lse, held, over, head_cols
):
    seg_len = attn_out.shape[1]
    local_heads = head_cols // HD
    pair = 2 * head_cols
    pad_rows = comp_ext.shape[1]
    entries = count + CSEGS - 1
    opening = first == 0
    done = count - 1 if opening else count
    rest = entries - CSEGS - 1 if opening else entries
    back = ((CSEGS + 1) * pad_rows + seg_len, pair) if opening else (16, pair)

    def pair_block(s):
        return (jnp.maximum(s - 1, 0) if opening else s, 0, 0)

    def stays(shape):
        return pl.BlockSpec(shape, lambda s: (0,) * len(shape))

    return pl.pallas_call(
        functools.partial(bwd_kernel, first),
        grid=(count,),
        in_specs=attention_specs(first, seg_len, head_cols, comp_ext.shape)
        + [pl.BlockSpec(memory_space=pltpu.SMEM)]
        + [by_segment(grad_mixed[0].shape[1:], first)] * 4
        + [
            by_segment((seg_len, head_cols), first),
            by_segment((local_heads, seg_len), first),
            fixed(held.shape),
            fixed(over.shape),
        ],
        out_specs=[
            by_segment((seg_len, head_cols)),
            pl.BlockSpec((1, seg_len, pair), pair_block),
            stays((seg_len, pair)),
            stays((rest, pad_rows, pair)),
            stays(back),
        ],
        out_shape=[
            jax.ShapeDtypeStruct((count, seg_len, head_cols), jnp.bfloat16),
            jax.ShapeDtypeStruct((done, seg_len, pair), jnp.bfloat16),
            jax.ShapeDtypeStruct((seg_len, pair), jnp.float32),
            jax.ShapeDtypeStruct((rest, pad_rows, pair), jnp.float32),
            jax.ShapeDtypeStruct(back, jnp.bfloat16),
        ],
        scratch_shapes=[
            pltpu.VMEM((seg_len, head_cols), jnp.bfloat16),
            pltpu.VMEM((entries, pad_rows, pair), jnp.float32),
        ],
        compiler_params=pltpu.CompilerParams(vmem_limit_bytes=VMEM_LIMIT),
        cost_estimate=pl.CostEstimate(
            flops=count * 2 * 10**9, bytes_accessed=count * 4 * 10**6, transcendentals=count * 16 * 10**5
        ),
        name="attend_bwd",
    )(place, slope, heads, heads, heads, recv_mem, comp_ext, head, *grad_mixed, attn_out, lse, held, over)


def row_norm(values):
    average = jnp.mean(values, axis=-1, keepdims=True)
    center = values - average
    spread = lax.rsqrt(jnp.mean(center * center, axis=-1, keepdims=True) + EPS)
    return center * spread, spread


def norm_back(grad, unit, spread, gain):
    scaled = grad * gain
    along = jnp.mean(scaled * unit, axis=-1, keepdims=True)
    return spread * (scaled - jnp.mean(scaled, axis=-1, keepdims=True) - unit * along)


def place_rows(head, pieces, target):
    for bits, piece in enumerate(pieces):
        rows = piece.shape[1]
        at = pl.multiple_of(jnp.bitwise_xor(head, bits) * rows, rows)
        target[pl.ds(at, rows), :] = piece[0].astype(target.dtype)


def hand_out(head, source, keep_ref, sent_ref):
    rows = keep_ref.shape[2]
    for bits, (ref, slot) in enumerate(
        ((keep_ref, 0), (sent_ref, 0), (keep_ref, 1), (sent_ref, 1))
    ):
        at = pl.multiple_of(jnp.bitwise_xor(head, bits) * rows, rows)
        ref[slot, 0] = source[pl.ds(at, rows), :].astype(ref.dtype)


def prep_kernel(
    head_ref, t0, t1, t2, t3, gain_ref, w_ref, heads_ref, normed_ref, grouped_ref, packed_ref, spread
):
    head = head_ref[0]
    quarter, width = t0.shape[1:]
    seg_len = heads_ref.shape[1]
    head_cols = w_ref.shape[2]
    pad_rows = grouped_ref.shape[1]
    tiles = width // 128
    for bits, piece in enumerate((t0, t1, t2, t3)):
        unit, _ = row_norm(piece[0].astype(jnp.float32))
        normed = (unit * gain_ref[...]).astype(jnp.bfloat16)
        at = pl.multiple_of(jnp.bitwise_xor(head, bits) * quarter, quarter)
        normed_ref[0, pl.ds(at, quarter), :] = normed
        wide = normed.astype(jnp.float32)
        for c in range(tiles):
            spread[c, pl.ds(at, quarter), :] = wide[:, c * 128 : (c + 1) * 128]
    last = spread[:, seg_len - 8 : seg_len, :]
    row = lax.broadcasted_iota(jnp.int32, last.shape, 1)
    spread[:, seg_len - 8 : seg_len, :] = jnp.where(row < 8 - seg_len % RATE, last, 0.0)
    spread[:, seg_len:, :] = jnp.zeros((tiles, spread.shape[1] - seg_len, 128), jnp.float32)
    rows = normed_ref[0]
    for n in range(3):
        heads_ref[0, :, n * head_cols : (n + 1) * head_cols] = jnp.dot(
            rows, w_ref[n], preferred_element_type=jnp.float32
        ).astype(jnp.bfloat16)
    total = jnp.zeros((pad_rows, head_cols), jnp.float32)
    for tap in range(RATE):
        for c in range(tiles):
            at = tap * width + c * 128
            grouped_ref[0, :, at : at + 128] = spread[
                c, pl.ds(tap, pad_rows, stride=RATE), :
            ].astype(jnp.bfloat16)
        total = total + jnp.dot(
            grouped_ref[0, :, tap * width : (tap + 1) * width],
            w_ref[3 + tap],
            preferred_element_type=jnp.float32,
        )
    packed_ref[0] = total.astype(jnp.bfloat16)


def fixed(shape):
    return pl.BlockSpec(shape, lambda s: (0,) * len(shape), pipeline_mode=pl.Buffered(1))


def by_segment(shape, first=0):
    return pl.BlockSpec((1,) + shape, lambda s: (s + first,) + (0,) * len(shape))


def piece_specs(quarter, width):
    spec = pl.BlockSpec((2, 1, quarter, width), lambda s: (0, s, 0, 0))
    return [spec, spec]


def piece_shapes(seg_count, quarter, width):
    shape = jax.ShapeDtypeStruct((2, seg_count, quarter, width), jnp.bfloat16)
    return [shape, shape]


def prepare(head, tokens, gain, weights, pad_rows):
    seg_count, quarter, width = tokens[0].shape
    seg_len = quarter * len(tokens)
    head_cols = weights.shape[2]
    bf16 = jnp.bfloat16
    return pl.pallas_call(
        prep_kernel,
        grid=(seg_count,),
        in_specs=[pl.BlockSpec(memory_space=pltpu.SMEM)]
        + [by_segment((quarter, width))] * 4
        + [fixed((1, width)), fixed(weights.shape)],
        out_specs=[
            by_segment((seg_len, 3 * head_cols)),
            by_segment((seg_len, width)),
            by_segment((pad_rows, RATE * width)),
            by_segment((pad_rows, head_cols)),
        ],
        out_shape=[
            jax.ShapeDtypeStruct((seg_count, seg_len, 3 * head_cols), bf16),
            jax.ShapeDtypeStruct((seg_count, seg_len, width), bf16),
            jax.ShapeDtypeStruct((seg_count, pad_rows, RATE * width), bf16),
            jax.ShapeDtypeStruct((seg_count, pad_rows, head_cols), bf16),
        ],
        scratch_shapes=[pltpu.VMEM((width // 128, RATE * pad_rows, 128), jnp.float32)],
        compiler_params=pltpu.CompilerParams(vmem_limit_bytes=VMEM_LIMIT),
        cost_estimate=pl.CostEstimate(flops=7 * 10**9, bytes_accessed=30 * 10**6, transcendentals=3072),
        name="prepare",
    )(head, *tokens, gain, weights)


def ffn_kernel(
    head_ref, a0, a1, a2, a3, o0, o1, o2, o3, t0, t1, t2, t3, g0, g1, g2, g3, gain_ref,
    up_ref, down_ref, f_keep, f_sent, n_keep, n_sent, hidden_ref, pack_ref,
    acc_up, acc_down,
):
    step = pl.program_id(0)
    head = head_ref[0]
    quarter, width = t0.shape[1:]
    ff_part = up_ref.shape[1]
    parts = up_ref.shape[0] // 2
    block = parts * ff_part

    @pl.when(step == 0)
    def _():
        acc_up[...] = jnp.zeros_like(acc_up)
        acc_down[...] = jnp.zeros_like(acc_down)

    starts = [
        pl.multiple_of(jnp.bitwise_xor(head, bits) * quarter, quarter) for bits in range(4)
    ]
    hidden = jnp.concatenate([t[0] for t in (t0, t1, t2, t3)], 0).astype(jnp.float32)
    for a, o in ((a0, o0), (a1, o1), (a2, o2), (a3, o3)):
        part = jnp.concatenate([a[0, pl.ds(at, quarter), :] for at in starts], 0)
        hidden = hidden + jnp.dot(
            part, o[...].reshape(a.shape[2], width), preferred_element_type=jnp.float32
        )
    hidden_ref[0] = hidden[:quarter]
    unit, _ = row_norm(hidden)
    normed = (unit * gain_ref[...]).astype(jnp.bfloat16)
    grad = jnp.concatenate([g[0] for g in (g0, g1, g2, g3)], 0)
    result = jnp.zeros(hidden.shape, jnp.float32)
    g_normed = jnp.zeros(hidden.shape, jnp.float32)
    for n in range(2):
        own = slice(n * parts, (n + 1) * parts)
        up = up_ref[own].reshape(block, width)
        down = down_ref[own].reshape(block, width)
        lifted = lax.dot_general(normed, up, COLS_IN, preferred_element_type=jnp.float32)
        sig = 0.5 * jnp.tanh(0.5 * lifted) + 0.5
        smooth = lifted * sig
        active = smooth.astype(jnp.bfloat16)
        g_active = lax.dot_general(grad, down, COLS_IN, preferred_element_type=jnp.float32)
        g_lifted = (g_active * (sig + smooth * (1.0 - sig))).astype(jnp.bfloat16)
        result = result + jnp.dot(active, down, preferred_element_type=jnp.float32)
        g_normed = g_normed + jnp.dot(g_lifted, up, preferred_element_type=jnp.float32)
        acc_down[n] += lax.dot_general(active, grad, ROWS_IN, preferred_element_type=jnp.float32)
        acc_up[n] += lax.dot_general(g_lifted, normed, ROWS_IN, preferred_element_type=jnp.float32)
    for value, keep, sent in ((g_normed, n_keep, n_sent), (result, f_keep, f_sent)):
        value = value.astype(jnp.bfloat16)
        for bits, (ref, slot) in enumerate(((keep, 0), (sent, 0), (keep, 1), (sent, 1))):
            ref[slot, 0] = value[bits * quarter : (bits + 1) * quarter]

    @pl.when(step == pl.num_programs(0) - 1)
    def _():
        for n in range(2):
            own = slice(n * parts, (n + 1) * parts)
            shape = (parts, ff_part, width)
            pack_ref[own, :ff_part] = acc_up[n].astype(jnp.bfloat16).reshape(shape)
            pack_ref[own, ff_part:] = acc_down[n].astype(jnp.bfloat16).reshape(shape)


def wo_blocks(pack, part, ff_part, head_groups):
    blks, _, width = pack.shape
    start = 2 * ff_part
    if part % 16 == 0:
        specs = [
            pl.BlockSpec(
                (blks, part, width),
                functools.partial(lambda index, s: (0, index, 0), start // part + n),
                pipeline_mode=pl.Buffered(1),
            )
            for n in range(head_groups)
        ]
        return [pack] * head_groups, specs
    blocks = [
        pack[:, start + n * part : start + (n + 1) * part].reshape(blks * part, width)
        for n in range(head_groups)
    ]
    return blocks, [fixed((blks * part, width))] * head_groups


def feed_forward(head, attended, wo, wo_specs, tokens, grads, gain, pack, ff_part):
    quarter, width = tokens[0].shape[1:]
    count, seg_len, head_cols = attended[0].shape
    blks = pack.shape[0]
    half = blks // 2 * ff_part
    grad_shape = (blks, 2 * ff_part, width)
    pieces = piece_specs(quarter, width)
    shapes = piece_shapes(count, quarter, width)

    def weight(index):
        return pl.BlockSpec(
            (blks, ff_part, width), lambda s: (0, index, 0), pipeline_mode=pl.Buffered(1)
        )

    return pl.pallas_call(
        ffn_kernel,
        grid=(count,),
        in_specs=[pl.BlockSpec(memory_space=pltpu.SMEM)]
        + [by_segment((seg_len, head_cols))] * 4
        + wo_specs
        + [by_segment((quarter, width))] * 8
        + [fixed((1, width)), weight(0), weight(1)],
        out_specs=pieces + pieces
        + [by_segment((quarter, width)), pl.BlockSpec(grad_shape, lambda s: (0, 0, 0))],
        out_shape=shapes + shapes
        + [
            jax.ShapeDtypeStruct((count, quarter, width), jnp.float32),
            jax.ShapeDtypeStruct(grad_shape, jnp.bfloat16),
        ],
        scratch_shapes=[
            pltpu.VMEM((2, half, width), jnp.float32),
            pltpu.VMEM((2, half, width), jnp.float32),
        ],
        compiler_params=pltpu.CompilerParams(vmem_limit_bytes=VMEM_LIMIT),
        cost_estimate=pl.CostEstimate(
            flops=count * 75 * 10**8, bytes_accessed=2 * 10**7 + count * 5 * 10**6, transcendentals=10**6
        ),
        name="feed_forward",
    )(head, *attended, *wo, *tokens, *grads, gain, pack, pack)


def middle_kernel(
    keep_ref, got_ref, far_ref, hidden_ref, grad_ref, gain_ref, o0, o1, o2, o3,
    g_hidden_ref, g_branch_ref, g_gain_ref, m0, m1, m2, m3,
):
    count, quarter, width = hidden_ref.shape
    flat = (count * quarter, width)
    gn = (
        keep_ref[0].astype(jnp.float32)
        + got_ref[0].astype(jnp.float32)
        + far_ref[...].astype(jnp.float32)
    ).reshape(flat)
    unit, spread = row_norm(hidden_ref[...].reshape(flat))
    gain_part = jnp.sum(gn * unit, axis=0, keepdims=True)

    @pl.when(pl.program_id(0) == 0)
    def _():
        g_gain_ref[...] = jnp.zeros_like(g_gain_ref)

    g_gain_ref[...] += gain_part
    g_hidden = grad_ref[...].astype(jnp.float32).reshape(flat) + norm_back(
        gn, unit, spread, gain_ref[...]
    )
    g_hidden_ref[...] = g_hidden.reshape(g_hidden_ref.shape)
    g_branch = g_hidden.astype(jnp.bfloat16)
    g_branch_ref[...] = g_branch.reshape(g_branch_ref.shape)
    for o, m in ((o0, m0), (o1, m1), (o2, m2), (o3, m3)):
        m[...] = (
            lax.dot_general(
                g_branch, o[...].reshape(m.shape[2], width), COLS_IN, preferred_element_type=jnp.float32
            )
            .astype(jnp.bfloat16)
            .reshape(m.shape)
        )


def middle(keep, got, far, hidden, grad, gain, wo, wo_specs, head_cols):
    count, quarter, width = hidden.shape
    size = 2 if count % 2 == 0 else 1
    piece = pl.BlockSpec((1, size, quarter, width), lambda s: (0, s, 0, 0))
    block = pl.BlockSpec((size, quarter, width), lambda s: (s, 0, 0))
    mixed = jax.ShapeDtypeStruct((count, quarter, head_cols), jnp.bfloat16)
    return pl.pallas_call(
        middle_kernel,
        grid=(count // size,),
        in_specs=[piece, piece, block, block, block, fixed((1, width))] + wo_specs,
        out_specs=[block, block, pl.BlockSpec((1, width), lambda s: (0, 0))]
        + [pl.BlockSpec((size, quarter, head_cols), lambda s: (s, 0, 0))] * 4,
        out_shape=[
            jax.ShapeDtypeStruct(hidden.shape, jnp.float32),
            jax.ShapeDtypeStruct(hidden.shape, jnp.bfloat16),
            jax.ShapeDtypeStruct((1, width), jnp.float32),
        ]
        + [mixed] * 4,
        compiler_params=pltpu.CompilerParams(vmem_limit_bytes=VMEM_LIMIT),
        cost_estimate=pl.CostEstimate(flops=count * 27 * 10**7, bytes_accessed=24 * 10**6, transcendentals=0),
        name="middle",
    )(keep, got, far, hidden, grad, gain, *wo)


def g_normed_kernel(head_ref, gq_ref, gkv_ref, gp_ref, w_ref, keep_ref, sent_ref, spread, rows):
    head = head_ref[0]
    seg_len, head_cols = gq_ref.shape[1:]
    pad_rows = gp_ref.shape[1]
    width = w_ref.shape[1]
    total = lax.dot_general(gq_ref[0], w_ref[2], COLS_IN, preferred_element_type=jnp.float32)
    for n in range(2):
        part = gkv_ref[0, :, n * head_cols : (n + 1) * head_cols]
        total = total + lax.dot_general(part, w_ref[n], COLS_IN, preferred_element_type=jnp.float32)
    for tap in range(RATE):
        sent = lax.dot_general(gp_ref[0], w_ref[3 + tap], COLS_IN, preferred_element_type=jnp.float32)
        for c in range(width // 128):
            spread[c, pl.ds(tap, pad_rows, stride=RATE), :] = sent[:, c * 128 : (c + 1) * 128]
    for c in range(width // 128):
        own = slice(c * 128, (c + 1) * 128)
        rows[:, own] = total[:, own] + spread[c, :seg_len, :]
    hand_out(head, rows, keep_ref, sent_ref)


def g_normed_parts(head, grad_query, grad_pair, grad_packed, weights, quarter):
    seg_count, seg_len, head_cols = grad_query.shape
    width = weights.shape[1]
    pad_rows = grad_packed.shape[1]
    return pl.pallas_call(
        g_normed_kernel,
        grid=(seg_count,),
        in_specs=[
            pl.BlockSpec(memory_space=pltpu.SMEM),
            by_segment((seg_len, head_cols)),
            by_segment((seg_len, 2 * head_cols)),
            by_segment((pad_rows, head_cols)),
            fixed(weights.shape),
        ],
        out_specs=piece_specs(quarter, width),
        out_shape=piece_shapes(seg_count, quarter, width),
        scratch_shapes=[
            pltpu.VMEM((width // 128, RATE * pad_rows, 128), jnp.float32),
            pltpu.VMEM((seg_len, width), jnp.float32),
        ],
        compiler_params=pltpu.CompilerParams(vmem_limit_bytes=VMEM_LIMIT),
        cost_estimate=pl.CostEstimate(flops=7 * 10**9, bytes_accessed=20 * 10**6, transcendentals=0),
        name="g_normed",
    )(head, grad_query, grad_pair, grad_packed, weights)


def head_swap(value, bit):
    count = lax.axis_size("head")
    return lax.ppermute(value, "head", [(source, source ^ bit) for source in range(count)])


def to_all_heads(value):
    far = head_swap(value, 2)
    return value, head_swap(value, 1), far, head_swap(far, 1)


def sum_over_heads(keep, sent):
    got = head_swap(sent, 1).astype(jnp.float32)
    far = (keep[1].astype(jnp.float32) + got[1]).astype(jnp.bfloat16)
    return keep[0].astype(jnp.float32) + got[0] + head_swap(far, 2).astype(jnp.float32)


def per_device(tokens, wq, wk, wv, wo, w_up, w_down, gain_one, gain_two, w_comp, lengths, grad_out):
    seg_count, quarter, width = tokens.shape
    head_groups = lax.axis_size("head")
    blk_count = lax.axis_size("blk")
    seg_len = quarter * head_groups
    head_cols = width // head_groups
    local_heads = head_cols // HD
    comp_rows = seg_len // RATE
    pad_rows = (comp_rows + 15) // 16 * 16
    window = CSEGS + 1
    head_index = lax.axis_index("head")
    blk_index = lax.axis_index("blk")
    token_count = seg_count * quarter
    full_count = seg_count * seg_len
    comp_count = seg_count * pad_rows
    part = wq.shape[0]
    ff_part = w_down.shape[0]
    bf16 = jnp.bfloat16
    head = head_index[None].astype(jnp.int32)

    columns = (
        jnp.concatenate([wk, wv, wq, w_comp.reshape(RATE * part, width)], 0)
        .reshape(6 * part, head_groups, head_cols)
        .transpose(1, 0, 2)
    )
    gains = jnp.pad(
        jnp.concatenate([gain_one, gain_two])[None], ((0, 15), (0, head_cols - 2 * part))
    )
    columns = jnp.concatenate(
        [columns, jnp.broadcast_to(gains, (head_groups, 16, head_cols))], 1
    )
    columns = lax.all_to_all(columns, "head", split_axis=0, concat_axis=0, tiled=True)
    columns, tokens_held = lax.optimization_barrier((columns, tokens))
    first_all = lax.all_gather(columns, "blk", axis=0)
    second_all = lax.all_gather(
        jnp.concatenate([w_up.T, w_down, *to_all_heads(wo)], 0), "blk", axis=0
    )
    token_pieces = to_all_heads(tokens_held)
    grad_held, tokens_far = lax.optimization_barrier((grad_out, token_pieces[2]))
    token_pieces = token_pieces[:2] + (tokens_far,) + token_pieces[3:]
    grad_far = head_swap(grad_held, 2)
    gain_pair = first_all[:, :, 6 * part, : 2 * part].reshape(
        blk_count, head_groups, 2, part
    ).transpose(2, 1, 0, 3).reshape(2, 1, width).astype(jnp.float32)
    gain_first, gain_second = gain_pair[0], gain_pair[1]
    weights = (
        first_all[:, :, : 6 * part]
        .reshape(blk_count, head_groups, 6, part, head_cols)
        .transpose(2, 1, 0, 3, 4)
        .reshape(6, width, head_cols)
    )
    wkv = jnp.concatenate([weights[0], weights[1]], 1)
    wo_held, wo_specs = wo_blocks(second_all, part, ff_part, head_groups)

    heads, normed, grouped, packed_mine = prepare(
        head, token_pieces, gain_first, weights, pad_rows
    )
    compressed = packed_mine[:, :comp_rows]
    pair = 2 * head_cols
    tail_rows = packed_mine[seg_count - window :].reshape(window * pad_rows, head_cols)
    half_rows = window * pad_rows // 2
    onward = jnp.concatenate(
        [
            heads[seg_count - 1, :, :pair],
            jnp.concatenate([tail_rows[:half_rows], tail_rows[half_rows:]], 1),
        ],
        0,
    )
    recv = passed_along(onward, "blk", 1)
    def all_columns(value):
        value = value.reshape(-1, head_cols)
        whole = jnp.zeros((value.shape[0], width), bf16)
        for bits, piece in enumerate(to_all_heads(value)):
            start = jnp.bitwise_xor(head_index, bits) * head_cols
            whole = lax.dynamic_update_slice(whole, piece, (0, start))
        return whole

    def comp_pairs(rows):
        return (
            jnp.dot(rows, wkv, preferred_element_type=jnp.float32)
            .astype(bf16)
            .reshape(-1, pad_rows, 2 * head_cols)
        )

    grad_far, grad_held, packed_mine = lax.optimization_barrier((grad_far, grad_held, packed_mine))
    grad_pieces = (grad_held, head_swap(grad_held, 1), grad_far, head_swap(grad_far, 1))
    packed = all_columns(packed_mine)
    comp_pair = comp_pairs(packed)
    comp_pair, grad_pieces = lax.optimization_barrier((comp_pair, grad_pieces))
    order = jnp.arange(lengths.shape[0], dtype=jnp.int32)
    starts = jnp.sum(jnp.where(order[None, :] < order[:, None], lengths[None, :], 0), axis=1)
    seg_ids = blk_index * seg_count + jnp.arange(seg_count, dtype=jnp.int32)
    seg_place = seg_ids - jnp.max(
        jnp.where(starts[None, :] <= seg_ids[:, None], starts[None, :], 0), axis=1
    )
    head_ids = head_index * local_heads + jnp.arange(local_heads, dtype=jnp.int32)
    slopes = jnp.exp2(-head_ids.astype(jnp.float32)) / 64.0 * LOG2E
    late = attend_fwd(
        window, window, seg_count - window, seg_place, slopes, heads, heads[:1, :, : 2 * head_cols],
        comp_pair, head_cols,
    )
    recv, late = lax.optimization_barrier((recv, late))
    recv_mem = recv[None, :seg_len]
    recv_packed = jnp.concatenate([recv[seg_len:, :head_cols], recv[seg_len:, head_cols:]], 0)
    comp_ext = jnp.concatenate([comp_pairs(all_columns(recv_packed)), comp_pair], 0)
    middle_seg = window // 2

    def early(a, b, comp_ext):
        return attend_fwd(a, 0, b - a, seg_place, slopes, heads, recv_mem, comp_ext, head_cols)

    first = early(0, middle_seg, comp_ext)
    late_far = head_swap(late[0], 2)
    late_far, first, comp_ext = lax.optimization_barrier((late_far, first, comp_ext))
    attention = [first, early(middle_seg, window, comp_ext), late]
    attn_out = jnp.concatenate([out for out, _ in attention], 0)
    lse = jnp.concatenate([total for _, total in attention], 0)
    far = jnp.concatenate([head_swap(out, 2) for out, _ in attention[:2]] + [late_far], 0)
    attended = (attn_out, head_swap(attn_out, 1), far, head_swap(far, 1))
    f_keep, f_sent, n_keep, n_sent, hidden, first_grads = feed_forward(
        head, attended, wo_held, wo_specs, token_pieces, grad_pieces, gain_second, second_all, ff_part
    )
    first_sum = lax.psum_scatter(first_grads, "blk", scatter_dimension=0)
    got = head_swap(n_sent, 1)
    far = (n_keep[1].astype(jnp.float32) + got[1].astype(jnp.float32)).astype(bf16)
    grad_hidden, grad_branch, grad_gain_two, *mixed = middle(
        n_keep, got, head_swap(far, 2), hidden, grad_out, gain_second, wo_held, wo_specs, head_cols
    )
    grad_gain_two = grad_gain_two[0]
    mixed = mixed[:1] + [head_swap(mixed[bits], bits) for bits in (1, 2, 3)]
    grad_wo = [
        lax.dot_general(
            lax.dynamic_slice_in_dim(block, head_index * quarter, quarter, 1).reshape(
                token_count, head_cols
            ),
            grad_branch.reshape(token_count, width),
            ROWS_IN,
            preferred_element_type=jnp.float32,
        ).astype(bf16)
        for block in attended
    ]
    f_got = head_swap(f_sent, 1)
    f_far = (f_keep[1].astype(jnp.float32) + f_got[1].astype(jnp.float32)).astype(bf16)
    wo_sent = jnp.stack([grad_wo[1], grad_wo[3]])
    wo_got = head_swap(wo_sent, 1).astype(jnp.float32)
    wo_far = (grad_wo[2].astype(jnp.float32) + wo_got[1]).astype(bf16)
    f_far, wo_far, mixed = lax.optimization_barrier((f_far, wo_far, mixed))
    wo_far = head_swap(wo_far, 2).astype(jnp.float32)

    none = jnp.zeros((16, 2 * head_cols), jnp.float32)
    grad_query, pair_done, held, rest, back = attend_bwd(
        0, seg_count, head, seg_place, slopes, heads, recv_mem, comp_ext, mixed, attn_out, lse, none,
        none, head_cols,
    )
    back, f_far = lax.optimization_barrier((back, f_far))
    got_back = passed_along(back[: window * pad_rows], "blk", -1)
    mem_back, got_back = lax.optimization_barrier((back[window * pad_rows :], got_back))
    got_mem = passed_along(mem_back, "blk", -1)
    f_far = head_swap(f_far, 2)
    grad_hidden = grad_hidden.reshape(token_count, width)
    normed = normed.reshape(full_count, width)
    grad_wq = lax.dot_general(
        normed, grad_query.reshape(full_count, head_cols), ROWS_IN, preferred_element_type=jnp.float32
    )
    grad_wo = (grad_wo[0].astype(jnp.float32) + wo_got[0] + wo_far).astype(bf16)

    def by_owner(value):
        return value.astype(bf16).reshape(
            head_groups, blk_count, part, value.shape[1]
        ).transpose(1, 0, 2, 3)

    wq_rows = by_owner(grad_wq)
    wo_rows = grad_wo.reshape(blk_count, part, head_groups, head_cols).transpose(0, 2, 1, 3)
    wq_rows, wo_rows, got_back, first_sum = lax.optimization_barrier(
        (wq_rows, wo_rows, got_back, first_sum)
    )
    got_back = got_back.astype(jnp.float32)
    got_comp = got_back.reshape(window, pad_rows, 2 * head_cols)
    comp_pair_grad = jnp.pad(rest, ((0, seg_count - rest.shape[0]), (0, 0), (0, 0))) + jnp.pad(
        got_comp, ((seg_count - window, 0), (0, 0), (0, 0))
    )
    comp_grad_rows = comp_pair_grad.reshape(comp_count, 2 * head_cols).astype(bf16)
    grad_packed_part = lax.dot_general(
        comp_grad_rows, wkv, COLS_IN, preferred_element_type=jnp.float32
    ).astype(bf16)

    def columns_of(bits):
        start = jnp.bitwise_xor(head_index, bits) * head_cols
        return lax.dynamic_slice_in_dim(grad_packed_part, start, head_cols, 1)

    packed_got = head_swap(jnp.stack([columns_of(1), columns_of(3)]), 1).astype(jnp.float32)
    packed_far = (columns_of(2).astype(jnp.float32) + packed_got[1]).astype(bf16)
    got_mem, _ = lax.optimization_barrier((got_mem, packed_far))
    last_pair = (held + got_mem.astype(jnp.float32)).astype(bf16)
    grad_pair = jnp.concatenate([pair_done, last_pair[None]], 0)
    grad_packed = (
        columns_of(0).astype(jnp.float32)
        + packed_got[0]
        + head_swap(packed_far, 2).astype(jnp.float32)
    ).astype(bf16)
    grad_packed, f_far = lax.optimization_barrier((grad_packed, f_far))
    out_tokens = (
        hidden + f_keep[0].astype(jnp.float32) + f_got[0].astype(jnp.float32) + f_far.astype(jnp.float32)
    ).astype(bf16)
    keep, sent = g_normed_parts(
        head,
        grad_query,
        grad_pair,
        grad_packed.reshape(seg_count, pad_rows, head_cols),
        weights,
        quarter,
    )
    grad_normed = sum_over_heads(keep, sent).reshape(token_count, width)
    unit_one, spread_one = row_norm(tokens.reshape(token_count, width).astype(jnp.float32))
    grad_tokens = (
        (grad_hidden + norm_back(grad_normed, unit_one, spread_one, gain_first))
        .astype(bf16)
        .reshape(tokens.shape)
    )
    grad_kv = grad_pair.reshape(full_count, 2 * head_cols)
    grad_wkv = lax.dot_general(normed, grad_kv, ROWS_IN, preferred_element_type=jnp.float32)
    comp_term = lax.dot_general(packed, comp_grad_rows, ROWS_IN, preferred_element_type=jnp.float32)
    grad_comp = lax.dot_general(
        grouped.reshape(comp_count, RATE * width),
        grad_packed,
        ROWS_IN,
        preferred_element_type=jnp.float32,
    ).reshape(RATE, width, head_cols)
    grad_gain_one = (
        jnp.sum(grad_wq * weights[2].astype(jnp.float32), axis=1)
        + jnp.sum(grad_wkv * wkv.astype(jnp.float32), axis=1)
        + jnp.sum(grad_comp * weights[3:].astype(jnp.float32), axis=(0, 2))
    ) / gain_first[0]
    grad_wkv = grad_wkv + comp_term

    gain_rows = (
        jnp.stack([grad_gain_one, grad_gain_two])
        .reshape(2, head_groups, blk_count, part)
        .transpose(2, 1, 0, 3)
        .astype(bf16)
    )
    second_grads = jnp.concatenate(
        [
            wq_rows,
            by_owner(grad_wkv[:, :head_cols]),
            by_owner(grad_wkv[:, head_cols:]),
            by_owner(grad_comp[0]),
            by_owner(grad_comp[1]),
            by_owner(grad_comp[2]),
            jnp.pad(gain_rows, ((0, 0), (0, 0), (0, 14), (0, head_cols - part))),
            wo_rows,
        ],
        2,
    )
    first_sum = first_sum.astype(jnp.float32)
    own_rows = 6 * part + 16
    second_part = lax.psum_scatter(
        second_grads.reshape(-1, head_cols), "blk", scatter_dimension=0, tiled=True
    ).reshape(head_groups, own_rows + part, head_cols)
    second_sum = lax.all_to_all(
        second_part[:, :own_rows], "head", split_axis=0, concat_axis=0, tiled=True
    ).astype(jnp.float32)
    gain_sum = jnp.sum(second_sum[:, 6 * part : 6 * part + 2, :part], axis=0)
    weight_sum = (
        second_sum[:, : 6 * part]
        .reshape(head_groups, 6, part, head_cols)
        .transpose(1, 2, 0, 3)
        .reshape(6, part, width)
    )
    wo_sum = second_part[:, own_rows:].astype(jnp.float32).transpose(1, 0, 2).reshape(part, width)
    return (
        out_tokens,
        compressed,
        grad_tokens,
        weight_sum[0],
        weight_sum[1],
        weight_sum[2],
        wo_sum,
        first_sum[:ff_part].T,
        first_sum[ff_part:],
        gain_sum[0],
        gain_sum[1],
        weight_sum[3:],
    )


def solution(mesh):
    return jax.shard_map(
        per_device,
        mesh=mesh,
        in_specs=(
            P("blk", "head", None),
            P(("head", "blk"), None),
            P(("head", "blk"), None),
            P(("head", "blk"), None),
            P(("head", "blk"), None),
            P(None, ("head", "blk")),
            P(("head", "blk"), None),
            P(("head", "blk")),
            P(("head", "blk")),
            P(None, ("head", "blk"), None),
            P(),
            P("blk", "head", None),
        ),
        out_specs=(
            P("blk", "head", None),
            P("blk", None, "head"),
            P("blk", "head", None),
            P(("head", "blk"), None),
            P(("head", "blk"), None),
            P(("head", "blk"), None),
            P(("head", "blk"), None),
            P(None, ("head", "blk")),
            P(("head", "blk"), None),
            P(("head", "blk")),
            P(("head", "blk")),
            P(None, ("head", "blk"), None),
        ),
        check_vma=False,
    )
```

```python
import functools

import jax
import jax.numpy as jnp
from jax import lax
from jax.experimental import pallas as pl
from jax.experimental.pallas import tpu as pltpu
from jax.sharding import PartitionSpec as P

HD = 128
RATE = 3
CSEGS = 3


EPS = 1e-05
NEG = -1e30
ROWS_IN = (((0,), (0,)), ((), ()))
COLS_IN = (((1,), (1,)), ((), ()))


def passed_along(value, axis, steps):
    count = lax.axis_size(axis)
    leading, last = (max(0, -steps), min(count, count - steps))
    return lax.ppermute(value, axis, [(source, source + steps) for source in range(leading, last)])


LOG2E = 1.4426950408889634
PAD_ROWS = 176
VMEM_LIMIT = 56 * 1024 * 1024


def key_bias(rows, base, step, valid_rows, open_, slope):
    row = lax.broadcasted_iota(jnp.int32, (rows, 1), 0)
    place = (base + step * row).astype(jnp.float32)
    return jnp.where((row < valid_rows) & open_, place * slope, NEG)


def fwd_kernel(first, shift, place_ref, slope_ref, q_ref, own_ref, prev_ref, recv_ref, comp_ref, out_ref, lse_ref):
    step = pl.program_id(0) + first
    place = place_ref[step]
    seg_len = q_ref.shape[1]
    half = seg_len // 2
    pad_rows = comp_ref.shape[1]
    local_heads = q_ref.shape[2] // HD
    values_at = local_heads * HD
    factor = HD ** (-0.5) * LOG2E
    lower = lax.broadcasted_iota(jnp.int32, (half, half), 0) <= lax.broadcasted_iota(
        jnp.int32, (half, half), 1
    )
    for h in range(local_heads):
        kc = slice(h * HD, (h + 1) * HD)
        vc = slice(values_at + h * HD, values_at + (h + 1) * HD)
        slope = slope_ref[h]
        parts = []
        for piece in range(CSEGS):
            lag = CSEGS + 1 - piece
            bias = key_bias(pad_rows, RATE // 2 - lag * seg_len, RATE, seg_len // RATE, place >= lag, slope)
            at = step + piece - shift
            parts.append((comp_ref[at, :, kc], comp_ref[at, :, vc], bias))
        bias = key_bias(seg_len, -seg_len, 1, seg_len, place >= 1, slope)
        if first:
            parts.append((prev_ref[0, :, kc], prev_ref[0, :, vc], bias))
        else:
            is_first = step == 0
            parts.append(
                (
                    jnp.where(is_first, recv_ref[0, :, kc], prev_ref[0, :, kc]),
                    jnp.where(is_first, recv_ref[0, :, vc], prev_ref[0, :, vc]),
                    bias,
                )
            )
        own_bias = [
            key_bias(half, n * half, 1, half, place >= 0, slope) for n in range(2)
        ]
        for n in range(2):
            query = q_ref[0, n * half : (n + 1) * half, kc]
            group = list(parts)
            for m in range(n + 1):
                rows = slice(m * half, (m + 1) * half)
                group.append((own_ref[0, rows, kc], own_ref[0, rows, vc], own_bias[m]))
            scores = []
            top = None
            for index, (k, v, bias) in enumerate(group):
                raw = lax.dot_general(k, query, COLS_IN, preferred_element_type=jnp.float32)
                raw = raw * factor + bias
                if index == len(group) - 1:
                    raw = jnp.where(lower, raw, NEG)
                scores.append(raw)
                peak = jnp.max(raw, axis=0, keepdims=True)
                top = peak if top is None else jnp.maximum(top, peak)
            total = jnp.zeros_like(top)
            result = jnp.zeros((HD, half), jnp.float32)
            for raw, (k, v, bias) in zip(scores, group):
                weight = jnp.exp2(raw - top)
                total = total + jnp.sum(weight, axis=0, keepdims=True)
                result = result + lax.dot_general(
                    v, weight.astype(jnp.bfloat16), ROWS_IN, preferred_element_type=jnp.float32
                )
            result = result * (1.0 / total)
            out_ref[0, n * half : (n + 1) * half, kc] = result.T.astype(jnp.bfloat16)
            lse_ref[0, h : h + 1, n * half : (n + 1) * half] = top + jnp.log(total) * LOG2E


def bwd_kernel(
    first, place_ref, slope_ref, q_ref, own_ref, prev_ref, recv_ref, comp_ref, head_ref, g0, g1, g2, g3,
    att_ref, lse_ref, held_ref, over_ref, gq_ref, gkv_ref, tail_ref, rest_ref, back_ref, grad_ref, gcomp_ref,
):
    opening = first == 0
    step = pl.program_id(0) + first
    place = place_ref[step]
    seg_len = q_ref.shape[1]
    half = seg_len // 2
    pad_rows = comp_ref.shape[1]
    local_heads = q_ref.shape[2] // HD
    values_at = local_heads * HD
    scale = HD ** (-0.5)
    factor = scale * LOG2E
    is_first = step == 0
    lower = lax.broadcasted_iota(jnp.int32, (half, half), 0) <= lax.broadcasted_iota(
        jnp.int32, (half, half), 1
    )

    at_start = pl.program_id(0) == 0

    @pl.when(at_start)
    def _():
        gcomp_ref[...] = jnp.zeros_like(gcomp_ref)
        if opening:
            tail_ref[...] = jnp.zeros_like(tail_ref)
        else:
            tail_ref[...] = held_ref[...]
            gcomp_ref[: CSEGS - 1] = over_ref[...]

    place_rows(head_ref[0], (g0, g1, g2, g3), grad_ref)
    for h in range(local_heads):
        kc = slice(h * HD, (h + 1) * HD)
        vc = slice(values_at + h * HD, values_at + (h + 1) * HD)
        slope = slope_ref[h]
        query = q_ref[0, :, kc]
        grad = grad_ref[:, kc]
        lse = lse_ref[0, h : h + 1, :]
        product = grad.astype(jnp.float32) * att_ref[0, :, kc].astype(jnp.float32)
        delta = jnp.sum(product.T, axis=0, keepdims=True)

        def part(k, v, bias, cols, masked):
            raw = lax.dot_general(k, query[cols], COLS_IN, preferred_element_type=jnp.float32)
            raw = raw * factor + bias
            if masked:
                raw = jnp.where(lower, raw, NEG)
            prob = jnp.exp2(raw - lse[:, cols])
            grad_prob = lax.dot_general(v, grad[cols], COLS_IN, preferred_element_type=jnp.float32)
            grad_score = (prob * (grad_prob - delta[:, cols])).astype(jnp.bfloat16)
            gk = jnp.dot(grad_score, query[cols], preferred_element_type=jnp.float32) * scale
            gv = jnp.dot(prob.astype(jnp.bfloat16), grad[cols], preferred_element_type=jnp.float32)
            gq = lax.dot_general(k, grad_score, ROWS_IN, preferred_element_type=jnp.float32)
            return gk, gv, gq

        every = slice(0, seg_len)
        total = jnp.zeros((HD, seg_len), jnp.float32)
        for piece in range(CSEGS):
            lag = CSEGS + 1 - piece
            bias = key_bias(pad_rows, RATE // 2 - lag * seg_len, RATE, seg_len // RATE, place >= lag, slope)
            gk, gv, gq = part(comp_ref[step + piece, :, kc], comp_ref[step + piece, :, vc], bias, every, False)
            gcomp_ref[step - first + piece, :, kc] += gk
            gcomp_ref[step - first + piece, :, vc] += gv
            total = total + gq
        for n in range(2):
            rows = slice(n * half, (n + 1) * half)
            bias = key_bias(half, n * half - seg_len, 1, half, place >= 1, slope)
            k, v = prev_ref[0, rows, kc], prev_ref[0, rows, vc]
            if opening:
                k = jnp.where(is_first, recv_ref[0, rows, kc], k)
                v = jnp.where(is_first, recv_ref[0, rows, vc], v)
            gk, gv, gq = part(k, v, bias, every, False)
            gk = (tail_ref[rows, kc] + gk).astype(jnp.bfloat16)
            gv = (tail_ref[rows, vc] + gv).astype(jnp.bfloat16)
            gkv_ref[0, rows, kc] = gk
            gkv_ref[0, rows, vc] = gv
            if opening:
                at = (CSEGS + 1) * pad_rows + n * half
                send = slice(at, at + half)

                @pl.when(is_first)
                def _(gk=gk, gv=gv, send=send):
                    back_ref[send, kc] = gk
                    back_ref[send, vc] = gv

            total = total + gq
        lo, hi = slice(0, half), slice(half, seg_len)
        bias_lo = key_bias(half, 0, 1, half, place >= 0, slope)
        bias_hi = key_bias(half, half, 1, half, place >= 0, slope)
        gk0, gv0, gq0 = part(own_ref[0, lo, kc], own_ref[0, lo, vc], bias_lo, lo, True)
        gk1, gv1, gq1 = part(own_ref[0, lo, kc], own_ref[0, lo, vc], bias_lo, hi, False)
        gk2, gv2, gq2 = part(own_ref[0, hi, kc], own_ref[0, hi, vc], bias_hi, hi, True)
        tail_ref[lo, kc] = gk0 + gk1
        tail_ref[lo, vc] = gv0 + gv1
        tail_ref[hi, kc] = gk2
        tail_ref[hi, vc] = gv2
        gq_ref[0, lo, kc] = ((total[:, lo] + gq0) * scale).T.astype(jnp.bfloat16)
        gq_ref[0, hi, kc] = ((total[:, hi] + gq1 + gq2) * scale).T.astype(jnp.bfloat16)

    @pl.when(pl.program_id(0) == pl.num_programs(0) - 1)
    def _():
        if opening:
            for entry in range(CSEGS + 1):
                rows = slice(entry * pad_rows, (entry + 1) * pad_rows)
                back_ref[rows, :] = gcomp_ref[entry].astype(jnp.bfloat16)
            rest_ref[...] = gcomp_ref[CSEGS + 1 :]
        else:
            rest_ref[...] = gcomp_ref[...]
            back_ref[...] = jnp.zeros_like(back_ref)


def attention_specs(first, seg_len, head_cols, comp_shape):
    pair = 2 * head_cols
    return [
        pl.BlockSpec(memory_space=pltpu.SMEM),
        pl.BlockSpec(memory_space=pltpu.SMEM),
        pl.BlockSpec((1, seg_len, head_cols), lambda s: (s + first, 0, 2)),
        pl.BlockSpec((1, seg_len, pair), lambda s: (s + first, 0, 0)),
        pl.BlockSpec((1, seg_len, pair), lambda s: (jnp.maximum(s + first - 1, 0), 0, 0)),
        fixed((1, seg_len, pair)),
        fixed(comp_shape),
    ]


def attend_fwd(first, shift, count, place, slope, heads, recv_mem, comp_ext, head_cols):
    seg_len = heads.shape[1]
    local_heads = head_cols // HD
    return pl.pallas_call(
        functools.partial(fwd_kernel, first, shift),
        grid=(count,),
        in_specs=attention_specs(first, seg_len, head_cols, comp_ext.shape),
        out_specs=[by_segment((seg_len, head_cols)), by_segment((local_heads, seg_len))],
        out_shape=[
            jax.ShapeDtypeStruct((count, seg_len, head_cols), jnp.bfloat16),
            jax.ShapeDtypeStruct((count, local_heads, seg_len), jnp.float32),
        ],
        compiler_params=pltpu.CompilerParams(vmem_limit_bytes=VMEM_LIMIT),
        cost_estimate=pl.CostEstimate(
            flops=count * 10**9, bytes_accessed=count * 3 * 10**6, transcendentals=count * 16 * 10**5
        ),
        name="attend_fwd",
    )(place, slope, heads, heads, heads, recv_mem, comp_ext)


def attend_bwd(
    first, count, head, place, slope, heads, recv_mem, comp_ext, grad_mixed, attn_out, lse, held, over, head_cols
):
    seg_len = attn_out.shape[1]
    local_heads = head_cols // HD
    pair = 2 * head_cols
    pad_rows = comp_ext.shape[1]
    entries = count + CSEGS - 1
    opening = first == 0
    done = count - 1 if opening else count
    rest = entries - CSEGS - 1 if opening else entries
    back = ((CSEGS + 1) * pad_rows + seg_len, pair) if opening else (16, pair)

    def pair_block(s):
        return (jnp.maximum(s - 1, 0) if opening else s, 0, 0)

    def stays(shape):
        return pl.BlockSpec(shape, lambda s: (0,) * len(shape))

    return pl.pallas_call(
        functools.partial(bwd_kernel, first),
        grid=(count,),
        in_specs=attention_specs(first, seg_len, head_cols, comp_ext.shape)
        + [pl.BlockSpec(memory_space=pltpu.SMEM)]
        + [by_segment(grad_mixed[0].shape[1:], first)] * 4
        + [
            by_segment((seg_len, head_cols), first),
            by_segment((local_heads, seg_len), first),
            fixed(held.shape),
            fixed(over.shape),
        ],
        out_specs=[
            by_segment((seg_len, head_cols)),
            pl.BlockSpec((1, seg_len, pair), pair_block),
            stays((seg_len, pair)),
            stays((rest, pad_rows, pair)),
            stays(back),
        ],
        out_shape=[
            jax.ShapeDtypeStruct((count, seg_len, head_cols), jnp.bfloat16),
            jax.ShapeDtypeStruct((done, seg_len, pair), jnp.bfloat16),
            jax.ShapeDtypeStruct((seg_len, pair), jnp.float32),
            jax.ShapeDtypeStruct((rest, pad_rows, pair), jnp.float32),
            jax.ShapeDtypeStruct(back, jnp.bfloat16),
        ],
        scratch_shapes=[
            pltpu.VMEM((seg_len, head_cols), jnp.bfloat16),
            pltpu.VMEM((entries, pad_rows, pair), jnp.float32),
        ],
        compiler_params=pltpu.CompilerParams(vmem_limit_bytes=VMEM_LIMIT),
        cost_estimate=pl.CostEstimate(
            flops=count * 2 * 10**9, bytes_accessed=count * 4 * 10**6, transcendentals=count * 16 * 10**5
        ),
        name="attend_bwd",
    )(place, slope, heads, heads, heads, recv_mem, comp_ext, head, *grad_mixed, attn_out, lse, held, over)


def row_norm(values):
    average = jnp.mean(values, axis=-1, keepdims=True)
    center = values - average
    spread = lax.rsqrt(jnp.mean(center * center, axis=-1, keepdims=True) + EPS)
    return center * spread, spread


def norm_back(grad, unit, spread, gain):
    scaled = grad * gain
    along = jnp.mean(scaled * unit, axis=-1, keepdims=True)
    return spread * (scaled - jnp.mean(scaled, axis=-1, keepdims=True) - unit * along)


def place_rows(head, pieces, target):
    for bits, piece in enumerate(pieces):
        rows = piece.shape[1]
        at = pl.multiple_of(jnp.bitwise_xor(head, bits) * rows, rows)
        target[pl.ds(at, rows), :] = piece[0].astype(target.dtype)


def hand_out(head, source, keep_ref, sent_ref):
    rows = keep_ref.shape[2]
    for bits, (ref, slot) in enumerate(
        ((keep_ref, 0), (sent_ref, 0), (keep_ref, 1), (sent_ref, 1))
    ):
        at = pl.multiple_of(jnp.bitwise_xor(head, bits) * rows, rows)
        ref[slot, 0] = source[pl.ds(at, rows), :].astype(ref.dtype)


def prep_kernel(
    head_ref, t0, t1, t2, t3, gain_ref, w_ref, heads_ref, normed_ref, grouped_ref, packed_ref, spread
):
    head = head_ref[0]
    quarter, width = t0.shape[1:]
    seg_len = heads_ref.shape[1]
    head_cols = w_ref.shape[2]
    pad_rows = grouped_ref.shape[1]
    tiles = width // 128
    for bits, piece in enumerate((t0, t1, t2, t3)):
        unit, _ = row_norm(piece[0].astype(jnp.float32))
        normed = (unit * gain_ref[...]).astype(jnp.bfloat16)
        at = pl.multiple_of(jnp.bitwise_xor(head, bits) * quarter, quarter)
        normed_ref[0, pl.ds(at, quarter), :] = normed
        wide = normed.astype(jnp.float32)
        for c in range(tiles):
            spread[c, pl.ds(at, quarter), :] = wide[:, c * 128 : (c + 1) * 128]
    last = spread[:, seg_len - 8 : seg_len, :]
    row = lax.broadcasted_iota(jnp.int32, last.shape, 1)
    spread[:, seg_len - 8 : seg_len, :] = jnp.where(row < 8 - seg_len % RATE, last, 0.0)
    spread[:, seg_len:, :] = jnp.zeros((tiles, spread.shape[1] - seg_len, 128), jnp.float32)
    rows = normed_ref[0]
    for n in range(3):
        heads_ref[0, :, n * head_cols : (n + 1) * head_cols] = jnp.dot(
            rows, w_ref[n], preferred_element_type=jnp.float32
        ).astype(jnp.bfloat16)
    total = jnp.zeros((pad_rows, head_cols), jnp.float32)
    for tap in range(RATE):
        for c in range(tiles):
            at = tap * width + c * 128
            grouped_ref[0, :, at : at + 128] = spread[
                c, pl.ds(tap, pad_rows, stride=RATE), :
            ].astype(jnp.bfloat16)
        total = total + jnp.dot(
            grouped_ref[0, :, tap * width : (tap + 1) * width],
            w_ref[3 + tap],
            preferred_element_type=jnp.float32,
        )
    packed_ref[0] = total.astype(jnp.bfloat16)


def fixed(shape):
    return pl.BlockSpec(shape, lambda s: (0,) * len(shape), pipeline_mode=pl.Buffered(1))


def by_segment(shape, first=0):
    return pl.BlockSpec((1,) + shape, lambda s: (s + first,) + (0,) * len(shape))


def piece_specs(quarter, width):
    spec = pl.BlockSpec((2, 1, quarter, width), lambda s: (0, s, 0, 0))
    return [spec, spec]


def piece_shapes(seg_count, quarter, width):
    shape = jax.ShapeDtypeStruct((2, seg_count, quarter, width), jnp.bfloat16)
    return [shape, shape]


def prepare(head, tokens, gain, weights, pad_rows):
    seg_count, quarter, width = tokens[0].shape
    seg_len = quarter * len(tokens)
    head_cols = weights.shape[2]
    bf16 = jnp.bfloat16
    return pl.pallas_call(
        prep_kernel,
        grid=(seg_count,),
        in_specs=[pl.BlockSpec(memory_space=pltpu.SMEM)]
        + [by_segment((quarter, width))] * 4
        + [fixed((1, width)), fixed(weights.shape)],
        out_specs=[
            by_segment((seg_len, 3 * head_cols)),
            by_segment((seg_len, width)),
            by_segment((pad_rows, RATE * width)),
            by_segment((pad_rows, head_cols)),
        ],
        out_shape=[
            jax.ShapeDtypeStruct((seg_count, seg_len, 3 * head_cols), bf16),
            jax.ShapeDtypeStruct((seg_count, seg_len, width), bf16),
            jax.ShapeDtypeStruct((seg_count, pad_rows, RATE * width), bf16),
            jax.ShapeDtypeStruct((seg_count, pad_rows, head_cols), bf16),
        ],
        scratch_shapes=[pltpu.VMEM((width // 128, RATE * pad_rows, 128), jnp.float32)],
        compiler_params=pltpu.CompilerParams(vmem_limit_bytes=VMEM_LIMIT),
        cost_estimate=pl.CostEstimate(flops=7 * 10**9, bytes_accessed=30 * 10**6, transcendentals=3072),
        name="prepare",
    )(head, *tokens, gain, weights)


def ffn_kernel(
    head_ref, a0, a1, a2, a3, o0, o1, o2, o3, t0, t1, t2, t3, g0, g1, g2, g3, gain_ref,
    up_ref, down_ref, f_keep, f_sent, n_keep, n_sent, hidden_ref, pack_ref,
    acc_up, acc_down,
):
    step = pl.program_id(0)
    head = head_ref[0]
    quarter, width = t0.shape[1:]
    ff_part = up_ref.shape[1]
    parts = up_ref.shape[0] // 2
    block = parts * ff_part

    @pl.when(step == 0)
    def _():
        acc_up[...] = jnp.zeros_like(acc_up)
        acc_down[...] = jnp.zeros_like(acc_down)

    starts = [
        pl.multiple_of(jnp.bitwise_xor(head, bits) * quarter, quarter) for bits in range(4)
    ]
    hidden = jnp.concatenate([t[0] for t in (t0, t1, t2, t3)], 0).astype(jnp.float32)
    for a, o in ((a0, o0), (a1, o1), (a2, o2), (a3, o3)):
        part = jnp.concatenate([a[0, pl.ds(at, quarter), :] for at in starts], 0)
        hidden = hidden + jnp.dot(
            part, o[...].reshape(a.shape[2], width), preferred_element_type=jnp.float32
        )
    hidden_ref[0] = hidden[:quarter]
    unit, _ = row_norm(hidden)
    normed = (unit * gain_ref[...]).astype(jnp.bfloat16)
    grad = jnp.concatenate([g[0] for g in (g0, g1, g2, g3)], 0)
    result = jnp.zeros(hidden.shape, jnp.float32)
    g_normed = jnp.zeros(hidden.shape, jnp.float32)
    for n in range(2):
        own = slice(n * parts, (n + 1) * parts)
        up = up_ref[own].reshape(block, width)
        down = down_ref[own].reshape(block, width)
        lifted = lax.dot_general(normed, up, COLS_IN, preferred_element_type=jnp.float32)
        sig = 0.5 * jnp.tanh(0.5 * lifted) + 0.5
        smooth = lifted * sig
        active = smooth.astype(jnp.bfloat16)
        g_active = lax.dot_general(grad, down, COLS_IN, preferred_element_type=jnp.float32)
        g_lifted = (g_active * (sig + smooth * (1.0 - sig))).astype(jnp.bfloat16)
        result = result + jnp.dot(active, down, preferred_element_type=jnp.float32)
        g_normed = g_normed + jnp.dot(g_lifted, up, preferred_element_type=jnp.float32)
        acc_down[n] += lax.dot_general(active, grad, ROWS_IN, preferred_element_type=jnp.float32)
        acc_up[n] += lax.dot_general(g_lifted, normed, ROWS_IN, preferred_element_type=jnp.float32)
    for value, keep, sent in ((g_normed, n_keep, n_sent), (result, f_keep, f_sent)):
        value = value.astype(jnp.bfloat16)
        for bits, (ref, slot) in enumerate(((keep, 0), (sent, 0), (keep, 1), (sent, 1))):
            ref[slot, 0] = value[bits * quarter : (bits + 1) * quarter]

    @pl.when(step == pl.num_programs(0) - 1)
    def _():
        for n in range(2):
            own = slice(n * parts, (n + 1) * parts)
            shape = (parts, ff_part, width)
            pack_ref[own, :ff_part] = acc_up[n].astype(jnp.bfloat16).reshape(shape)
            pack_ref[own, ff_part:] = acc_down[n].astype(jnp.bfloat16).reshape(shape)


def wo_blocks(pack, part, ff_part, head_groups):
    blks, _, width = pack.shape
    start = 2 * ff_part
    if part % 16 == 0:
        specs = [
            pl.BlockSpec(
                (blks, part, width),
                functools.partial(lambda index, s: (0, index, 0), start // part + n),
                pipeline_mode=pl.Buffered(1),
            )
            for n in range(head_groups)
        ]
        return [pack] * head_groups, specs
    blocks = [
        pack[:, start + n * part : start + (n + 1) * part].reshape(blks * part, width)
        for n in range(head_groups)
    ]
    return blocks, [fixed((blks * part, width))] * head_groups


def feed_forward(head, attended, wo, wo_specs, tokens, grads, gain, pack, ff_part):
    quarter, width = tokens[0].shape[1:]
    count, seg_len, head_cols = attended[0].shape
    blks = pack.shape[0]
    half = blks // 2 * ff_part
    grad_shape = (blks, 2 * ff_part, width)
    pieces = piece_specs(quarter, width)
    shapes = piece_shapes(count, quarter, width)

    def weight(index):
        return pl.BlockSpec(
            (blks, ff_part, width), lambda s: (0, index, 0), pipeline_mode=pl.Buffered(1)
        )

    return pl.pallas_call(
        ffn_kernel,
        grid=(count,),
        in_specs=[pl.BlockSpec(memory_space=pltpu.SMEM)]
        + [by_segment((seg_len, head_cols))] * 4
        + wo_specs
        + [by_segment((quarter, width))] * 8
        + [fixed((1, width)), weight(0), weight(1)],
        out_specs=pieces + pieces
        + [by_segment((quarter, width)), pl.BlockSpec(grad_shape, lambda s: (0, 0, 0))],
        out_shape=shapes + shapes
        + [
            jax.ShapeDtypeStruct((count, quarter, width), jnp.float32),
            jax.ShapeDtypeStruct(grad_shape, jnp.bfloat16),
        ],
        scratch_shapes=[
            pltpu.VMEM((2, half, width), jnp.float32),
            pltpu.VMEM((2, half, width), jnp.float32),
        ],
        compiler_params=pltpu.CompilerParams(vmem_limit_bytes=VMEM_LIMIT),
        cost_estimate=pl.CostEstimate(
            flops=count * 75 * 10**8, bytes_accessed=2 * 10**7 + count * 5 * 10**6, transcendentals=10**6
        ),
        name="feed_forward",
    )(head, *attended, *wo, *tokens, *grads, gain, pack, pack)


def middle_kernel(
    keep_ref, got_ref, far_ref, hidden_ref, grad_ref, gain_ref, o0, o1, o2, o3,
    g_hidden_ref, g_branch_ref, g_gain_ref, m0, m1, m2, m3,
):
    count, quarter, width = hidden_ref.shape
    flat = (count * quarter, width)
    gn = (
        keep_ref[0].astype(jnp.float32)
        + got_ref[0].astype(jnp.float32)
        + far_ref[...].astype(jnp.float32)
    ).reshape(flat)
    unit, spread = row_norm(hidden_ref[...].reshape(flat))
    gain_part = jnp.sum(gn * unit, axis=0, keepdims=True)

    @pl.when(pl.program_id(0) == 0)
    def _():
        g_gain_ref[...] = jnp.zeros_like(g_gain_ref)

    g_gain_ref[...] += gain_part
    g_hidden = grad_ref[...].astype(jnp.float32).reshape(flat) + norm_back(
        gn, unit, spread, gain_ref[...]
    )
    g_hidden_ref[...] = g_hidden.reshape(g_hidden_ref.shape)
    g_branch = g_hidden.astype(jnp.bfloat16)
    g_branch_ref[...] = g_branch.reshape(g_branch_ref.shape)
    for o, m in ((o0, m0), (o1, m1), (o2, m2), (o3, m3)):
        m[...] = (
            lax.dot_general(
                g_branch, o[...].reshape(m.shape[2], width), COLS_IN, preferred_element_type=jnp.float32
            )
            .astype(jnp.bfloat16)
            .reshape(m.shape)
        )


def middle(keep, got, far, hidden, grad, gain, wo, wo_specs, head_cols):
    count, quarter, width = hidden.shape
    size = 2 if count % 2 == 0 else 1
    piece = pl.BlockSpec((1, size, quarter, width), lambda s: (0, s, 0, 0))
    block = pl.BlockSpec((size, quarter, width), lambda s: (s, 0, 0))
    mixed = jax.ShapeDtypeStruct((count, quarter, head_cols), jnp.bfloat16)
    return pl.pallas_call(
        middle_kernel,
        grid=(count // size,),
        in_specs=[piece, piece, block, block, block, fixed((1, width))] + wo_specs,
        out_specs=[block, block, pl.BlockSpec((1, width), lambda s: (0, 0))]
        + [pl.BlockSpec((size, quarter, head_cols), lambda s: (s, 0, 0))] * 4,
        out_shape=[
            jax.ShapeDtypeStruct(hidden.shape, jnp.float32),
            jax.ShapeDtypeStruct(hidden.shape, jnp.bfloat16),
            jax.ShapeDtypeStruct((1, width), jnp.float32),
        ]
        + [mixed] * 4,
        compiler_params=pltpu.CompilerParams(vmem_limit_bytes=VMEM_LIMIT),
        cost_estimate=pl.CostEstimate(flops=count * 27 * 10**7, bytes_accessed=24 * 10**6, transcendentals=0),
        name="middle",
    )(keep, got, far, hidden, grad, gain, *wo)


def g_normed_kernel(head_ref, gq_ref, gkv_ref, gp_ref, w_ref, keep_ref, sent_ref, spread, rows):
    head = head_ref[0]
    seg_len, head_cols = gq_ref.shape[1:]
    pad_rows = gp_ref.shape[1]
    width = w_ref.shape[1]
    total = lax.dot_general(gq_ref[0], w_ref[2], COLS_IN, preferred_element_type=jnp.float32)
    for n in range(2):
        part = gkv_ref[0, :, n * head_cols : (n + 1) * head_cols]
        total = total + lax.dot_general(part, w_ref[n], COLS_IN, preferred_element_type=jnp.float32)
    for tap in range(RATE):
        sent = lax.dot_general(gp_ref[0], w_ref[3 + tap], COLS_IN, preferred_element_type=jnp.float32)
        for c in range(width // 128):
            spread[c, pl.ds(tap, pad_rows, stride=RATE), :] = sent[:, c * 128 : (c + 1) * 128]
    for c in range(width // 128):
        own = slice(c * 128, (c + 1) * 128)
        rows[:, own] = total[:, own] + spread[c, :seg_len, :]
    hand_out(head, rows, keep_ref, sent_ref)


def g_normed_parts(head, grad_query, grad_pair, grad_packed, weights, quarter):
    seg_count, seg_len, head_cols = grad_query.shape
    width = weights.shape[1]
    pad_rows = grad_packed.shape[1]
    return pl.pallas_call(
        g_normed_kernel,
        grid=(seg_count,),
        in_specs=[
            pl.BlockSpec(memory_space=pltpu.SMEM),
            by_segment((seg_len, head_cols)),
            by_segment((seg_len, 2 * head_cols)),
            by_segment((pad_rows, head_cols)),
            fixed(weights.shape),
        ],
        out_specs=piece_specs(quarter, width),
        out_shape=piece_shapes(seg_count, quarter, width),
        scratch_shapes=[
            pltpu.VMEM((width // 128, RATE * pad_rows, 128), jnp.float32),
            pltpu.VMEM((seg_len, width), jnp.float32),
        ],
        compiler_params=pltpu.CompilerParams(vmem_limit_bytes=VMEM_LIMIT),
        cost_estimate=pl.CostEstimate(flops=7 * 10**9, bytes_accessed=20 * 10**6, transcendentals=0),
        name="g_normed",
    )(head, grad_query, grad_pair, grad_packed, weights)


def head_swap(value, bit):
    count = lax.axis_size("head")
    return lax.ppermute(value, "head", [(source, source ^ bit) for source in range(count)])


def to_all_heads(value):
    far = head_swap(value, 2)
    return value, head_swap(value, 1), far, head_swap(far, 1)


def sum_over_heads(keep, sent):
    got = head_swap(sent, 1).astype(jnp.float32)
    far = (keep[1].astype(jnp.float32) + got[1]).astype(jnp.bfloat16)
    return keep[0].astype(jnp.float32) + got[0] + head_swap(far, 2).astype(jnp.float32)


def per_device(tokens, wq, wk, wv, wo, w_up, w_down, gain_one, gain_two, w_comp, lengths, grad_out):
    seg_count, quarter, width = tokens.shape
    head_groups = lax.axis_size("head")
    blk_count = lax.axis_size("blk")
    seg_len = quarter * head_groups
    head_cols = width // head_groups
    local_heads = head_cols // HD
    comp_rows = seg_len // RATE
    pad_rows = (comp_rows + 15) // 16 * 16
    window = CSEGS + 1
    head_index = lax.axis_index("head")
    blk_index = lax.axis_index("blk")
    token_count = seg_count * quarter
    full_count = seg_count * seg_len
    comp_count = seg_count * pad_rows
    part = wq.shape[0]
    ff_part = w_down.shape[0]
    bf16 = jnp.bfloat16
    head = head_index[None].astype(jnp.int32)

    columns = (
        jnp.concatenate([wk, wv, wq, w_comp.reshape(RATE * part, width)], 0)
        .reshape(6 * part, head_groups, head_cols)
        .transpose(1, 0, 2)
    )
    gains = jnp.pad(
        jnp.concatenate([gain_one, gain_two])[None], ((0, 15), (0, head_cols - 2 * part))
    )
    columns = jnp.concatenate(
        [columns, jnp.broadcast_to(gains, (head_groups, 16, head_cols))], 1
    )
    columns = lax.all_to_all(columns, "head", split_axis=0, concat_axis=0, tiled=True)
    columns, tokens_held = lax.optimization_barrier((columns, tokens))
    first_all = lax.all_gather(columns, "blk", axis=0)
    second_all = lax.all_gather(
        jnp.concatenate([w_up.T, w_down, *to_all_heads(wo)], 0), "blk", axis=0
    )
    token_pieces = to_all_heads(tokens_held)
    grad_held, tokens_far = lax.optimization_barrier((grad_out, token_pieces[2]))
    token_pieces = token_pieces[:2] + (tokens_far,) + token_pieces[3:]
    grad_far = head_swap(grad_held, 2)
    gain_pair = first_all[:, :, 6 * part, : 2 * part].reshape(
        blk_count, head_groups, 2, part
    ).transpose(2, 1, 0, 3).reshape(2, 1, width).astype(jnp.float32)
    gain_first, gain_second = gain_pair[0], gain_pair[1]
    weights = (
        first_all[:, :, : 6 * part]
        .reshape(blk_count, head_groups, 6, part, head_cols)
        .transpose(2, 1, 0, 3, 4)
        .reshape(6, width, head_cols)
    )
    wkv = jnp.concatenate([weights[0], weights[1]], 1)
    wo_held, wo_specs = wo_blocks(second_all, part, ff_part, head_groups)

    heads, normed, grouped, packed_mine = prepare(
        head, token_pieces, gain_first, weights, pad_rows
    )
    compressed = packed_mine[:, :comp_rows]
    pair = 2 * head_cols
    tail_rows = packed_mine[seg_count - window :].reshape(window * pad_rows, head_cols)
    half_rows = window * pad_rows // 2
    onward = jnp.concatenate(
        [
            heads[seg_count - 1, :, :pair],
            jnp.concatenate([tail_rows[:half_rows], tail_rows[half_rows:]], 1),
        ],
        0,
    )
    recv = passed_along(onward, "blk", 1)
    def all_columns(value):
        value = value.reshape(-1, head_cols)
        whole = jnp.zeros((value.shape[0], width), bf16)
        for bits, piece in enumerate(to_all_heads(value)):
            start = jnp.bitwise_xor(head_index, bits) * head_cols
            whole = lax.dynamic_update_slice(whole, piece, (0, start))
        return whole

    def comp_pairs(rows):
        return (
            jnp.dot(rows, wkv, preferred_element_type=jnp.float32)
            .astype(bf16)
            .reshape(-1, pad_rows, 2 * head_cols)
        )

    grad_far, grad_held, packed_mine = lax.optimization_barrier((grad_far, grad_held, packed_mine))
    grad_pieces = (grad_held, head_swap(grad_held, 1), grad_far, head_swap(grad_far, 1))
    packed = all_columns(packed_mine)
    comp_pair = comp_pairs(packed)
    comp_pair, grad_pieces = lax.optimization_barrier((comp_pair, grad_pieces))
    order = jnp.arange(lengths.shape[0], dtype=jnp.int32)
    starts = jnp.sum(jnp.where(order[None, :] < order[:, None], lengths[None, :], 0), axis=1)
    seg_ids = blk_index * seg_count + jnp.arange(seg_count, dtype=jnp.int32)
    seg_place = seg_ids - jnp.max(
        jnp.where(starts[None, :] <= seg_ids[:, None], starts[None, :], 0), axis=1
    )
    head_ids = head_index * local_heads + jnp.arange(local_heads, dtype=jnp.int32)
    slopes = jnp.exp2(-head_ids.astype(jnp.float32)) / 64.0 * LOG2E
    late = attend_fwd(
        window, window, seg_count - window, seg_place, slopes, heads, heads[:1, :, : 2 * head_cols],
        comp_pair, head_cols,
    )
    recv, late = lax.optimization_barrier((recv, late))
    recv_mem = recv[None, :seg_len]
    recv_packed = jnp.concatenate([recv[seg_len:, :head_cols], recv[seg_len:, head_cols:]], 0)
    comp_ext = jnp.concatenate([comp_pairs(all_columns(recv_packed)), comp_pair], 0)
    middle_seg = window // 2

    def early(a, b, comp_ext):
        return attend_fwd(a, 0, b - a, seg_place, slopes, heads, recv_mem, comp_ext, head_cols)

    first = early(0, middle_seg, comp_ext)
    late_far = head_swap(late[0], 2)
    late_far, first, comp_ext = lax.optimization_barrier((late_far, first, comp_ext))
    attention = [first, early(middle_seg, window, comp_ext), late]
    attn_out = jnp.concatenate([out for out, _ in attention], 0)
    lse = jnp.concatenate([total for _, total in attention], 0)
    far = jnp.concatenate([head_swap(out, 2) for out, _ in attention[:2]] + [late_far], 0)
    attended = (attn_out, head_swap(attn_out, 1), far, head_swap(far, 1))
    f_keep, f_sent, n_keep, n_sent, hidden, first_grads = feed_forward(
        head, attended, wo_held, wo_specs, token_pieces, grad_pieces, gain_second, second_all, ff_part
    )
    first_sum = lax.psum_scatter(first_grads, "blk", scatter_dimension=0)
    got = head_swap(n_sent, 1)
    far = (n_keep[1].astype(jnp.float32) + got[1].astype(jnp.float32)).astype(bf16)
    grad_hidden, grad_branch, grad_gain_two, *mixed = middle(
        n_keep, got, head_swap(far, 2), hidden, grad_out, gain_second, wo_held, wo_specs, head_cols
    )
    grad_gain_two = grad_gain_two[0]
    mixed = mixed[:1] + [head_swap(mixed[bits], bits) for bits in (1, 2, 3)]
    grad_wo = [
        lax.dot_general(
            lax.dynamic_slice_in_dim(block, head_index * quarter, quarter, 1).reshape(
                token_count, head_cols
            ),
            grad_branch.reshape(token_count, width),
            ROWS_IN,
            preferred_element_type=jnp.float32,
        ).astype(bf16)
        for block in attended
    ]
    f_got = head_swap(f_sent, 1)
    f_far = (f_keep[1].astype(jnp.float32) + f_got[1].astype(jnp.float32)).astype(bf16)
    wo_sent = jnp.stack([grad_wo[1], grad_wo[3]])
    wo_got = head_swap(wo_sent, 1).astype(jnp.float32)
    wo_far = (grad_wo[2].astype(jnp.float32) + wo_got[1]).astype(bf16)
    f_far, wo_far, mixed = lax.optimization_barrier((f_far, wo_far, mixed))
    wo_far = head_swap(wo_far, 2).astype(jnp.float32)

    none = jnp.zeros((16, 2 * head_cols), jnp.float32)
    grad_query, pair_done, held, rest, back = attend_bwd(
        0, seg_count, head, seg_place, slopes, heads, recv_mem, comp_ext, mixed, attn_out, lse, none,
        none, head_cols,
    )
    got_back = passed_along(back[: window * pad_rows], "blk", -1)
    mem_back, got_back = lax.optimization_barrier((back[window * pad_rows :], got_back))
    got_mem = passed_along(mem_back, "blk", -1)
    grad_hidden = grad_hidden.reshape(token_count, width)
    normed = normed.reshape(full_count, width)
    grad_wq = lax.dot_general(
        normed, grad_query.reshape(full_count, head_cols), ROWS_IN, preferred_element_type=jnp.float32
    )
    grad_wo = (grad_wo[0].astype(jnp.float32) + wo_got[0] + wo_far).astype(bf16)

    def by_owner(value):
        return value.astype(bf16).reshape(
            head_groups, blk_count, part, value.shape[1]
        ).transpose(1, 0, 2, 3)

    wq_rows = by_owner(grad_wq)
    wo_rows = grad_wo.reshape(blk_count, part, head_groups, head_cols).transpose(0, 2, 1, 3)
    wq_rows, wo_rows, got_back, first_sum = lax.optimization_barrier(
        (wq_rows, wo_rows, got_back, first_sum)
    )
    got_back = got_back.astype(jnp.float32)
    got_comp = got_back.reshape(window, pad_rows, 2 * head_cols)
    comp_pair_grad = jnp.pad(rest, ((0, seg_count - rest.shape[0]), (0, 0), (0, 0))) + jnp.pad(
        got_comp, ((seg_count - window, 0), (0, 0), (0, 0))
    )
    comp_grad_rows = comp_pair_grad.reshape(comp_count, 2 * head_cols).astype(bf16)
    grad_packed_part = lax.dot_general(
        comp_grad_rows, wkv, COLS_IN, preferred_element_type=jnp.float32
    ).astype(bf16)

    def columns_of(bits):
        start = jnp.bitwise_xor(head_index, bits) * head_cols
        return lax.dynamic_slice_in_dim(grad_packed_part, start, head_cols, 1)

    packed_got = head_swap(jnp.stack([columns_of(1), columns_of(3)]), 1).astype(jnp.float32)
    packed_far = (columns_of(2).astype(jnp.float32) + packed_got[1]).astype(bf16)
    got_mem, _ = lax.optimization_barrier((got_mem, packed_far))
    last_pair = (held + got_mem.astype(jnp.float32)).astype(bf16)
    grad_pair = jnp.concatenate([pair_done, last_pair[None]], 0)
    grad_packed = (
        columns_of(0).astype(jnp.float32)
        + packed_got[0]
        + head_swap(packed_far, 2).astype(jnp.float32)
    ).astype(bf16)
    f_far, grad_packed = lax.optimization_barrier((f_far, grad_packed))
    f_far = head_swap(f_far, 2)
    out_tokens = (
        hidden + f_keep[0].astype(jnp.float32) + f_got[0].astype(jnp.float32) + f_far.astype(jnp.float32)
    ).astype(bf16)
    keep, sent = g_normed_parts(
        head,
        grad_query,
        grad_pair,
        grad_packed.reshape(seg_count, pad_rows, head_cols),
        weights,
        quarter,
    )
    grad_normed = sum_over_heads(keep, sent).reshape(token_count, width)
    unit_one, spread_one = row_norm(tokens.reshape(token_count, width).astype(jnp.float32))
    grad_tokens = (
        (grad_hidden + norm_back(grad_normed, unit_one, spread_one, gain_first))
        .astype(bf16)
        .reshape(tokens.shape)
    )
    grad_kv = grad_pair.reshape(full_count, 2 * head_cols)
    grad_wkv = lax.dot_general(normed, grad_kv, ROWS_IN, preferred_element_type=jnp.float32)
    comp_term = lax.dot_general(packed, comp_grad_rows, ROWS_IN, preferred_element_type=jnp.float32)
    grad_comp = lax.dot_general(
        grouped.reshape(comp_count, RATE * width),
        grad_packed,
        ROWS_IN,
        preferred_element_type=jnp.float32,
    ).reshape(RATE, width, head_cols)
    grad_gain_one = (
        jnp.sum(grad_wq * weights[2].astype(jnp.float32), axis=1)
        + jnp.sum(grad_wkv * wkv.astype(jnp.float32), axis=1)
        + jnp.sum(grad_comp * weights[3:].astype(jnp.float32), axis=(0, 2))
    ) / gain_first[0]
    grad_wkv = grad_wkv + comp_term

    gain_rows = (
        jnp.stack([grad_gain_one, grad_gain_two])
        .reshape(2, head_groups, blk_count, part)
        .transpose(2, 1, 0, 3)
        .astype(bf16)
    )
    second_grads = jnp.concatenate(
        [
            wq_rows,
            by_owner(grad_wkv[:, :head_cols]),
            by_owner(grad_wkv[:, head_cols:]),
            by_owner(grad_comp[0]),
            by_owner(grad_comp[1]),
            by_owner(grad_comp[2]),
            jnp.pad(gain_rows, ((0, 0), (0, 0), (0, 14), (0, head_cols - part))),
            wo_rows,
        ],
        2,
    )
    first_sum = first_sum.astype(jnp.float32)
    own_rows = 6 * part + 16
    second_part = lax.psum_scatter(
        second_grads.reshape(-1, head_cols), "blk", scatter_dimension=0, tiled=True
    ).reshape(head_groups, own_rows + part, head_cols)
    second_sum = lax.all_to_all(
        second_part[:, :own_rows], "head", split_axis=0, concat_axis=0, tiled=True
    ).astype(jnp.float32)
    gain_sum = jnp.sum(second_sum[:, 6 * part : 6 * part + 2, :part], axis=0)
    weight_sum = (
        second_sum[:, : 6 * part]
        .reshape(head_groups, 6, part, head_cols)
        .transpose(1, 2, 0, 3)
        .reshape(6, part, width)
    )
    wo_sum = second_part[:, own_rows:].astype(jnp.float32).transpose(1, 0, 2).reshape(part, width)
    return (
        out_tokens,
        compressed,
        grad_tokens,
        weight_sum[0],
        weight_sum[1],
        weight_sum[2],
        wo_sum,
        first_sum[:ff_part].T,
        first_sum[ff_part:],
        gain_sum[0],
        gain_sum[1],
        weight_sum[3:],
    )


def solution(mesh):
    return jax.shard_map(
        per_device,
        mesh=mesh,
        in_specs=(
            P("blk", "head", None),
            P(("head", "blk"), None),
            P(("head", "blk"), None),
            P(("head", "blk"), None),
            P(("head", "blk"), None),
            P(None, ("head", "blk")),
            P(("head", "blk"), None),
            P(("head", "blk")),
            P(("head", "blk")),
            P(None, ("head", "blk"), None),
            P(),
            P("blk", "head", None),
        ),
        out_specs=(
            P("blk", "head", None),
            P("blk", None, "head"),
            P("blk", "head", None),
            P(("head", "blk"), None),
            P(("head", "blk"), None),
            P(("head", "blk"), None),
            P(("head", "blk"), None),
            P(None, ("head", "blk")),
            P(("head", "blk"), None),
            P(("head", "blk")),
            P(("head", "blk")),
            P(None, ("head", "blk"), None),
        ),
        check_vma=False,
    )
```
